32 devices in a mesh: dp: 2 (over y), row: 4 (over z), col: 4 (over x, core).
Axes of the slice: x: 2, y: 2, z: 4, core: 2. Of those that a mesh axis runs over, the one named last changes fastest.
Arguments:
- resid_in: bfloat16 [8192, 2048], P(('dp', 'col'), 'row')
- cotangent: bfloat16 [8192, 2048], P(('dp', 'col'), 'row'), may hold values from -6 to 6
- seq_lens: int32 [2, 4], P('dp'), may hold values from 256 to 1024, as said below
- qkv_weight: float32 [2048, 3072], P(('row', 'dp'), 'col'), may hold values from -0.125 to 0.125
- qkv_moment: float32 [2048, 3072], P(('row', 'dp'), 'col'), may hold values from -36.20387 to 36.20387
- qkv_square: float32 [2048, 3072], P(('row', 'dp'), 'col'), may hold values from 75.3664 to 1204.224
- out_weight: float32 [2048, 2048], P(('col', 'dp'), 'row'), may hold values from -1 to 1
- out_moment: float32 [2048, 2048], P(('col', 'dp'), 'row'), may hold values from -5.939697 to 5.939697
- out_square: float32 [2048, 2048], P(('col', 'dp'), 'row'), may hold values from 2.16 to 34.4
- gate_weight: float32 [2048, 8192], P(('row', 'dp'), 'col'), may hold values from -0.125 to 0.125
- gate_moment: float32 [2048, 8192], P(('row', 'dp'), 'col'), may hold values from -15.386643 to 15.386643
- gate_square: float32 [2048, 8192], P(('row', 'dp'), 'col'), may hold values from 13.9264 to 221.184
- up_weight: float32 [2048, 8192], P(('row', 'dp'), 'col'), may hold values from -0.125 to 0.125
- up_moment: float32 [2048, 8192], P(('row', 'dp'), 'col'), may hold values from -15.386643 to 15.386643
- up_square: float32 [2048, 8192], P(('row', 'dp'), 'col'), may hold values from 13.9264 to 221.184
- down_weight: float32 [8192, 2048], P(('col', 'dp'), 'row'), may hold values from -0.0625 to 0.0625
- down_moment: float32 [8192, 2048], P(('col', 'dp'), 'row'), may hold values from -29.86819 to 29.86819
- down_square: float32 [8192, 2048], P(('col', 'dp'), 'row'), may hold values from 54.0672 to 860.16
- norm_gains: float32 [2, 2048], P(None, 'row')
- gain_moment: float32 [2, 2048], P(None, 'row'), may hold values from -35.29877 to 35.29877
- gain_square: float32 [2, 2048], P(None, 'row'), may hold values from 73.728 to 1146.88
Outputs:
- resid_out: bfloat16 [8192, 2048], P(('dp', 'col'), 'row')
- resid_grad: float32 [8192, 2048], P(('dp', 'col'), 'row')
- qkv_new: float32 [2048, 3072], P(('row', 'dp'), 'col')
- qkv_moment_new: float32 [2048, 3072], P(('row', 'dp'), 'col')
- qkv_square_new: float32 [2048, 3072], P(('row', 'dp'), 'col')
- out_new: float32 [2048, 2048], P(('col', 'dp'), 'row')
- out_moment_new: float32 [2048, 2048], P(('col', 'dp'), 'row')
- out_square_new: float32 [2048, 2048], P(('col', 'dp'), 'row')
- gate_new: float32 [2048, 8192], P(('row', 'dp'), 'col')
- gate_moment_new: float32 [2048, 8192], P(('row', 'dp'), 'col')
- gate_square_new: float32 [2048, 8192], P(('row', 'dp'), 'col')
- up_new: float32 [2048, 8192], P(('row', 'dp'), 'col')
- up_moment_new: float32 [2048, 8192], P(('row', 'dp'), 'col')
- up_square_new: float32 [2048, 8192], P(('row', 'dp'), 'col')
- down_new: float32 [8192, 2048], P(('col', 'dp'), 'row')
- down_moment_new: float32 [8192, 2048], P(('col', 'dp'), 'row')
- down_square_new: float32 [8192, 2048], P(('col', 'dp'), 'row')
- gains_new: float32 [2, 2048], P(None, 'row')
- gain_moment_new: float32 [2, 2048], P(None, 'row')
- gain_square_new: float32 [2, 2048], P(None, 'row')
The draws below stay inside these ranges and needn't reach their ends.
Inputs may be any that keep to these rules, and one draw needn't show every extreme that they name: `seq_lens`: each replica's 4 lengths sum to at most 4096, and one of them equals 1024.
All inputs are finite; a program needn't handle non-finite values.
Results may differ from the reference program's by a relative error of at most 0.03.
Values may be sent and summed in bfloat16 or wider, within the bound.
A program may use at most 384 MiB of HBM per device.

```python
import math
from functools import partial
import jax
import jax.numpy as jnp
from jax import lax

D = 2048
FF = 8192
H_Q = 32
H_KV = 8
HD = 64
GROUP = 4
Q = 2048
QKV = 3072
LMAX = 1024
LMIN = 256
BLK = 512
SEQS = 4
CAP = 4096
TOKENS = 8192
STEP = 10
N_DP = 2


def draw_resid_in(key, part):
    key = jax.random.fold_in(key, 11)
    first_key = jax.random.fold_in(key, 0)
    ladder = jnp.arange(D, dtype=jnp.float32) / (D - 1)
    base = jax.random.normal(first_key, (TOKENS, D), jnp.float32)
    column = 0.6 + 1.2 * ladder
    return (base * column[None, :]).astype(jnp.bfloat16)


def draw_seq_lens(key, part):
    key = jax.random.fold_in(key, 5)
    first_key, second_key = jax.random.split(key)
    lengths = jax.random.randint(first_key, (N_DP, SEQS), LMIN, LMAX + 1, dtype=jnp.int32)
    longest = jax.random.randint(second_key, (N_DP, 1), 0, SEQS, dtype=jnp.int32)
    places = jnp.arange(SEQS, dtype=jnp.int32)[None, :]
    return jnp.where(places == longest, LMAX, lengths).astype(jnp.int32)


def draw_norm_gains(key, part):
    key = jax.random.fold_in(key, 7)
    ladder = jnp.arange(D, dtype=jnp.float32) / (D - 1)
    noise = jax.random.uniform(key, (2, D), jnp.float32, 0.8, 1.2)
    return (0.6 + 1.2 * ladder)[None, :] * noise


def block_scale(stream_key, extent, shards, smallest, high):
    loudness, own = 1.0, jax.random.fold_in(stream_key, 6)
    for dim, blocks in shards:
        heights = jnp.exp(jax.random.uniform(jax.random.fold_in(own, dim), (blocks,), jnp.float32, smallest / len(shards), high / len(shards)))
        loudness = loudness * jnp.repeat(heights, extent[dim] // blocks).reshape([-1 if axis == dim else 1 for axis in range(len(extent))])
    return loudness


def normal_values(stream_key, extent, deviation, limit, cuts=(), kind=jnp.bfloat16):
    entries = deviation * jax.random.normal(stream_key, extent, jnp.float32)
    if cuts:
        entries = entries * block_scale(stream_key, extent, cuts, -0.22, 0.18)
    return jnp.clip(entries, -limit, limit).astype(kind)


def setup_inputs(seed: int = 0) -> dict:
    seeds = jax.random.split(jax.random.key(seed), 22)
    return {
        "resid_in": draw_resid_in(jax.random.fold_in(seeds[21], 71), 0),
        "cotangent": normal_values(seeds[1], (TOKENS, D), 1.0, 6.0, ((0, 8), (1, 4))),
        "seq_lens": draw_seq_lens(jax.random.fold_in(seeds[21], 71), 0),
        "qkv_weight": normal_values(seeds[3], (D, QKV), D ** -0.5, 0.125, ((0, 8), (1, 4)), jnp.float32),
        "qkv_moment": normal_values(seeds[4], (D, QKV), (0.066 * TOKENS ** 0.5), 36.20387, ((0, 8), (1, 4)), jnp.float32),
        "qkv_square": jnp.clip(jnp.exp(math.log(1204.224) - 2.771229 * jax.random.uniform(seeds[5], (D, QKV), jnp.float32) ** block_scale(seeds[5], (D, QKV), ((0, 8), (1, 4)), -0.2, 0.2)), 75.3664, 1204.224),
        "out_weight": normal_values(seeds[6], (Q, D), (max(Q * 16 // LMAX, 1)) ** -0.5, 1.0, ((0, 8), (1, 4)), jnp.float32),
        "out_moment": normal_values(seeds[7], (Q, D), (0.35 * (TOKENS / LMAX) ** 0.5), 5.939697, ((0, 8), (1, 4)), jnp.float32),
        "out_square": jnp.clip(jnp.exp(math.log(34.4) - 2.7679483 * jax.random.uniform(seeds[8], (Q, D), jnp.float32) ** block_scale(seeds[8], (Q, D), ((0, 8), (1, 4)), -0.2, 0.2)), 2.16, 34.4),
        "gate_weight": normal_values(seeds[9], (D, FF), D ** -0.5, 0.125, ((0, 8), (1, 4)), jnp.float32),
        "gate_moment": normal_values(seeds[10], (D, FF), (0.056 * (TOKENS * D / FF) ** 0.5), 15.386643, ((0, 8), (1, 4)), jnp.float32),
        "gate_square": jnp.clip(jnp.exp(math.log(221.184) - 2.76520863 * jax.random.uniform(seeds[11], (D, FF), jnp.float32) ** block_scale(seeds[11], (D, FF), ((0, 8), (1, 4)), -0.2, 0.2)), 13.9264, 221.184),
        "up_weight": normal_values(seeds[12], (D, FF), D ** -0.5, 0.125, ((0, 8), (1, 4)), jnp.float32),
        "up_moment": normal_values(seeds[13], (D, FF), (0.056 * (TOKENS * D / FF) ** 0.5), 15.386643, ((0, 8), (1, 4)), jnp.float32),
        "up_square": jnp.clip(jnp.exp(math.log(221.184) - 2.76520863 * jax.random.uniform(seeds[14], (D, FF), jnp.float32) ** block_scale(seeds[14], (D, FF), ((0, 8), (1, 4)), -0.2, 0.2)), 13.9264, 221.184),
        "down_weight": normal_values(seeds[15], (FF, D), FF ** -0.5, 0.0625, ((0, 8), (1, 4)), jnp.float32),
        "down_moment": normal_values(seeds[16], (FF, D), (0.056 * TOKENS ** 0.5), 29.86819, ((0, 8), (1, 4)), jnp.float32),
        "down_square": jnp.clip(jnp.exp(math.log(860.16) - 2.7668907 * jax.random.uniform(seeds[17], (FF, D), jnp.float32) ** block_scale(seeds[17], (FF, D), ((0, 8), (1, 4)), -0.2, 0.2)), 54.0672, 860.16),
        "norm_gains": draw_norm_gains(jax.random.fold_in(seeds[21], 71), 0),
        "gain_moment": normal_values(seeds[19], (2, D), (0.065 * TOKENS ** 0.5), 35.29877, ((1, 4),), jnp.float32),
        "gain_square": jnp.clip(jnp.exp(math.log(1146.88) - 2.744418 * jax.random.uniform(seeds[20], (2, D), jnp.float32) ** block_scale(seeds[20], (2, D), ((1, 4),), -0.2, 0.2)), 73.728, 1146.88),
    }


EPS_NORM = 1e-05
ROPE_BASE = 500000.0
BETA_ONE = 0.9
BETA_TWO = 0.95
ADAM_EPS = 1e-08
WEIGHT_DECAY = 0.1
RATE_MATRIX = 0.05
RATE_OUTPUT = 0.4
RATE_GAIN = 0.8
MASKED = -1e+30

@jax.custom_vjp
def low(v):
    return lax.optimization_barrier(v.astype(jnp.bfloat16)).astype(jnp.float32)

@jax.custom_vjp
def low_back(v):
    return v

def low_keep(v):
    return (low(v), None)

def low_pass(kept, grad):
    return (grad,)

def back_keep(v):
    return (v, None)

def back_low(kept, grad):
    return (low(grad),)
low.defvjp(low_keep, low_pass)
low_back.defvjp(back_keep, back_low)

def slot_info(lengths, total_slots):
    ends = jnp.cumsum(lengths, dtype=jnp.int32)
    slots = jnp.arange(total_slots, dtype=jnp.int32)
    passed = (slots[:, None] >= ends[None, :]).astype(jnp.int32)
    segment = lax.optimization_barrier(jnp.sum(passed, axis=1, dtype=jnp.int32))
    position = slots - lax.optimization_barrier(jnp.sum(passed * lengths[None, :], axis=1, dtype=jnp.int32))
    usable = slots < ends[-1]
    return (segment, position, usable)

def rope_tables(position):
    exponent = jnp.arange(0, HD, 2, dtype=jnp.float32) / HD
    freq_table = 1.0 / ROPE_BASE ** exponent
    angle = position.astype(jnp.float32)[:, None] * freq_table[None, :]
    cosine = jnp.cos(angle)
    sine = jnp.sin(angle)
    return (jnp.concatenate([cosine, cosine], axis=1), jnp.concatenate([sine, sine], axis=1))

def rotate(vectors, cosine, sine):
    half_width = vectors.shape[-1] // 2
    turned = jnp.concatenate([-vectors[..., half_width:], vectors[..., :half_width]], axis=-1)
    return vectors * cosine[:, None, :] + turned * sine[:, None, :]

def block_mask(segment, usable, start, window_start, window):
    query_slot = start + jnp.arange(BLK, dtype=jnp.int32)
    key_slot = window_start + jnp.arange(window, dtype=jnp.int32)
    query_seg = lax.dynamic_slice_in_dim(segment, start, BLK, 0)
    key_seg = lax.dynamic_slice_in_dim(segment, window_start, window, 0)
    query_usable = lax.dynamic_slice_in_dim(usable, start, BLK, 0)
    joined = (query_seg[:, None] == key_seg[None, :]) & (key_slot[None, :] <= query_slot[:, None]) & query_usable[:, None]
    return joined | (query_slot[:, None] == key_slot[None, :])

def matmul_high(left, right):
    return jnp.dot(left, right, precision=lax.Precision.HIGHEST)

def rms_scale(vectors):
    return lax.rsqrt(lax.optimization_barrier(jnp.mean(vectors * vectors, axis=1, keepdims=True)) + EPS_NORM)

def attend_block(q_rows, k_win, v_win, allowed):
    score_scale = HD ** (-0.5)
    raw_scores = jnp.einsum('qkgd,wkd->kgqw', q_rows, k_win, precision=lax.Precision.HIGHEST)
    scores = low_back(raw_scores * score_scale)
    scores = jnp.where(allowed[None, None], scores, MASKED)
    top_score = lax.optimization_barrier(jnp.max(scores, axis=-1, keepdims=True))
    exponent_terms = jnp.exp(scores - top_score)
    weights_soft = exponent_terms / lax.optimization_barrier(jnp.sum(exponent_terms, axis=-1, keepdims=True))
    return jnp.einsum('kgqw,wkd->qkgd', low(weights_soft), v_win, precision=lax.Precision.HIGHEST)

def attention(queries, keys, values, segment, usable):
    blocks = CAP // BLK
    window = BLK + LMAX
    q_rep = queries.reshape(N_DP, CAP, H_KV, GROUP, HD)
    k_rep = keys.reshape(N_DP, CAP, H_KV, HD)
    v_rep = values.reshape(N_DP, CAP, H_KV, HD)
    block_fn = jax.checkpoint(attend_block)

    def one_block(block_index):
        replica = block_index // blocks
        start = block_index % blocks * BLK
        window_start = jnp.maximum(start - LMAX, 0)
        q_rows = lax.dynamic_slice_in_dim(lax.dynamic_index_in_dim(q_rep, replica, 0, False), start, BLK, 0)
        k_win = lax.dynamic_slice_in_dim(lax.dynamic_index_in_dim(k_rep, replica, 0, False), window_start, window, 0)
        v_win = lax.dynamic_slice_in_dim(lax.dynamic_index_in_dim(v_rep, replica, 0, False), window_start, window, 0)
        seg_rep = lax.dynamic_index_in_dim(segment, replica, 0, False)
        usable_rep = lax.dynamic_index_in_dim(usable, replica, 0, False)
        allowed = block_mask(seg_rep, usable_rep, start, window_start, window)
        return block_fn(q_rows, k_win, v_win, allowed)
    outputs = lax.map(one_block, jnp.arange(N_DP * blocks, dtype=jnp.int32))
    return outputs.reshape(TOKENS, H_Q * HD)

def layer(source, qkv_w, out_w, gate_w, up_w, down_w, gains, segment, usable, cosine, sine):
    normed_one = low(source * rms_scale(source) * gains[0])
    projected = low_back(matmul_high(normed_one, low(qkv_w)))
    grouped = projected.reshape(TOKENS, H_KV, GROUP * HD + 2 * HD)
    queries = grouped[:, :, :GROUP * HD].reshape(TOKENS, H_Q, HD)
    keys = grouped[:, :, GROUP * HD:GROUP * HD + HD]
    values = grouped[:, :, GROUP * HD + HD:]
    queries = low(rotate(queries, cosine, sine)).reshape(TOKENS, H_KV, GROUP, HD)
    keys = low(rotate(keys, cosine, sine))
    values = low(values)
    attended = attention(queries, keys, values, segment, usable)
    attended = low(low_back(attended))
    middle = source + low_back(matmul_high(attended, low(out_w)))
    normed_two = low(middle * rms_scale(middle) * gains[1])
    gate = low_back(matmul_high(normed_two, low(gate_w)))
    up_value = low_back(matmul_high(normed_two, low(up_w)))
    hidden = low(jax.nn.silu(gate) * up_value)
    return middle + low_back(matmul_high(hidden, low(down_w)))

def adamw(weights, gradient, moment, square, step_rate, decay_rate):
    moment_new = BETA_ONE * moment + (1.0 - BETA_ONE) * gradient
    square_new = BETA_TWO * square + (1.0 - BETA_TWO) * gradient * gradient
    moment_hat = moment_new / (1.0 - BETA_ONE ** STEP)
    square_hat = square_new / (1.0 - BETA_TWO ** STEP)
    weights_new = weights - step_rate * (moment_hat / (jnp.sqrt(square_hat) + ADAM_EPS) + decay_rate * weights)
    return (weights_new, moment_new, square_new)

def reference(resid_in, cotangent, seq_lens, qkv_weight, qkv_moment, qkv_square, out_weight, out_moment, out_square, gate_weight, gate_moment, gate_square, up_weight, up_moment, up_square, down_weight, down_moment, down_square, norm_gains, gain_moment, gain_square):
    segment, position, usable = jax.vmap(partial(slot_info, total_slots=CAP))(seq_lens)
    cosine, sine = rope_tables(position.reshape(TOKENS))
    source = resid_in.astype(jnp.float32)

    def forward(source_in, qkv_w, out_w, gate_w, up_w, down_w, gains):
        return layer(source_in, qkv_w, out_w, gate_w, up_w, down_w, gains, segment, usable, cosine, sine)
    result, pull_back = jax.vjp(forward, source, qkv_weight, out_weight, gate_weight, up_weight, down_weight, norm_gains)
    grad_top = cotangent.astype(jnp.float32) * usable.reshape(TOKENS, 1).astype(jnp.float32)
    grad_source, grad_qkv, grad_out, grad_gate, grad_up, grad_down, grad_gains = pull_back(grad_top)
    qkv_set = adamw(qkv_weight, grad_qkv, qkv_moment, qkv_square, RATE_MATRIX, WEIGHT_DECAY)
    out_set = adamw(out_weight, grad_out, out_moment, out_square, RATE_OUTPUT, WEIGHT_DECAY)
    gate_set = adamw(gate_weight, grad_gate, gate_moment, gate_square, RATE_MATRIX, WEIGHT_DECAY)
    up_set = adamw(up_weight, grad_up, up_moment, up_square, RATE_MATRIX, WEIGHT_DECAY)
    down_set = adamw(down_weight, grad_down, down_moment, down_square, RATE_MATRIX, WEIGHT_DECAY)
    gain_set = adamw(norm_gains, grad_gains, gain_moment, gain_square, RATE_GAIN, 0.0)
    return (result.astype(jnp.bfloat16), grad_source, qkv_set[0], qkv_set[1], qkv_set[2], out_set[0], out_set[1], out_set[2], gate_set[0], gate_set[1], gate_set[2], up_set[0], up_set[1], up_set[2], down_set[0], down_set[1], down_set[2], gain_set[0], gain_set[1], gain_set[2])
```

```python
import functools

import jax
import jax.numpy as jnp
from jax import lax
from jax.experimental import pallas as pl
from jax.experimental.pallas import tpu as pltpu
from jax.sharding import PartitionSpec as P

D = 2048
FF = 8192
HD = 64
GROUP = 4
LMAX = 1024
STEP = 10
KEYS = 256

EPS_NORM = 1e-05
ROPE_BASE = 500000.0
BETA_ONE = 0.9
BETA_TWO = 0.95
ADAM_EPS = 1e-08
WEIGHT_DECAY = 0.1
RATE_MATRIX = 0.05
RATE_OUTPUT = 0.4
RATE_GAIN = 0.8
MASKED = -1e30
SCALE = HD ** (-0.5)

BF = jnp.bfloat16
F32 = jnp.float32


def dot(left, right, left_dim, right_dim):
    return lax.dot_general(
        left, right, (((left_dim,), (right_dim,)), ((), ())), preferred_element_type=F32
    )


def half_groups(reps):
    return [[rep, rep + reps] for rep in range(reps)]


def rep_groups(reps):
    return [[half * reps + rep for rep in range(reps)] for half in range(2)]


def plane_gather(values_in, reps):
    if reps == 1:
        return lax.all_gather(values_in, ("dp", "col"), axis=0, tiled=True)
    gathered = lax.all_gather(values_in, "col", axis=0, tiled=True)
    return lax.all_gather(gathered, "dp", axis=0, tiled=True, axis_index_groups=half_groups(reps))


def plane_scatter(values_in, reps):
    if reps == 1:
        return lax.psum_scatter(values_in, ("dp", "col"), scatter_dimension=0, tiled=True)
    scattered = lax.psum_scatter(
        values_in, "dp", scatter_dimension=0, tiled=True, axis_index_groups=half_groups(reps)
    )
    return lax.psum_scatter(scattered, "col", scatter_dimension=0, tiled=True)


def gather_in_block(weight, reps):
    swapped = lax.all_to_all(
        weight.astype(BF), "dp", split_axis=1, concat_axis=0, tiled=True, axis_index_groups=half_groups(reps)
    )
    if reps > 1:
        own = weight.shape[0]
        swapped = lax.all_gather(swapped, "dp", axis=0, axis_index_groups=rep_groups(reps))
        swapped = swapped.reshape(reps, 2, own, -1).swapaxes(0, 1).reshape(2 * reps * own, -1)
    return lax.all_gather(swapped, "row", axis=0, tiled=True)


def scatter_in_block(gradient, reps):
    part = lax.psum_scatter(gradient.astype(BF), "row", scatter_dimension=0, tiled=True)
    part = lax.all_to_all(
        part, "dp", split_axis=0, concat_axis=1, tiled=True, axis_index_groups=half_groups(reps)
    )
    if reps > 1:
        part = lax.psum_scatter(
            part, "dp", scatter_dimension=0, tiled=True, axis_index_groups=rep_groups(reps)
        )
    return part


def gather_down(weight, reps):
    own = weight.astype(BF)
    if reps > 1:
        own = lax.all_gather(own, "dp", axis=0, tiled=True, axis_index_groups=rep_groups(reps))
    return lax.all_gather(own, "row", axis=0)


def scatter_down(gradient, reps):
    part = lax.psum_scatter(gradient.astype(BF), "row", scatter_dimension=0, tiled=False)
    if reps > 1:
        part = lax.psum_scatter(
            part, "dp", scatter_dimension=0, tiled=True, axis_index_groups=rep_groups(reps)
        )
    return part


def rope_tables(position):
    exponent = jnp.arange(0, HD, 2, dtype=F32) / HD
    freq_table = 1.0 / ROPE_BASE**exponent
    angle = position.astype(F32)[:, None] * freq_table[None, :]
    cosine = jnp.cos(angle)
    sine = jnp.sin(angle)
    return (jnp.concatenate([cosine, cosine], axis=1), jnp.concatenate([sine, sine], axis=1))


def rotate(vectors, cosine, sine):
    half_width = HD // 2
    turned = jnp.concatenate([-vectors[..., half_width:], vectors[..., :half_width]], axis=-1)
    return vectors * cosine[:, None, None, :] + turned * sine[:, None, None, :]


def rotate_back(gradient, cosine, sine):
    half_width = HD // 2
    turned = gradient * sine[:, None, None, :]
    moved = jnp.concatenate([turned[..., half_width:], -turned[..., :half_width]], axis=-1)
    return gradient * cosine[:, None, None, :] + moved


def head_rows(block):
    turned = block.astype(F32).T
    return [turned[head * HD : (head + 1) * HD].astype(BF) for head in range(GROUP)]


def allowed_entries(key_block, low_ref, query_first):
    tokens = low_ref.shape[-1]
    key_slot = key_block * KEYS + lax.broadcasted_iota(jnp.int32, (KEYS, tokens), 0)
    query_slot = query_first + lax.broadcasted_iota(jnp.int32, (KEYS, tokens), 1)
    return (key_slot >= low_ref[...]) & (key_slot <= query_slot)


def key_rows(block):
    return pl.ds(pl.multiple_of(block * KEYS, KEYS), KEYS)


def attend_kernel(bounds, query_ref, pair_ref, low_ref, out_ref, log_ref, score_ref, mix_ref):
    step = pl.program_id(1)
    first, last, query_first = bounds[0, step], bounds[1, step], bounds[2, step]
    tokens = query_ref.shape[0]
    blank = jnp.zeros((HD, tokens), BF)
    queries = [jnp.concatenate([rows, blank], axis=0) for rows in head_rows(query_ref[...])]

    def score_block(block, tops):
        pairs = pair_ref[key_rows(block), :]
        allowed = allowed_entries(block, low_ref, query_first)
        new_tops = []
        for head in range(GROUP):
            scores = jnp.where(allowed, dot(pairs, queries[head], 1, 0), MASKED)
            score_ref[head, key_rows(block - first), :] = scores
            new_tops.append(jnp.maximum(tops[head], jnp.max(scores, axis=0, keepdims=True)))
        return tuple(new_tops)

    start = tuple(jnp.full((1, tokens), MASKED, F32) for _ in range(GROUP))
    tops = lax.fori_loop(first, last, score_block, start)
    mix_ref[...] = jnp.zeros_like(mix_ref)

    def mix_block(block, totals):
        pairs = pair_ref[key_rows(block), :]
        new_totals = []
        for head in range(GROUP):
            terms = jnp.exp(score_ref[head, key_rows(block - first), :] - tops[head])
            new_totals.append(totals[head] + jnp.sum(terms, axis=0, keepdims=True))
            mix_ref[head] += dot(pairs, terms.astype(BF), 0, 0)
        return tuple(new_totals)

    start = tuple(jnp.zeros((1, tokens), F32) for _ in range(GROUP))
    totals = lax.fori_loop(first, last, mix_block, start)
    mixed = jnp.concatenate(
        [mix_ref[head, HD:, :] / totals[head] for head in range(GROUP)], axis=0
    )
    out_ref[...] = mixed.T.astype(BF)
    for head in range(GROUP):
        log_ref[head : head + 1, :] = tops[head] + jnp.log(totals[head])


def attend_back_kernel(
    bounds, query_ref, grad_ref, pair_ref, low_ref, log_ref, dquery_ref, dpair_ref, prob_ref, dprob_ref, dmix_ref
):
    step = pl.program_id(1)
    first, last, query_first = bounds[0, step], bounds[1, step], bounds[2, step]
    tokens = query_ref.shape[0]
    blank = jnp.zeros((HD, tokens), BF)
    queries = [jnp.concatenate([rows, blank], axis=0) for rows in head_rows(query_ref[...])]
    grads = [jnp.concatenate([blank, rows], axis=0) for rows in head_rows(grad_ref[...])]

    @pl.when(step == 0)
    def _():
        dpair_ref[...] = jnp.zeros_like(dpair_ref)

    def prob_block(block, inners):
        pairs = pair_ref[key_rows(block), :]
        allowed = allowed_entries(block, low_ref, query_first)
        new_inners = []
        for head in range(GROUP):
            scores = dot(pairs, queries[head], 1, 0)
            probs = jnp.where(allowed, jnp.exp(scores - log_ref[head : head + 1, :]), 0.0)
            dprobs = dot(pairs, grads[head], 1, 0)
            prob_ref[head, key_rows(block - first), :] = probs
            dprob_ref[head, key_rows(block - first), :] = dprobs
            new_inners.append(inners[head] + jnp.sum(probs * dprobs, axis=0, keepdims=True))
        return tuple(new_inners)

    start = tuple(jnp.zeros((1, tokens), F32) for _ in range(GROUP))
    inners = lax.fori_loop(first, last, prob_block, start)
    dmix_ref[...] = jnp.zeros_like(dmix_ref)
    all_queries = jnp.concatenate(queries, axis=1)
    all_grads = jnp.concatenate(grads, axis=1)

    def back_block(block, carry):
        rows = key_rows(block)
        pairs = pair_ref[rows, :]
        all_probs, all_scores = [], []
        for head in range(GROUP):
            probs = prob_ref[head, key_rows(block - first), :]
            dprobs = dprob_ref[head, key_rows(block - first), :]
            dscores = (probs * (dprobs - inners[head])).astype(BF)
            dmix_ref[head] += dot(pairs, dscores, 0, 0)
            all_probs.append(probs.astype(BF))
            all_scores.append(dscores)
        dpair_ref[rows, :] += dot(jnp.concatenate(all_scores, axis=1), all_queries, 1, 1) + dot(
            jnp.concatenate(all_probs, axis=1), all_grads, 1, 1
        )
        return carry

    lax.fori_loop(first, last, back_block, 0)
    dquery = jnp.concatenate([dmix_ref[head, :HD, :] for head in range(GROUP)], axis=0)
    dquery_ref[...] = dquery.T * SCALE


def attend(queries, pairs, low, bounds):
    tokens, width = queries.shape
    kv_heads, slots, _ = pairs.shape
    blocks, _, rows = low.shape
    span = LMAX + KEYS
    return pl.pallas_call(
        attend_kernel,
        grid_spec=pltpu.PrefetchScalarGridSpec(
            num_scalar_prefetch=1,
            grid=(kv_heads, blocks),
            in_specs=[
                pl.BlockSpec((rows, GROUP * HD), lambda kv, block, _: (block, kv)),
                pl.BlockSpec((None, slots, 2 * HD), lambda kv, block, _: (kv, 0, 0)),
                pl.BlockSpec((None, 1, rows), lambda kv, block, _: (block, 0, 0)),
            ],
            out_specs=[
                pl.BlockSpec((rows, GROUP * HD), lambda kv, block, _: (block, kv)),
                pl.BlockSpec((None, None, GROUP, rows), lambda kv, block, _: (kv, block, 0, 0)),
            ],
            scratch_shapes=[
                pltpu.VMEM((GROUP, span, rows), F32),
                pltpu.VMEM((GROUP, 2 * HD, rows), F32),
            ],
        ),
        out_shape=[
            jax.ShapeDtypeStruct((tokens, width), BF),
            jax.ShapeDtypeStruct((kv_heads, blocks, GROUP, rows), F32),
        ],
        compiler_params=pltpu.CompilerParams(vmem_limit_bytes=48 * 2**20),
        cost_estimate=pl.CostEstimate(flops=3 * 10**9, bytes_accessed=8 * 2**20, transcendentals=5 * 10**6),
        name="attend",
    )(bounds, queries, pairs, low)


def attend_back(queries, grads, pairs, low, log_total, bounds):
    tokens, width = queries.shape
    kv_heads, slots, _ = pairs.shape
    blocks, _, rows = low.shape
    span = LMAX + KEYS
    return pl.pallas_call(
        attend_back_kernel,
        grid_spec=pltpu.PrefetchScalarGridSpec(
            num_scalar_prefetch=1,
            grid=(kv_heads, blocks),
            in_specs=[
                pl.BlockSpec((rows, GROUP * HD), lambda kv, block, _: (block, kv)),
                pl.BlockSpec((rows, GROUP * HD), lambda kv, block, _: (block, kv)),
                pl.BlockSpec((None, slots, 2 * HD), lambda kv, block, _: (kv, 0, 0)),
                pl.BlockSpec((None, 1, rows), lambda kv, block, _: (block, 0, 0)),
                pl.BlockSpec((None, None, GROUP, rows), lambda kv, block, _: (kv, block, 0, 0)),
            ],
            out_specs=[
                pl.BlockSpec((rows, GROUP * HD), lambda kv, block, _: (block, kv)),
                pl.BlockSpec((None, slots, 2 * HD), lambda kv, block, _: (kv, 0, 0)),
            ],
            scratch_shapes=[
                pltpu.VMEM((GROUP, span, rows), F32),
                pltpu.VMEM((GROUP, span, rows), F32),
                pltpu.VMEM((GROUP, 2 * HD, rows), F32),
            ],
        ),
        out_shape=[
            jax.ShapeDtypeStruct((tokens, width), F32),
            jax.ShapeDtypeStruct((kv_heads, slots, 2 * HD), F32),
        ],
        compiler_params=pltpu.CompilerParams(vmem_limit_bytes=48 * 2**20),
        cost_estimate=pl.CostEstimate(flops=8 * 10**9, bytes_accessed=12 * 2**20, transcendentals=5 * 10**6),
        name="attend_back",
    )(bounds, queries, grads, pairs, low, log_total)


def normalize(vectors):
    scaling = lax.rsqrt(jnp.mean(vectors * vectors, axis=1, keepdims=True) + EPS_NORM)
    return (vectors * scaling, scaling)


def normalize_back(gradient, unit, scaling, gain):
    weighted = gradient * gain[None, :]
    inner = jnp.mean(weighted * unit, axis=1, keepdims=True)
    return (scaling * (weighted - unit * inner), jnp.sum(gradient * unit, axis=0))


def adamw(weights, gradient, moment, square, step_rate, decay_rate):
    gradient = gradient.astype(F32)
    moment_new = BETA_ONE * moment + (1.0 - BETA_ONE) * gradient
    square_new = BETA_TWO * square + (1.0 - BETA_TWO) * gradient * gradient
    moment_hat = moment_new / (1.0 - BETA_ONE**STEP)
    square_hat = square_new / (1.0 - BETA_TWO**STEP)
    weights_new = weights - step_rate * (
        moment_hat / (jnp.sqrt(square_hat) + ADAM_EPS) + decay_rate * weights
    )
    return (weights_new, moment_new, square_new)


def local(
    resid_in,
    cotangent,
    seq_lens,
    qkv_weight,
    qkv_moment,
    qkv_square,
    out_weight,
    out_moment,
    out_square,
    gate_weight,
    gate_moment,
    gate_square,
    up_weight,
    up_moment,
    up_square,
    down_weight,
    down_moment,
    down_square,
    norm_gains,
    gain_moment,
    gain_square,
):
    cols, rows, replicas = lax.axis_size("col"), lax.axis_size("row"), lax.axis_size("dp")
    reps = replicas // 2
    row, col = lax.axis_index("row"), lax.axis_index("col")
    chunk = resid_in.shape[0]
    slots = chunk * cols
    sub = chunk // rows
    group_tokens = sub * cols

    lengths = seq_lens[0]
    ends = jnp.cumsum(lengths, dtype=jnp.int32)
    firsts = (jnp.arange(cols, dtype=jnp.int32) * chunk + row * sub).astype(jnp.int32)
    slot = (firsts[:, None] + jnp.arange(sub, dtype=jnp.int32)[None, :]).reshape(group_tokens)
    passed = (slot[:, None] >= ends[None, :]).astype(jnp.int32)
    seq_start = jnp.sum(passed * lengths[None, :], axis=1, dtype=jnp.int32)
    usable = slot < ends[-1]
    cosine, sine = rope_tables(slot - seq_start)
    low = jnp.where(usable, seq_start, slot).reshape(cols, 1, sub)
    bounds = jnp.stack([low[:, 0, 0] // KEYS, (firsts + sub - 1) // KEYS + 1, firsts]).astype(jnp.int32)
    usable_mine = lax.dynamic_slice_in_dim(usable, col * sub, sub, 0).astype(F32)[:, None]

    gains = lax.all_gather(norm_gains, "row", axis=1, tiled=True)
    source = lax.all_to_all(resid_in, "row", split_axis=0, concat_axis=1, tiled=True).astype(F32)

    qkv_w = lax.all_gather(qkv_weight.astype(BF), ("row", "dp"), axis=0, tiled=True)
    out_w = lax.all_gather(out_weight.astype(BF), ("row", "dp"), axis=0)
    out_w = out_w.reshape(rows, replicas * out_weight.shape[0], -1).swapaxes(0, 1)
    out_w = out_w.reshape(replicas * out_weight.shape[0], D)
    gate_w = gather_in_block(gate_weight, reps)
    up_w = gather_in_block(up_weight, reps)
    down_w = gather_down(down_weight, reps)
    down_w = down_w.swapaxes(0, 1).reshape(-1, D)

    unit_one, scale_one = normalize(source)
    normed_one = lax.all_gather((unit_one * gains[0][None, :]).astype(BF), "col", axis=0, tiled=True)
    projected = dot(normed_one, qkv_w, 1, 0)
    kv_heads = projected.shape[1] // ((GROUP + 2) * HD)
    parts = projected.reshape(group_tokens, kv_heads, GROUP + 2, HD)
    turned = rotate(parts[:, :, : GROUP + 1], cosine, sine).astype(BF)
    queries = (turned[:, :, :GROUP] * BF(SCALE)).reshape(group_tokens, kv_heads * GROUP * HD)
    pairs = jnp.concatenate([turned[:, :, GROUP], parts[:, :, GROUP + 1].astype(BF)], axis=2)
    pairs = lax.all_gather(pairs.reshape(group_tokens, kv_heads * 2 * HD), "row", axis=0)
    pairs = pairs.reshape(rows, cols, sub, kv_heads, 2 * HD).transpose(3, 1, 0, 2, 4)
    pairs = pairs.reshape(kv_heads, slots, 2 * HD)
    attended, log_total = attend(queries, pairs, low, bounds)
    mixed = lax.psum_scatter(dot(attended, out_w, 1, 0).astype(BF), "col", scatter_dimension=0, tiled=True)
    middle = source + mixed.astype(F32)

    unit_two, scale_two = normalize(middle)
    normed_two = plane_gather((unit_two * gains[1][None, :]).astype(BF), reps)
    grad_top = lax.all_to_all(cotangent, "row", split_axis=0, concat_axis=1, tiled=True).astype(F32) * usable_mine
    grad_top_all = plane_gather(grad_top.astype(BF), reps)
    gate_val = dot(normed_two, gate_w, 1, 0)
    up_val = dot(normed_two, up_w, 1, 0)
    sigma = jax.nn.sigmoid(gate_val)
    activated = gate_val * sigma
    hidden = (activated * up_val).astype(BF)
    grad_down = dot(hidden, grad_top_all, 0, 0)
    grad_down = grad_down.reshape(-1, rows, D // rows).swapaxes(0, 1)
    grad_down = scatter_down(grad_down, reps)
    grad_hidden = dot(grad_top_all, down_w, 1, 1)
    grad_gate_val = (grad_hidden * up_val * sigma * (1.0 + gate_val * (1.0 - sigma))).astype(BF)
    grad_up_val = (grad_hidden * activated).astype(BF)
    grad_normed_two = plane_scatter(
        (dot(grad_gate_val, gate_w, 1, 1) + dot(grad_up_val, up_w, 1, 1)).astype(BF), reps
    ).astype(F32)
    grad_gate = scatter_in_block(dot(normed_two, grad_gate_val, 0, 0), reps)
    grad_up = scatter_in_block(dot(normed_two, grad_up_val, 0, 0), reps)
    lifted = plane_scatter(dot(hidden, down_w, 1, 0).astype(BF), reps)
    result = (middle + lifted.astype(F32)).astype(BF)
    result = lax.all_to_all(result, "row", split_axis=1, concat_axis=0, tiled=True)

    back_two, gain_grad_two = normalize_back(grad_normed_two, unit_two, scale_two, gains[1])
    grad_middle = grad_top + back_two
    grad_middle_all = lax.all_gather(grad_middle.astype(BF), "col", axis=0, tiled=True)
    grad_attended = dot(grad_middle_all, out_w, 1, 1).astype(BF)
    grad_query, grad_pairs = attend_back(queries, grad_attended, pairs, low, log_total, bounds)
    grad_pairs = grad_pairs.astype(BF).reshape(kv_heads, cols, rows, sub, 2 * HD).transpose(2, 1, 3, 0, 4)
    grad_pairs = lax.psum_scatter(
        grad_pairs.reshape(rows, group_tokens, kv_heads * 2 * HD), "row", scatter_dimension=0, tiled=False
    )
    grad_pairs = grad_pairs.astype(F32).reshape(group_tokens, kv_heads, 2, HD)
    grad_turned = jnp.concatenate(
        [grad_query.reshape(group_tokens, kv_heads, GROUP, HD), grad_pairs[:, :, :1]], axis=2
    )
    grad_proj = jnp.concatenate([rotate_back(grad_turned, cosine, sine), grad_pairs[:, :, 1:]], axis=2)
    grad_proj = grad_proj.astype(BF).reshape(group_tokens, kv_heads * (GROUP + 2) * HD)
    grad_normed_one = lax.psum_scatter(
        dot(grad_proj, qkv_w, 1, 1).astype(BF), "col", scatter_dimension=0, tiled=True
    ).astype(F32)
    grad_out = dot(attended, grad_middle_all, 0, 0).astype(BF)
    grad_out = grad_out.reshape(grad_out.shape[0], rows, D // rows).swapaxes(0, 1)
    grad_out = lax.psum_scatter(
        grad_out.reshape(-1, D // rows), ("row", "dp"), scatter_dimension=0, tiled=True
    )
    grad_qkv = lax.psum_scatter(
        dot(normed_one, grad_proj, 0, 0).astype(BF), ("row", "dp"), scatter_dimension=0, tiled=True
    )
    back_one, gain_grad_one = normalize_back(grad_normed_one, unit_one, scale_one, gains[0])
    resid_grad = lax.all_to_all(
        (grad_middle + back_one).astype(BF), "row", split_axis=1, concat_axis=0, tiled=True
    ).astype(F32)

    gain_grads = lax.psum(jnp.stack([gain_grad_one, gain_grad_two]), ("dp", "row", "col"))
    gain_grads = lax.dynamic_slice_in_dim(gain_grads, row * norm_gains.shape[1], norm_gains.shape[1], 1)
    qkv_set = adamw(qkv_weight, grad_qkv, qkv_moment, qkv_square, RATE_MATRIX, WEIGHT_DECAY)
    out_set = adamw(out_weight, grad_out, out_moment, out_square, RATE_OUTPUT, WEIGHT_DECAY)
    gate_set = adamw(gate_weight, grad_gate, gate_moment, gate_square, RATE_MATRIX, WEIGHT_DECAY)
    up_set = adamw(up_weight, grad_up, up_moment, up_square, RATE_MATRIX, WEIGHT_DECAY)
    down_set = adamw(down_weight, grad_down, down_moment, down_square, RATE_MATRIX, WEIGHT_DECAY)
    gain_set = adamw(norm_gains, gain_grads, gain_moment, gain_square, RATE_GAIN, 0.0)
    return (result, resid_grad, *qkv_set, *out_set, *gate_set, *up_set, *down_set, *gain_set)


def solution(mesh):
    tokens = P(("dp", "col"), "row")
    wide = P(("row", "dp"), "col")
    tall = P(("col", "dp"), "row")
    gain = P(None, "row")
    weights = (wide,) * 3 + (tall,) * 3 + (wide,) * 6 + (tall,) * 3 + (gain,) * 3
    return jax.shard_map(
        local,
        mesh=mesh,
        in_specs=(tokens, tokens, P("dp", None)) + weights,
        out_specs=(tokens, tokens) + weights,
        check_vma=False,
    )
```

```python
import functools

import jax
import jax.numpy as jnp
from jax import lax
from jax.experimental import pallas as pl
from jax.experimental.pallas import tpu as pltpu
from jax.sharding import PartitionSpec as P

D = 2048
FF = 8192
HD = 64
GROUP = 4
LMAX = 1024
STEP = 10
KEYS = 256

EPS_NORM = 1e-05
ROPE_BASE = 500000.0
BETA_ONE = 0.9
BETA_TWO = 0.95
ADAM_EPS = 1e-08
WEIGHT_DECAY = 0.1
RATE_MATRIX = 0.05
RATE_OUTPUT = 0.4
RATE_GAIN = 0.8
MASKED = -1e30
SCALE = HD ** (-0.5)

BF = jnp.bfloat16
F32 = jnp.float32


def dot(left, right, left_dim, right_dim):
    return lax.dot_general(
        left, right, (((left_dim,), (right_dim,)), ((), ())), preferred_element_type=F32
    )


def half_groups(reps):
    return [[rep, rep + reps] for rep in range(reps)]


def rep_groups(reps):
    return [[half * reps + rep for rep in range(reps)] for half in range(2)]


def plane_gather(values_in, reps):
    if reps == 1:
        return lax.all_gather(values_in, ("dp", "col"), axis=0, tiled=True)
    gathered = lax.all_gather(values_in, "col", axis=0, tiled=True)
    return lax.all_gather(gathered, "dp", axis=0, tiled=True, axis_index_groups=half_groups(reps))


def plane_scatter(values_in, reps):
    if reps == 1:
        return lax.psum_scatter(values_in, ("dp", "col"), scatter_dimension=0, tiled=True)
    scattered = lax.psum_scatter(
        values_in, "dp", scatter_dimension=0, tiled=True, axis_index_groups=half_groups(reps)
    )
    return lax.psum_scatter(scattered, "col", scatter_dimension=0, tiled=True)


def partner_swap(values_in, reps):
    pairs = [pair for rep in range(reps) for pair in ((rep, rep + reps), (rep + reps, rep))]
    return lax.ppermute(values_in, "dp", pairs)


def both_halves(mine, theirs, half, axis):
    first = jnp.where(half == 0, mine, theirs)
    second = jnp.where(half == 0, theirs, mine)
    return jnp.concatenate([first, second], axis=axis)


def gather_in_block(weight, reps):
    half = lax.axis_index("dp") // reps
    own, width = weight.shape[0], weight.shape[1] // 2
    low = weight.astype(BF)
    mine = lax.dynamic_slice_in_dim(low, half * width, width, 1)
    theirs = partner_swap(lax.dynamic_slice_in_dim(low, (1 - half) * width, width, 1), reps)
    both = both_halves(mine, theirs, half, 0)
    if reps > 1:
        both = lax.all_gather(both, "dp", axis=0, axis_index_groups=rep_groups(reps))
        both = both.reshape(reps, 2, own, width).swapaxes(0, 1).reshape(2 * reps * own, width)
    return lax.all_gather(both, "row", axis=0, tiled=True)


def scatter_in_block(gradient, reps):
    half = lax.axis_index("dp") // reps
    part = lax.psum_scatter(gradient.astype(BF), "row", scatter_dimension=0, tiled=True)
    height = part.shape[0] // 2
    mine = lax.dynamic_slice_in_dim(part, half * height, height, 0)
    theirs = partner_swap(lax.dynamic_slice_in_dim(part, (1 - half) * height, height, 0), reps)
    part = both_halves(mine, theirs, half, 1)
    if reps > 1:
        part = lax.psum_scatter(
            part, "dp", scatter_dimension=0, tiled=True, axis_index_groups=rep_groups(reps)
        )
    return part


def gather_tall(weight, reps):
    own = weight.astype(BF)
    if reps > 1:
        own = lax.all_gather(own, "dp", axis=0, tiled=True, axis_index_groups=rep_groups(reps))
    return lax.all_gather(own, "row", axis=0)


def scatter_tall(gradient, reps):
    rows = lax.axis_size("row")
    gradient = gradient.astype(BF).reshape(gradient.shape[0], rows, D // rows).swapaxes(0, 1)
    part = lax.psum_scatter(gradient, "row", scatter_dimension=0, tiled=False)
    if reps > 1:
        part = lax.psum_scatter(
            part, "dp", scatter_dimension=0, tiled=True, axis_index_groups=rep_groups(reps)
        )
    return part


MESH = pl.DeviceIdType.MESH
COLS = 4


def plane(reps):
    replica, col = lax.axis_index("dp"), lax.axis_index("col")
    half, rep = lax.div(replica, reps), lax.rem(replica, reps)
    core = lax.rem(col, 2)
    other = col + 1 - 2 * core

    def place(half_of, col_of):
        return (half_of * COLS + col_of, {"dp": half_of * reps + rep, "col": col_of})

    def turn(value, by, modulus):
        return lax.rem(value + by, modulus)

    return {
        "O": place(half, col),
        "P": place(turn(half, 1 - core, 2), turn(col, 2 * core, COLS)),
        "Q": place(turn(half, core, 2), turn(col, 2 - 2 * core, COLS)),
        "D": place(1 - half, turn(col, 2, COLS)),
        "SO": place(half, other),
        "SP": place(turn(half, core, 2), turn(other, 2 - 2 * core, COLS)),
        "SQ": place(turn(half, 1 - core, 2), turn(other, 2 * core, COLS)),
        "SD": place(1 - half, turn(other, 2, COLS)),
    }


def meet(devices):
    barrier = pltpu.get_barrier_semaphore()
    for device in devices:
        pl.semaphore_signal(barrier, inc=1, device_id=device, device_id_type=MESH)
    pl.semaphore_wait(barrier, len(devices))


GATHER_KINDS = ("P", "Q", "D", "SO", "SP", "SQ", "SD")


def run_gather(reps, pieces, own_ref, held_ref, send_sems, recv_sems, use):
    where = plane(reps)
    height = own_ref.shape[0] // pieces

    def message(kind, piece, source, block, device):
        rows = pl.ds(piece * height, height)
        index = GATHER_KINDS.index(kind)
        return pltpu.make_async_remote_copy(
            src_ref=source.at[rows],
            dst_ref=held_ref.at[block, rows],
            send_sem=send_sems.at[index, piece],
            recv_sem=recv_sems.at[index, piece],
            device_id=device,
            device_id_type=MESH,
        )

    near_p, near_q, sibling = where["P"][1], where["Q"][1], where["SO"][1]
    meet((near_p, near_q, sibling))
    sent = []

    def send(kind, piece, source, block, device):
        copy = message(kind, piece, source, block, device)
        copy.start()
        sent.append(copy)

    def arrive(kind, piece):
        block = where[kind][0]
        message(kind, piece, held_ref.at[block], block, sibling).wait_recv()
        return held_ref.at[block], block

    own = where["O"][0]
    for piece in range(pieces):
        send("P", piece, own_ref, own, near_p)
        send("Q", piece, own_ref, own, near_q)
        send("SO", piece, own_ref, own, sibling)
    use(0, own, own_ref)
    for piece in range(pieces):
        ref, block = arrive("P", piece)
        send("D", piece, ref, block, near_q)
        send("SP", piece, ref, block, sibling)
    use(1, block, ref)
    for piece in range(pieces):
        ref, block = arrive("Q", piece)
        send("SQ", piece, ref, block, sibling)
    use(2, block, ref)
    step = 3
    for kind in ("SO", "SP", "SQ", "D", "SD"):
        for piece in range(pieces):
            ref, block = arrive(kind, piece)
            if kind == "D":
                send("SD", piece, ref, block, sibling)
        use(step, block, ref)
        step += 1
    for copy in sent:
        copy.wait_send()


def stage(step, block, value_of, slots_ref, out_ref, sems, pending):
    slot = step % 2
    if step >= 2:
        pending[step - 2].wait()
    value_of(slots_ref.at[slot])
    copy = pltpu.make_async_copy(slots_ref.at[slot], out_ref.at[block], sems.at[slot])
    copy.start()
    pending[step] = copy


SCATTER_SWAPS = ("D", "Q", "P", "O")
SCATTER_HOPS = ("D", "Q", "P")


def run_scatter(reps, pieces, partial, finish, total_ref, give_ref, take_ref, hop_out, hop_in, sems):
    swap_send, swap_recv, hop_send, hop_recv = sems
    where = plane(reps)
    near = {"P": where["P"][1], "Q": where["Q"][1], "D": where["Q"][1]}
    sibling = where["SO"][1]
    height = total_ref.shape[1] // pieces
    meet((near["P"], near["Q"], sibling))
    sent = []

    def swap(kind):
        index = SCATTER_SWAPS.index(kind)
        return pltpu.make_async_remote_copy(
            src_ref=give_ref.at[index],
            dst_ref=take_ref.at[index],
            send_sem=swap_send.at[index],
            recv_sem=swap_recv.at[index],
            device_id=sibling,
            device_id_type=MESH,
        )

    def hop(kind, piece):
        index = SCATTER_HOPS.index(kind)
        rows = pl.ds(piece * height, height)
        return pltpu.make_async_remote_copy(
            src_ref=hop_out.at[index, rows],
            dst_ref=hop_in.at[index, rows],
            send_sem=hop_send.at[index, piece],
            recv_sem=hop_recv.at[index, piece],
            device_id=near[kind],
            device_id_type=MESH,
        )

    def give(step, kind):
        index = SCATTER_SWAPS.index(kind)

        def put(columns, value):
            give_ref[index, :, columns] = value.astype(BF)

        partial(step, where["S" + kind][0], put)
        copy = swap(kind)
        copy.start()
        sent.append(copy)

    def keep(step, kind):
        index = SCATTER_SWAPS.index(kind)

        def put(columns, value):
            total_ref[index, :, columns] = value

        partial(step, where[kind][0], put)

    def settle(kind):
        index = SCATTER_SWAPS.index(kind)
        swap(kind).wait_recv()
        for piece in range(pieces):
            rows = pl.ds(piece * height, height)
            value = total_ref[index, rows, :] + take_ref[index, rows, :].astype(F32)
            if kind == "P":
                hop("D", piece).wait_recv()
                value += hop_in[SCATTER_HOPS.index("D"), rows, :].astype(F32)
            if kind == "O":
                for source in ("Q", "P"):
                    hop(source, piece).wait_recv()
                    value += hop_in[SCATTER_HOPS.index(source), rows, :].astype(F32)
                finish(rows, value)
            else:
                hop_out[SCATTER_HOPS.index(kind), rows, :] = value.astype(BF)
                copy = hop(kind, piece)
                copy.start()
                sent.append(copy)

    give(0, "D")
    keep(1, "D")
    give(2, "Q")
    settle("D")
    keep(3, "Q")
    give(4, "P")
    settle("Q")
    keep(5, "P")
    give(6, "O")
    keep(7, "O")
    settle("P")
    settle("O")
    for copy in sent:
        copy.wait_send()


def rope_tables(position):
    exponent = jnp.arange(0, HD, 2, dtype=F32) / HD
    freq_table = 1.0 / ROPE_BASE**exponent
    angle = position.astype(F32)[:, None] * freq_table[None, :]
    cosine = jnp.cos(angle)
    sine = jnp.sin(angle)
    return (jnp.concatenate([cosine, cosine], axis=1), jnp.concatenate([sine, sine], axis=1))


def rotate(vectors, cosine, sine):
    half_width = HD // 2
    turned = jnp.concatenate([-vectors[..., half_width:], vectors[..., :half_width]], axis=-1)
    return vectors * cosine[:, None, None, :] + turned * sine[:, None, None, :]


def rotate_back(gradient, cosine, sine):
    half_width = HD // 2
    turned = gradient * sine[:, None, None, :]
    moved = jnp.concatenate([turned[..., half_width:], -turned[..., :half_width]], axis=-1)
    return gradient * cosine[:, None, None, :] + moved


def head_rows(block):
    turned = block.astype(F32).T
    return [turned[head * HD : (head + 1) * HD].astype(BF) for head in range(GROUP)]


def allowed_entries(key_block, low_ref, query_first):
    tokens = low_ref.shape[-1]
    key_slot = key_block * KEYS + lax.broadcasted_iota(jnp.int32, (KEYS, tokens), 0)
    query_slot = query_first + lax.broadcasted_iota(jnp.int32, (KEYS, tokens), 1)
    return (key_slot >= low_ref[...]) & (key_slot <= query_slot)


def key_rows(block):
    return pl.ds(pl.multiple_of(block * KEYS, KEYS), KEYS)


def attend_kernel(bounds, query_ref, pair_ref, low_ref, out_ref, log_ref, score_ref, mix_ref):
    step = pl.program_id(1)
    place = pl.program_id(0) * pl.num_programs(1) + step
    first, last, query_first = bounds[0, place], bounds[1, place], bounds[2, place]
    tokens = query_ref.shape[0]
    blank = jnp.zeros((HD, tokens), BF)
    queries = [jnp.concatenate([rows, blank], axis=0) for rows in head_rows(query_ref[...])]

    def score_block(block, tops):
        pairs = pair_ref[key_rows(block), :]
        allowed = allowed_entries(block, low_ref, query_first)
        new_tops = []
        for head in range(GROUP):
            scores = jnp.where(allowed, dot(pairs, queries[head], 1, 0), MASKED)
            score_ref[head, key_rows(block - first), :] = scores
            new_tops.append(jnp.maximum(tops[head], jnp.max(scores, axis=0, keepdims=True)))
        return tuple(new_tops)

    start = tuple(jnp.full((1, tokens), MASKED, F32) for _ in range(GROUP))
    tops = lax.fori_loop(first, last, score_block, start)
    mix_ref[...] = jnp.zeros_like(mix_ref)

    def mix_block(block, totals):
        pairs = pair_ref[key_rows(block), :]
        new_totals = []
        for head in range(GROUP):
            terms = jnp.exp(score_ref[head, key_rows(block - first), :] - tops[head])
            new_totals.append(totals[head] + jnp.sum(terms, axis=0, keepdims=True))
            mix_ref[head] += dot(pairs, terms.astype(BF), 0, 0)
        return tuple(new_totals)

    start = tuple(jnp.zeros((1, tokens), F32) for _ in range(GROUP))
    totals = lax.fori_loop(first, last, mix_block, start)
    mixed = jnp.concatenate(
        [mix_ref[head, HD:, :] / totals[head] for head in range(GROUP)], axis=0
    )
    out_ref[...] = mixed.T.astype(BF)
    for head in range(GROUP):
        log_ref[head : head + 1, :] = tops[head] + jnp.log(totals[head])


def attend_back_kernel(
    bounds, query_ref, grad_ref, pair_ref, low_ref, log_ref, dquery_ref, dpair_ref, prob_ref, dprob_ref, dmix_ref
):
    step = pl.program_id(1)
    place = pl.program_id(0) * pl.num_programs(1) + step
    first, last, query_first = bounds[0, place], bounds[1, place], bounds[2, place]
    tokens = query_ref.shape[0]
    blank = jnp.zeros((HD, tokens), BF)
    queries = [jnp.concatenate([rows, blank], axis=0) for rows in head_rows(query_ref[...])]
    grads = [jnp.concatenate([blank, rows], axis=0) for rows in head_rows(grad_ref[...])]

    @pl.when(step == 0)
    def _():
        dpair_ref[...] = jnp.zeros_like(dpair_ref)

    def prob_block(block, inners):
        pairs = pair_ref[key_rows(block), :]
        allowed = allowed_entries(block, low_ref, query_first)
        new_inners = []
        for head in range(GROUP):
            scores = dot(pairs, queries[head], 1, 0)
            probs = jnp.where(allowed, jnp.exp(scores - log_ref[head : head + 1, :]), 0.0)
            dprobs = dot(pairs, grads[head], 1, 0)
            prob_ref[head, key_rows(block - first), :] = probs
            dprob_ref[head, key_rows(block - first), :] = dprobs
            new_inners.append(inners[head] + jnp.sum(probs * dprobs, axis=0, keepdims=True))
        return tuple(new_inners)

    start = tuple(jnp.zeros((1, tokens), F32) for _ in range(GROUP))
    inners = lax.fori_loop(first, last, prob_block, start)
    dmix_ref[...] = jnp.zeros_like(dmix_ref)
    all_queries = jnp.concatenate(queries, axis=1)
    all_grads = jnp.concatenate(grads, axis=1)

    def back_block(block, carry):
        rows = key_rows(block)
        pairs = pair_ref[rows, :]
        all_probs, all_scores = [], []
        for head in range(GROUP):
            probs = prob_ref[head, key_rows(block - first), :]
            dprobs = dprob_ref[head, key_rows(block - first), :]
            dscores = (probs * (dprobs - inners[head])).astype(BF)
            dmix_ref[head] += dot(pairs, dscores, 0, 0)
            all_probs.append(probs.astype(BF))
            all_scores.append(dscores)
        dpair_ref[rows, :] += dot(jnp.concatenate(all_scores, axis=1), all_queries, 1, 1) + dot(
            jnp.concatenate(all_probs, axis=1), all_grads, 1, 1
        )
        return carry

    lax.fori_loop(first, last, back_block, 0)
    dquery = jnp.concatenate([dmix_ref[head, :HD, :] for head in range(GROUP)], axis=0)
    dquery_ref[...] = dquery.T * SCALE


def attend(queries, pairs, low, bounds):
    tokens, width = queries.shape
    replicas, slots, _ = pairs.shape
    rows = low.shape[2]
    blocks = low.shape[0] // replicas
    span = LMAX + KEYS
    return pl.pallas_call(
        attend_kernel,
        grid_spec=pltpu.PrefetchScalarGridSpec(
            num_scalar_prefetch=1,
            grid=(replicas, blocks),
            in_specs=[
                pl.BlockSpec((rows, GROUP * HD), lambda rep, block, _: (rep * blocks + block, 0)),
                pl.BlockSpec((None, slots, 2 * HD), lambda rep, block, _: (rep, 0, 0)),
                pl.BlockSpec((None, 1, rows), lambda rep, block, _: (rep * blocks + block, 0, 0)),
            ],
            out_specs=[
                pl.BlockSpec((rows, GROUP * HD), lambda rep, block, _: (rep * blocks + block, 0)),
                pl.BlockSpec((None, None, GROUP, rows), lambda rep, block, _: (rep, block, 0, 0)),
            ],
            scratch_shapes=[
                pltpu.VMEM((GROUP, span, rows), F32),
                pltpu.VMEM((GROUP, 2 * HD, rows), F32),
            ],
        ),
        out_shape=[
            jax.ShapeDtypeStruct((tokens, width), BF),
            jax.ShapeDtypeStruct((replicas, blocks, GROUP, rows), F32),
        ],
        compiler_params=pltpu.CompilerParams(vmem_limit_bytes=48 * 2**20),
        cost_estimate=pl.CostEstimate(flops=3 * 10**9, bytes_accessed=8 * 2**20, transcendentals=5 * 10**6),
        name="attend",
    )(bounds, queries, pairs, low)


def attend_back(queries, grads, pairs, low, log_total, bounds):
    tokens, width = queries.shape
    replicas, slots, _ = pairs.shape
    rows = low.shape[2]
    blocks = low.shape[0] // replicas
    span = LMAX + KEYS
    return pl.pallas_call(
        attend_back_kernel,
        grid_spec=pltpu.PrefetchScalarGridSpec(
            num_scalar_prefetch=1,
            grid=(replicas, blocks),
            in_specs=[
                pl.BlockSpec((rows, GROUP * HD), lambda rep, block, _: (rep * blocks + block, 0)),
                pl.BlockSpec((rows, GROUP * HD), lambda rep, block, _: (rep * blocks + block, 0)),
                pl.BlockSpec((None, slots, 2 * HD), lambda rep, block, _: (rep, 0, 0)),
                pl.BlockSpec((None, 1, rows), lambda rep, block, _: (rep * blocks + block, 0, 0)),
                pl.BlockSpec((None, None, GROUP, rows), lambda rep, block, _: (rep, block, 0, 0)),
            ],
            out_specs=[
                pl.BlockSpec((rows, GROUP * HD), lambda rep, block, _: (rep * blocks + block, 0)),
                pl.BlockSpec((None, slots, 2 * HD), lambda rep, block, _: (rep, 0, 0)),
            ],
            scratch_shapes=[
                pltpu.VMEM((GROUP, span, rows), F32),
                pltpu.VMEM((GROUP, span, rows), F32),
                pltpu.VMEM((GROUP, 2 * HD, rows), F32),
            ],
        ),
        out_shape=[
            jax.ShapeDtypeStruct((tokens, width), F32),
            jax.ShapeDtypeStruct((replicas, slots, 2 * HD), F32),
        ],
        compiler_params=pltpu.CompilerParams(vmem_limit_bytes=48 * 2**20),
        cost_estimate=pl.CostEstimate(flops=8 * 10**9, bytes_accessed=12 * 2**20, transcendentals=5 * 10**6),
        name="attend_back",
    )(bounds, queries, grads, pairs, low, log_total)


PIECES = 4


def takes(micros):
    return pl.CostEstimate(flops=1, bytes_accessed=int(micros * 3.6e6), transcendentals=0)


def params(collective_id):
    return pltpu.CompilerParams(
        collective_id=collective_id, has_side_effects=True, vmem_limit_bytes=60 * 2**20
    )


def tile(index, width):
    return pl.ds(pl.multiple_of(index * width, width), width)


HBM = pl.BlockSpec(memory_space=pl.ANY)
VMEM = pl.BlockSpec(memory_space=pltpu.VMEM)


def exchange_kernel(token_ref, gain_ref, source_ref, normed_ref, gains_ref, held, held_gains, send_sems, recv_sems, local_sems):
    rows, row = lax.axis_size("row"), lax.axis_index("row")
    sub, width = held.shape[0], token_ref.shape[1]
    partners = [lax.rem(row + shift, rows) for shift in range(1, rows)]
    meet([{"row": partner} for partner in partners])
    own_cols = tile(row, width)
    copies = []
    for shift, partner in enumerate(partners):
        for index, (source, target) in enumerate(
            ((token_ref.at[tile(partner, sub)], held), (gain_ref, held_gains))
        ):
            copy = pltpu.make_async_remote_copy(
                src_ref=source,
                dst_ref=target.at[:, own_cols],
                send_sem=send_sems.at[index, shift],
                recv_sem=recv_sems.at[index, shift],
                device_id={"row": partner},
                device_id_type=MESH,
            )
            copy.start()
            copies.append(copy)
    for index, (source, target) in enumerate(((token_ref.at[tile(row, sub)], held), (gain_ref, held_gains))):
        copy = pltpu.make_async_copy(source, target.at[:, own_cols], local_sems.at[index])
        copy.start()
        copies.append(copy)
    for copy in copies:
        copy.wait()
    source_ref[...] = held[...]
    gains_ref[...] = held_gains[...]
    source = held[...].astype(F32)
    scaling = lax.rsqrt(jnp.mean(source * source, axis=1, keepdims=True) + EPS_NORM)
    normed_ref[...] = (source * scaling * held_gains[0:1, :]).astype(BF)


def exchange(tokens, gains, rows):
    sub, width = tokens.shape[0] // rows, tokens.shape[1]
    return pl.pallas_call(
        exchange_kernel,
        out_shape=[
            jax.ShapeDtypeStruct((sub, rows * width), BF),
            jax.ShapeDtypeStruct((sub, rows * width), BF),
            jax.ShapeDtypeStruct((gains.shape[0], rows * width), F32),
        ],
        in_specs=[VMEM, VMEM],
        out_specs=[VMEM, VMEM, VMEM],
        scratch_shapes=[
            pltpu.VMEM((sub, rows * width), BF),
            pltpu.VMEM((gains.shape[0], rows * width), F32),
            pltpu.SemaphoreType.DMA((2, rows - 1)),
            pltpu.SemaphoreType.DMA((2, rows - 1)),
            pltpu.SemaphoreType.DMA((2,)),
        ],
        compiler_params=params(1),
        cost_estimate=takes(30),
        name="exchange",
    )(tokens, gains)


def gather_scratch(sub):
    return [
        pltpu.VMEM((2 * COLS, sub, D), BF),
        pltpu.SemaphoreType.DMA((len(GATHER_KINDS), PIECES)),
        pltpu.SemaphoreType.DMA((len(GATHER_KINDS), PIECES)),
        pltpu.SemaphoreType.DMA((2 * COLS,)),
    ]


def gather_call(kernel, own, weights, outs, collective_id, micros, name):
    sub = own.shape[0]
    blocks = 2 * COLS
    return pl.pallas_call(
        kernel,
        out_shape=[jax.ShapeDtypeStruct((blocks, sub, D), BF)]
        + [jax.ShapeDtypeStruct((blocks, sub, width), kind) for width, kind in outs],
        in_specs=[VMEM] * (1 + len(weights)),
        out_specs=[HBM] * (1 + len(outs)),
        scratch_shapes=gather_scratch(sub)
        + [pltpu.VMEM((2, sub, width), kind) for width, kind in outs]
        + [pltpu.SemaphoreType.DMA((2,)) for _ in outs],
        compiler_params=params(collective_id),
        cost_estimate=takes(micros),
        name=name,
    )(own, *weights)


def project_kernel(reps, own_ref, weight_ref, all_ref, proj_ref, held, send_sems, recv_sems, out_sems, slots, slot_sems):
    pending, copies = {}, []

    def use(step, block, ref):
        copy = pltpu.make_async_copy(ref, all_ref.at[block], out_sems.at[step])
        copy.start()
        copies.append(copy)

        def value_of(slot):
            slot[...] = dot(ref[...], weight_ref[...], 1, 0)

        stage(step, block, value_of, slots, proj_ref, slot_sems, pending)

    run_gather(reps, PIECES, own_ref, held, send_sems, recv_sems, use)
    for copy in copies + [pending[6], pending[7]]:
        copy.wait()


def back_out_kernel(reps, own_ref, weight_ref, all_ref, grad_ref, held, send_sems, recv_sems, out_sems, slots, slot_sems):
    pending, copies = {}, []
    rows, _, width = weight_ref.shape

    def use(step, block, ref):
        copy = pltpu.make_async_copy(ref, all_ref.at[block], out_sems.at[step])
        copy.start()
        copies.append(copy)

        def value_of(slot):
            total = dot(ref[:, :width], weight_ref[0], 1, 1)
            for part in range(1, rows):
                total += dot(ref[:, part * width : (part + 1) * width], weight_ref[part], 1, 1)
            slot[...] = total.astype(BF)

        stage(step, block, value_of, slots, grad_ref, slot_sems, pending)

    run_gather(reps, PIECES, own_ref, held, send_sems, recv_sems, use)
    for copy in copies + [pending[6], pending[7]]:
        copy.wait()


def forward_kernel(
    reps, own_ref, gate_w_ref, up_w_ref, all_ref, gate_ref, up_ref, hidden_ref,
    held, send_sems, recv_sems, out_sems, gates, ups, hiddens, gate_sems, up_sems, hidden_sems,
):
    pending, copies = {}, []
    span = 256

    def use(step, block, ref):
        copy = pltpu.make_async_copy(ref, all_ref.at[block], out_sems.at[step])
        copy.start()
        copies.append(copy)
        slot = step % 2
        outs = ((gates, gate_ref, gate_sems), (ups, up_ref, up_sems), (hiddens, hidden_ref, hidden_sems))
        if step >= 2:
            for copy in pending[step - 2]:
                copy.wait()

        def one_tile(index, carry):
            columns = tile(index, span)
            gate = dot(ref[...], gate_w_ref[:, columns], 1, 0)
            up = dot(ref[...], up_w_ref[:, columns], 1, 0)
            gates[slot, :, columns] = gate
            ups[slot, :, columns] = up
            hiddens[slot, :, columns] = (gate * jax.nn.sigmoid(gate) * up).astype(BF)
            return carry

        lax.fori_loop(0, gate_w_ref.shape[1] // span, one_tile, 0)
        pending[step] = []
        for slots, target, sems in outs:
            copy = pltpu.make_async_copy(slots.at[slot], target.at[block], sems.at[slot])
            copy.start()
            pending[step].append(copy)

    run_gather(reps, PIECES, own_ref, held, send_sems, recv_sems, use)
    for copy in copies + pending[6] + pending[7]:
        copy.wait()


def scatter_scratch(sub):
    return [
        pltpu.VMEM((4, sub, D), F32),
        pltpu.VMEM((4, sub, D), BF),
        pltpu.VMEM((4, sub, D), BF),
        pltpu.VMEM((3, sub, D), BF),
        pltpu.VMEM((3, sub, D), BF),
        pltpu.SemaphoreType.DMA((4,)),
        pltpu.SemaphoreType.DMA((4,)),
        pltpu.SemaphoreType.DMA((3, PIECES)),
        pltpu.SemaphoreType.DMA((3, PIECES)),
    ]


def mix_out_kernel(reps, attended_ref, weight_ref, source_ref, gains_ref, middle_ref, normed_ref, *scratch):
    parts, _, width = weight_ref.shape

    def partial(step, block, put):
        for part in range(parts):
            put(pl.ds(part * width, width), dot(attended_ref[block], weight_ref[part], 1, 0))

    def finish(rows, value):
        middle = source_ref[rows, :].astype(F32) + value
        middle_ref[rows, :] = middle
        scaling = lax.rsqrt(jnp.mean(middle * middle, axis=1, keepdims=True) + EPS_NORM)
        normed_ref[rows, :] = (middle * scaling * gains_ref[1:2, :]).astype(BF)

    run_scatter(reps, PIECES, partial, finish, *scratch[:5], scratch[5:])


def mix_out(attended, weight, source, gains, reps):
    sub = source.shape[0]
    return pl.pallas_call(
        functools.partial(mix_out_kernel, reps),
        out_shape=[jax.ShapeDtypeStruct((sub, D), F32), jax.ShapeDtypeStruct((sub, D), BF)],
        in_specs=[VMEM] * 4,
        out_specs=[VMEM] * 2,
        scratch_shapes=scatter_scratch(sub),
        compiler_params=params(3),
        cost_estimate=takes(40),
        name="mix_out",
    )(attended, weight, source, gains)


def norm_back(value, vectors, gain):
    scaling = lax.rsqrt(jnp.mean(vectors * vectors, axis=1, keepdims=True) + EPS_NORM)
    unit = vectors * scaling
    weighted = value * gain
    inner = jnp.mean(weighted * unit, axis=1, keepdims=True)
    return scaling * (weighted - unit * inner), jnp.sum(value * unit, axis=0, keepdims=True)


def backward_kernel(
    reps, gate_ref, up_ref, top_ref, gate_w_ref, up_w_ref, down_w_ref, middle_ref, own_top_ref, gains_ref,
    ggate_ref, gup_ref, grad_ref, low_ref, gain_ref,
    total, give, take, hop_out, hop_in, swap_send, swap_recv, hop_send, hop_recv,
    gates, ups, tops, ggates, gups, in_sems, out_sems,
):
    where = plane(reps)
    order = [where[kind][0] for kind in ("SD", "D", "SQ", "Q", "SP", "P", "SO", "O")]
    parts, inner_width, width = down_w_ref.shape
    span, loads, stores = 256, {}, {}

    def load(step):
        slot, loads[step] = step % 2, []
        for index, (source, target) in enumerate(((gate_ref, gates), (up_ref, ups), (top_ref, tops))):
            copy = pltpu.make_async_copy(source.at[order[step]], target.at[slot], in_sems.at[index, slot])
            copy.start()
            loads[step].append(copy)

    load(0)
    gain_ref[...] = jnp.zeros_like(gain_ref)

    def partial(step, block, put):
        slot = step % 2
        for copy in loads[step]:
            copy.wait()
        if step < 7:
            load(step + 1)
        if step >= 2:
            for copy in stores[step - 2]:
                copy.wait()

        def one_tile(index, carry):
            columns = tile(index, span)
            grad = dot(tops[slot, :, :width], down_w_ref[0, columns, :], 1, 1)
            for part in range(1, parts):
                grad += dot(tops[slot, :, part * width : (part + 1) * width], down_w_ref[part, columns, :], 1, 1)
            gate = gates[slot, :, columns]
            up = ups[slot, :, columns]
            sigma = jax.nn.sigmoid(gate)
            ggates[slot, :, columns] = (grad * up * sigma * (1.0 + gate * (1.0 - sigma))).astype(BF)
            gups[slot, :, columns] = (grad * gate * sigma).astype(BF)
            return carry

        lax.fori_loop(0, inner_width // span, one_tile, 0)
        stores[step] = []
        for index, (source, target) in enumerate(((ggates, ggate_ref), (gups, gup_ref))):
            copy = pltpu.make_async_copy(source.at[slot], target.at[block], out_sems.at[index, slot])
            copy.start()
            stores[step].append(copy)

        def out_tile(index, carry):
            columns = tile(index, span)
            put(
                columns,
                dot(ggates[slot], gate_w_ref[columns, :], 1, 1) + dot(gups[slot], up_w_ref[columns, :], 1, 1),
            )
            return carry

        lax.fori_loop(0, D // span, out_tile, 0)

    def finish(rows, value):
        back, gain_part = norm_back(value, middle_ref[rows, :], gains_ref[1:2, :])
        grad = own_top_ref[rows, :].astype(F32) + back
        grad_ref[rows, :] = grad
        low_ref[rows, :] = grad.astype(BF)
        gain_ref[0:1, :] += gain_part

    run_scatter(
        reps, PIECES, partial, finish, total, give, take, hop_out, hop_in,
        (swap_send, swap_recv, hop_send, hop_recv),
    )
    for copy in stores[6] + stores[7]:
        copy.wait()


def feed_back(gate, up, top, gate_w, up_w, down_w, middle, own_top, gains, reps):
    blocks, sub, width = gate.shape
    return pl.pallas_call(
        functools.partial(backward_kernel, reps),
        out_shape=[
            jax.ShapeDtypeStruct((blocks, sub, width), BF),
            jax.ShapeDtypeStruct((blocks, sub, width), BF),
            jax.ShapeDtypeStruct((sub, D), F32),
            jax.ShapeDtypeStruct((sub, D), BF),
            jax.ShapeDtypeStruct((8, D), F32),
        ],
        in_specs=[HBM] * 3 + [VMEM] * 6,
        out_specs=[HBM] * 2 + [VMEM] * 3,
        scratch_shapes=scatter_scratch(sub)
        + [
            pltpu.VMEM((2, sub, width), F32),
            pltpu.VMEM((2, sub, width), F32),
            pltpu.VMEM((2, sub, D), BF),
            pltpu.VMEM((2, sub, width), BF),
            pltpu.VMEM((2, sub, width), BF),
            pltpu.SemaphoreType.DMA((3, 2)),
            pltpu.SemaphoreType.DMA((2, 2)),
        ],
        compiler_params=params(5),
        cost_estimate=takes(45),
        name="feed_back",
    )(gate, up, top, gate_w, up_w, down_w, middle, own_top, gains)


def project_back_kernel(reps, grad_ref, weight_ref, source_ref, middle_ref, gains_ref, resid_ref, gain_ref, *scratch):
    span = 512
    gain_ref[...] = jnp.zeros_like(gain_ref)

    def partial(step, block, put):
        for index in range(D // span):
            columns = pl.ds(index * span, span)
            put(columns, dot(grad_ref[block], weight_ref[columns, :], 1, 1))

    def finish(rows, value):
        back, gain_part = norm_back(value, source_ref[rows, :].astype(F32), gains_ref[0:1, :])
        resid_ref[rows, :] = (middle_ref[rows, :] + back).astype(BF)
        gain_ref[0:1, :] += gain_part

    run_scatter(reps, PIECES, partial, finish, *scratch[:5], scratch[5:])


def project_back(grad_proj, weight, source, grad_middle, gains, reps):
    sub = source.shape[0]
    return pl.pallas_call(
        functools.partial(project_back_kernel, reps),
        out_shape=[jax.ShapeDtypeStruct((sub, D), BF), jax.ShapeDtypeStruct((8, D), F32)],
        in_specs=[VMEM] * 5,
        out_specs=[VMEM] * 2,
        scratch_shapes=scatter_scratch(sub),
        compiler_params=params(7),
        cost_estimate=takes(40),
        name="project_back",
    )(grad_proj, weight, source, grad_middle, gains)


def adamw(weights, gradient, moment, square, step_rate, decay_rate):
    gradient = gradient.astype(F32)
    moment_new = BETA_ONE * moment + (1.0 - BETA_ONE) * gradient
    square_new = BETA_TWO * square + (1.0 - BETA_TWO) * gradient * gradient
    moment_hat = moment_new / (1.0 - BETA_ONE**STEP)
    square_hat = square_new / (1.0 - BETA_TWO**STEP)
    weights_new = weights - step_rate * (
        moment_hat / (jnp.sqrt(square_hat) + ADAM_EPS) + decay_rate * weights
    )
    return (weights_new, moment_new, square_new)


def local(
    resid_in,
    cotangent,
    seq_lens,
    qkv_weight,
    qkv_moment,
    qkv_square,
    out_weight,
    out_moment,
    out_square,
    gate_weight,
    gate_moment,
    gate_square,
    up_weight,
    up_moment,
    up_square,
    down_weight,
    down_moment,
    down_square,
    norm_gains,
    gain_moment,
    gain_square,
):
    cols, rows, replicas = lax.axis_size("col"), lax.axis_size("row"), lax.axis_size("dp")
    reps = replicas // 2
    half = lax.axis_index("dp") // reps
    row, col = lax.axis_index("row"), lax.axis_index("col")
    chunk = resid_in.shape[0]
    slots = chunk * cols
    sub = chunk // rows
    blocks = 2 * cols
    plane_tokens = sub * blocks

    lengths = both_halves(seq_lens, partner_swap(seq_lens, reps), half, 0)
    ends = jnp.cumsum(lengths, axis=1, dtype=jnp.int32)
    firsts = jnp.arange(cols, dtype=jnp.int32) * chunk + row * sub
    slot = (firsts[:, None] + jnp.arange(sub, dtype=jnp.int32)[None, :]).reshape(1, cols * sub)
    passed = (slot[:, :, None] >= ends[:, None, :]).astype(jnp.int32)
    seq_start = jnp.sum(passed * lengths[:, None, :], axis=2, dtype=jnp.int32)
    usable = slot < ends[:, -1:]
    cosine, sine = rope_tables((slot - seq_start).reshape(plane_tokens))
    low = jnp.where(usable, seq_start, slot).reshape(blocks, 1, sub)
    firsts = jnp.concatenate([firsts, firsts])
    bounds = jnp.stack([low[:, 0, 0] // KEYS, (firsts + sub - 1) // KEYS + 1, firsts]).astype(jnp.int32)
    usable_mine = lax.dynamic_slice_in_dim(usable.reshape(plane_tokens), (half * cols + col) * sub, sub, 0)

    qkv_w = gather_in_block(qkv_weight, reps)
    out_w = gather_tall(out_weight, reps)
    gate_w = gather_in_block(gate_weight, reps)
    up_w = gather_in_block(up_weight, reps)
    down_w = gather_tall(down_weight, reps)

    padded = jnp.concatenate([norm_gains, jnp.zeros((6, norm_gains.shape[1]), F32)])
    source, normed_own, gains = exchange(resid_in, padded, rows)
    head_width = (GROUP + 2) * HD
    normed_one, projected = gather_call(
        functools.partial(project_kernel, reps), normed_own, [qkv_w], [(head_width, F32)], 2, 36, "project"
    )
    parts = projected.reshape(plane_tokens, 1, GROUP + 2, HD)
    turned = rotate(parts[:, :, : GROUP + 1], cosine, sine).astype(BF)
    queries = (turned[:, :, :GROUP] * BF(SCALE)).reshape(plane_tokens, GROUP * HD)
    pairs = jnp.concatenate([turned[:, :, GROUP], parts[:, :, GROUP + 1].astype(BF)], axis=2)
    pairs = lax.all_gather(pairs.reshape(blocks, sub, 2 * HD), "row", axis=0)
    pairs = pairs.reshape(rows, 2, cols, sub, 2 * HD).transpose(1, 2, 0, 3, 4).reshape(2, slots, 2 * HD)
    attended, log_total = attend(queries, pairs, low, bounds)
    middle, normed_own = mix_out(attended.reshape(blocks, sub, GROUP * HD), out_w, source, gains, reps)

    grad_top = lax.all_to_all(cotangent, "row", split_axis=0, concat_axis=1, tiled=True)
    grad_top = jnp.where(usable_mine[:, None], grad_top, jnp.zeros((), BF))
    grad_top_all = plane_gather(grad_top, reps)
    inner = gate_w.shape[1]
    normed_two, gate_val, up_val, hidden = gather_call(
        functools.partial(forward_kernel, reps), normed_own, [gate_w, up_w],
        [(inner, F32), (inner, F32), (inner, BF)], 4, 38, "feed_forward",
    )
    normed_two = normed_two.reshape(plane_tokens, D)
    hidden = hidden.reshape(plane_tokens, inner)
    grad_down = scatter_tall(dot(hidden, grad_top_all, 0, 0), reps)
    grad_gate_val, grad_up_val, grad_middle, grad_middle_own, gain_grad_two = feed_back(
        gate_val, up_val, grad_top_all.reshape(blocks, sub, D), gate_w, up_w, down_w, middle, grad_top, gains, reps
    )
    grad_gate = scatter_in_block(dot(normed_two, grad_gate_val.reshape(plane_tokens, inner), 0, 0), reps)
    grad_up = scatter_in_block(dot(normed_two, grad_up_val.reshape(plane_tokens, inner), 0, 0), reps)
    lifted = plane_scatter(dot(hidden, down_w.swapaxes(0, 1).reshape(inner, D), 1, 0).astype(BF), reps)
    result = (middle + lifted.astype(F32)).astype(BF)
    result = lax.all_to_all(result, "row", split_axis=1, concat_axis=0, tiled=True)

    grad_middle_all, grad_attended = gather_call(
        functools.partial(back_out_kernel, reps), grad_middle_own, [out_w], [(GROUP * HD, BF)], 6, 36, "back_out"
    )
    grad_attended = grad_attended.reshape(plane_tokens, GROUP * HD)
    grad_query, grad_pairs = attend_back(queries, grad_attended, pairs, low, log_total, bounds)
    grad_pairs = grad_pairs.astype(BF).reshape(2, cols, rows, sub, 2 * HD).transpose(2, 0, 1, 3, 4)
    grad_pairs = lax.psum_scatter(
        grad_pairs.reshape(rows, plane_tokens, 2 * HD), "row", scatter_dimension=0, tiled=False
    )
    grad_pairs = grad_pairs.astype(F32).reshape(plane_tokens, 1, 2, HD)
    grad_turned = jnp.concatenate(
        [grad_query.reshape(plane_tokens, 1, GROUP, HD), grad_pairs[:, :, :1]], axis=2
    )
    grad_proj = jnp.concatenate([rotate_back(grad_turned, cosine, sine), grad_pairs[:, :, 1:]], axis=2)
    grad_proj = grad_proj.astype(BF).reshape(plane_tokens, head_width)
    resid_grad, gain_grad_one = project_back(
        grad_proj.reshape(blocks, sub, head_width), qkv_w, source, grad_middle, gains, reps
    )
    grad_out = scatter_tall(dot(attended, grad_middle_all.reshape(plane_tokens, D), 0, 0), reps)
    grad_qkv = scatter_in_block(dot(normed_one.reshape(plane_tokens, D), grad_proj, 0, 0), reps)
    resid_grad = lax.all_to_all(resid_grad, "row", split_axis=1, concat_axis=0, tiled=True).astype(F32)

    gain_grads = lax.psum(jnp.concatenate([gain_grad_one[:1], gain_grad_two[:1]]), ("dp", "row", "col"))
    gain_grads = lax.dynamic_slice_in_dim(gain_grads, row * norm_gains.shape[1], norm_gains.shape[1], 1)
    qkv_set = adamw(qkv_weight, grad_qkv, qkv_moment, qkv_square, RATE_MATRIX, WEIGHT_DECAY)
    out_set = adamw(out_weight, grad_out, out_moment, out_square, RATE_OUTPUT, WEIGHT_DECAY)
    gate_set = adamw(gate_weight, grad_gate, gate_moment, gate_square, RATE_MATRIX, WEIGHT_DECAY)
    up_set = adamw(up_weight, grad_up, up_moment, up_square, RATE_MATRIX, WEIGHT_DECAY)
    down_set = adamw(down_weight, grad_down, down_moment, down_square, RATE_MATRIX, WEIGHT_DECAY)
    gain_set = adamw(norm_gains, gain_grads, gain_moment, gain_square, RATE_GAIN, 0.0)
    return (result, resid_grad, *qkv_set, *out_set, *gate_set, *up_set, *down_set, *gain_set)


def solution(mesh):
    tokens = P(("dp", "col"), "row")
    wide = P(("row", "dp"), "col")
    tall = P(("col", "dp"), "row")
    gain = P(None, "row")
    weights = (wide,) * 3 + (tall,) * 3 + (wide,) * 6 + (tall,) * 3 + (gain,) * 3
    return jax.shard_map(
        local,
        mesh=mesh,
        in_specs=(tokens, tokens, P("dp", None)) + weights,
        out_specs=(tokens, tokens) + weights,
        check_vma=False,
    )
```

```python
import functools

import jax
import jax.numpy as jnp
from jax import lax
from jax.experimental import pallas as pl
from jax.experimental.pallas import tpu as pltpu
from jax.sharding import PartitionSpec as P

D = 2048
FF = 8192
HD = 64
GROUP = 4
LMAX = 1024
STEP = 10
KEYS = 256
SLICES = 2
PIECES = 4
COLS = 4

EPS_NORM = 1e-05
ROPE_BASE = 500000.0
BETA_ONE = 0.9
BETA_TWO = 0.95
ADAM_EPS = 1e-08
WEIGHT_DECAY = 0.1
RATE_MATRIX = 0.05
RATE_OUTPUT = 0.4
RATE_GAIN = 0.8
MASKED = -1e30
SCALE = HD ** (-0.5)

BF = jnp.bfloat16
F32 = jnp.float32


def dot(left, right, left_dim, right_dim):
    return lax.dot_general(
        left, right, (((left_dim,), (right_dim,)), ((), ())), preferred_element_type=F32
    )


def half_groups(reps):
    return [[rep, rep + reps] for rep in range(reps)]


def rep_groups(reps):
    return [[half * reps + rep for rep in range(reps)] for half in range(2)]


def partner_swap(values_in, reps):
    pairs = [pair for rep in range(reps) for pair in ((rep, rep + reps), (rep + reps, rep))]
    return lax.ppermute(values_in, "dp", pairs)


def both_halves(mine, theirs, half, axis):
    first = jnp.where(half == 0, mine, theirs)
    second = jnp.where(half == 0, theirs, mine)
    return jnp.concatenate([first, second], axis=axis)


def half_columns(weight, reps):
    half = lax.axis_index("dp") // reps
    own, width = weight.shape[0], weight.shape[1] // 2
    low = weight.astype(BF)
    mine = lax.dynamic_slice_in_dim(low, half * width, width, 1)
    theirs = partner_swap(lax.dynamic_slice_in_dim(low, (1 - half) * width, width, 1), reps)
    both = both_halves(mine, theirs, half, 0)
    if reps > 1:
        both = lax.all_gather(both, "dp", axis=0, axis_index_groups=rep_groups(reps))
        both = both.reshape(reps, 2, own, width).swapaxes(0, 1).reshape(2 * reps * own, width)
    return both


def own_rows(part, reps):
    half = lax.axis_index("dp") // reps
    height = part.shape[0] // 2
    mine = lax.dynamic_slice_in_dim(part, half * height, height, 0)
    theirs = partner_swap(lax.dynamic_slice_in_dim(part, (1 - half) * height, height, 0), reps)
    part = both_halves(mine, theirs, half, 1)
    if reps > 1:
        part = lax.psum_scatter(
            part, "dp", scatter_dimension=0, tiled=True, axis_index_groups=rep_groups(reps)
        )
    return part


def tall_block(weight, reps):
    own = weight.astype(BF)
    if reps > 1:
        own = lax.all_gather(own, "dp", axis=0, tiled=True, axis_index_groups=rep_groups(reps))
    return own


def own_tall(part, reps):
    if reps > 1:
        part = lax.psum_scatter(
            part, "dp", scatter_dimension=0, tiled=True, axis_index_groups=rep_groups(reps)
        )
    return part


def row_blocks(matrix, rows):
    return matrix.reshape(matrix.shape[0], rows, -1).swapaxes(0, 1)


def rope_tables(position):
    exponent = jnp.arange(0, HD, 2, dtype=F32) / HD
    freq_table = 1.0 / ROPE_BASE**exponent
    angle = position.astype(F32)[:, None] * freq_table[None, :]
    cosine = jnp.cos(angle)
    sine = jnp.sin(angle)
    return (jnp.concatenate([cosine] * 4, axis=1), jnp.concatenate([-sine, sine, -sine, sine], axis=1))


def rotate(vectors, cosine, sine):
    width = vectors.shape[1]
    lane = lax.broadcasted_iota(jnp.int32, vectors.shape, 1)
    lower = lax.rem(lane, HD) < HD // 2
    turned = jnp.where(
        lower, pltpu.roll(vectors, width - HD // 2, 1), pltpu.roll(vectors, HD // 2, 1)
    )
    copies = width // cosine.shape[1]
    cosine = jnp.concatenate([cosine] * copies, axis=1)
    sine = jnp.concatenate([sine] * copies, axis=1)
    return jnp.where(lane < (GROUP + 1) * HD, vectors * cosine + turned * sine, vectors)


MESH = pl.DeviceIdType.MESH
HBM = pl.BlockSpec(memory_space=pl.ANY)
VMEM = pl.BlockSpec(memory_space=pltpu.VMEM)
DMA = pltpu.SemaphoreType.DMA


def takes(micros):
    return pl.CostEstimate(flops=1, bytes_accessed=int(micros * 3.6e6), transcendentals=0)


def params(collective_id):
    return pltpu.CompilerParams(
        collective_id=collective_id, has_side_effects=True, vmem_limit_bytes=60 * 2**20
    )


def tile(index, width):
    return pl.ds(pl.multiple_of(index * width, width), width)


def plane(reps):
    replica, col = lax.axis_index("dp"), lax.axis_index("col")
    half, rep = lax.div(replica, reps), lax.rem(replica, reps)
    core = lax.rem(col, 2)
    other = col + 1 - 2 * core

    def place(half_of, col_of):
        chip = half_of * (COLS // 2) + lax.div(col_of, 2)
        return (chip, lax.rem(col_of, 2), {"dp": half_of * reps + rep, "col": col_of})

    def turn(value, by, modulus):
        return lax.rem(value + by, modulus)

    return {
        "O": place(half, col),
        "P": place(turn(half, 1 - core, 2), turn(col, 2 * core, COLS)),
        "Q": place(turn(half, core, 2), turn(col, 2 - 2 * core, COLS)),
        "D": place(1 - half, turn(col, 2, COLS)),
        "SO": place(half, other),
        "SP": place(turn(half, core, 2), turn(other, 2 - 2 * core, COLS)),
        "SQ": place(turn(half, 1 - core, 2), turn(other, 2 * core, COLS)),
        "SD": place(1 - half, turn(other, 2, COLS)),
    }


def near(reps):
    where = plane(reps)
    return [where["P"][2], where["Q"][2], where["SO"][2]]


def row_partners():
    rows, row = lax.axis_size("row"), lax.axis_index("row")
    return [lax.rem(row + shift, rows) for shift in range(1, rows)]


def meet(devices):
    barrier = pltpu.get_barrier_semaphore()
    for device in devices:
        pl.semaphore_signal(barrier, inc=1, device_id=device, device_id_type=MESH)
    pl.semaphore_wait(barrier, len(devices))


GATHER_KINDS = ("P", "Q", "D", "SO", "SP", "SQ", "SD")


def run_gather(reps, own_ref, held_ref, sems, use):
    send_sems, recv_sems, local_sem = sems
    where = plane(reps)
    sub = own_ref.shape[0]
    height = sub // PIECES

    def spot(kind, piece):
        chip, core, _ = where[kind]
        return held_ref.at[chip, pl.ds(pl.multiple_of(core * sub + piece * height, height), height)]

    def message(kind, piece, source, target, device):
        index = GATHER_KINDS.index(kind)
        return pltpu.make_async_remote_copy(
            src_ref=source,
            dst_ref=target,
            send_sem=send_sems.at[index, piece],
            recv_sem=recv_sems.at[index, piece],
            device_id=device,
            device_id_type=MESH,
        )

    near_p, near_q, sibling = where["P"][2], where["Q"][2], where["SO"][2]
    sent = []

    def send(kind, piece, source, held_by, device):
        copy = message(kind, piece, source, spot(held_by, piece), device)
        copy.start()
        sent.append(copy)

    def arrive(kind, piece):
        message(kind, piece, spot(kind, piece), spot(kind, piece), sibling).wait_recv()

    own_copy = pltpu.make_async_copy(own_ref, held_ref.at[where["O"][0], tile(where["O"][1], sub)], local_sem)
    own_copy.start()
    for piece in range(PIECES):
        source = own_ref.at[pl.ds(piece * height, height)]
        send("P", piece, source, "O", near_p)
        send("Q", piece, source, "O", near_q)
        send("SO", piece, source, "O", sibling)
    own_copy.wait()
    for piece in range(PIECES):
        arrive("SO", piece)
    use(0, where["O"][0])
    for piece in range(PIECES):
        arrive("P", piece)
        send("D", piece, spot("P", piece), "P", near_q)
        send("SP", piece, spot("P", piece), "P", sibling)
    for piece in range(PIECES):
        arrive("Q", piece)
        send("SQ", piece, spot("Q", piece), "Q", sibling)
    for piece in range(PIECES):
        arrive("SQ", piece)
    use(1, where["P"][0])
    for piece in range(PIECES):
        arrive("SP", piece)
    use(2, where["Q"][0])
    for piece in range(PIECES):
        arrive("D", piece)
        send("SD", piece, spot("D", piece), "D", sibling)
    for piece in range(PIECES):
        arrive("SD", piece)
    use(3, where["D"][0])
    for copy in sent:
        copy.wait_send()


def gather_scratch(sub):
    count = len(GATHER_KINDS)
    return [pltpu.VMEM((COLS, 2 * sub, D), BF), DMA((count, PIECES)), DMA((count, PIECES)), DMA]


SCATTER_SWAPS = ("D", "Q", "P", "O")
SCATTER_HOPS = ("D", "Q", "P")


def scatter_order(reps):
    where = plane(reps)
    return [where[kind][0] for kind in SCATTER_SWAPS]


def run_scatter(reps, partial, finish, scratch):
    total_ref, give_ref, take_ref, hop_out, hop_in, both_ref, swap_send, swap_recv, hop_send, hop_recv = scratch
    where = plane(reps)
    core = where["O"][1]
    device = {"P": where["P"][2], "Q": where["Q"][2], "D": where["Q"][2]}
    sibling = where["SO"][2]
    sub = total_ref.shape[1]
    height = sub // PIECES
    sibling_kind = {"D": "D", "Q": "P", "P": "Q", "O": "O"}
    sent = []

    def swap(kind):
        index = SCATTER_SWAPS.index(kind)
        return pltpu.make_async_remote_copy(
            src_ref=give_ref.at[index],
            dst_ref=take_ref.at[index],
            send_sem=swap_send.at[index],
            recv_sem=swap_recv.at[index],
            device_id=sibling,
            device_id_type=MESH,
        )

    def hop(kind, piece):
        index = SCATTER_HOPS.index(kind)
        rows = pl.ds(piece * height, height)
        return pltpu.make_async_remote_copy(
            src_ref=hop_out.at[index, rows],
            dst_ref=hop_in.at[index, rows],
            send_sem=hop_send.at[index, piece],
            recv_sem=hop_recv.at[index, piece],
            device_id=device[kind],
            device_id_type=MESH,
        )

    def compute(step, kind):
        mine, theirs = SCATTER_SWAPS.index(kind), SCATTER_SWAPS.index(sibling_kind[kind])

        def put(columns, value):
            both_ref[...] = value
            total_ref[mine, :, columns] = both_ref[tile(core, sub), :]
            give_ref[theirs, :, columns] = both_ref[tile(1 - core, sub), :].astype(BF)

        partial(step, where[kind][0], put)
        copy = swap(sibling_kind[kind])
        copy.start()
        sent.append(copy)

    def settle(kind):
        index = SCATTER_SWAPS.index(kind)
        swap(kind).wait_recv()
        for piece in range(PIECES):
            rows = pl.ds(piece * height, height)
            value = total_ref[index, rows, :] + take_ref[index, rows, :].astype(F32)
            if kind == "P":
                hop("D", piece).wait_recv()
                value += hop_in[SCATTER_HOPS.index("D"), rows, :].astype(F32)
            if kind == "O":
                for source in ("Q", "P"):
                    hop(source, piece).wait_recv()
                    value += hop_in[SCATTER_HOPS.index(source), rows, :].astype(F32)
                finish(rows, value)
            else:
                hop_out[SCATTER_HOPS.index(kind), rows, :] = value.astype(BF)
                copy = hop(kind, piece)
                copy.start()
                sent.append(copy)

    compute(0, "D")
    compute(1, "Q")
    settle("D")
    compute(2, "P")
    settle("Q")
    compute(3, "O")
    settle("P")
    settle("O")
    for copy in sent:
        copy.wait_send()


SPAN = 512


def scatter_scratch(sub):
    return [
        pltpu.VMEM((4, sub, D), F32),
        pltpu.VMEM((4, sub, D), BF),
        pltpu.VMEM((4, sub, D), BF),
        pltpu.VMEM((3, sub, D), BF),
        pltpu.VMEM((3, sub, D), BF),
        pltpu.VMEM((2 * sub, SPAN), F32),
        DMA((4,)),
        DMA((4,)),
        DMA((3, PIECES)),
        DMA((3, PIECES)),
    ]


SCATTER_REFS = 10


def head_rows(block):
    turned = block.astype(F32).T
    return [turned[head * HD : (head + 1) * HD].astype(BF) for head in range(GROUP)]


def allowed_entries(key_block, low_ref, query_first):
    tokens = low_ref.shape[-1]
    key_slot = key_block * KEYS + lax.broadcasted_iota(jnp.int32, (KEYS, tokens), 0)
    query_slot = query_first + lax.broadcasted_iota(jnp.int32, (KEYS, tokens), 1)
    return (key_slot >= low_ref[...]) & (key_slot <= query_slot)


def key_rows(block):
    return pl.ds(pl.multiple_of(block * KEYS, KEYS), KEYS)


def attend_kernel(bounds, query_ref, pair_ref, low_ref, out_ref, log_ref, score_ref, mix_ref):
    step = pl.program_id(1)
    place = pl.program_id(0) * pl.num_programs(1) + step
    first, last, query_first = bounds[0, place], bounds[1, place], bounds[2, place]
    tokens = query_ref.shape[0]
    blank = jnp.zeros((HD, tokens), BF)
    queries = [jnp.concatenate([rows, blank], axis=0) for rows in head_rows(query_ref[...])]

    def score_block(block, tops):
        pairs = pair_ref[key_rows(block), :]
        allowed = allowed_entries(block, low_ref, query_first)
        new_tops = []
        for head in range(GROUP):
            scores = jnp.where(allowed, dot(pairs, queries[head], 1, 0), MASKED)
            score_ref[head, key_rows(block - first), :] = scores
            new_tops.append(jnp.maximum(tops[head], jnp.max(scores, axis=0, keepdims=True)))
        return tuple(new_tops)

    start = tuple(jnp.full((1, tokens), MASKED, F32) for _ in range(GROUP))
    tops = lax.fori_loop(first, last, score_block, start)
    mix_ref[...] = jnp.zeros_like(mix_ref)

    def mix_block(block, totals):
        pairs = pair_ref[key_rows(block), :]
        new_totals = []
        for head in range(GROUP):
            terms = jnp.exp(score_ref[head, key_rows(block - first), :] - tops[head])
            new_totals.append(totals[head] + jnp.sum(terms, axis=0, keepdims=True))
            mix_ref[head] += dot(pairs, terms.astype(BF), 0, 0)
        return tuple(new_totals)

    start = tuple(jnp.zeros((1, tokens), F32) for _ in range(GROUP))
    totals = lax.fori_loop(first, last, mix_block, start)
    mixed = jnp.concatenate(
        [mix_ref[head, HD:, :] / totals[head] for head in range(GROUP)], axis=0
    )
    out_ref[...] = mixed.T.astype(BF)
    for head in range(GROUP):
        log_ref[head : head + 1, :] = tops[head] + jnp.log(totals[head])


def attend_back_kernel(
    bounds, query_ref, grad_ref, pair_ref, low_ref, log_ref, dquery_ref, dpair_ref, prob_ref, dprob_ref, dmix_ref
):
    step = pl.program_id(1)
    place = pl.program_id(0) * pl.num_programs(1) + step
    first, last, query_first = bounds[0, place], bounds[1, place], bounds[2, place]
    tokens = query_ref.shape[0]
    blank = jnp.zeros((HD, tokens), BF)
    queries = [jnp.concatenate([rows, blank], axis=0) for rows in head_rows(query_ref[...])]
    grads = [jnp.concatenate([blank, rows], axis=0) for rows in head_rows(grad_ref[...])]

    @pl.when(step == 0)
    def _():
        dpair_ref[...] = jnp.zeros_like(dpair_ref)

    def prob_block(block, inners):
        pairs = pair_ref[key_rows(block), :]
        allowed = allowed_entries(block, low_ref, query_first)
        new_inners = []
        for head in range(GROUP):
            scores = dot(pairs, queries[head], 1, 0)
            probs = jnp.where(allowed, jnp.exp(scores - log_ref[head : head + 1, :]), 0.0)
            dprobs = dot(pairs, grads[head], 1, 0)
            prob_ref[head, key_rows(block - first), :] = probs
            dprob_ref[head, key_rows(block - first), :] = dprobs
            new_inners.append(inners[head] + jnp.sum(probs * dprobs, axis=0, keepdims=True))
        return tuple(new_inners)

    start = tuple(jnp.zeros((1, tokens), F32) for _ in range(GROUP))
    inners = lax.fori_loop(first, last, prob_block, start)
    dmix_ref[...] = jnp.zeros_like(dmix_ref)
    all_queries = jnp.concatenate(queries, axis=1)
    all_grads = jnp.concatenate(grads, axis=1)

    def back_block(block, carry):
        rows = key_rows(block)
        pairs = pair_ref[rows, :]
        all_probs, all_scores = [], []
        for head in range(GROUP):
            probs = prob_ref[head, key_rows(block - first), :]
            dprobs = dprob_ref[head, key_rows(block - first), :]
            dscores = (probs * (dprobs - inners[head])).astype(BF)
            dmix_ref[head] += dot(pairs, dscores, 0, 0)
            all_probs.append(probs.astype(BF))
            all_scores.append(dscores)
        dpair_ref[rows, :] += dot(jnp.concatenate(all_scores, axis=1), all_queries, 1, 1) + dot(
            jnp.concatenate(all_probs, axis=1), all_grads, 1, 1
        )
        return carry

    lax.fori_loop(first, last, back_block, 0)
    dquery = jnp.concatenate([dmix_ref[head, :HD, :] for head in range(GROUP)], axis=0)
    dquery_ref[...] = dquery.T * SCALE


def attend(queries, pairs, low, bounds):
    tokens, width = queries.shape
    replicas, slots, _ = pairs.shape
    rows = low.shape[2]
    blocks = low.shape[0] // replicas
    span = LMAX + KEYS
    return pl.pallas_call(
        attend_kernel,
        grid_spec=pltpu.PrefetchScalarGridSpec(
            num_scalar_prefetch=1,
            grid=(replicas, blocks),
            in_specs=[
                pl.BlockSpec((rows, GROUP * HD), lambda rep, block, _: (rep * blocks + block, 0)),
                pl.BlockSpec((None, slots, 2 * HD), lambda rep, block, _: (rep, 0, 0)),
                pl.BlockSpec((None, 1, rows), lambda rep, block, _: (rep * blocks + block, 0, 0)),
            ],
            out_specs=[
                pl.BlockSpec((rows, GROUP * HD), lambda rep, block, _: (rep * blocks + block, 0)),
                pl.BlockSpec((None, None, GROUP, rows), lambda rep, block, _: (rep, block, 0, 0)),
            ],
            scratch_shapes=[
                pltpu.VMEM((GROUP, span, rows), F32),
                pltpu.VMEM((GROUP, 2 * HD, rows), F32),
            ],
        ),
        out_shape=[
            jax.ShapeDtypeStruct((tokens, width), BF),
            jax.ShapeDtypeStruct((replicas, blocks, GROUP, rows), F32),
        ],
        compiler_params=pltpu.CompilerParams(vmem_limit_bytes=48 * 2**20),
        cost_estimate=takes(14),
        name="attend",
    )(bounds, queries, pairs, low)


def attend_back(queries, grads, pairs, low, log_total, bounds):
    tokens, width = queries.shape
    replicas, slots, _ = pairs.shape
    rows = low.shape[2]
    blocks = low.shape[0] // replicas
    span = LMAX + KEYS
    return pl.pallas_call(
        attend_back_kernel,
        grid_spec=pltpu.PrefetchScalarGridSpec(
            num_scalar_prefetch=1,
            grid=(replicas, blocks),
            in_specs=[
                pl.BlockSpec((rows, GROUP * HD), lambda rep, block, _: (rep * blocks + block, 0)),
                pl.BlockSpec((rows, GROUP * HD), lambda rep, block, _: (rep * blocks + block, 0)),
                pl.BlockSpec((None, slots, 2 * HD), lambda rep, block, _: (rep, 0, 0)),
                pl.BlockSpec((None, 1, rows), lambda rep, block, _: (rep * blocks + block, 0, 0)),
                pl.BlockSpec((None, None, GROUP, rows), lambda rep, block, _: (rep, block, 0, 0)),
            ],
            out_specs=[
                pl.BlockSpec((rows, GROUP * HD), lambda rep, block, _: (rep * blocks + block, 0)),
                pl.BlockSpec((None, slots, 2 * HD), lambda rep, block, _: (rep, 0, 0)),
            ],
            scratch_shapes=[
                pltpu.VMEM((GROUP, span, rows), F32),
                pltpu.VMEM((GROUP, span, rows), F32),
                pltpu.VMEM((GROUP, 2 * HD, rows), F32),
            ],
        ),
        out_shape=[
            jax.ShapeDtypeStruct((tokens, width), F32),
            jax.ShapeDtypeStruct((replicas, slots, 2 * HD), F32),
        ],
        compiler_params=pltpu.CompilerParams(vmem_limit_bytes=48 * 2**20),
        cost_estimate=takes(23),
        name="attend_back",
    )(bounds, queries, grads, pairs, low, log_total)


def norm_of(vectors):
    scaling = lax.rsqrt(jnp.mean(vectors * vectors, axis=1, keepdims=True) + EPS_NORM)
    return vectors * scaling, scaling


def norm_back(value, vectors, gain):
    unit, scaling = norm_of(vectors)
    weighted = value * gain
    inner = jnp.mean(weighted * unit, axis=1, keepdims=True)
    return scaling * (weighted - unit * inner), jnp.sum(value * unit, axis=0, keepdims=True)


def exchange_kernel(
    token_ref, top_ref, gain_ref, usable_ref, source_ref, normed_ref, grad_top_ref, gains_ref,
    held, held_top, held_gains, send_sems, recv_sems, local_sems,
):
    row = lax.axis_index("row")
    sub, width = held.shape[0], token_ref.shape[1]
    partners = row_partners()
    meet([{"row": partner} for partner in partners])
    own_cols = tile(row, width)
    arrays = ((token_ref, held), (gain_ref, held_gains), (top_ref, held_top))
    copies = []
    for index, (source, target) in enumerate(arrays):
        started = []
        for shift, partner in enumerate(partners):
            copy = pltpu.make_async_remote_copy(
                src_ref=source if index == 1 else source.at[tile(partner, sub)],
                dst_ref=target.at[:, own_cols],
                send_sem=send_sems.at[index, shift],
                recv_sem=recv_sems.at[index, shift],
                device_id={"row": partner},
                device_id_type=MESH,
            )
            copy.start()
            started.append(copy)
        copy = pltpu.make_async_copy(
            source if index == 1 else source.at[tile(row, sub)], target.at[:, own_cols], local_sems.at[index]
        )
        copy.start()
        copies.append(started + [copy])
    for copy in copies[0] + copies[1]:
        copy.wait()
    source_ref[...] = held[...]
    gains_ref[...] = held_gains[...]
    unit, _ = norm_of(held[...].astype(F32))
    normed_ref[...] = (unit * held_gains[0:1, :]).astype(BF)
    for copy in copies[2]:
        copy.wait()
    grad_top_ref[...] = (held_top[...].astype(F32) * usable_ref[...]).astype(BF)


def exchange(tokens, top, gains, usable, rows):
    sub, width = tokens.shape[0] // rows, tokens.shape[1]
    block = jax.ShapeDtypeStruct((sub, rows * width), BF)
    return pl.pallas_call(
        exchange_kernel,
        out_shape=[block, block, block, jax.ShapeDtypeStruct((gains.shape[0], rows * width), F32)],
        in_specs=[VMEM] * 4,
        out_specs=[VMEM] * 4,
        scratch_shapes=[
            pltpu.VMEM((sub, rows * width), BF),
            pltpu.VMEM((sub, rows * width), BF),
            pltpu.VMEM((gains.shape[0], rows * width), F32),
            DMA((3, rows - 1)),
            DMA((3, rows - 1)),
            DMA((3,)),
        ],
        compiler_params=params(1),
        cost_estimate=takes(55),
        name="exchange",
    )(tokens, top, gains, usable)


def project_kernel(
    reps, own_ref, top_ref, weight_ref, cosine_ref, sine_ref,
    all_ref, top_all_ref, query_ref, pair_ref,
    held, send_sems, recv_sems, local_sem, top_held, top_send, top_recv, top_local,
    queries, pairs, out_sems, pair_send, pair_recv,
):
    row = lax.axis_index("row")
    partners = row_partners()
    meet(near(reps) + [{"row": partner} for partner in partners])
    sub = own_ref.shape[0]
    copies, pushes = [], []

    def out(source, target, index):
        copy = pltpu.make_async_copy(source, target, out_sems.at[index])
        copy.start()
        copies.append(copy)

    def use(step, chip):
        out(held.at[chip], all_ref.at[chip], step)
        rows = tile(chip, 2 * sub)
        turned = rotate(dot(held[chip], weight_ref[...], 1, 0), cosine_ref[rows, :], sine_ref[rows, :])
        queries[chip] = (turned[:, : GROUP * HD] * SCALE).astype(BF)
        out(queries.at[chip], query_ref.at[chip], COLS + step)
        pair = turned[:, GROUP * HD :].astype(BF)
        spot = pairs.at[chip, :, row]
        spot[...] = pair.reshape(2, sub, 2 * HD)
        for shift, partner in enumerate(partners):
            copy = pltpu.make_async_remote_copy(
                src_ref=spot,
                dst_ref=spot,
                send_sem=pair_send.at[step, shift],
                recv_sem=pair_recv.at[step, shift],
                device_id={"row": partner},
                device_id_type=MESH,
            )
            copy.start()
            pushes.append(copy)

    run_gather(reps, own_ref, held, (send_sems, recv_sems, local_sem), use)

    def use_top(step, chip):
        out(top_held.at[chip], top_all_ref.at[chip], 2 * COLS + step)

    run_gather(reps, top_ref, top_held, (top_send, top_recv, top_local), use_top)
    for copy in pushes:
        copy.wait()
    out(pairs, pair_ref, 3 * COLS)
    for copy in copies:
        copy.wait()


def project(normed_own, top_own, weight, cosine, sine, reps, rows):
    sub = normed_own.shape[0]
    return pl.pallas_call(
        functools.partial(project_kernel, reps),
        out_shape=[
            jax.ShapeDtypeStruct((COLS, 2 * sub, D), BF),
            jax.ShapeDtypeStruct((COLS, 2 * sub, D), BF),
            jax.ShapeDtypeStruct((COLS, 2 * sub, GROUP * HD), BF),
            jax.ShapeDtypeStruct((COLS, 2, rows, sub, 2 * HD), BF),
        ],
        in_specs=[VMEM] * 5,
        out_specs=[HBM] * 4,
        scratch_shapes=gather_scratch(sub)
        + gather_scratch(sub)
        + [
            pltpu.VMEM((COLS, 2 * sub, GROUP * HD), BF),
            pltpu.VMEM((COLS, 2, rows, sub, 2 * HD), BF),
            DMA((3 * COLS + 1,)),
            DMA((COLS, rows - 1)),
            DMA((COLS, rows - 1)),
        ],
        compiler_params=params(2),
        cost_estimate=takes(75),
        name="project",
    )(normed_own, top_own, weight, cosine, sine)


def mix_out_kernel(reps, attended_ref, weight_ref, source_ref, gains_ref, middle_ref, normed_ref, *scratch):
    meet(near(reps))
    parts, _, width = weight_ref.shape

    def partial(step, chip, put):
        for part in range(parts):
            put(pl.ds(part * width, width), dot(attended_ref[chip], weight_ref[part], 1, 0))

    def finish(rows, value):
        middle = source_ref[rows, :].astype(F32) + value
        middle_ref[rows, :] = middle
        normed_ref[rows, :] = (norm_of(middle)[0] * gains_ref[1:2, :]).astype(BF)

    run_scatter(reps, partial, finish, scratch)


def mix_out(attended, weight, source, gains, reps):
    sub = source.shape[0]
    return pl.pallas_call(
        functools.partial(mix_out_kernel, reps),
        out_shape=[jax.ShapeDtypeStruct((sub, D), F32), jax.ShapeDtypeStruct((sub, D), BF)],
        in_specs=[VMEM] * 4,
        out_specs=[VMEM] * 2,
        scratch_shapes=scatter_scratch(sub),
        compiler_params=params(3),
        cost_estimate=takes(44),
        name="mix_out",
    )(attended, weight, source, gains)


def gated(tokens, top, weight_ref, put):
    parts, rows, width = weight_ref.shape
    units, span = rows // 3, 256

    def one_tile(index, carry):
        columns = tile(index, span)
        gate_w = weight_ref[:, :units, columns].reshape(D, span)
        up_w = weight_ref[:, units : 2 * units, columns].reshape(D, span)
        gate = dot(tokens, gate_w, 1, 0)
        up = dot(tokens, up_w, 1, 0)
        down_rows = pl.ds(pl.multiple_of(2 * units + index * span, span), span)
        grad = dot(top[:, :width], weight_ref[0, down_rows, :], 1, 1)
        for part in range(1, parts):
            grad += dot(top[:, part * width : (part + 1) * width], weight_ref[part, down_rows, :], 1, 1)
        sigma = 1.0 / (1.0 + jnp.exp(-gate))
        active = gate * sigma
        put(
            columns,
            (active * up).astype(BF),
            (grad * up * sigma * (1.0 + gate * (1.0 - sigma))).astype(BF),
            (grad * active).astype(BF),
        )
        return carry

    lax.fori_loop(0, units // span, one_tile, 0)


def first_slice_kernel(
    reps, own_ref, top_ref, weight_ref, all_ref, hidden_ref, ggate_ref, gup_ref,
    held, send_sems, recv_sems, local_sem, tops, hiddens, ggates, gups, top_sems, out_sems,
):
    meet(near(reps))
    where = plane(reps)
    order = [where[kind][0] for kind in ("O", "P", "Q", "D")]
    loads = [pltpu.make_async_copy(top_ref.at[chip], tops.at[chip], top_sems.at[step]) for step, chip in enumerate(order)]
    for copy in loads:
        copy.start()
    copies = []

    def use(step, chip):
        def out(source, target, index):
            copy = pltpu.make_async_copy(source.at[chip], target.at[chip], out_sems.at[index, step])
            copy.start()
            copies.append(copy)

        out(held, all_ref, 0)
        loads[step].wait()

        def put(columns, hidden, ggate, gup):
            hiddens[chip, :, columns] = hidden
            ggates[chip, :, columns] = ggate
            gups[chip, :, columns] = gup

        gated(held[chip], tops[chip], weight_ref, put)
        out(hiddens, hidden_ref, 1)
        out(ggates, ggate_ref, 2)
        out(gups, gup_ref, 3)

    run_gather(reps, own_ref, held, (send_sems, recv_sems, local_sem), use)
    for copy in copies:
        copy.wait()


def first_slice(normed_own, top_all, weight, reps):
    sub = normed_own.shape[0]
    units = weight.shape[1] // 3
    piece = jax.ShapeDtypeStruct((COLS, 2 * sub, units), BF)
    return pl.pallas_call(
        functools.partial(first_slice_kernel, reps),
        out_shape=[jax.ShapeDtypeStruct((COLS, 2 * sub, D), BF)] + [piece] * 3,
        in_specs=[VMEM, HBM, VMEM],
        out_specs=[HBM] * 4,
        scratch_shapes=gather_scratch(sub)
        + [pltpu.VMEM((COLS, 2 * sub, D), BF)]
        + [pltpu.VMEM((COLS, 2 * sub, units), BF)] * 3
        + [DMA((COLS,)), DMA((4, COLS))],
        compiler_params=params(4),
        cost_estimate=takes(50),
        name="first_slice",
    )(normed_own, top_all, weight)


def second_slice_kernel(
    reps, token_ref, top_ref, ggate_one_ref, gup_one_ref, weight_one_ref, weight_ref, middle_ref, own_top_ref, gains_ref,
    hidden_ref, ggate_ref, gup_ref, grad_ref, low_ref, gain_ref, *scratch,
):
    tokens, tops, ggate_ones, gup_ones, weight_one, hiddens, ggates, gups, in_sems, out_sems, weight_sem = scratch[SCATTER_REFS:]
    meet(near(reps))
    order = scatter_order(reps)
    parts, rows, width = weight_ref.shape
    units = rows // 3
    loads, copies = {}, []
    sources = ((token_ref, tokens), (top_ref, tops), (ggate_one_ref, ggate_ones), (gup_one_ref, gup_ones))

    def load(step):
        loads[step] = []
        for index, (source, target) in enumerate(sources):
            copy = pltpu.make_async_copy(source.at[order[step]], target.at[step % 2], in_sems.at[index, step % 2])
            copy.start()
            loads[step].append(copy)

    load(0)
    weight_copy = pltpu.make_async_copy(weight_one_ref.at[:, pl.ds(0, 2 * units)], weight_one, weight_sem)
    weight_copy.start()
    gain_ref[...] = jnp.zeros_like(gain_ref)

    def partial(step, chip, put):
        slot = step % 2
        for copy in loads[step]:
            copy.wait()
        if step < 3:
            load(step + 1)

        def keep(columns, hidden, ggate, gup):
            hiddens[chip, :, columns] = hidden
            ggates[chip, :, columns] = ggate
            gups[chip, :, columns] = gup

        gated(tokens[slot], tops[slot], weight_ref, keep)
        for index, (source, target) in enumerate(((hiddens, hidden_ref), (ggates, ggate_ref), (gups, gup_ref))):
            copy = pltpu.make_async_copy(source.at[chip], target.at[chip], out_sems.at[index, step])
            copy.start()
            copies.append(copy)
        if step == 0:
            weight_copy.wait()
        for part in range(parts):
            value = dot(ggates[chip], weight_ref[part, :units, :], 1, 1)
            value += dot(gups[chip], weight_ref[part, units : 2 * units, :], 1, 1)
            value += dot(ggate_ones[slot], weight_one[part, :units, :], 1, 1)
            value += dot(gup_ones[slot], weight_one[part, units:, :], 1, 1)
            put(pl.ds(part * width, width), value)

    def finish(rows_of, value):
        back, gain_part = norm_back(value, middle_ref[rows_of, :], gains_ref[1:2, :])
        grad = own_top_ref[rows_of, :].astype(F32) + back
        grad_ref[rows_of, :] = grad
        low_ref[rows_of, :] = grad.astype(BF)
        gain_ref[0:1, :] += gain_part

    run_scatter(reps, partial, finish, scratch[:SCATTER_REFS])
    for copy in copies:
        copy.wait()


def second_slice(normed_all, top_all, ggate_one, gup_one, weight_one, weight, middle, own_top, gains, reps):
    sub = middle.shape[0]
    parts, rows, width = weight.shape
    units = rows // 3
    piece = jax.ShapeDtypeStruct((COLS, 2 * sub, units), BF)
    return pl.pallas_call(
        functools.partial(second_slice_kernel, reps),
        out_shape=[piece] * 3
        + [
            jax.ShapeDtypeStruct((sub, D), F32),
            jax.ShapeDtypeStruct((sub, D), BF),
            jax.ShapeDtypeStruct((8, D), F32),
        ],
        in_specs=[HBM] * 5 + [VMEM] * 4,
        out_specs=[HBM] * 3 + [VMEM] * 3,
        scratch_shapes=scatter_scratch(sub)
        + [pltpu.VMEM((2, 2 * sub, D), BF)] * 2
        + [pltpu.VMEM((2, 2 * sub, units), BF)] * 2
        + [pltpu.VMEM((parts, 2 * units, width), BF)]
        + [pltpu.VMEM((COLS, 2 * sub, units), BF)] * 3
        + [DMA((4, 2)), DMA((3, COLS)), DMA],
        compiler_params=params(5),
        cost_estimate=takes(65),
        name="second_slice",
    )(normed_all, top_all, ggate_one, gup_one, weight_one, weight, middle, own_top, gains)


def back_out_kernel(
    reps, own_ref, weight_ref, all_ref, grad_ref, held, send_sems, recv_sems, local_sem, grads, out_sems
):
    meet(near(reps))
    parts, _, width = weight_ref.shape
    copies = []

    def use(step, chip):
        def out(source, target, index):
            copy = pltpu.make_async_copy(source.at[chip], target.at[chip], out_sems.at[index, step])
            copy.start()
            copies.append(copy)

        out(held, all_ref, 0)
        total = dot(held[chip, :, :width], weight_ref[0], 1, 1)
        for part in range(1, parts):
            total += dot(held[chip, :, part * width : (part + 1) * width], weight_ref[part], 1, 1)
        grads[chip] = total.astype(BF)
        out(grads, grad_ref, 1)

    run_gather(reps, own_ref, held, (send_sems, recv_sems, local_sem), use)
    for copy in copies:
        copy.wait()


def back_out(grad_own, weight, reps):
    sub = grad_own.shape[0]
    return pl.pallas_call(
        functools.partial(back_out_kernel, reps),
        out_shape=[
            jax.ShapeDtypeStruct((COLS, 2 * sub, D), BF),
            jax.ShapeDtypeStruct((COLS, 2 * sub, weight.shape[1]), BF),
        ],
        in_specs=[VMEM] * 2,
        out_specs=[HBM] * 2,
        scratch_shapes=gather_scratch(sub)
        + [pltpu.VMEM((COLS, 2 * sub, weight.shape[1]), BF), DMA((2, COLS))],
        compiler_params=params(6),
        cost_estimate=takes(41),
        name="back_out",
    )(grad_own, weight)


def lift_kernel(
    reps, hidden_one_ref, hidden_two_ref, weight_one_ref, weight_two_ref, middle_ref, dpair_ref, result_ref, sum_ref, *scratch
):
    weight_one, weight_two, low, taken, weight_sems, row_send, row_recv = scratch[SCATTER_REFS:]
    row = lax.axis_index("row")
    partners = row_partners()
    meet(near(reps) + [{"row": partner} for partner in partners])
    parts, units, width = weight_one.shape
    loads = []
    for index, (source, target) in enumerate(((weight_one_ref, weight_one), (weight_two_ref, weight_two))):
        copy = pltpu.make_async_copy(source.at[:, pl.ds(2 * units, units)], target, weight_sems.at[index])
        copy.start()
        loads.append(copy)
    pushes = []
    for shift, partner in enumerate(partners):
        low[shift] = dpair_ref[:, :, partner].astype(BF)
        copy = pltpu.make_async_remote_copy(
            src_ref=low.at[shift],
            dst_ref=taken.at[shift],
            send_sem=row_send.at[shift],
            recv_sem=row_recv.at[shift],
            device_id={"row": partner},
            device_id_type=MESH,
        )
        copy.start()
        pushes.append(copy)
    for copy in loads:
        copy.wait()

    def partial(step, chip, put):
        for part in range(parts):
            value = dot(hidden_one_ref[chip], weight_one[part], 1, 0)
            put(pl.ds(part * width, width), value + dot(hidden_two_ref[chip], weight_two[part], 1, 0))

    def finish(rows, value):
        result_ref[rows, :] = (middle_ref[rows, :] + value).astype(BF)

    run_scatter(reps, partial, finish, scratch[:SCATTER_REFS])
    for copy in pushes:
        copy.wait()
    total = dpair_ref[:, :, row]
    for shift in range(len(partners)):
        total += taken[shift].astype(F32)
    sum_ref[...] = total


def lift(hidden_one, hidden_two, weight_one, weight_two, middle, dpairs, reps):
    sub = middle.shape[0]
    parts, rows, width = weight_one.shape
    chips, cores, row_count, _, lanes = dpairs.shape
    return pl.pallas_call(
        functools.partial(lift_kernel, reps),
        out_shape=[
            jax.ShapeDtypeStruct((sub, D), BF),
            jax.ShapeDtypeStruct((chips, cores, sub, lanes), F32),
        ],
        in_specs=[VMEM] * 2 + [HBM] * 2 + [VMEM] * 2,
        out_specs=[VMEM] * 2,
        scratch_shapes=scatter_scratch(sub)
        + [pltpu.VMEM((parts, rows // 3, width), BF)] * 2
        + [pltpu.VMEM((row_count - 1, chips, cores, sub, lanes), BF)] * 2
        + [DMA((2,)), DMA((row_count - 1,)), DMA((row_count - 1,))],
        compiler_params=params(7),
        cost_estimate=takes(50),
        name="lift",
    )(hidden_one, hidden_two, weight_one, weight_two, middle, dpairs)


def project_back_kernel(
    reps, dquery_ref, dpair_ref, cosine_ref, sine_ref, weight_ref, source_ref, middle_ref, gains_ref,
    proj_ref, resid_ref, gain_ref, *scratch,
):
    meet(near(reps))
    gain_ref[...] = jnp.zeros_like(gain_ref)
    sub = source_ref.shape[0]

    def partial(step, chip, put):
        rows = tile(chip, 2 * sub)
        pair = dpair_ref[chip].reshape(2 * sub, 2 * HD)
        grad = jnp.concatenate([dquery_ref[rows, :], pair], axis=1)
        proj_ref[chip] = rotate(grad, cosine_ref[rows, :], -sine_ref[rows, :]).astype(BF)
        for index in range(D // SPAN):
            columns = pl.ds(index * SPAN, SPAN)
            put(columns, dot(proj_ref[chip], weight_ref[columns, :], 1, 1))

    def finish(rows, value):
        back, gain_part = norm_back(value, source_ref[rows, :].astype(F32), gains_ref[0:1, :])
        resid_ref[rows, :] = (middle_ref[rows, :] + back).astype(BF)
        gain_ref[0:1, :] += gain_part

    run_scatter(reps, partial, finish, scratch)


def project_back(dquery, dpairs, cosine, sine, weight, source, grad_middle, gains, reps):
    sub = source.shape[0]
    return pl.pallas_call(
        functools.partial(project_back_kernel, reps),
        out_shape=[
            jax.ShapeDtypeStruct((COLS, 2 * sub, weight.shape[1]), BF),
            jax.ShapeDtypeStruct((sub, D), BF),
            jax.ShapeDtypeStruct((8, D), F32),
        ],
        in_specs=[VMEM] * 8,
        out_specs=[VMEM] * 3,
        scratch_shapes=scatter_scratch(sub),
        compiler_params=params(8),
        cost_estimate=takes(45),
        name="project_back",
    )(dquery, dpairs, cosine, sine, weight, source, grad_middle, gains)


def adamw(weights, gradient, moment, square, step_rate, decay_rate):
    gradient = gradient.astype(F32)
    moment_new = BETA_ONE * moment + (1.0 - BETA_ONE) * gradient
    square_new = BETA_TWO * square + (1.0 - BETA_TWO) * gradient * gradient
    moment_hat = moment_new / (1.0 - BETA_ONE**STEP)
    square_hat = square_new / (1.0 - BETA_TWO**STEP)
    weights_new = weights - step_rate * (
        moment_hat / (jnp.sqrt(square_hat) + ADAM_EPS) + decay_rate * weights
    )
    return (weights_new, moment_new, square_new)


def local(
    resid_in,
    cotangent,
    seq_lens,
    qkv_weight,
    qkv_moment,
    qkv_square,
    out_weight,
    out_moment,
    out_square,
    gate_weight,
    gate_moment,
    gate_square,
    up_weight,
    up_moment,
    up_square,
    down_weight,
    down_moment,
    down_square,
    norm_gains,
    gain_moment,
    gain_square,
):
    cols, rows, replicas = lax.axis_size("col"), lax.axis_size("row"), lax.axis_size("dp")
    reps = replicas // 2
    half = lax.axis_index("dp") // reps
    row, col = lax.axis_index("row"), lax.axis_index("col")
    chunk = resid_in.shape[0]
    slots = chunk * cols
    sub = chunk // rows
    blocks = 2 * cols
    plane_tokens = sub * blocks
    head_width = (GROUP + 2) * HD

    qkv_block = half_columns(qkv_weight, reps)
    out_block = tall_block(out_weight, reps)
    split = out_block.shape[1] // 2
    stacked = jnp.concatenate([out_block[:, :split], out_block[:, split:]], axis=0)
    first_w = lax.all_gather(jnp.concatenate([qkv_block, stacked], axis=1), "row", axis=0)
    qkv_w = first_w[:, :, :head_width].reshape(D, head_width)
    heads = out_block.shape[0]
    out_w = jnp.concatenate([first_w[:, :heads, head_width:], first_w[:, heads:, head_width:]], axis=2)
    gate_block, up_block = half_columns(gate_weight, reps), half_columns(up_weight, reps)
    down_block = tall_block(down_weight, reps)
    units = gate_block.shape[1] // SLICES
    slice_w = []
    for index in range(SLICES):
        span = slice(index * units, (index + 1) * units)
        block = jnp.concatenate([gate_block[:, span], up_block[:, span], down_block[span]], axis=0)
        slice_w.append(lax.all_gather(block, "row", axis=0))

    lengths = both_halves(seq_lens, partner_swap(seq_lens, reps), half, 0)
    ends = jnp.cumsum(lengths, axis=1, dtype=jnp.int32)
    firsts = jnp.arange(cols, dtype=jnp.int32) * chunk + row * sub
    slot = (firsts[:, None] + jnp.arange(sub, dtype=jnp.int32)[None, :]).reshape(1, cols * sub)
    passed = (slot[:, :, None] >= ends[:, None, :]).astype(jnp.int32)
    seq_start = jnp.sum(passed * lengths[:, None, :], axis=2, dtype=jnp.int32)
    usable = slot < ends[:, -1:]
    cosine, sine = rope_tables((slot - seq_start).reshape(plane_tokens))
    low = jnp.where(usable, seq_start, slot).reshape(blocks, 1, sub)
    firsts = jnp.concatenate([firsts, firsts])
    bounds = jnp.stack([low[:, 0, 0] // KEYS, (firsts + sub - 1) // KEYS + 1, firsts]).astype(jnp.int32)
    usable_mine = (col * chunk + row * sub + jnp.arange(sub, dtype=jnp.int32)) < jnp.sum(seq_lens)

    padded = jnp.concatenate([norm_gains, jnp.zeros((6, norm_gains.shape[1]), F32)])
    source, normed_own, grad_top, gains = exchange(
        resid_in, cotangent, padded, usable_mine.astype(F32)[:, None], rows
    )
    normed_one, grad_top_all, queries, pairs = project(normed_own, grad_top, qkv_w, cosine, sine, reps, rows)
    queries = queries.reshape(plane_tokens, GROUP * HD)
    pairs = pairs.reshape(2, slots, 2 * HD)
    attended, log_total = attend(queries, pairs, low, bounds)
    middle, normed_own = mix_out(attended.reshape(cols, 2 * sub, GROUP * HD), out_w, source, gains, reps)

    flat_top = grad_top_all.reshape(plane_tokens, D)

    def slice_grads(normed_all, hidden, ggate, gup):
        flat = normed_all.reshape(plane_tokens, D)
        parts = [
            dot(flat, ggate.reshape(plane_tokens, units), 0, 0).astype(BF).reshape(rows, -1, units),
            dot(flat, gup.reshape(plane_tokens, units), 0, 0).astype(BF).reshape(rows, -1, units),
            row_blocks(dot(hidden.reshape(plane_tokens, units), flat_top, 0, 0).astype(BF), rows),
        ]
        return jnp.concatenate(parts, axis=1)

    normed_two, hidden_one, ggate_one, gup_one = first_slice(normed_own, grad_top_all, slice_w[0], reps)
    grads_one = slice_grads(normed_two, hidden_one, ggate_one, gup_one)
    normed_two, grads_one = lax.optimization_barrier((normed_two, grads_one))
    hidden_two, ggate_two, gup_two, grad_middle, grad_middle_own, gain_grad_two = second_slice(
        normed_two, grad_top_all, ggate_one, gup_one, slice_w[0], slice_w[1], middle, grad_top, gains, reps
    )
    grads_two = slice_grads(normed_two, hidden_two, ggate_two, gup_two)
    grad_middle_own, grads_two = lax.optimization_barrier((grad_middle_own, grads_two))
    slice_g = [lax.psum_scatter(part, "row", scatter_dimension=0) for part in (grads_one, grads_two)]

    grad_middle_all, grad_attended = back_out(grad_middle_own, out_w, reps)
    grad_query, grad_pairs = attend_back(
        queries, grad_attended.reshape(plane_tokens, GROUP * HD), pairs, low, log_total, bounds
    )
    result, grad_pairs = lift(
        hidden_one, hidden_two, slice_w[0], slice_w[1], middle,
        grad_pairs.reshape(cols, 2, rows, sub, 2 * HD), reps,
    )
    result = lax.all_to_all(result, "row", split_axis=1, concat_axis=0, tiled=True)
    grad_proj, resid_grad, gain_grad_one = project_back(
        grad_query, grad_pairs, cosine, sine, qkv_w, source, grad_middle, gains, reps
    )
    resid_grad = lax.all_to_all(resid_grad, "row", split_axis=1, concat_axis=0, tiled=True).astype(F32)
    grad_out = row_blocks(dot(attended, grad_middle_all.reshape(plane_tokens, D), 0, 0).astype(BF), rows)
    grad_out = own_tall(lax.psum_scatter(grad_out, "row", scatter_dimension=0), reps)
    grad_qkv = dot(normed_one.reshape(plane_tokens, D), grad_proj.reshape(plane_tokens, head_width), 0, 0)
    grad_qkv = own_rows(lax.psum_scatter(grad_qkv.astype(BF), "row", scatter_dimension=0, tiled=True), reps)
    wide = sum(part.shape[0] for part in slice_g) // (3 * SLICES)
    grad_gate = own_rows(jnp.concatenate([part[:wide] for part in slice_g], axis=1), reps)
    grad_up = own_rows(jnp.concatenate([part[wide : 2 * wide] for part in slice_g], axis=1), reps)
    grad_down = own_tall(jnp.concatenate([part[2 * wide :] for part in slice_g], axis=0), reps)

    gain_grads = lax.psum(jnp.concatenate([gain_grad_one[:1], gain_grad_two[:1]]), ("dp", "row", "col"))
    gain_grads = lax.dynamic_slice_in_dim(gain_grads, row * norm_gains.shape[1], norm_gains.shape[1], 1)
    qkv_set = adamw(qkv_weight, grad_qkv, qkv_moment, qkv_square, RATE_MATRIX, WEIGHT_DECAY)
    out_set = adamw(out_weight, grad_out, out_moment, out_square, RATE_OUTPUT, WEIGHT_DECAY)
    gate_set = adamw(gate_weight, grad_gate, gate_moment, gate_square, RATE_MATRIX, WEIGHT_DECAY)
    up_set = adamw(up_weight, grad_up, up_moment, up_square, RATE_MATRIX, WEIGHT_DECAY)
    down_set = adamw(down_weight, grad_down, down_moment, down_square, RATE_MATRIX, WEIGHT_DECAY)
    gain_set = adamw(norm_gains, gain_grads, gain_moment, gain_square, RATE_GAIN, 0.0)
    return (result, resid_grad, *qkv_set, *out_set, *gate_set, *up_set, *down_set, *gain_set)


def solution(mesh):
    tokens = P(("dp", "col"), "row")
    wide = P(("row", "dp"), "col")
    tall = P(("col", "dp"), "row")
    gain = P(None, "row")
    weights = (wide,) * 3 + (tall,) * 3 + (wide,) * 6 + (tall,) * 3 + (gain,) * 3
    return jax.shard_map(
        local,
        mesh=mesh,
        in_specs=(tokens, tokens, P("dp", None)) + weights,
        out_specs=(tokens, tokens) + weights,
        check_vma=False,
    )
```

```python
import functools

import jax
import jax.numpy as jnp
from jax import lax
from jax.experimental import pallas as pl
from jax.experimental.pallas import tpu as pltpu
from jax.sharding import PartitionSpec as P

D = 2048
FF = 8192
HD = 64
GROUP = 4
LMAX = 1024
STEP = 10
KEYS = 256
SLICES = 2
PIECES = 4
COLS = 4

EPS_NORM = 1e-05
ROPE_BASE = 500000.0
BETA_ONE = 0.9
BETA_TWO = 0.95
ADAM_EPS = 1e-08
WEIGHT_DECAY = 0.1
RATE_MATRIX = 0.05
RATE_OUTPUT = 0.4
RATE_GAIN = 0.8
MASKED = -1e30
SCALE = HD ** (-0.5)

BF = jnp.bfloat16
F32 = jnp.float32


def dot(left, right, left_dim, right_dim):
    return lax.dot_general(
        left, right, (((left_dim,), (right_dim,)), ((), ())), preferred_element_type=F32
    )


def half_groups(reps):
    return [[rep, rep + reps] for rep in range(reps)]


def rep_groups(reps):
    return [[half * reps + rep for rep in range(reps)] for half in range(2)]


def partner_swap(values_in, reps):
    pairs = [pair for rep in range(reps) for pair in ((rep, rep + reps), (rep + reps, rep))]
    return lax.ppermute(values_in, "dp", pairs)


def both_halves(mine, theirs, half, axis):
    first = jnp.where(half == 0, mine, theirs)
    second = jnp.where(half == 0, theirs, mine)
    return jnp.concatenate([first, second], axis=axis)


def half_columns(weight, reps):
    half = lax.axis_index("dp") // reps
    own, width = weight.shape[0], weight.shape[1] // 2
    low = weight.astype(BF)
    mine = lax.dynamic_slice_in_dim(low, half * width, width, 1)
    theirs = partner_swap(lax.dynamic_slice_in_dim(low, (1 - half) * width, width, 1), reps)
    both = both_halves(mine, theirs, half, 0)
    if reps > 1:
        both = lax.all_gather(both, "dp", axis=0, axis_index_groups=rep_groups(reps))
        both = both.reshape(reps, 2, own, width).swapaxes(0, 1).reshape(2 * reps * own, width)
    return both


def own_rows(part, reps):
    half = lax.axis_index("dp") // reps
    height = part.shape[0] // 2
    mine = lax.dynamic_slice_in_dim(part, half * height, height, 0)
    theirs = partner_swap(lax.dynamic_slice_in_dim(part, (1 - half) * height, height, 0), reps)
    part = both_halves(mine, theirs, half, 1)
    if reps > 1:
        part = lax.psum_scatter(
            part, "dp", scatter_dimension=0, tiled=True, axis_index_groups=rep_groups(reps)
        )
    return part


def tall_block(weight, reps):
    own = weight.astype(BF)
    if reps > 1:
        own = lax.all_gather(own, "dp", axis=0, tiled=True, axis_index_groups=rep_groups(reps))
    return own


def own_tall(part, reps):
    if reps > 1:
        part = lax.psum_scatter(
            part, "dp", scatter_dimension=0, tiled=True, axis_index_groups=rep_groups(reps)
        )
    return part


def row_blocks(matrix, rows):
    return matrix.reshape(matrix.shape[0], rows, -1).swapaxes(0, 1)


def rope_tables(position):
    exponent = jnp.arange(0, HD, 2, dtype=F32) / HD
    freq_table = 1.0 / ROPE_BASE**exponent
    angle = position.astype(F32)[:, None] * freq_table[None, :]
    cosine = jnp.cos(angle)
    sine = jnp.sin(angle)
    return (jnp.concatenate([cosine] * 4, axis=1), jnp.concatenate([-sine, sine, -sine, sine], axis=1))


def rotate(vectors, cosine, sine):
    width = vectors.shape[1]
    lane = lax.broadcasted_iota(jnp.int32, vectors.shape, 1)
    lower = lax.rem(lane, HD) < HD // 2
    turned = jnp.where(
        lower, pltpu.roll(vectors, width - HD // 2, 1), pltpu.roll(vectors, HD // 2, 1)
    )
    copies = width // cosine.shape[1]
    cosine = jnp.concatenate([cosine] * copies, axis=1)
    sine = jnp.concatenate([sine] * copies, axis=1)
    return jnp.where(lane < (GROUP + 1) * HD, vectors * cosine + turned * sine, vectors)


MESH = pl.DeviceIdType.MESH
HBM = pl.BlockSpec(memory_space=pl.ANY)
VMEM = pl.BlockSpec(memory_space=pltpu.VMEM)
DMA = pltpu.SemaphoreType.DMA


def takes(micros):
    return pl.CostEstimate(flops=1, bytes_accessed=int(micros * 3.6e6), transcendentals=0)


def params(collective_id):
    return pltpu.CompilerParams(
        collective_id=collective_id, has_side_effects=True, vmem_limit_bytes=60 * 2**20
    )


def tile(index, width):
    return pl.ds(pl.multiple_of(index * width, width), width)


def plane(reps):
    replica, col = lax.axis_index("dp"), lax.axis_index("col")
    half, rep = lax.div(replica, reps), lax.rem(replica, reps)
    core = lax.rem(col, 2)
    other = col + 1 - 2 * core

    def place(half_of, col_of):
        chip = half_of * (COLS // 2) + lax.div(col_of, 2)
        return (chip, lax.rem(col_of, 2), {"dp": half_of * reps + rep, "col": col_of})

    def turn(value, by, modulus):
        return lax.rem(value + by, modulus)

    return {
        "O": place(half, col),
        "P": place(turn(half, 1 - core, 2), turn(col, 2 * core, COLS)),
        "Q": place(turn(half, core, 2), turn(col, 2 - 2 * core, COLS)),
        "D": place(1 - half, turn(col, 2, COLS)),
        "SO": place(half, other),
        "SP": place(turn(half, core, 2), turn(other, 2 - 2 * core, COLS)),
        "SQ": place(turn(half, 1 - core, 2), turn(other, 2 * core, COLS)),
        "SD": place(1 - half, turn(other, 2, COLS)),
    }


def near(reps):
    where = plane(reps)
    return [where["P"][2], where["Q"][2], where["SO"][2]]


def row_partners():
    rows, row = lax.axis_size("row"), lax.axis_index("row")
    return [lax.rem(row + shift, rows) for shift in range(1, rows)]


def meet(devices):
    barrier = pltpu.get_barrier_semaphore()
    for device in devices:
        pl.semaphore_signal(barrier, inc=1, device_id=device, device_id_type=MESH)
    pl.semaphore_wait(barrier, len(devices))


GATHER_KINDS = ("P", "Q", "D", "SO", "SP", "SQ", "SD")


def run_gather(reps, own_ref, held_ref, sems, use):
    send_sems, recv_sems, local_sem = sems
    where = plane(reps)
    sub = own_ref.shape[0]
    height = sub // PIECES

    def spot(kind, piece):
        chip, core, _ = where[kind]
        return held_ref.at[chip, pl.ds(pl.multiple_of(core * sub + piece * height, height), height)]

    def message(kind, piece, source, target, device):
        index = GATHER_KINDS.index(kind)
        return pltpu.make_async_remote_copy(
            src_ref=source,
            dst_ref=target,
            send_sem=send_sems.at[index, piece],
            recv_sem=recv_sems.at[index, piece],
            device_id=device,
            device_id_type=MESH,
        )

    near_p, near_q, sibling = where["P"][2], where["Q"][2], where["SO"][2]
    sent = []

    def send(kind, piece, source, held_by, device):
        copy = message(kind, piece, source, spot(held_by, piece), device)
        copy.start()
        sent.append(copy)

    def arrive(kind, piece):
        message(kind, piece, spot(kind, piece), spot(kind, piece), sibling).wait_recv()

    own_copy = pltpu.make_async_copy(own_ref, held_ref.at[where["O"][0], tile(where["O"][1], sub)], local_sem)
    own_copy.start()
    for piece in range(PIECES):
        source = own_ref.at[pl.ds(piece * height, height)]
        send("P", piece, source, "O", near_p)
        send("Q", piece, source, "O", near_q)
        send("SO", piece, source, "O", sibling)
    own_copy.wait()
    for piece in range(PIECES):
        arrive("SO", piece)
    use(0, where["O"][0])
    for piece in range(PIECES):
        arrive("P", piece)
        send("D", piece, spot("P", piece), "P", near_q)
        send("SP", piece, spot("P", piece), "P", sibling)
    for piece in range(PIECES):
        arrive("Q", piece)
        send("SQ", piece, spot("Q", piece), "Q", sibling)
    for piece in range(PIECES):
        arrive("SQ", piece)
    use(1, where["P"][0])
    for piece in range(PIECES):
        arrive("SP", piece)
    use(2, where["Q"][0])
    for piece in range(PIECES):
        arrive("D", piece)
        send("SD", piece, spot("D", piece), "D", sibling)
    for piece in range(PIECES):
        arrive("SD", piece)
    use(3, where["D"][0])
    for copy in sent:
        copy.wait_send()


def gather_scratch(sub):
    count = len(GATHER_KINDS)
    return [pltpu.VMEM((COLS, 2 * sub, D), BF), DMA((count, PIECES)), DMA((count, PIECES)), DMA]


SCATTER_SWAPS = ("D", "Q", "P", "O")
SCATTER_HOPS = ("D", "Q", "P")


def scatter_order(reps):
    where = plane(reps)
    return [where[kind][0] for kind in SCATTER_SWAPS]


def run_scatter(reps, partial, finish, scratch):
    total_ref, give_ref, take_ref, hop_out, hop_in, both_ref, swap_send, swap_recv, hop_send, hop_recv = scratch
    where = plane(reps)
    core = where["O"][1]
    device = {"P": where["P"][2], "Q": where["Q"][2], "D": where["Q"][2]}
    sibling = where["SO"][2]
    sub = total_ref.shape[1]
    height = sub // PIECES
    sibling_kind = {"D": "D", "Q": "P", "P": "Q", "O": "O"}
    sent = []

    def swap(kind):
        index = SCATTER_SWAPS.index(kind)
        return pltpu.make_async_remote_copy(
            src_ref=give_ref.at[index],
            dst_ref=take_ref.at[index],
            send_sem=swap_send.at[index],
            recv_sem=swap_recv.at[index],
            device_id=sibling,
            device_id_type=MESH,
        )

    def hop(kind, piece):
        index = SCATTER_HOPS.index(kind)
        rows = pl.ds(piece * height, height)
        return pltpu.make_async_remote_copy(
            src_ref=hop_out.at[index, rows],
            dst_ref=hop_in.at[index, rows],
            send_sem=hop_send.at[index, piece],
            recv_sem=hop_recv.at[index, piece],
            device_id=device[kind],
            device_id_type=MESH,
        )

    def compute(step, kind):
        mine, theirs = SCATTER_SWAPS.index(kind), SCATTER_SWAPS.index(sibling_kind[kind])

        def put(columns, value):
            both_ref[...] = value
            total_ref[mine, :, columns] = both_ref[tile(core, sub), :]
            give_ref[theirs, :, columns] = both_ref[tile(1 - core, sub), :].astype(BF)

        partial(step, where[kind][0], put)
        copy = swap(sibling_kind[kind])
        copy.start()
        sent.append(copy)

    def settle(kind):
        index = SCATTER_SWAPS.index(kind)
        swap(kind).wait_recv()
        for piece in range(PIECES):
            rows = pl.ds(piece * height, height)
            value = total_ref[index, rows, :] + take_ref[index, rows, :].astype(F32)
            if kind == "P":
                hop("D", piece).wait_recv()
                value += hop_in[SCATTER_HOPS.index("D"), rows, :].astype(F32)
            if kind == "O":
                for source in ("Q", "P"):
                    hop(source, piece).wait_recv()
                    value += hop_in[SCATTER_HOPS.index(source), rows, :].astype(F32)
                finish(rows, value)
            else:
                hop_out[SCATTER_HOPS.index(kind), rows, :] = value.astype(BF)
                copy = hop(kind, piece)
                copy.start()
                sent.append(copy)

    compute(0, "D")
    compute(1, "Q")
    settle("D")
    compute(2, "P")
    settle("Q")
    compute(3, "O")
    settle("P")
    settle("O")
    for copy in sent:
        copy.wait_send()


SPAN = 512


def scatter_scratch(sub):
    return [
        pltpu.VMEM((4, sub, D), F32),
        pltpu.VMEM((4, sub, D), BF),
        pltpu.VMEM((4, sub, D), BF),
        pltpu.VMEM((3, sub, D), BF),
        pltpu.VMEM((3, sub, D), BF),
        pltpu.VMEM((2 * sub, SPAN), F32),
        DMA((4,)),
        DMA((4,)),
        DMA((3, PIECES)),
        DMA((3, PIECES)),
    ]


SCATTER_REFS = 10


def head_rows(block):
    turned = block.astype(F32).T
    return [turned[head * HD : (head + 1) * HD].astype(BF) for head in range(GROUP)]


def allowed_entries(key_block, low_ref, query_first):
    tokens = low_ref.shape[-1]
    key_slot = key_block * KEYS + lax.broadcasted_iota(jnp.int32, (KEYS, tokens), 0)
    query_slot = query_first + lax.broadcasted_iota(jnp.int32, (KEYS, tokens), 1)
    return (key_slot >= low_ref[...]) & (key_slot <= query_slot)


def key_rows(block):
    return pl.ds(pl.multiple_of(block * KEYS, KEYS), KEYS)


def attend_kernel(bounds, query_ref, pair_ref, low_ref, out_ref, log_ref, score_ref, mix_ref):
    step = pl.program_id(1)
    place = pl.program_id(0) * pl.num_programs(1) + step
    first, last, query_first = bounds[0, place], bounds[1, place], bounds[2, place]
    tokens = query_ref.shape[0]
    blank = jnp.zeros((HD, tokens), BF)
    queries = [jnp.concatenate([rows, blank], axis=0) for rows in head_rows(query_ref[...])]

    def score_block(block, tops):
        pairs = pair_ref[key_rows(block), :]
        allowed = allowed_entries(block, low_ref, query_first)
        new_tops = []
        for head in range(GROUP):
            scores = jnp.where(allowed, dot(pairs, queries[head], 1, 0), MASKED)
            score_ref[head, key_rows(block - first), :] = scores
            new_tops.append(jnp.maximum(tops[head], jnp.max(scores, axis=0, keepdims=True)))
        return tuple(new_tops)

    start = tuple(jnp.full((1, tokens), MASKED, F32) for _ in range(GROUP))
    tops = lax.fori_loop(first, last, score_block, start)
    mix_ref[...] = jnp.zeros_like(mix_ref)

    def mix_block(block, totals):
        pairs = pair_ref[key_rows(block), :]
        new_totals = []
        for head in range(GROUP):
            terms = jnp.exp(score_ref[head, key_rows(block - first), :] - tops[head])
            new_totals.append(totals[head] + jnp.sum(terms, axis=0, keepdims=True))
            mix_ref[head] += dot(pairs, terms.astype(BF), 0, 0)
        return tuple(new_totals)

    start = tuple(jnp.zeros((1, tokens), F32) for _ in range(GROUP))
    totals = lax.fori_loop(first, last, mix_block, start)
    mixed = jnp.concatenate(
        [mix_ref[head, HD:, :] / totals[head] for head in range(GROUP)], axis=0
    )
    out_ref[...] = mixed.T.astype(BF)
    for head in range(GROUP):
        log_ref[head : head + 1, :] = tops[head] + jnp.log(totals[head])


def attend_back_kernel(
    bounds, query_ref, grad_ref, pair_ref, low_ref, log_ref, dquery_ref, dpair_ref, prob_ref, dprob_ref, dmix_ref
):
    step = pl.program_id(1)
    place = pl.program_id(0) * pl.num_programs(1) + step
    first, last, query_first = bounds[0, place], bounds[1, place], bounds[2, place]
    tokens = query_ref.shape[0]
    blank = jnp.zeros((HD, tokens), BF)
    queries = [jnp.concatenate([rows, blank], axis=0) for rows in head_rows(query_ref[...])]
    grads = [jnp.concatenate([blank, rows], axis=0) for rows in head_rows(grad_ref[...])]

    @pl.when(step == 0)
    def _():
        dpair_ref[...] = jnp.zeros_like(dpair_ref)

    def prob_block(block, inners):
        pairs = pair_ref[key_rows(block), :]
        allowed = allowed_entries(block, low_ref, query_first)
        new_inners = []
        for head in range(GROUP):
            scores = dot(pairs, queries[head], 1, 0)
            probs = jnp.where(allowed, jnp.exp(scores - log_ref[head : head + 1, :]), 0.0)
            dprobs = dot(pairs, grads[head], 1, 0)
            prob_ref[head, key_rows(block - first), :] = probs
            dprob_ref[head, key_rows(block - first), :] = dprobs
            new_inners.append(inners[head] + jnp.sum(probs * dprobs, axis=0, keepdims=True))
        return tuple(new_inners)

    start = tuple(jnp.zeros((1, tokens), F32) for _ in range(GROUP))
    inners = lax.fori_loop(first, last, prob_block, start)
    dmix_ref[...] = jnp.zeros_like(dmix_ref)
    all_queries = jnp.concatenate(queries, axis=1)
    all_grads = jnp.concatenate(grads, axis=1)

    def back_block(block, carry):
        rows = key_rows(block)
        pairs = pair_ref[rows, :]
        all_probs, all_scores = [], []
        for head in range(GROUP):
            probs = prob_ref[head, key_rows(block - first), :]
            dprobs = dprob_ref[head, key_rows(block - first), :]
            dscores = (probs * (dprobs - inners[head])).astype(BF)
            dmix_ref[head] += dot(pairs, dscores, 0, 0)
            all_probs.append(probs.astype(BF))
            all_scores.append(dscores)
        dpair_ref[rows, :] += dot(jnp.concatenate(all_scores, axis=1), all_queries, 1, 1) + dot(
            jnp.concatenate(all_probs, axis=1), all_grads, 1, 1
        )
        return carry

    lax.fori_loop(first, last, back_block, 0)
    dquery = jnp.concatenate([dmix_ref[head, :HD, :] for head in range(GROUP)], axis=0)
    dquery_ref[...] = dquery.T * SCALE


def attend(queries, pairs, low, bounds):
    tokens, width = queries.shape
    replicas, slots, _ = pairs.shape
    rows = low.shape[2]
    blocks = low.shape[0] // replicas
    span = LMAX + KEYS
    return pl.pallas_call(
        attend_kernel,
        grid_spec=pltpu.PrefetchScalarGridSpec(
            num_scalar_prefetch=1,
            grid=(replicas, blocks),
            in_specs=[
                pl.BlockSpec((rows, GROUP * HD), lambda rep, block, _: (rep * blocks + block, 0)),
                pl.BlockSpec((None, slots, 2 * HD), lambda rep, block, _: (rep, 0, 0)),
                pl.BlockSpec((None, 1, rows), lambda rep, block, _: (rep * blocks + block, 0, 0)),
            ],
            out_specs=[
                pl.BlockSpec((rows, GROUP * HD), lambda rep, block, _: (rep * blocks + block, 0)),
                pl.BlockSpec((None, None, GROUP, rows), lambda rep, block, _: (rep, block, 0, 0)),
            ],
            scratch_shapes=[
                pltpu.VMEM((GROUP, span, rows), F32),
                pltpu.VMEM((GROUP, 2 * HD, rows), F32),
            ],
        ),
        out_shape=[
            jax.ShapeDtypeStruct((tokens, width), BF),
            jax.ShapeDtypeStruct((replicas, blocks, GROUP, rows), F32),
        ],
        compiler_params=pltpu.CompilerParams(vmem_limit_bytes=48 * 2**20),
        cost_estimate=takes(14),
        name="attend",
    )(bounds, queries, pairs, low)


def attend_back(queries, grads, pairs, low, log_total, bounds):
    tokens, width = queries.shape
    replicas, slots, _ = pairs.shape
    rows = low.shape[2]
    blocks = low.shape[0] // replicas
    span = LMAX + KEYS
    return pl.pallas_call(
        attend_back_kernel,
        grid_spec=pltpu.PrefetchScalarGridSpec(
            num_scalar_prefetch=1,
            grid=(replicas, blocks),
            in_specs=[
                pl.BlockSpec((rows, GROUP * HD), lambda rep, block, _: (rep * blocks + block, 0)),
                pl.BlockSpec((rows, GROUP * HD), lambda rep, block, _: (rep * blocks + block, 0)),
                pl.BlockSpec((None, slots, 2 * HD), lambda rep, block, _: (rep, 0, 0)),
                pl.BlockSpec((None, 1, rows), lambda rep, block, _: (rep * blocks + block, 0, 0)),
                pl.BlockSpec((None, None, GROUP, rows), lambda rep, block, _: (rep, block, 0, 0)),
            ],
            out_specs=[
                pl.BlockSpec((rows, GROUP * HD), lambda rep, block, _: (rep * blocks + block, 0)),
                pl.BlockSpec((None, slots, 2 * HD), lambda rep, block, _: (rep, 0, 0)),
            ],
            scratch_shapes=[
                pltpu.VMEM((GROUP, span, rows), F32),
                pltpu.VMEM((GROUP, span, rows), F32),
                pltpu.VMEM((GROUP, 2 * HD, rows), F32),
            ],
        ),
        out_shape=[
            jax.ShapeDtypeStruct((tokens, width), F32),
            jax.ShapeDtypeStruct((replicas, slots, 2 * HD), F32),
        ],
        compiler_params=pltpu.CompilerParams(vmem_limit_bytes=48 * 2**20),
        cost_estimate=takes(23),
        name="attend_back",
    )(bounds, queries, grads, pairs, low, log_total)


def norm_of(vectors):
    scaling = lax.rsqrt(jnp.mean(vectors * vectors, axis=1, keepdims=True) + EPS_NORM)
    return vectors * scaling, scaling


def norm_back(value, vectors, gain):
    unit, scaling = norm_of(vectors)
    weighted = value * gain
    inner = jnp.mean(weighted * unit, axis=1, keepdims=True)
    return scaling * (weighted - unit * inner), jnp.sum(value * unit, axis=0, keepdims=True)


def exchange_kernel(
    token_ref, top_ref, gain_ref, usable_ref, source_ref, normed_ref, grad_top_ref, gains_ref,
    held, held_top, held_gains, send_sems, recv_sems, local_sems,
):
    row = lax.axis_index("row")
    sub, width = held.shape[0], token_ref.shape[1]
    partners = row_partners()
    meet([{"row": partner} for partner in partners])
    own_cols = tile(row, width)
    arrays = ((token_ref, held), (gain_ref, held_gains), (top_ref, held_top))
    copies = []
    for index, (source, target) in enumerate(arrays):
        started = []
        for shift, partner in enumerate(partners):
            copy = pltpu.make_async_remote_copy(
                src_ref=source if index == 1 else source.at[tile(partner, sub)],
                dst_ref=target.at[:, own_cols],
                send_sem=send_sems.at[index, shift],
                recv_sem=recv_sems.at[index, shift],
                device_id={"row": partner},
                device_id_type=MESH,
            )
            copy.start()
            started.append(copy)
        copy = pltpu.make_async_copy(
            source if index == 1 else source.at[tile(row, sub)], target.at[:, own_cols], local_sems.at[index]
        )
        copy.start()
        copies.append(started + [copy])
    for copy in copies[0] + copies[1]:
        copy.wait()
    source_ref[...] = held[...]
    gains_ref[...] = held_gains[...]
    unit, _ = norm_of(held[...].astype(F32))
    normed_ref[...] = (unit * held_gains[0:1, :]).astype(BF)
    for copy in copies[2]:
        copy.wait()
    grad_top_ref[...] = (held_top[...].astype(F32) * usable_ref[...]).astype(BF)


def exchange(tokens, top, gains, usable, rows):
    sub, width = tokens.shape[0] // rows, tokens.shape[1]
    block = jax.ShapeDtypeStruct((sub, rows * width), BF)
    return pl.pallas_call(
        exchange_kernel,
        out_shape=[block, block, block, jax.ShapeDtypeStruct((gains.shape[0], rows * width), F32)],
        in_specs=[VMEM] * 4,
        out_specs=[VMEM] * 4,
        scratch_shapes=[
            pltpu.VMEM((sub, rows * width), BF),
            pltpu.VMEM((sub, rows * width), BF),
            pltpu.VMEM((gains.shape[0], rows * width), F32),
            DMA((3, rows - 1)),
            DMA((3, rows - 1)),
            DMA((3,)),
        ],
        compiler_params=params(1),
        cost_estimate=takes(55),
        name="exchange",
    )(tokens, top, gains, usable)


def project_kernel(
    reps, own_ref, top_ref, weight_ref, cosine_ref, sine_ref,
    all_ref, top_all_ref, query_ref, pair_ref,
    held, send_sems, recv_sems, local_sem, top_held, top_send, top_recv, top_local,
    queries, pairs, out_sems, pair_send, pair_recv,
):
    row = lax.axis_index("row")
    partners = row_partners()
    meet(near(reps) + [{"row": partner} for partner in partners])
    sub = own_ref.shape[0]
    copies, pushes = [], []

    def out(source, target, index):
        copy = pltpu.make_async_copy(source, target, out_sems.at[index])
        copy.start()
        copies.append(copy)

    def use(step, chip):
        out(held.at[chip], all_ref.at[chip], step)
        rows = tile(chip, 2 * sub)
        turned = rotate(dot(held[chip], weight_ref[...], 1, 0), cosine_ref[rows, :], sine_ref[rows, :])
        queries[chip] = (turned[:, : GROUP * HD] * SCALE).astype(BF)
        out(queries.at[chip], query_ref.at[chip], COLS + step)
        pair = turned[:, GROUP * HD :].astype(BF)
        spot = pairs.at[chip, :, row]
        spot[...] = pair.reshape(2, sub, 2 * HD)
        for shift, partner in enumerate(partners):
            copy = pltpu.make_async_remote_copy(
                src_ref=spot,
                dst_ref=spot,
                send_sem=pair_send.at[step, shift],
                recv_sem=pair_recv.at[step, shift],
                device_id={"row": partner},
                device_id_type=MESH,
            )
            copy.start()
            pushes.append(copy)

    run_gather(reps, own_ref, held, (send_sems, recv_sems, local_sem), use)

    def use_top(step, chip):
        out(top_held.at[chip], top_all_ref.at[chip], 2 * COLS + step)

    run_gather(reps, top_ref, top_held, (top_send, top_recv, top_local), use_top)
    for copy in pushes:
        copy.wait()
    out(pairs, pair_ref, 3 * COLS)
    for copy in copies:
        copy.wait()


def project(normed_own, top_own, weight, cosine, sine, reps, rows):
    sub = normed_own.shape[0]
    return pl.pallas_call(
        functools.partial(project_kernel, reps),
        out_shape=[
            jax.ShapeDtypeStruct((COLS, 2 * sub, D), BF),
            jax.ShapeDtypeStruct((COLS, 2 * sub, D), BF),
            jax.ShapeDtypeStruct((COLS, 2 * sub, GROUP * HD), BF),
            jax.ShapeDtypeStruct((COLS, 2, rows, sub, 2 * HD), BF),
        ],
        in_specs=[VMEM] * 5,
        out_specs=[HBM] * 4,
        scratch_shapes=gather_scratch(sub)
        + gather_scratch(sub)
        + [
            pltpu.VMEM((COLS, 2 * sub, GROUP * HD), BF),
            pltpu.VMEM((COLS, 2, rows, sub, 2 * HD), BF),
            DMA((3 * COLS + 1,)),
            DMA((COLS, rows - 1)),
            DMA((COLS, rows - 1)),
        ],
        compiler_params=params(2),
        cost_estimate=takes(75),
        name="project",
    )(normed_own, top_own, weight, cosine, sine)


def mix_out_kernel(reps, attended_ref, weight_ref, source_ref, gains_ref, middle_ref, normed_ref, *scratch):
    meet(near(reps))
    parts, _, width = weight_ref.shape

    def partial(step, chip, put):
        for part in range(parts):
            put(pl.ds(part * width, width), dot(attended_ref[chip], weight_ref[part], 1, 0))

    def finish(rows, value):
        middle = source_ref[rows, :].astype(F32) + value
        middle_ref[rows, :] = middle
        normed_ref[rows, :] = (norm_of(middle)[0] * gains_ref[1:2, :]).astype(BF)

    run_scatter(reps, partial, finish, scratch)


def mix_out(attended, weight, source, gains, reps):
    sub = source.shape[0]
    return pl.pallas_call(
        functools.partial(mix_out_kernel, reps),
        out_shape=[jax.ShapeDtypeStruct((sub, D), F32), jax.ShapeDtypeStruct((sub, D), BF)],
        in_specs=[VMEM] * 4,
        out_specs=[VMEM] * 2,
        scratch_shapes=scatter_scratch(sub),
        compiler_params=params(3),
        cost_estimate=takes(44),
        name="mix_out",
    )(attended, weight, source, gains)


def gated(tokens, top, weight_ref, put):
    parts, rows, width = weight_ref.shape
    units, span = rows // 3, 256

    def one_tile(index, carry):
        columns = tile(index, span)
        gate_w = weight_ref[:, :units, columns].reshape(D, span)
        up_w = weight_ref[:, units : 2 * units, columns].reshape(D, span)
        gate = dot(tokens, gate_w, 1, 0)
        up = dot(tokens, up_w, 1, 0)
        down_rows = pl.ds(pl.multiple_of(2 * units + index * span, span), span)
        grad = dot(top[:, :width], weight_ref[0, down_rows, :], 1, 1)
        for part in range(1, parts):
            grad += dot(top[:, part * width : (part + 1) * width], weight_ref[part, down_rows, :], 1, 1)
        sigma = 1.0 / (1.0 + jnp.exp(-gate))
        active = gate * sigma
        put(
            columns,
            (active * up).astype(BF),
            (grad * up * sigma * (1.0 + gate * (1.0 - sigma))).astype(BF),
            (grad * active).astype(BF),
        )
        return carry

    lax.fori_loop(0, units // span, one_tile, 0)


def first_slice_kernel(
    reps, own_ref, top_ref, weight_ref, all_ref, hidden_ref, ggate_ref, gup_ref,
    held, send_sems, recv_sems, local_sem, tops, hiddens, ggates, gups, top_sems, out_sems,
):
    meet(near(reps))
    where = plane(reps)
    order = [where[kind][0] for kind in ("O", "P", "Q", "D")]
    loads = [pltpu.make_async_copy(top_ref.at[chip], tops.at[chip], top_sems.at[step]) for step, chip in enumerate(order)]
    for copy in loads:
        copy.start()
    copies = []

    def use(step, chip):
        def out(source, target, index):
            copy = pltpu.make_async_copy(source.at[chip], target.at[chip], out_sems.at[index, step])
            copy.start()
            copies.append(copy)

        out(held, all_ref, 0)
        loads[step].wait()

        def put(columns, hidden, ggate, gup):
            hiddens[chip, :, columns] = hidden
            ggates[chip, :, columns] = ggate
            gups[chip, :, columns] = gup

        gated(held[chip], tops[chip], weight_ref, put)
        out(hiddens, hidden_ref, 1)
        out(ggates, ggate_ref, 2)
        out(gups, gup_ref, 3)

    run_gather(reps, own_ref, held, (send_sems, recv_sems, local_sem), use)
    for copy in copies:
        copy.wait()


def first_slice(normed_own, top_all, weight, reps):
    sub = normed_own.shape[0]
    units = weight.shape[1] // 3
    piece = jax.ShapeDtypeStruct((COLS, 2 * sub, units), BF)
    return pl.pallas_call(
        functools.partial(first_slice_kernel, reps),
        out_shape=[jax.ShapeDtypeStruct((COLS, 2 * sub, D), BF)] + [piece] * 3,
        in_specs=[VMEM, HBM, VMEM],
        out_specs=[HBM] * 4,
        scratch_shapes=gather_scratch(sub)
        + [pltpu.VMEM((COLS, 2 * sub, D), BF)]
        + [pltpu.VMEM((COLS, 2 * sub, units), BF)] * 3
        + [DMA((COLS,)), DMA((4, COLS))],
        compiler_params=params(4),
        cost_estimate=takes(50),
        name="first_slice",
    )(normed_own, top_all, weight)


def second_slice_kernel(
    reps, token_ref, top_ref, ggate_one_ref, gup_one_ref, weight_one_ref, weight_ref, middle_ref, own_top_ref, gains_ref,
    hidden_ref, ggate_ref, gup_ref, grad_ref, low_ref, gain_ref, *scratch,
):
    tokens, tops, ggate_ones, gup_ones, weight_one, hiddens, ggates, gups, in_sems, out_sems, weight_sem = scratch[SCATTER_REFS:]
    meet(near(reps))
    order = scatter_order(reps)
    parts, rows, width = weight_ref.shape
    units = rows // 3
    loads, copies = {}, []
    sources = ((token_ref, tokens), (top_ref, tops), (ggate_one_ref, ggate_ones), (gup_one_ref, gup_ones))

    def load(step):
        loads[step] = []
        for index, (source, target) in enumerate(sources):
            copy = pltpu.make_async_copy(source.at[order[step]], target.at[step % 2], in_sems.at[index, step % 2])
            copy.start()
            loads[step].append(copy)

    load(0)
    weight_copy = pltpu.make_async_copy(weight_one_ref.at[:, pl.ds(0, 2 * units)], weight_one, weight_sem)
    weight_copy.start()
    gain_ref[...] = jnp.zeros_like(gain_ref)

    def partial(step, chip, put):
        slot = step % 2
        for copy in loads[step]:
            copy.wait()
        if step < 3:
            load(step + 1)

        def keep(columns, hidden, ggate, gup):
            hiddens[chip, :, columns] = hidden
            ggates[chip, :, columns] = ggate
            gups[chip, :, columns] = gup

        gated(tokens[slot], tops[slot], weight_ref, keep)
        for index, (source, target) in enumerate(((hiddens, hidden_ref), (ggates, ggate_ref), (gups, gup_ref))):
            copy = pltpu.make_async_copy(source.at[chip], target.at[chip], out_sems.at[index, step])
            copy.start()
            copies.append(copy)
        if step == 0:
            weight_copy.wait()
        for part in range(parts):
            value = dot(ggates[chip], weight_ref[part, :units, :], 1, 1)
            value += dot(gups[chip], weight_ref[part, units : 2 * units, :], 1, 1)
            value += dot(ggate_ones[slot], weight_one[part, :units, :], 1, 1)
            value += dot(gup_ones[slot], weight_one[part, units:, :], 1, 1)
            put(pl.ds(part * width, width), value)

    def finish(rows_of, value):
        back, gain_part = norm_back(value, middle_ref[rows_of, :], gains_ref[1:2, :])
        grad = own_top_ref[rows_of, :].astype(F32) + back
        grad_ref[rows_of, :] = grad
        low_ref[rows_of, :] = grad.astype(BF)
        gain_ref[0:1, :] += gain_part

    run_scatter(reps, partial, finish, scratch[:SCATTER_REFS])
    for copy in copies:
        copy.wait()


def second_slice(normed_all, top_all, ggate_one, gup_one, weight_one, weight, middle, own_top, gains, reps):
    sub = middle.shape[0]
    parts, rows, width = weight.shape
    units = rows // 3
    piece = jax.ShapeDtypeStruct((COLS, 2 * sub, units), BF)
    return pl.pallas_call(
        functools.partial(second_slice_kernel, reps),
        out_shape=[piece] * 3
        + [
            jax.ShapeDtypeStruct((sub, D), F32),
            jax.ShapeDtypeStruct((sub, D), BF),
            jax.ShapeDtypeStruct((8, D), F32),
        ],
        in_specs=[HBM] * 5 + [VMEM] * 4,
        out_specs=[HBM] * 3 + [VMEM] * 3,
        scratch_shapes=scatter_scratch(sub)
        + [pltpu.VMEM((2, 2 * sub, D), BF)] * 2
        + [pltpu.VMEM((2, 2 * sub, units), BF)] * 2
        + [pltpu.VMEM((parts, 2 * units, width), BF)]
        + [pltpu.VMEM((COLS, 2 * sub, units), BF)] * 3
        + [DMA((4, 2)), DMA((3, COLS)), DMA],
        compiler_params=params(5),
        cost_estimate=takes(65),
        name="second_slice",
    )(normed_all, top_all, ggate_one, gup_one, weight_one, weight, middle, own_top, gains)


def back_out_kernel(
    reps, own_ref, weight_ref, all_ref, grad_ref, held, send_sems, recv_sems, local_sem, grads, out_sems
):
    meet(near(reps))
    parts, _, width = weight_ref.shape
    copies = []

    def use(step, chip):
        def out(source, target, index):
            copy = pltpu.make_async_copy(source.at[chip], target.at[chip], out_sems.at[index, step])
            copy.start()
            copies.append(copy)

        out(held, all_ref, 0)
        total = dot(held[chip, :, :width], weight_ref[0], 1, 1)
        for part in range(1, parts):
            total += dot(held[chip, :, part * width : (part + 1) * width], weight_ref[part], 1, 1)
        grads[chip] = total.astype(BF)
        out(grads, grad_ref, 1)

    run_gather(reps, own_ref, held, (send_sems, recv_sems, local_sem), use)
    for copy in copies:
        copy.wait()


def back_out(grad_own, weight, reps):
    sub = grad_own.shape[0]
    return pl.pallas_call(
        functools.partial(back_out_kernel, reps),
        out_shape=[
            jax.ShapeDtypeStruct((COLS, 2 * sub, D), BF),
            jax.ShapeDtypeStruct((COLS, 2 * sub, weight.shape[1]), BF),
        ],
        in_specs=[VMEM] * 2,
        out_specs=[HBM] * 2,
        scratch_shapes=gather_scratch(sub)
        + [pltpu.VMEM((COLS, 2 * sub, weight.shape[1]), BF), DMA((2, COLS))],
        compiler_params=params(6),
        cost_estimate=takes(41),
        name="back_out",
    )(grad_own, weight)


def lift_kernel(
    reps, hidden_one_ref, hidden_two_ref, weight_one_ref, weight_two_ref, middle_ref, dpair_ref, result_ref, sum_ref, *scratch
):
    weight_one, weight_two, low, taken, weight_sems, row_send, row_recv = scratch[SCATTER_REFS:]
    row = lax.axis_index("row")
    partners = row_partners()
    meet(near(reps) + [{"row": partner} for partner in partners])
    parts, units, width = weight_one.shape
    loads = []
    for index, (source, target) in enumerate(((weight_one_ref, weight_one), (weight_two_ref, weight_two))):
        copy = pltpu.make_async_copy(source.at[:, pl.ds(2 * units, units)], target, weight_sems.at[index])
        copy.start()
        loads.append(copy)
    pushes = []
    for shift, partner in enumerate(partners):
        low[shift] = dpair_ref[:, :, partner].astype(BF)
        copy = pltpu.make_async_remote_copy(
            src_ref=low.at[shift],
            dst_ref=taken.at[shift],
            send_sem=row_send.at[shift],
            recv_sem=row_recv.at[shift],
            device_id={"row": partner},
            device_id_type=MESH,
        )
        copy.start()
        pushes.append(copy)
    for copy in loads:
        copy.wait()

    def partial(step, chip, put):
        for part in range(parts):
            value = dot(hidden_one_ref[chip], weight_one[part], 1, 0)
            put(pl.ds(part * width, width), value + dot(hidden_two_ref[chip], weight_two[part], 1, 0))

    def finish(rows, value):
        result_ref[rows, :] = (middle_ref[rows, :] + value).astype(BF)

    run_scatter(reps, partial, finish, scratch[:SCATTER_REFS])
    for copy in pushes:
        copy.wait()
    total = dpair_ref[:, :, row]
    for shift in range(len(partners)):
        total += taken[shift].astype(F32)
    sum_ref[...] = total


def lift(hidden_one, hidden_two, weight_one, weight_two, middle, dpairs, reps):
    sub = middle.shape[0]
    parts, rows, width = weight_one.shape
    chips, cores, row_count, _, lanes = dpairs.shape
    return pl.pallas_call(
        functools.partial(lift_kernel, reps),
        out_shape=[
            jax.ShapeDtypeStruct((sub, D), BF),
            jax.ShapeDtypeStruct((chips, cores, sub, lanes), F32),
        ],
        in_specs=[VMEM] * 2 + [HBM] * 2 + [VMEM] * 2,
        out_specs=[VMEM] * 2,
        scratch_shapes=scatter_scratch(sub)
        + [pltpu.VMEM((parts, rows // 3, width), BF)] * 2
        + [pltpu.VMEM((row_count - 1, chips, cores, sub, lanes), BF)] * 2
        + [DMA((2,)), DMA((row_count - 1,)), DMA((row_count - 1,))],
        compiler_params=params(7),
        cost_estimate=takes(50),
        name="lift",
    )(hidden_one, hidden_two, weight_one, weight_two, middle, dpairs)


def project_back_kernel(
    reps, dquery_ref, dpair_ref, cosine_ref, sine_ref, weight_ref, source_ref, middle_ref, gains_ref,
    proj_ref, resid_ref, gain_ref, *scratch,
):
    meet(near(reps))
    gain_ref[...] = jnp.zeros_like(gain_ref)
    sub = source_ref.shape[0]

    def partial(step, chip, put):
        rows = tile(chip, 2 * sub)
        pair = dpair_ref[chip].reshape(2 * sub, 2 * HD)
        grad = jnp.concatenate([dquery_ref[rows, :], pair], axis=1)
        proj_ref[chip] = rotate(grad, cosine_ref[rows, :], -sine_ref[rows, :]).astype(BF)
        for index in range(D // SPAN):
            columns = pl.ds(index * SPAN, SPAN)
            put(columns, dot(proj_ref[chip], weight_ref[columns, :], 1, 1))

    def finish(rows, value):
        back, gain_part = norm_back(value, source_ref[rows, :].astype(F32), gains_ref[0:1, :])
        resid_ref[rows, :] = (middle_ref[rows, :] + back).astype(BF)
        gain_ref[0:1, :] += gain_part

    run_scatter(reps, partial, finish, scratch)


def project_back(dquery, dpairs, cosine, sine, weight, source, grad_middle, gains, reps):
    sub = source.shape[0]
    return pl.pallas_call(
        functools.partial(project_back_kernel, reps),
        out_shape=[
            jax.ShapeDtypeStruct((COLS, 2 * sub, weight.shape[1]), BF),
            jax.ShapeDtypeStruct((sub, D), BF),
            jax.ShapeDtypeStruct((8, D), F32),
        ],
        in_specs=[VMEM] * 8,
        out_specs=[VMEM] * 3,
        scratch_shapes=scatter_scratch(sub),
        compiler_params=params(8),
        cost_estimate=takes(45),
        name="project_back",
    )(dquery, dpairs, cosine, sine, weight, source, grad_middle, gains)


def adamw(weights, gradient, moment, square, step_rate, decay_rate):
    gradient = gradient.astype(F32)
    moment_new = BETA_ONE * moment + (1.0 - BETA_ONE) * gradient
    square_new = BETA_TWO * square + (1.0 - BETA_TWO) * gradient * gradient
    moment_hat = moment_new / (1.0 - BETA_ONE**STEP)
    square_hat = square_new / (1.0 - BETA_TWO**STEP)
    weights_new = weights - step_rate * (
        moment_hat / (jnp.sqrt(square_hat) + ADAM_EPS) + decay_rate * weights
    )
    return (weights_new, moment_new, square_new)


def local(
    resid_in,
    cotangent,
    seq_lens,
    qkv_weight,
    qkv_moment,
    qkv_square,
    out_weight,
    out_moment,
    out_square,
    gate_weight,
    gate_moment,
    gate_square,
    up_weight,
    up_moment,
    up_square,
    down_weight,
    down_moment,
    down_square,
    norm_gains,
    gain_moment,
    gain_square,
):
    cols, rows, replicas = lax.axis_size("col"), lax.axis_size("row"), lax.axis_size("dp")
    reps = replicas // 2
    half = lax.axis_index("dp") // reps
    row, col = lax.axis_index("row"), lax.axis_index("col")
    chunk = resid_in.shape[0]
    slots = chunk * cols
    sub = chunk // rows
    blocks = 2 * cols
    plane_tokens = sub * blocks
    head_width = (GROUP + 2) * HD

    qkv_block = half_columns(qkv_weight, reps)
    out_block = tall_block(out_weight, reps)
    split = out_block.shape[1] // 2
    stacked = jnp.concatenate([out_block[:, :split], out_block[:, split:]], axis=0)
    first_w = lax.all_gather(jnp.concatenate([qkv_block, stacked], axis=1), "row", axis=0)
    qkv_w = first_w[:, :, :head_width].reshape(D, head_width)
    heads = out_block.shape[0]
    out_w = jnp.concatenate([first_w[:, :heads, head_width:], first_w[:, heads:, head_width:]], axis=2)
    gate_block, up_block = half_columns(gate_weight, reps), half_columns(up_weight, reps)
    down_block = tall_block(down_weight, reps)
    units = gate_block.shape[1] // SLICES
    slice_w = []
    for index in range(SLICES):
        span = slice(index * units, (index + 1) * units)
        block = jnp.concatenate([gate_block[:, span], up_block[:, span], down_block[span]], axis=0)
        slice_w.append(lax.all_gather(block, "row", axis=0))

    lengths = both_halves(seq_lens, partner_swap(seq_lens, reps), half, 0)
    ends = jnp.cumsum(lengths, axis=1, dtype=jnp.int32)
    firsts = jnp.arange(cols, dtype=jnp.int32) * chunk + row * sub
    slot = (firsts[:, None] + jnp.arange(sub, dtype=jnp.int32)[None, :]).reshape(1, cols * sub)
    passed = (slot[:, :, None] >= ends[:, None, :]).astype(jnp.int32)
    seq_start = jnp.sum(passed * lengths[:, None, :], axis=2, dtype=jnp.int32)
    usable = slot < ends[:, -1:]
    cosine, sine = rope_tables((slot - seq_start).reshape(plane_tokens))
    low = jnp.where(usable, seq_start, slot).reshape(blocks, 1, sub)
    firsts = jnp.concatenate([firsts, firsts])
    bounds = jnp.stack([low[:, 0, 0] // KEYS, (firsts + sub - 1) // KEYS + 1, firsts]).astype(jnp.int32)
    usable_mine = (col * chunk + row * sub + jnp.arange(sub, dtype=jnp.int32)) < jnp.sum(seq_lens)

    padded = jnp.concatenate([norm_gains, jnp.zeros((6, norm_gains.shape[1]), F32)])
    source, normed_own, grad_top, gains = exchange(
        resid_in, cotangent, padded, usable_mine.astype(F32)[:, None], rows
    )
    normed_one, grad_top_all, queries, pairs = project(normed_own, grad_top, qkv_w, cosine, sine, reps, rows)
    queries = queries.reshape(plane_tokens, GROUP * HD)
    pairs = pairs.reshape(2, slots, 2 * HD)
    attended, log_total = attend(queries, pairs, low, bounds)
    middle, normed_own = mix_out(attended.reshape(cols, 2 * sub, GROUP * HD), out_w, source, gains, reps)

    flat_top = grad_top_all.reshape(plane_tokens, D)

    def slice_grads(normed_all, hidden, ggate, gup):
        flat = normed_all.reshape(plane_tokens, D)
        parts = [
            dot(flat, ggate.reshape(plane_tokens, units), 0, 0).astype(BF).reshape(rows, -1, units),
            dot(flat, gup.reshape(plane_tokens, units), 0, 0).astype(BF).reshape(rows, -1, units),
            row_blocks(dot(hidden.reshape(plane_tokens, units), flat_top, 0, 0).astype(BF), rows),
        ]
        return jnp.concatenate(parts, axis=1)

    normed_two, hidden_one, ggate_one, gup_one = first_slice(normed_own, grad_top_all, slice_w[0], reps)
    grads_one = slice_grads(normed_two, hidden_one, ggate_one, gup_one)
    normed_two, grads_one = lax.optimization_barrier((normed_two, grads_one))
    hidden_two, ggate_two, gup_two, grad_middle, grad_middle_own, gain_grad_two = second_slice(
        normed_two, grad_top_all, ggate_one, gup_one, slice_w[0], slice_w[1], middle, grad_top, gains, reps
    )
    grads_two = slice_grads(normed_two, hidden_two, ggate_two, gup_two)
    grad_middle_own, grads_two = lax.optimization_barrier((grad_middle_own, grads_two))
    slice_g = [lax.psum_scatter(part, "row", scatter_dimension=0) for part in (grads_one, grads_two)]

    grad_middle_all, grad_attended = back_out(grad_middle_own, out_w, reps)
    grad_attended, slice_g[0] = lax.optimization_barrier((grad_attended, slice_g[0]))
    grad_query, grad_pairs = attend_back(
        queries, grad_attended.reshape(plane_tokens, GROUP * HD), pairs, low, log_total, bounds
    )
    result, grad_pairs = lift(
        hidden_one, hidden_two, slice_w[0], slice_w[1], middle,
        grad_pairs.reshape(cols, 2, rows, sub, 2 * HD), reps,
    )
    result = lax.all_to_all(result, "row", split_axis=1, concat_axis=0, tiled=True)
    grad_query, slice_g[1] = lax.optimization_barrier((grad_query, slice_g[1]))
    grad_proj, resid_grad, gain_grad_one = project_back(
        grad_query, grad_pairs, cosine, sine, qkv_w, source, grad_middle, gains, reps
    )
    resid_grad = lax.all_to_all(resid_grad, "row", split_axis=1, concat_axis=0, tiled=True).astype(F32)
    attended, slice_g[1] = lax.optimization_barrier((attended, slice_g[1]))
    grad_out = row_blocks(dot(attended, grad_middle_all.reshape(plane_tokens, D), 0, 0).astype(BF), rows)
    grad_out = own_tall(lax.psum_scatter(grad_out, "row", scatter_dimension=0), reps)
    grad_qkv = dot(normed_one.reshape(plane_tokens, D), grad_proj.reshape(plane_tokens, head_width), 0, 0)
    grad_qkv = own_rows(lax.psum_scatter(grad_qkv.astype(BF), "row", scatter_dimension=0, tiled=True), reps)
    wide = sum(part.shape[0] for part in slice_g) // (3 * SLICES)
    grad_gate = own_rows(jnp.concatenate([part[:wide] for part in slice_g], axis=1), reps)
    grad_up = own_rows(jnp.concatenate([part[wide : 2 * wide] for part in slice_g], axis=1), reps)
    grad_down = own_tall(jnp.concatenate([part[2 * wide :] for part in slice_g], axis=0), reps)

    gain_grads = lax.psum(jnp.concatenate([gain_grad_one[:1], gain_grad_two[:1]]), ("dp", "row", "col"))
    gain_grads = lax.dynamic_slice_in_dim(gain_grads, row * norm_gains.shape[1], norm_gains.shape[1], 1)
    qkv_set = adamw(qkv_weight, grad_qkv, qkv_moment, qkv_square, RATE_MATRIX, WEIGHT_DECAY)
    out_set = adamw(out_weight, grad_out, out_moment, out_square, RATE_OUTPUT, WEIGHT_DECAY)
    gate_set = adamw(gate_weight, grad_gate, gate_moment, gate_square, RATE_MATRIX, WEIGHT_DECAY)
    up_set = adamw(up_weight, grad_up, up_moment, up_square, RATE_MATRIX, WEIGHT_DECAY)
    down_set = adamw(down_weight, grad_down, down_moment, down_square, RATE_MATRIX, WEIGHT_DECAY)
    gain_set = adamw(norm_gains, gain_grads, gain_moment, gain_square, RATE_GAIN, 0.0)
    return (result, resid_grad, *qkv_set, *out_set, *gate_set, *up_set, *down_set, *gain_set)


def solution(mesh):
    tokens = P(("dp", "col"), "row")
    wide = P(("row", "dp"), "col")
    tall = P(("col", "dp"), "row")
    gain = P(None, "row")
    weights = (wide,) * 3 + (tall,) * 3 + (wide,) * 6 + (tall,) * 3 + (gain,) * 3
    return jax.shard_map(
        local,
        mesh=mesh,
        in_specs=(tokens, tokens, P("dp", None)) + weights,
        out_specs=(tokens, tokens) + weights,
        check_vma=False,
    )
```

```python
import functools

import jax
import jax.numpy as jnp
from jax import lax
from jax.experimental import pallas as pl
from jax.experimental.pallas import tpu as pltpu
from jax.sharding import PartitionSpec as P

D = 2048
FF = 8192
HD = 64
GROUP = 4
LMAX = 1024
STEP = 10
KEYS = 256
SLICES = 2
PIECES = 4
COLS = 4

EPS_NORM = 1e-05
ROPE_BASE = 500000.0
BETA_ONE = 0.9
BETA_TWO = 0.95
ADAM_EPS = 1e-08
WEIGHT_DECAY = 0.1
RATE_MATRIX = 0.05
RATE_OUTPUT = 0.4
RATE_GAIN = 0.8
MASKED = -1e30
SCALE = HD ** (-0.5)

BF = jnp.bfloat16
F32 = jnp.float32


def dot(left, right, left_dim, right_dim):
    return lax.dot_general(
        left, right, (((left_dim,), (right_dim,)), ((), ())), preferred_element_type=F32
    )


def half_groups(reps):
    return [[rep, rep + reps] for rep in range(reps)]


def rep_groups(reps):
    return [[half * reps + rep for rep in range(reps)] for half in range(2)]


def partner_swap(values_in, reps):
    pairs = [pair for rep in range(reps) for pair in ((rep, rep + reps), (rep + reps, rep))]
    return lax.ppermute(values_in, "dp", pairs)


def both_halves(mine, theirs, half, axis):
    first = jnp.where(half == 0, mine, theirs)
    second = jnp.where(half == 0, theirs, mine)
    return jnp.concatenate([first, second], axis=axis)


def half_columns(weight, reps):
    half = lax.axis_index("dp") // reps
    own, width = weight.shape[0], weight.shape[1] // 2
    low = weight.astype(BF)
    mine = lax.dynamic_slice_in_dim(low, half * width, width, 1)
    theirs = partner_swap(lax.dynamic_slice_in_dim(low, (1 - half) * width, width, 1), reps)
    both = both_halves(mine, theirs, half, 0)
    if reps > 1:
        both = lax.all_gather(both, "dp", axis=0, axis_index_groups=rep_groups(reps))
        both = both.reshape(reps, 2, own, width).swapaxes(0, 1).reshape(2 * reps * own, width)
    return both


def own_rows(part, reps):
    half = lax.axis_index("dp") // reps
    height = part.shape[0] // 2
    mine = lax.dynamic_slice_in_dim(part, half * height, height, 0)
    theirs = partner_swap(lax.dynamic_slice_in_dim(part, (1 - half) * height, height, 0), reps)
    part = both_halves(mine, theirs, half, 1)
    if reps > 1:
        part = lax.psum_scatter(
            part, "dp", scatter_dimension=0, tiled=True, axis_index_groups=rep_groups(reps)
        )
    return part


def tall_block(weight, reps):
    own = weight.astype(BF)
    if reps > 1:
        own = lax.all_gather(own, "dp", axis=0, tiled=True, axis_index_groups=rep_groups(reps))
    return own


def own_tall(part, reps):
    if reps > 1:
        part = lax.psum_scatter(
            part, "dp", scatter_dimension=0, tiled=True, axis_index_groups=rep_groups(reps)
        )
    return part


def row_blocks(matrix, rows):
    return matrix.reshape(matrix.shape[0], rows, -1).swapaxes(0, 1)


def rope_tables(position):
    exponent = jnp.arange(0, HD, 2, dtype=F32) / HD
    freq_table = 1.0 / ROPE_BASE**exponent
    angle = position.astype(F32)[:, None] * freq_table[None, :]
    cosine = jnp.cos(angle)
    sine = jnp.sin(angle)
    return (jnp.concatenate([cosine] * 4, axis=1), jnp.concatenate([-sine, sine, -sine, sine], axis=1))


def rotate(vectors, cosine, sine):
    width = vectors.shape[1]
    lane = lax.broadcasted_iota(jnp.int32, vectors.shape, 1)
    lower = lax.rem(lane, HD) < HD // 2
    turned = jnp.where(
        lower, pltpu.roll(vectors, width - HD // 2, 1), pltpu.roll(vectors, HD // 2, 1)
    )
    copies = width // cosine.shape[1]
    cosine = jnp.concatenate([cosine] * copies, axis=1)
    sine = jnp.concatenate([sine] * copies, axis=1)
    return jnp.where(lane < (GROUP + 1) * HD, vectors * cosine + turned * sine, vectors)


MESH = pl.DeviceIdType.MESH
HBM = pl.BlockSpec(memory_space=pl.ANY)
VMEM = pl.BlockSpec(memory_space=pltpu.VMEM)
DMA = pltpu.SemaphoreType.DMA


def takes(micros):
    return pl.CostEstimate(flops=1, bytes_accessed=int(micros * 3.6e6), transcendentals=0)


def params(collective_id):
    return pltpu.CompilerParams(
        collective_id=collective_id, has_side_effects=True, vmem_limit_bytes=60 * 2**20
    )


def tile(index, width):
    return pl.ds(pl.multiple_of(index * width, width), width)


def plane(reps):
    replica, col = lax.axis_index("dp"), lax.axis_index("col")
    half, rep = lax.div(replica, reps), lax.rem(replica, reps)
    core = lax.rem(col, 2)
    other = col + 1 - 2 * core

    def place(half_of, col_of):
        chip = half_of * (COLS // 2) + lax.div(col_of, 2)
        return (chip, lax.rem(col_of, 2), {"dp": half_of * reps + rep, "col": col_of})

    def turn(value, by, modulus):
        return lax.rem(value + by, modulus)

    return {
        "O": place(half, col),
        "P": place(turn(half, 1 - core, 2), turn(col, 2 * core, COLS)),
        "Q": place(turn(half, core, 2), turn(col, 2 - 2 * core, COLS)),
        "D": place(1 - half, turn(col, 2, COLS)),
        "SO": place(half, other),
        "SP": place(turn(half, core, 2), turn(other, 2 - 2 * core, COLS)),
        "SQ": place(turn(half, 1 - core, 2), turn(other, 2 * core, COLS)),
        "SD": place(1 - half, turn(other, 2, COLS)),
    }


def near(reps):
    where = plane(reps)
    return [where["P"][2], where["Q"][2], where["SO"][2]]


def row_partners():
    rows, row = lax.axis_size("row"), lax.axis_index("row")
    return [lax.rem(row + shift, rows) for shift in range(1, rows)]


def signal(devices):
    barrier = pltpu.get_barrier_semaphore()
    for device in devices:
        pl.semaphore_signal(barrier, inc=1, device_id=device, device_id_type=MESH)


def meet(devices):
    signal(devices)
    pl.semaphore_wait(pltpu.get_barrier_semaphore(), len(devices))


GATHER_KINDS = ("P", "Q", "D", "SO", "SP", "SQ", "SD")


def run_gather(reps, own_ref, held_ref, sems, use):
    send_sems, recv_sems, local_sem = sems
    where = plane(reps)
    sub = own_ref.shape[0]
    height = sub // PIECES

    def spot(kind, piece):
        chip, core, _ = where[kind]
        return held_ref.at[chip, pl.ds(pl.multiple_of(core * sub + piece * height, height), height)]

    def message(kind, piece, source, target, device):
        index = GATHER_KINDS.index(kind)
        return pltpu.make_async_remote_copy(
            src_ref=source,
            dst_ref=target,
            send_sem=send_sems.at[index, piece],
            recv_sem=recv_sems.at[index, piece],
            device_id=device,
            device_id_type=MESH,
        )

    near_p, near_q, sibling = where["P"][2], where["Q"][2], where["SO"][2]
    sent = []

    def send(kind, piece, source, held_by, device):
        copy = message(kind, piece, source, spot(held_by, piece), device)
        copy.start()
        sent.append(copy)

    def arrive(kind, piece):
        message(kind, piece, spot(kind, piece), spot(kind, piece), sibling).wait_recv()

    own_copy = pltpu.make_async_copy(own_ref, held_ref.at[where["O"][0], tile(where["O"][1], sub)], local_sem)
    own_copy.start()
    for piece in range(PIECES):
        source = own_ref.at[pl.ds(piece * height, height)]
        send("P", piece, source, "O", near_p)
        send("Q", piece, source, "O", near_q)
        send("SO", piece, source, "O", sibling)
    own_copy.wait()
    for piece in range(PIECES):
        arrive("SO", piece)
    use(0, where["O"][0])
    for piece in range(PIECES):
        arrive("P", piece)
        send("D", piece, spot("P", piece), "P", near_q)
        send("SP", piece, spot("P", piece), "P", sibling)
    for piece in range(PIECES):
        arrive("Q", piece)
        send("SQ", piece, spot("Q", piece), "Q", sibling)
    for piece in range(PIECES):
        arrive("SQ", piece)
    use(1, where["P"][0])
    for piece in range(PIECES):
        arrive("SP", piece)
    use(2, where["Q"][0])
    for piece in range(PIECES):
        arrive("D", piece)
        send("SD", piece, spot("D", piece), "D", sibling)
    for piece in range(PIECES):
        arrive("SD", piece)
    use(3, where["D"][0])
    for copy in sent:
        copy.wait_send()


def gather_scratch(sub):
    count = len(GATHER_KINDS)
    return [pltpu.VMEM((COLS, 2 * sub, D), BF), DMA((count, PIECES)), DMA((count, PIECES)), DMA]


SCATTER_SWAPS = ("D", "Q", "P", "O")
SCATTER_HOPS = ("D", "Q", "P")


def scatter_order(reps):
    where = plane(reps)
    return [where[kind][0] for kind in SCATTER_SWAPS]


def run_scatter(reps, partial, finish, scratch):
    total_ref, give_ref, take_ref, hop_out, hop_in, both_ref, swap_send, swap_recv, hop_send, hop_recv = scratch
    where = plane(reps)
    core = where["O"][1]
    device = {"P": where["P"][2], "Q": where["Q"][2], "D": where["Q"][2]}
    sibling = where["SO"][2]
    sub = total_ref.shape[1]
    height = sub // PIECES
    sibling_kind = {"D": "D", "Q": "P", "P": "Q", "O": "O"}
    sent = []

    def swap(kind):
        index = SCATTER_SWAPS.index(kind)
        return pltpu.make_async_remote_copy(
            src_ref=give_ref.at[index],
            dst_ref=take_ref.at[index],
            send_sem=swap_send.at[index],
            recv_sem=swap_recv.at[index],
            device_id=sibling,
            device_id_type=MESH,
        )

    def hop(kind, piece):
        index = SCATTER_HOPS.index(kind)
        rows = pl.ds(piece * height, height)
        return pltpu.make_async_remote_copy(
            src_ref=hop_out.at[index, rows],
            dst_ref=hop_in.at[index, rows],
            send_sem=hop_send.at[index, piece],
            recv_sem=hop_recv.at[index, piece],
            device_id=device[kind],
            device_id_type=MESH,
        )

    def compute(step, kind):
        mine, theirs = SCATTER_SWAPS.index(kind), SCATTER_SWAPS.index(sibling_kind[kind])

        def put(columns, value):
            both_ref[...] = value
            total_ref[mine, :, columns] = both_ref[tile(core, sub), :]
            give_ref[theirs, :, columns] = both_ref[tile(1 - core, sub), :].astype(BF)

        partial(step, where[kind][0], put)
        copy = swap(sibling_kind[kind])
        copy.start()
        sent.append(copy)

    def settle(kind):
        index = SCATTER_SWAPS.index(kind)
        swap(kind).wait_recv()
        for piece in range(PIECES):
            rows = pl.ds(piece * height, height)
            value = total_ref[index, rows, :] + take_ref[index, rows, :].astype(F32)
            if kind == "P":
                hop("D", piece).wait_recv()
                value += hop_in[SCATTER_HOPS.index("D"), rows, :].astype(F32)
            if kind == "O":
                for source in ("Q", "P"):
                    hop(source, piece).wait_recv()
                    value += hop_in[SCATTER_HOPS.index(source), rows, :].astype(F32)
                finish(piece, rows, value)
            else:
                hop_out[SCATTER_HOPS.index(kind), rows, :] = value.astype(BF)
                copy = hop(kind, piece)
                copy.start()
                sent.append(copy)

    compute(0, "D")
    compute(1, "Q")
    settle("D")
    compute(2, "P")
    settle("Q")
    compute(3, "O")
    settle("P")
    settle("O")
    for copy in sent:
        copy.wait_send()


SPAN = 512


def scatter_scratch(sub):
    return [
        pltpu.VMEM((4, sub, D), F32),
        pltpu.VMEM((4, sub, D), BF),
        pltpu.VMEM((4, sub, D), BF),
        pltpu.VMEM((3, sub, D), BF),
        pltpu.VMEM((3, sub, D), BF),
        pltpu.VMEM((2 * sub, SPAN), F32),
        DMA((4,)),
        DMA((4,)),
        DMA((3, PIECES)),
        DMA((3, PIECES)),
    ]


SCATTER_REFS = 10


def home_ends(row, col, cols):
    return [(col, other) for other in range(cols)], [(other, row) for other in range(cols)]


def greet(pairs_to, row, col, waits):
    barrier = pltpu.get_barrier_semaphore()
    for to_row, to_col in pairs_to:

        @pl.when((to_row != row) | (to_col != col))
        def _():
            pl.semaphore_signal(
                barrier, inc=1, device_id={"row": to_row, "col": to_col}, device_id_type=MESH
            )

    pl.semaphore_wait(barrier, waits - (row == col).astype(jnp.int32))


def home_scratch(sub, rows):
    return [
        pltpu.VMEM((sub, D), BF),
        pltpu.VMEM((sub * COLS, D // rows), BF),
        DMA((rows, PIECES)),
        DMA((COLS, PIECES)),
        DMA((PIECES,)),
    ]


HOME_REFS = 5


class Home:
    def __init__(self, scratch):
        self.stage, self.home, self.send_sems, self.recv_sems, self.local_sems = scratch
        self.row, self.col = lax.axis_index("row"), lax.axis_index("col")
        self.rows = lax.axis_size("row")
        self.sub = self.stage.shape[0]
        self.height, self.width = self.sub // PIECES, D // self.rows
        self.senders, self.targets = home_ends(self.row, self.col, COLS)

    def meet(self, others):
        greet(self.senders, self.row, self.col, COLS + others)

    def target(self, piece):
        first = pl.multiple_of(self.col * self.sub + piece * self.height, self.height)
        return self.home.at[pl.ds(first, self.height)]

    def copies(self, piece, index):
        to_row, to_col = self.targets[index]
        source = self.stage.at[pl.ds(piece * self.height, self.height), pl.ds(index * self.width, self.width)]
        remote = pltpu.make_async_remote_copy(
            src_ref=source,
            dst_ref=self.target(piece),
            send_sem=self.send_sems.at[index, piece],
            recv_sem=self.recv_sems.at[self.col, piece],
            device_id={"row": to_row, "col": to_col},
            device_id_type=MESH,
        )
        local = pltpu.make_async_copy(source, self.target(piece), self.local_sems.at[piece])
        return (to_row == self.row) & (to_col == self.col), remote, local

    def send(self, piece):
        for index in range(self.rows):
            own, remote, local = self.copies(piece, index)

            @pl.when(own)
            def _():
                local.start()

            @pl.when(jnp.logical_not(own))
            def _():
                remote.start()

    def wait(self):
        for piece in range(PIECES):
            for index in range(self.rows):
                own, remote, local = self.copies(piece, index)

                @pl.when(own)
                def _():
                    local.wait()

                @pl.when(jnp.logical_not(own))
                def _():
                    remote.wait_send()

            for index in range(COLS):
                from_row, from_col = self.senders[index]
                spot = self.home.at[pl.ds(index * self.sub + piece * self.height, self.height)]
                arrived = pltpu.make_async_remote_copy(
                    src_ref=spot,
                    dst_ref=spot,
                    send_sem=self.send_sems.at[0, piece],
                    recv_sem=self.recv_sems.at[index, piece],
                    device_id={"row": from_row, "col": from_col},
                    device_id_type=MESH,
                )

                @pl.when((from_row != self.row) | (from_col != self.col))
                def _():
                    arrived.wait_recv()


def head_rows(block):
    turned = block.astype(F32).T
    return [turned[head * HD : (head + 1) * HD].astype(BF) for head in range(GROUP)]


def allowed_entries(key_block, low_ref, query_first):
    tokens = low_ref.shape[-1]
    key_slot = key_block * KEYS + lax.broadcasted_iota(jnp.int32, (KEYS, tokens), 0)
    query_slot = query_first + lax.broadcasted_iota(jnp.int32, (KEYS, tokens), 1)
    return (key_slot >= low_ref[...]) & (key_slot <= query_slot)


def key_rows(block):
    return pl.ds(pl.multiple_of(block * KEYS, KEYS), KEYS)


def attend_kernel(bounds, query_ref, pair_ref, low_ref, out_ref, log_ref, score_ref, mix_ref):
    step = pl.program_id(1)
    place = pl.program_id(0) * pl.num_programs(1) + step
    first, last, query_first = bounds[0, place], bounds[1, place], bounds[2, place]
    tokens = query_ref.shape[0]
    blank = jnp.zeros((HD, tokens), BF)
    queries = [jnp.concatenate([rows, blank], axis=0) for rows in head_rows(query_ref[...])]

    def score_block(block, tops):
        pairs = pair_ref[key_rows(block), :]
        allowed = allowed_entries(block, low_ref, query_first)
        new_tops = []
        for head in range(GROUP):
            scores = jnp.where(allowed, dot(pairs, queries[head], 1, 0), MASKED)
            score_ref[head, key_rows(block - first), :] = scores
            new_tops.append(jnp.maximum(tops[head], jnp.max(scores, axis=0, keepdims=True)))
        return tuple(new_tops)

    start = tuple(jnp.full((1, tokens), MASKED, F32) for _ in range(GROUP))
    tops = lax.fori_loop(first, last, score_block, start)
    mix_ref[...] = jnp.zeros_like(mix_ref)

    def mix_block(block, totals):
        pairs = pair_ref[key_rows(block), :]
        new_totals = []
        for head in range(GROUP):
            terms = jnp.exp(score_ref[head, key_rows(block - first), :] - tops[head])
            new_totals.append(totals[head] + jnp.sum(terms, axis=0, keepdims=True))
            mix_ref[head] += dot(pairs, terms.astype(BF), 0, 0)
        return tuple(new_totals)

    start = tuple(jnp.zeros((1, tokens), F32) for _ in range(GROUP))
    totals = lax.fori_loop(first, last, mix_block, start)
    mixed = jnp.concatenate(
        [mix_ref[head, HD:, :] / totals[head] for head in range(GROUP)], axis=0
    )
    out_ref[...] = mixed.T.astype(BF)
    for head in range(GROUP):
        log_ref[head : head + 1, :] = tops[head] + jnp.log(totals[head])


def attend_back_kernel(
    bounds, query_ref, grad_ref, pair_ref, low_ref, log_ref, dquery_ref, dpair_ref, prob_ref, dprob_ref, dmix_ref
):
    step = pl.program_id(1)
    place = pl.program_id(0) * pl.num_programs(1) + step
    first, last, query_first = bounds[0, place], bounds[1, place], bounds[2, place]
    tokens = query_ref.shape[0]
    blank = jnp.zeros((HD, tokens), BF)
    queries = [jnp.concatenate([rows, blank], axis=0) for rows in head_rows(query_ref[...])]
    grads = [jnp.concatenate([blank, rows], axis=0) for rows in head_rows(grad_ref[...])]

    @pl.when(step == 0)
    def _():
        dpair_ref[...] = jnp.zeros_like(dpair_ref)

    def prob_block(block, inners):
        pairs = pair_ref[key_rows(block), :]
        allowed = allowed_entries(block, low_ref, query_first)
        new_inners = []
        for head in range(GROUP):
            scores = dot(pairs, queries[head], 1, 0)
            probs = jnp.where(allowed, jnp.exp(scores - log_ref[head : head + 1, :]), 0.0)
            dprobs = dot(pairs, grads[head], 1, 0)
            prob_ref[head, key_rows(block - first), :] = probs
            dprob_ref[head, key_rows(block - first), :] = dprobs
            new_inners.append(inners[head] + jnp.sum(probs * dprobs, axis=0, keepdims=True))
        return tuple(new_inners)

    start = tuple(jnp.zeros((1, tokens), F32) for _ in range(GROUP))
    inners = lax.fori_loop(first, last, prob_block, start)
    dmix_ref[...] = jnp.zeros_like(dmix_ref)
    all_queries = jnp.concatenate(queries, axis=1)
    all_grads = jnp.concatenate(grads, axis=1)

    def back_block(block, carry):
        rows = key_rows(block)
        pairs = pair_ref[rows, :]
        all_probs, all_scores = [], []
        for head in range(GROUP):
            probs = prob_ref[head, key_rows(block - first), :]
            dprobs = dprob_ref[head, key_rows(block - first), :]
            dscores = (probs * (dprobs - inners[head])).astype(BF)
            dmix_ref[head] += dot(pairs, dscores, 0, 0)
            all_probs.append(probs.astype(BF))
            all_scores.append(dscores)
        dpair_ref[rows, :] += dot(jnp.concatenate(all_scores, axis=1), all_queries, 1, 1) + dot(
            jnp.concatenate(all_probs, axis=1), all_grads, 1, 1
        )
        return carry

    lax.fori_loop(first, last, back_block, 0)
    dquery = jnp.concatenate([dmix_ref[head, :HD, :] for head in range(GROUP)], axis=0)
    dquery_ref[...] = dquery.T * SCALE


def attend(queries, pairs, low, bounds):
    tokens, width = queries.shape
    replicas, slots, _ = pairs.shape
    rows = low.shape[2]
    blocks = low.shape[0] // replicas
    span = LMAX + KEYS
    return pl.pallas_call(
        attend_kernel,
        grid_spec=pltpu.PrefetchScalarGridSpec(
            num_scalar_prefetch=1,
            grid=(replicas, blocks),
            in_specs=[
                pl.BlockSpec((rows, GROUP * HD), lambda rep, block, _: (rep * blocks + block, 0)),
                pl.BlockSpec((None, slots, 2 * HD), lambda rep, block, _: (rep, 0, 0)),
                pl.BlockSpec((None, 1, rows), lambda rep, block, _: (rep * blocks + block, 0, 0)),
            ],
            out_specs=[
                pl.BlockSpec((rows, GROUP * HD), lambda rep, block, _: (rep * blocks + block, 0)),
                pl.BlockSpec((None, None, GROUP, rows), lambda rep, block, _: (rep, block, 0, 0)),
            ],
            scratch_shapes=[
                pltpu.VMEM((GROUP, span, rows), F32),
                pltpu.VMEM((GROUP, 2 * HD, rows), F32),
            ],
        ),
        out_shape=[
            jax.ShapeDtypeStruct((tokens, width), BF),
            jax.ShapeDtypeStruct((replicas, blocks, GROUP, rows), F32),
        ],
        compiler_params=pltpu.CompilerParams(vmem_limit_bytes=48 * 2**20),
        cost_estimate=takes(14),
        name="attend",
    )(bounds, queries, pairs, low)


def attend_back(queries, grads, pairs, low, log_total, bounds):
    tokens, width = queries.shape
    replicas, slots, _ = pairs.shape
    rows = low.shape[2]
    blocks = low.shape[0] // replicas
    span = LMAX + KEYS
    return pl.pallas_call(
        attend_back_kernel,
        grid_spec=pltpu.PrefetchScalarGridSpec(
            num_scalar_prefetch=1,
            grid=(replicas, blocks),
            in_specs=[
                pl.BlockSpec((rows, GROUP * HD), lambda rep, block, _: (rep * blocks + block, 0)),
                pl.BlockSpec((rows, GROUP * HD), lambda rep, block, _: (rep * blocks + block, 0)),
                pl.BlockSpec((None, slots, 2 * HD), lambda rep, block, _: (rep, 0, 0)),
                pl.BlockSpec((None, 1, rows), lambda rep, block, _: (rep * blocks + block, 0, 0)),
                pl.BlockSpec((None, None, GROUP, rows), lambda rep, block, _: (rep, block, 0, 0)),
            ],
            out_specs=[
                pl.BlockSpec((rows, GROUP * HD), lambda rep, block, _: (rep * blocks + block, 0)),
                pl.BlockSpec((None, slots, 2 * HD), lambda rep, block, _: (rep, 0, 0)),
            ],
            scratch_shapes=[
                pltpu.VMEM((GROUP, span, rows), F32),
                pltpu.VMEM((GROUP, span, rows), F32),
                pltpu.VMEM((GROUP, 2 * HD, rows), F32),
            ],
        ),
        out_shape=[
            jax.ShapeDtypeStruct((tokens, width), F32),
            jax.ShapeDtypeStruct((replicas, slots, 2 * HD), F32),
        ],
        compiler_params=pltpu.CompilerParams(vmem_limit_bytes=48 * 2**20),
        cost_estimate=takes(23),
        name="attend_back",
    )(bounds, queries, grads, pairs, low, log_total)


def norm_of(vectors):
    scaling = lax.rsqrt(jnp.mean(vectors * vectors, axis=1, keepdims=True) + EPS_NORM)
    return vectors * scaling, scaling


def norm_back(value, vectors, gain):
    unit, scaling = norm_of(vectors)
    weighted = value * gain
    inner = jnp.mean(weighted * unit, axis=1, keepdims=True)
    return scaling * (weighted - unit * inner), jnp.sum(value * unit, axis=0, keepdims=True)


def exchange_kernel(
    token_ref, top_ref, gain_ref, usable_ref, source_ref, normed_ref, grad_top_ref, gains_ref,
    held, held_top, held_gains, send_sems, recv_sems, gain_send, gain_recv, local_sems,
):
    row, col, rows = lax.axis_index("row"), lax.axis_index("col"), lax.axis_size("row")
    sub, width = held.shape[0], token_ref.shape[1]
    senders = [(other, row) for other in range(rows)]
    signal([{"row": partner} for partner in row_partners()])
    greet(senders, row, col, COLS + rows - 1)
    own_cols = tile(row, width)
    gain_copies = []
    for shift, partner in enumerate(row_partners()):
        copy = pltpu.make_async_remote_copy(
            src_ref=gain_ref,
            dst_ref=held_gains.at[:, own_cols],
            send_sem=gain_send.at[shift],
            recv_sem=gain_recv.at[shift],
            device_id={"row": partner},
            device_id_type=MESH,
        )
        copy.start()
        gain_copies.append(copy)
    copy = pltpu.make_async_copy(gain_ref, held_gains.at[:, own_cols], local_sems.at[2])
    copy.start()
    gain_copies.append(copy)

    def copies(array, index):
        source, target = ((token_ref, held), (top_ref, held_top))[array]
        remote = pltpu.make_async_remote_copy(
            src_ref=source.at[pl.ds(index * sub, sub)],
            dst_ref=target.at[:, own_cols],
            send_sem=send_sems.at[array, index],
            recv_sem=recv_sems.at[array, row],
            device_id={"row": col, "col": index},
            device_id_type=MESH,
        )
        local = pltpu.make_async_copy(
            source.at[pl.ds(index * sub, sub)], target.at[:, own_cols], local_sems.at[array]
        )
        return (row == col) & (col == index), remote, local

    for array in range(2):
        for index in range(COLS):
            own, remote, local = copies(array, index)

            @pl.when(own)
            def _():
                local.start()

            @pl.when(jnp.logical_not(own))
            def _():
                remote.start()

    def settle(array):
        target = (held, held_top)[array]
        for index in range(COLS):
            own, remote, local = copies(array, index)

            @pl.when(own)
            def _():
                local.wait()

            @pl.when(jnp.logical_not(own))
            def _():
                remote.wait_send()

        for from_row, from_col in senders:
            spot = target.at[:, pl.ds(from_row * width, width)]
            arrived = pltpu.make_async_remote_copy(
                src_ref=spot,
                dst_ref=spot,
                send_sem=send_sems.at[array, 0],
                recv_sem=recv_sems.at[array, from_row],
                device_id={"row": from_row, "col": from_col},
                device_id_type=MESH,
            )

            @pl.when((from_row != row) | (from_col != col))
            def _():
                arrived.wait_recv()

    for copy in gain_copies:
        copy.wait()
    settle(0)
    source_ref[...] = held[...]
    gains_ref[...] = held_gains[...]
    unit, _ = norm_of(held[...].astype(F32))
    normed_ref[...] = (unit * held_gains[0:1, :]).astype(BF)
    settle(1)
    grad_top_ref[...] = (held_top[...].astype(F32) * usable_ref[...]).astype(BF)


def exchange(tokens, top, gains, usable, rows):
    sub, width = tokens.shape[0] // COLS, tokens.shape[1]
    block = jax.ShapeDtypeStruct((sub, rows * width), BF)
    return pl.pallas_call(
        exchange_kernel,
        out_shape=[block, block, block, jax.ShapeDtypeStruct((gains.shape[0], rows * width), F32)],
        in_specs=[VMEM] * 4,
        out_specs=[VMEM] * 4,
        scratch_shapes=[
            pltpu.VMEM((sub, rows * width), BF),
            pltpu.VMEM((sub, rows * width), BF),
            pltpu.VMEM((gains.shape[0], rows * width), F32),
            DMA((2, COLS)),
            DMA((2, rows)),
            DMA((rows - 1,)),
            DMA((rows - 1,)),
            DMA((3,)),
        ],
        compiler_params=params(1),
        cost_estimate=takes(55),
        name="exchange",
    )(tokens, top, gains, usable)


def project_kernel(
    reps, own_ref, top_ref, weight_ref, cosine_ref, sine_ref,
    all_ref, top_all_ref, query_ref, pair_ref,
    held, send_sems, recv_sems, local_sem, top_held, top_send, top_recv, top_local,
    queries, pairs, halo, out_sems, pair_sems, halo_sems, pair_send, pair_recv,
):
    row, rows = lax.axis_index("row"), lax.axis_size("row")
    meet(near(reps) + [{"row": partner} for partner in row_partners()])
    sub = own_ref.shape[0]
    copies, chips = [], []
    has_next, has_last = row < rows - 1, row > 0

    @pl.when(row == 0)
    def _():
        halo[...] = jnp.zeros_like(halo)

    def out(source, target, sem):
        copy = pltpu.make_async_copy(source, target, sem)
        copy.start()
        copies.append(copy)

    def push(step, chip):
        return pltpu.make_async_remote_copy(
            src_ref=pairs.at[chip],
            dst_ref=halo.at[chip],
            send_sem=pair_send.at[step],
            recv_sem=pair_recv.at[step],
            device_id={"row": lax.rem(row + 1, rows)},
            device_id_type=MESH,
        )

    def use(step, chip):
        chips.append(chip)
        out(held.at[chip], all_ref.at[chip], out_sems.at[step])
        places = tile(chip, 2 * sub)
        turned = rotate(dot(held[chip], weight_ref[...], 1, 0), cosine_ref[places, :], sine_ref[places, :])
        queries[chip] = (turned[:, : GROUP * HD] * SCALE).astype(BF)
        out(queries.at[chip], query_ref.at[chip], out_sems.at[COLS + step])
        pairs[chip] = turned[:, GROUP * HD :].astype(BF)
        out(pairs.at[chip], pair_ref.at[lax.div(chip, 2), 1, lax.rem(chip, 2)], pair_sems.at[step])

        @pl.when(has_next)
        def _():
            push(step, chip).start()

    run_gather(reps, own_ref, held, (send_sems, recv_sems, local_sem), use)

    def use_top(step, chip):
        out(top_held.at[chip], top_all_ref.at[chip], out_sems.at[2 * COLS + step])

    run_gather(reps, top_ref, top_held, (top_send, top_recv, top_local), use_top)
    for step, chip in enumerate(chips):

        @pl.when(has_next)
        def _():
            push(step, chip).wait_send()

        @pl.when(has_last)
        def _():
            push(step, chip).wait_recv()

    for chip in range(COLS):
        out(halo.at[chip], pair_ref.at[chip // 2, 0, chip % 2], halo_sems.at[chip])
    for copy in copies:
        copy.wait()


def project(normed_own, top_own, weight, cosine, sine, reps):
    sub = normed_own.shape[0]
    return pl.pallas_call(
        functools.partial(project_kernel, reps),
        out_shape=[
            jax.ShapeDtypeStruct((COLS, 2 * sub, D), BF),
            jax.ShapeDtypeStruct((COLS, 2 * sub, D), BF),
            jax.ShapeDtypeStruct((COLS, 2 * sub, GROUP * HD), BF),
            jax.ShapeDtypeStruct((2, 2, COLS // 2, 2 * sub, 2 * HD), BF),
        ],
        in_specs=[VMEM] * 5,
        out_specs=[HBM] * 4,
        scratch_shapes=gather_scratch(sub)
        + gather_scratch(sub)
        + [
            pltpu.VMEM((COLS, 2 * sub, GROUP * HD), BF),
            pltpu.VMEM((COLS, 2 * sub, 2 * HD), BF),
            pltpu.VMEM((COLS, 2 * sub, 2 * HD), BF),
            DMA((3 * COLS,)),
            DMA((COLS,)),
            DMA((COLS,)),
            DMA((COLS,)),
            DMA((COLS,)),
        ],
        compiler_params=params(2),
        cost_estimate=takes(75),
        name="project",
    )(normed_own, top_own, weight, cosine, sine)


def mix_out_kernel(reps, attended_ref, weight_ref, source_ref, gains_ref, middle_ref, normed_ref, *scratch):
    meet(near(reps))
    parts, _, width = weight_ref.shape

    def partial(step, chip, put):
        for part in range(parts):
            put(pl.ds(part * width, width), dot(attended_ref[chip], weight_ref[part], 1, 0))

    def finish(piece, rows, value):
        middle = source_ref[rows, :].astype(F32) + value
        middle_ref[rows, :] = middle
        normed_ref[rows, :] = (norm_of(middle)[0] * gains_ref[1:2, :]).astype(BF)

    run_scatter(reps, partial, finish, scratch)


def mix_out(attended, weight, source, gains, reps):
    sub = source.shape[0]
    return pl.pallas_call(
        functools.partial(mix_out_kernel, reps),
        out_shape=[jax.ShapeDtypeStruct((sub, D), F32), jax.ShapeDtypeStruct((sub, D), BF)],
        in_specs=[VMEM] * 4,
        out_specs=[VMEM] * 2,
        scratch_shapes=scatter_scratch(sub),
        compiler_params=params(3),
        cost_estimate=takes(44),
        name="mix_out",
    )(attended, weight, source, gains)


def gated(tokens, top, weight_ref, put):
    parts, rows, width = weight_ref.shape
    units, span = rows // 3, 256

    def one_tile(index, carry):
        columns = tile(index, span)
        gate_w = weight_ref[:, :units, columns].reshape(D, span)
        up_w = weight_ref[:, units : 2 * units, columns].reshape(D, span)
        gate = dot(tokens, gate_w, 1, 0)
        up = dot(tokens, up_w, 1, 0)
        down_rows = pl.ds(pl.multiple_of(2 * units + index * span, span), span)
        grad = dot(top[:, :width], weight_ref[0, down_rows, :], 1, 1)
        for part in range(1, parts):
            grad += dot(top[:, part * width : (part + 1) * width], weight_ref[part, down_rows, :], 1, 1)
        sigma = 1.0 / (1.0 + jnp.exp(-gate))
        active = gate * sigma
        put(
            columns,
            (active * up).astype(BF),
            (grad * up * sigma * (1.0 + gate * (1.0 - sigma))).astype(BF),
            (grad * active).astype(BF),
        )
        return carry

    lax.fori_loop(0, units // span, one_tile, 0)


def first_slice_kernel(
    reps, own_ref, top_ref, weight_ref, all_ref, hidden_ref, ggate_ref, gup_ref,
    held, send_sems, recv_sems, local_sem, tops, hiddens, ggates, gups, top_sems, out_sems,
):
    meet(near(reps))
    where = plane(reps)
    order = [where[kind][0] for kind in ("O", "P", "Q", "D")]
    loads = [pltpu.make_async_copy(top_ref.at[chip], tops.at[chip], top_sems.at[step]) for step, chip in enumerate(order)]
    for copy in loads:
        copy.start()
    copies = []

    def use(step, chip):
        def out(source, target, index):
            copy = pltpu.make_async_copy(source.at[chip], target.at[chip], out_sems.at[index, step])
            copy.start()
            copies.append(copy)

        out(held, all_ref, 0)
        loads[step].wait()

        def put(columns, hidden, ggate, gup):
            hiddens[chip, :, columns] = hidden
            ggates[chip, :, columns] = ggate
            gups[chip, :, columns] = gup

        gated(held[chip], tops[chip], weight_ref, put)
        out(hiddens, hidden_ref, 1)
        out(ggates, ggate_ref, 2)
        out(gups, gup_ref, 3)

    run_gather(reps, own_ref, held, (send_sems, recv_sems, local_sem), use)
    for copy in copies:
        copy.wait()


def first_slice(normed_own, top_all, weight, reps):
    sub = normed_own.shape[0]
    units = weight.shape[1] // 3
    piece = jax.ShapeDtypeStruct((COLS, 2 * sub, units), BF)
    return pl.pallas_call(
        functools.partial(first_slice_kernel, reps),
        out_shape=[jax.ShapeDtypeStruct((COLS, 2 * sub, D), BF)] + [piece] * 3,
        in_specs=[VMEM, HBM, VMEM],
        out_specs=[HBM] * 4,
        scratch_shapes=gather_scratch(sub)
        + [pltpu.VMEM((COLS, 2 * sub, D), BF)]
        + [pltpu.VMEM((COLS, 2 * sub, units), BF)] * 3
        + [DMA((COLS,)), DMA((4, COLS))],
        compiler_params=params(4),
        cost_estimate=takes(50),
        name="first_slice",
    )(normed_own, top_all, weight)


def second_slice_kernel(
    reps, token_ref, top_ref, ggate_one_ref, gup_one_ref, weight_one_ref, weight_ref, middle_ref, own_top_ref, gains_ref,
    hidden_ref, ggate_ref, gup_ref, grad_ref, low_ref, gain_ref, *scratch,
):
    tokens, tops, ggate_ones, gup_ones, weight_one, hiddens, ggates, gups, in_sems, out_sems, weight_sem = scratch[SCATTER_REFS:]
    meet(near(reps))
    order = scatter_order(reps)
    parts, rows, width = weight_ref.shape
    units = rows // 3
    loads, copies = {}, []
    sources = ((token_ref, tokens), (top_ref, tops), (ggate_one_ref, ggate_ones), (gup_one_ref, gup_ones))

    def load(step):
        loads[step] = []
        for index, (source, target) in enumerate(sources):
            copy = pltpu.make_async_copy(source.at[order[step]], target.at[step % 2], in_sems.at[index, step % 2])
            copy.start()
            loads[step].append(copy)

    load(0)
    weight_copy = pltpu.make_async_copy(weight_one_ref.at[:, pl.ds(0, 2 * units)], weight_one, weight_sem)
    weight_copy.start()
    gain_ref[...] = jnp.zeros_like(gain_ref)

    def partial(step, chip, put):
        slot = step % 2
        for copy in loads[step]:
            copy.wait()
        if step < 3:
            load(step + 1)

        def keep(columns, hidden, ggate, gup):
            hiddens[chip, :, columns] = hidden
            ggates[chip, :, columns] = ggate
            gups[chip, :, columns] = gup

        gated(tokens[slot], tops[slot], weight_ref, keep)
        for index, (source, target) in enumerate(((hiddens, hidden_ref), (ggates, ggate_ref), (gups, gup_ref))):
            copy = pltpu.make_async_copy(source.at[chip], target.at[chip], out_sems.at[index, step])
            copy.start()
            copies.append(copy)
        if step == 0:
            weight_copy.wait()
        for part in range(parts):
            value = dot(ggates[chip], weight_ref[part, :units, :], 1, 1)
            value += dot(gups[chip], weight_ref[part, units : 2 * units, :], 1, 1)
            value += dot(ggate_ones[slot], weight_one[part, :units, :], 1, 1)
            value += dot(gup_ones[slot], weight_one[part, units:, :], 1, 1)
            put(pl.ds(part * width, width), value)

    def finish(piece, rows_of, value):
        back, gain_part = norm_back(value, middle_ref[rows_of, :], gains_ref[1:2, :])
        grad = own_top_ref[rows_of, :].astype(F32) + back
        grad_ref[rows_of, :] = grad
        low_ref[rows_of, :] = grad.astype(BF)
        gain_ref[0:1, :] += gain_part

    run_scatter(reps, partial, finish, scratch[:SCATTER_REFS])
    for copy in copies:
        copy.wait()


def second_slice(normed_all, top_all, ggate_one, gup_one, weight_one, weight, middle, own_top, gains, reps):
    sub = middle.shape[0]
    parts, rows, width = weight.shape
    units = rows // 3
    piece = jax.ShapeDtypeStruct((COLS, 2 * sub, units), BF)
    return pl.pallas_call(
        functools.partial(second_slice_kernel, reps),
        out_shape=[piece] * 3
        + [
            jax.ShapeDtypeStruct((sub, D), F32),
            jax.ShapeDtypeStruct((sub, D), BF),
            jax.ShapeDtypeStruct((8, D), F32),
        ],
        in_specs=[HBM] * 5 + [VMEM] * 4,
        out_specs=[HBM] * 3 + [VMEM] * 3,
        scratch_shapes=scatter_scratch(sub)
        + [pltpu.VMEM((2, 2 * sub, D), BF)] * 2
        + [pltpu.VMEM((2, 2 * sub, units), BF)] * 2
        + [pltpu.VMEM((parts, 2 * units, width), BF)]
        + [pltpu.VMEM((COLS, 2 * sub, units), BF)] * 3
        + [DMA((4, 2)), DMA((3, COLS)), DMA],
        compiler_params=params(5),
        cost_estimate=takes(65),
        name="second_slice",
    )(normed_all, top_all, ggate_one, gup_one, weight_one, weight, middle, own_top, gains)


def back_out_kernel(
    reps, own_ref, weight_ref, all_ref, grad_ref, held, send_sems, recv_sems, local_sem, grads, out_sems
):
    meet(near(reps))
    parts, _, width = weight_ref.shape
    copies = []

    def use(step, chip):
        def out(source, target, index):
            copy = pltpu.make_async_copy(source.at[chip], target.at[chip], out_sems.at[index, step])
            copy.start()
            copies.append(copy)

        out(held, all_ref, 0)
        total = dot(held[chip, :, :width], weight_ref[0], 1, 1)
        for part in range(1, parts):
            total += dot(held[chip, :, part * width : (part + 1) * width], weight_ref[part], 1, 1)
        grads[chip] = total.astype(BF)
        out(grads, grad_ref, 1)

    run_gather(reps, own_ref, held, (send_sems, recv_sems, local_sem), use)
    for copy in copies:
        copy.wait()


def back_out(grad_own, weight, reps):
    sub = grad_own.shape[0]
    return pl.pallas_call(
        functools.partial(back_out_kernel, reps),
        out_shape=[
            jax.ShapeDtypeStruct((COLS, 2 * sub, D), BF),
            jax.ShapeDtypeStruct((COLS, 2 * sub, weight.shape[1]), BF),
        ],
        in_specs=[VMEM] * 2,
        out_specs=[HBM] * 2,
        scratch_shapes=gather_scratch(sub)
        + [pltpu.VMEM((COLS, 2 * sub, weight.shape[1]), BF), DMA((2, COLS))],
        compiler_params=params(6),
        cost_estimate=takes(41),
        name="back_out",
    )(grad_own, weight)


def lift_kernel(
    reps, hidden_one_ref, hidden_two_ref, weight_one_ref, weight_two_ref, middle_ref, result_ref, *scratch
):
    weight_one, weight_two, weight_sems = scratch[SCATTER_REFS + HOME_REFS :]
    parts, units, width = weight_one.shape
    loads = []
    for index, (source, target) in enumerate(((weight_one_ref, weight_one), (weight_two_ref, weight_two))):
        copy = pltpu.make_async_copy(source.at[:, pl.ds(2 * units, units)], target, weight_sems.at[index])
        copy.start()
        loads.append(copy)
    signal(near(reps))
    home = Home(scratch[SCATTER_REFS : SCATTER_REFS + HOME_REFS])
    home.meet(3)
    for copy in loads:
        copy.wait()

    def partial(step, chip, put):
        for part in range(parts):
            value = dot(hidden_one_ref[chip], weight_one[part], 1, 0)
            put(pl.ds(part * width, width), value + dot(hidden_two_ref[chip], weight_two[part], 1, 0))

    def finish(piece, rows, value):
        home.stage[rows, :] = (middle_ref[rows, :] + value).astype(BF)
        home.send(piece)

    run_scatter(reps, partial, finish, scratch[:SCATTER_REFS])
    home.wait()
    result_ref[...] = home.home[...]


def lift(hidden_one, hidden_two, weight_one, weight_two, middle, reps):
    sub = middle.shape[0]
    parts, rows, width = weight_one.shape
    return pl.pallas_call(
        functools.partial(lift_kernel, reps),
        out_shape=jax.ShapeDtypeStruct((sub * COLS, width), BF),
        in_specs=[VMEM] * 2 + [HBM] * 2 + [VMEM],
        out_specs=VMEM,
        scratch_shapes=scatter_scratch(sub)
        + home_scratch(sub, parts)
        + [pltpu.VMEM((parts, rows // 3, width), BF)] * 2
        + [DMA((2,))],
        compiler_params=params(7),
        cost_estimate=takes(50),
        name="lift",
    )(hidden_one, hidden_two, weight_one, weight_two, middle)


def turn_back_kernel(dquery_ref, dpair_ref, cosine_ref, sine_ref, proj_ref, low, taken, send_sem, recv_sem):
    row, rows = lax.axis_index("row"), lax.axis_size("row")
    meet([{"row": partner} for partner in row_partners()])
    chips, height, _ = proj_ref.shape
    low[...] = dpair_ref[:, 0].astype(BF)
    push = pltpu.make_async_remote_copy(
        src_ref=low,
        dst_ref=taken,
        send_sem=send_sem,
        recv_sem=recv_sem,
        device_id={"row": lax.rem(row + rows - 1, rows)},
        device_id_type=MESH,
    )

    @pl.when(row > 0)
    def _():
        push.start()

    @pl.when(row == rows - 1)
    def _():
        taken[...] = jnp.zeros_like(taken)

    @pl.when(row < rows - 1)
    def _():
        push.wait_recv()

    for chip in range(chips):
        places = pl.ds(chip * height, height)
        pair_rows = pl.ds(chip % 2 * height, height)
        pair = dpair_ref[chip // 2, 1, pair_rows, :] + taken[chip // 2, pair_rows, :].astype(F32)
        grad = jnp.concatenate([dquery_ref[places, :], pair], axis=1)
        proj_ref[chip] = rotate(grad, cosine_ref[places, :], -sine_ref[places, :]).astype(BF)

    @pl.when(row > 0)
    def _():
        push.wait_send()


def turn_back(dquery, dpairs, cosine, sine):
    tokens, width = dquery.shape
    halves, _, slots, lanes = dpairs.shape
    return pl.pallas_call(
        turn_back_kernel,
        out_shape=jax.ShapeDtypeStruct((COLS, tokens // COLS, width + lanes), BF),
        in_specs=[VMEM] * 4,
        out_specs=VMEM,
        scratch_shapes=[pltpu.VMEM((halves, slots, lanes), BF)] * 2 + [DMA, DMA],
        compiler_params=params(9),
        cost_estimate=takes(20),
        name="turn_back",
    )(dquery, dpairs, cosine, sine)


PEERS = ("SO", "P", "SP", "Q", "SQ", "D", "SD")


def project_back_kernel(
    reps, proj_ref, weight_ref, source_ref, middle_ref, gains_ref, gain_two_ref, resid_ref, gain_ref, *scratch
):
    gain_own, gain_rows, gain_plane, row_send, row_recv, plane_send, plane_recv = scratch[SCATTER_REFS + HOME_REFS :]
    where = plane(reps)
    row = lax.axis_index("row")
    partners = row_partners()
    signal([where[kind][2] for kind in PEERS] + [{"row": partner} for partner in partners])
    home = Home(scratch[SCATTER_REFS : SCATTER_REFS + HOME_REFS])
    home.meet(len(PEERS) + len(partners))
    gain_own[...] = jnp.zeros_like(gain_own)
    gain_own[1:2, :] = gain_two_ref[0:1, :]

    def partial(step, chip, put):
        for index in range(D // SPAN):
            columns = pl.ds(index * SPAN, SPAN)
            put(columns, dot(proj_ref[chip], weight_ref[columns, :], 1, 1))

    def finish(piece, rows, value):
        back, gain_part = norm_back(value, source_ref[rows, :].astype(F32), gains_ref[0:1, :])
        home.stage[rows, :] = (middle_ref[rows, :] + back).astype(BF)
        home.send(piece)
        gain_own[0:1, :] += gain_part

    run_scatter(reps, partial, finish, scratch[:SCATTER_REFS])
    width = gain_ref.shape[1]
    copies = []
    for shift, partner in enumerate(partners):
        copy = pltpu.make_async_remote_copy(
            src_ref=gain_own.at[:, tile(partner, width)],
            dst_ref=gain_rows.at[shift],
            send_sem=row_send.at[shift],
            recv_sem=row_recv.at[shift],
            device_id={"row": partner},
            device_id_type=MESH,
        )
        copy.start()
        copies.append(copy)
    for copy in copies:
        copy.wait()
    total = gain_own[:, tile(row, width)]
    for shift in range(len(partners)):
        total += gain_rows[shift]
    own = where["O"][0] * 2 + where["O"][1]
    gain_plane[own] = total

    def share(index, place):
        return pltpu.make_async_remote_copy(
            src_ref=gain_plane.at[place],
            dst_ref=gain_plane.at[place],
            send_sem=plane_send.at[index],
            recv_sem=plane_recv.at[place],
            device_id=where[PEERS[index]][2],
            device_id_type=MESH,
        )

    for index in range(len(PEERS)):
        share(index, own).start()
    for index, kind in enumerate(PEERS):
        share(index, where[kind][0] * 2 + where[kind][1]).wait_recv()
    total = gain_plane[0]
    for place in range(1, 2 * COLS):
        total += gain_plane[place]
    gain_ref[...] = total
    for index in range(len(PEERS)):
        share(index, own).wait_send()
    home.wait()
    resid_ref[...] = home.home[...]


def project_back(grad_proj, weight, source, grad_middle, gains, gain_two, reps, rows):
    sub = source.shape[0]
    width = D // rows
    return pl.pallas_call(
        functools.partial(project_back_kernel, reps),
        out_shape=[jax.ShapeDtypeStruct((sub * COLS, width), BF), jax.ShapeDtypeStruct((8, width), F32)],
        in_specs=[VMEM] * 6,
        out_specs=[VMEM] * 2,
        scratch_shapes=scatter_scratch(sub)
        + home_scratch(sub, rows)
        + [
            pltpu.VMEM((8, D), F32),
            pltpu.VMEM((rows - 1, 8, width), F32),
            pltpu.VMEM((2 * COLS, 8, width), F32),
            DMA((rows - 1,)),
            DMA((rows - 1,)),
            DMA((len(PEERS),)),
            DMA((2 * COLS,)),
        ],
        compiler_params=params(8),
        cost_estimate=takes(55),
        name="project_back",
    )(grad_proj, weight, source, grad_middle, gains, gain_two)


def adamw(weights, gradient, moment, square, step_rate, decay_rate):
    gradient = gradient.astype(F32)
    moment_new = BETA_ONE * moment + (1.0 - BETA_ONE) * gradient
    square_new = BETA_TWO * square + (1.0 - BETA_TWO) * gradient * gradient
    moment_hat = moment_new / (1.0 - BETA_ONE**STEP)
    square_hat = square_new / (1.0 - BETA_TWO**STEP)
    weights_new = weights - step_rate * (
        moment_hat / (jnp.sqrt(square_hat) + ADAM_EPS) + decay_rate * weights
    )
    return (weights_new, moment_new, square_new)


def local(
    resid_in,
    cotangent,
    seq_lens,
    qkv_weight,
    qkv_moment,
    qkv_square,
    out_weight,
    out_moment,
    out_square,
    gate_weight,
    gate_moment,
    gate_square,
    up_weight,
    up_moment,
    up_square,
    down_weight,
    down_moment,
    down_square,
    norm_gains,
    gain_moment,
    gain_square,
):
    cols, rows, replicas = lax.axis_size("col"), lax.axis_size("row"), lax.axis_size("dp")
    reps = replicas // 2
    half = lax.axis_index("dp") // reps
    row, col = lax.axis_index("row"), lax.axis_index("col")
    chunk = resid_in.shape[0]
    sub = chunk // cols
    blocks = 2 * cols
    plane_tokens = sub * blocks
    head_width = (GROUP + 2) * HD

    qkv_block = half_columns(qkv_weight, reps)
    out_block = tall_block(out_weight, reps)
    split = out_block.shape[1] // 2
    stacked = jnp.concatenate([out_block[:, :split], out_block[:, split:]], axis=0)
    first_w = lax.all_gather(jnp.concatenate([qkv_block, stacked], axis=1), "row", axis=0)
    qkv_w = first_w[:, :, :head_width].reshape(D, head_width)
    heads = out_block.shape[0]
    out_w = jnp.concatenate([first_w[:, :heads, head_width:], first_w[:, heads:, head_width:]], axis=2)
    gate_block, up_block = half_columns(gate_weight, reps), half_columns(up_weight, reps)
    down_block = tall_block(down_weight, reps)
    units = gate_block.shape[1] // SLICES
    slice_w = []
    for index in range(SLICES):
        span = slice(index * units, (index + 1) * units)
        block = jnp.concatenate([gate_block[:, span], up_block[:, span], down_block[span]], axis=0)
        slice_w.append(lax.all_gather(block, "row", axis=0))

    lengths = both_halves(seq_lens, partner_swap(seq_lens, reps), half, 0)
    ends = jnp.cumsum(lengths, axis=1, dtype=jnp.int32)
    slot = (row * chunk + jnp.arange(chunk, dtype=jnp.int32)).reshape(1, chunk)
    passed = (slot[:, :, None] >= ends[:, None, :]).astype(jnp.int32)
    seq_start = jnp.sum(passed * lengths[:, None, :], axis=2, dtype=jnp.int32)
    usable = slot < ends[:, -1:]
    cosine, sine = rope_tables((slot - seq_start).reshape(plane_tokens))
    low = (jnp.where(usable, seq_start, slot) - (row - 1) * chunk).reshape(blocks, 1, sub)
    firsts = jnp.tile(chunk + jnp.arange(cols, dtype=jnp.int32) * sub, 2)
    bounds = jnp.stack([low[:, 0, 0] // KEYS, (firsts + sub - 1) // KEYS + 1, firsts]).astype(jnp.int32)
    usable_mine = (row * chunk + col * sub + jnp.arange(sub, dtype=jnp.int32)) < jnp.sum(seq_lens)

    padded = jnp.concatenate([norm_gains, jnp.zeros((6, norm_gains.shape[1]), F32)])
    source, normed_own, grad_top, gains = exchange(
        resid_in, cotangent, padded, usable_mine.astype(F32)[:, None], rows
    )
    normed_one, grad_top_all, queries, pairs = project(normed_own, grad_top, qkv_w, cosine, sine, reps)
    queries = queries.reshape(plane_tokens, GROUP * HD)
    pairs = pairs.reshape(2, 2 * chunk, 2 * HD)
    attended, log_total = attend(queries, pairs, low, bounds)
    middle, normed_own = mix_out(attended.reshape(cols, 2 * sub, GROUP * HD), out_w, source, gains, reps)

    flat_top = grad_top_all.reshape(plane_tokens, D)

    def slice_grads(normed_all, hidden, ggate, gup):
        flat = normed_all.reshape(plane_tokens, D)
        parts = [
            dot(flat, ggate.reshape(plane_tokens, units), 0, 0).astype(BF).reshape(rows, -1, units),
            dot(flat, gup.reshape(plane_tokens, units), 0, 0).astype(BF).reshape(rows, -1, units),
            row_blocks(dot(hidden.reshape(plane_tokens, units), flat_top, 0, 0).astype(BF), rows),
        ]
        return jnp.concatenate(parts, axis=1)

    normed_two, hidden_one, ggate_one, gup_one = first_slice(normed_own, grad_top_all, slice_w[0], reps)
    grads_one = slice_grads(normed_two, hidden_one, ggate_one, gup_one)
    normed_two, grads_one = lax.optimization_barrier((normed_two, grads_one))
    hidden_two, ggate_two, gup_two, grad_middle, grad_middle_own, gain_grad_two = second_slice(
        normed_two, grad_top_all, ggate_one, gup_one, slice_w[0], slice_w[1], middle, grad_top, gains, reps
    )
    grads_two = slice_grads(normed_two, hidden_two, ggate_two, gup_two)
    grad_middle_own, grads_two = lax.optimization_barrier((grad_middle_own, grads_two))
    slice_g = [lax.psum_scatter(part, "row", scatter_dimension=0) for part in (grads_one, grads_two)]

    grad_middle_all, grad_attended = back_out(grad_middle_own, out_w, reps)
    result = lift(hidden_one, hidden_two, slice_w[0], slice_w[1], middle, reps)
    grad_attended, slice_g[0], result = lax.optimization_barrier((grad_attended, slice_g[0], result))
    grad_query, grad_pairs = attend_back(
        queries, grad_attended.reshape(plane_tokens, GROUP * HD), pairs, low, log_total, bounds
    )
    grad_proj = turn_back(grad_query, grad_pairs.reshape(2, 2, chunk, 2 * HD), cosine, sine)
    grad_qkv = dot(normed_one.reshape(plane_tokens, D), grad_proj.reshape(plane_tokens, head_width), 0, 0).astype(BF)
    grad_proj, grad_qkv = lax.optimization_barrier((grad_proj, grad_qkv))
    resid_grad, gain_grads = project_back(
        grad_proj, qkv_w, source, grad_middle, gains, gain_grad_two, reps, rows
    )
    resid_grad = resid_grad.astype(F32)
    attended, slice_g[1] = lax.optimization_barrier((attended, slice_g[1]))
    grad_out = row_blocks(dot(attended, grad_middle_all.reshape(plane_tokens, D), 0, 0).astype(BF), rows)
    grad_out = own_tall(lax.psum_scatter(grad_out, "row", scatter_dimension=0), reps)
    grad_qkv = own_rows(lax.psum_scatter(grad_qkv, "row", scatter_dimension=0, tiled=True), reps)
    wide = sum(part.shape[0] for part in slice_g) // (3 * SLICES)
    grad_gate = own_rows(jnp.concatenate([part[:wide] for part in slice_g], axis=1), reps)
    grad_up = own_rows(jnp.concatenate([part[wide : 2 * wide] for part in slice_g], axis=1), reps)
    grad_down = own_tall(jnp.concatenate([part[2 * wide :] for part in slice_g], axis=0), reps)

    gain_grads = gain_grads[:2]
    if reps > 1:
        gain_grads = lax.psum(gain_grads, "dp", axis_index_groups=rep_groups(reps))
    qkv_set = adamw(qkv_weight, grad_qkv, qkv_moment, qkv_square, RATE_MATRIX, WEIGHT_DECAY)
    out_set = adamw(out_weight, grad_out, out_moment, out_square, RATE_OUTPUT, WEIGHT_DECAY)
    gate_set = adamw(gate_weight, grad_gate, gate_moment, gate_square, RATE_MATRIX, WEIGHT_DECAY)
    up_set = adamw(up_weight, grad_up, up_moment, up_square, RATE_MATRIX, WEIGHT_DECAY)
    down_set = adamw(down_weight, grad_down, down_moment, down_square, RATE_MATRIX, WEIGHT_DECAY)
    gain_set = adamw(norm_gains, gain_grads, gain_moment, gain_square, RATE_GAIN, 0.0)
    return (result, resid_grad, *qkv_set, *out_set, *gate_set, *up_set, *down_set, *gain_set)


def solution(mesh):
    tokens = P(("dp", "col"), "row")
    wide = P(("row", "dp"), "col")
    tall = P(("col", "dp"), "row")
    gain = P(None, "row")
    weights = (wide,) * 3 + (tall,) * 3 + (wide,) * 6 + (tall,) * 3 + (gain,) * 3
    return jax.shard_map(
        local,
        mesh=mesh,
        in_specs=(tokens, tokens, P("dp", None)) + weights,
        out_specs=(tokens, tokens) + weights,
        check_vma=False,
    )
```

```python
import functools

import jax
import jax.numpy as jnp
from jax import lax
from jax.experimental import pallas as pl
from jax.experimental.pallas import tpu as pltpu
from jax.sharding import PartitionSpec as P

D = 2048
FF = 8192
HD = 64
GROUP = 4
LMAX = 1024
STEP = 10
KEYS = 256
SLICES = 2
PIECES = 4
COLS = 4

EPS_NORM = 1e-05
ROPE_BASE = 500000.0
BETA_ONE = 0.9
BETA_TWO = 0.95
ADAM_EPS = 1e-08
WEIGHT_DECAY = 0.1
RATE_MATRIX = 0.05
RATE_OUTPUT = 0.4
RATE_GAIN = 0.8
MASKED = -1e30
SCALE = HD ** (-0.5)

BF = jnp.bfloat16
F32 = jnp.float32


def dot(left, right, left_dim, right_dim):
    return lax.dot_general(
        left, right, (((left_dim,), (right_dim,)), ((), ())), preferred_element_type=F32
    )


def half_groups(reps):
    return [[rep, rep + reps] for rep in range(reps)]


def rep_groups(reps):
    return [[half * reps + rep for rep in range(reps)] for half in range(2)]


def partner_swap(values_in, reps):
    pairs = [pair for rep in range(reps) for pair in ((rep, rep + reps), (rep + reps, rep))]
    return lax.ppermute(values_in, "dp", pairs)


def both_halves(mine, theirs, half, axis):
    first = jnp.where(half == 0, mine, theirs)
    second = jnp.where(half == 0, theirs, mine)
    return jnp.concatenate([first, second], axis=axis)


def half_columns(weight, reps, after=None):
    half = lax.axis_index("dp") // reps
    own, width = weight.shape[0], weight.shape[1] // 2
    low = weight.astype(BF)
    mine = lax.dynamic_slice_in_dim(low, half * width, width, 1)
    theirs = partner_swap(lax.dynamic_slice_in_dim(low, (1 - half) * width, width, 1), reps)
    if after is not None:
        theirs, _ = lax.optimization_barrier((theirs, after))
    both = both_halves(mine, theirs, half, 0)
    if reps > 1:
        both = lax.all_gather(both, "dp", axis=0, axis_index_groups=rep_groups(reps))
        both = both.reshape(reps, 2, own, width).swapaxes(0, 1).reshape(2 * reps * own, width)
    return both


def own_rows(part, reps):
    half = lax.axis_index("dp") // reps
    height = part.shape[0] // 2
    mine = lax.dynamic_slice_in_dim(part, half * height, height, 0)
    theirs = partner_swap(lax.dynamic_slice_in_dim(part, (1 - half) * height, height, 0), reps)
    part = both_halves(mine, theirs, half, 1)
    if reps > 1:
        part = lax.psum_scatter(
            part, "dp", scatter_dimension=0, tiled=True, axis_index_groups=rep_groups(reps)
        )
    return part


def tall_block(weight, reps):
    own = weight.astype(BF)
    if reps > 1:
        own = lax.all_gather(own, "dp", axis=0, tiled=True, axis_index_groups=rep_groups(reps))
    return own


def own_tall(part, reps):
    if reps > 1:
        part = lax.psum_scatter(
            part, "dp", scatter_dimension=0, tiled=True, axis_index_groups=rep_groups(reps)
        )
    return part


def row_blocks(matrix, rows):
    return matrix.reshape(matrix.shape[0], rows, -1).swapaxes(0, 1)


def rope_tables(position):
    exponent = jnp.arange(0, HD, 2, dtype=F32) / HD
    freq_table = 1.0 / ROPE_BASE**exponent
    angle = position.astype(F32)[:, None] * freq_table[None, :]
    cosine = jnp.cos(angle)
    sine = jnp.sin(angle)
    return (jnp.concatenate([cosine] * 4, axis=1), jnp.concatenate([-sine, sine, -sine, sine], axis=1))


def rotate(vectors, cosine, sine):
    width = vectors.shape[1]
    lane = lax.broadcasted_iota(jnp.int32, vectors.shape, 1)
    lower = lax.rem(lane, HD) < HD // 2
    turned = jnp.where(
        lower, pltpu.roll(vectors, width - HD // 2, 1), pltpu.roll(vectors, HD // 2, 1)
    )
    copies = width // cosine.shape[1]
    cosine = jnp.concatenate([cosine] * copies, axis=1)
    sine = jnp.concatenate([sine] * copies, axis=1)
    return jnp.where(lane < (GROUP + 1) * HD, vectors * cosine + turned * sine, vectors)


MESH = pl.DeviceIdType.MESH
HBM = pl.BlockSpec(memory_space=pl.ANY)
VMEM = pl.BlockSpec(memory_space=pltpu.VMEM)
DMA = pltpu.SemaphoreType.DMA


def takes(micros):
    return pl.CostEstimate(flops=1, bytes_accessed=int(micros * 3.6e6), transcendentals=0)


def params(collective_id):
    return pltpu.CompilerParams(
        collective_id=collective_id, has_side_effects=True, vmem_limit_bytes=60 * 2**20
    )


def tile(index, width):
    return pl.ds(pl.multiple_of(index * width, width), width)


def plane(reps):
    replica, col = lax.axis_index("dp"), lax.axis_index("col")
    half, rep = lax.div(replica, reps), lax.rem(replica, reps)
    core = lax.rem(col, 2)
    other = col + 1 - 2 * core

    def place(half_of, col_of):
        chip = half_of * (COLS // 2) + lax.div(col_of, 2)
        return (chip, lax.rem(col_of, 2), {"dp": half_of * reps + rep, "col": col_of})

    def turn(value, by, modulus):
        return lax.rem(value + by, modulus)

    return {
        "O": place(half, col),
        "P": place(turn(half, 1 - core, 2), turn(col, 2 * core, COLS)),
        "Q": place(turn(half, core, 2), turn(col, 2 - 2 * core, COLS)),
        "D": place(1 - half, turn(col, 2, COLS)),
        "SO": place(half, other),
        "SP": place(turn(half, core, 2), turn(other, 2 - 2 * core, COLS)),
        "SQ": place(turn(half, 1 - core, 2), turn(other, 2 * core, COLS)),
        "SD": place(1 - half, turn(other, 2, COLS)),
    }


def near(reps):
    where = plane(reps)
    return [where["P"][2], where["Q"][2], where["SO"][2]]


def row_partners():
    rows, row = lax.axis_size("row"), lax.axis_index("row")
    return [lax.rem(row + shift, rows) for shift in range(1, rows)]


def signal(devices):
    barrier = pltpu.get_barrier_semaphore()
    for device in devices:
        pl.semaphore_signal(barrier, inc=1, device_id=device, device_id_type=MESH)


def meet(devices):
    signal(devices)
    pl.semaphore_wait(pltpu.get_barrier_semaphore(), len(devices))


GATHER_KINDS = ("P", "Q", "D", "SO", "SP", "SQ", "SD")


def run_gather(reps, own_ref, held_ref, sems, use):
    send_sems, recv_sems, local_sem = sems
    where = plane(reps)
    sub = own_ref.shape[0]
    height = sub // PIECES

    def spot(kind, piece):
        chip, core, _ = where[kind]
        return held_ref.at[chip, pl.ds(pl.multiple_of(core * sub + piece * height, height), height)]

    def message(kind, piece, source, target, device):
        index = GATHER_KINDS.index(kind)
        return pltpu.make_async_remote_copy(
            src_ref=source,
            dst_ref=target,
            send_sem=send_sems.at[index, piece],
            recv_sem=recv_sems.at[index, piece],
            device_id=device,
            device_id_type=MESH,
        )

    near_p, near_q, sibling = where["P"][2], where["Q"][2], where["SO"][2]
    sent = []

    def send(kind, piece, source, held_by, device):
        copy = message(kind, piece, source, spot(held_by, piece), device)
        copy.start()
        sent.append(copy)

    def arrive(kind, piece):
        message(kind, piece, spot(kind, piece), spot(kind, piece), sibling).wait_recv()

    own_copy = pltpu.make_async_copy(own_ref, held_ref.at[where["O"][0], tile(where["O"][1], sub)], local_sem)
    own_copy.start()
    for piece in range(PIECES):
        source = own_ref.at[pl.ds(piece * height, height)]
        send("P", piece, source, "O", near_p)
        send("Q", piece, source, "O", near_q)
        send("SO", piece, source, "O", sibling)
    own_copy.wait()
    for piece in range(PIECES):
        arrive("SO", piece)
    use(0, where["O"][0])
    for piece in range(PIECES):
        arrive("P", piece)
        send("D", piece, spot("P", piece), "P", near_q)
        send("SP", piece, spot("P", piece), "P", sibling)
    for piece in range(PIECES):
        arrive("Q", piece)
        send("SQ", piece, spot("Q", piece), "Q", sibling)
    for piece in range(PIECES):
        arrive("SQ", piece)
    use(1, where["P"][0])
    for piece in range(PIECES):
        arrive("SP", piece)
    use(2, where["Q"][0])
    for piece in range(PIECES):
        arrive("D", piece)
        send("SD", piece, spot("D", piece), "D", sibling)
    for piece in range(PIECES):
        arrive("SD", piece)
    use(3, where["D"][0])
    for copy in sent:
        copy.wait_send()


def gather_scratch(sub):
    count = len(GATHER_KINDS)
    return [pltpu.VMEM((COLS, 2 * sub, D), BF), DMA((count, PIECES)), DMA((count, PIECES)), DMA]


SCATTER_SWAPS = ("D", "Q", "P", "O")
SCATTER_HOPS = ("D", "Q", "P")


def scatter_order(reps):
    where = plane(reps)
    return [where[kind][0] for kind in SCATTER_SWAPS]


def run_scatter(reps, partial, finish, scratch, meanwhile=None):
    total_ref, give_ref, take_ref, hop_out, hop_in, both_ref, swap_send, swap_recv, hop_send, hop_recv = scratch
    where = plane(reps)
    core = where["O"][1]
    device = {"P": where["P"][2], "Q": where["Q"][2], "D": where["Q"][2]}
    sibling = where["SO"][2]
    sub = total_ref.shape[1]
    height = sub // PIECES
    sibling_kind = {"D": "D", "Q": "P", "P": "Q", "O": "O"}
    sent = []

    def swap(kind):
        index = SCATTER_SWAPS.index(kind)
        return pltpu.make_async_remote_copy(
            src_ref=give_ref.at[index],
            dst_ref=take_ref.at[index],
            send_sem=swap_send.at[index],
            recv_sem=swap_recv.at[index],
            device_id=sibling,
            device_id_type=MESH,
        )

    def hop(kind, piece):
        index = SCATTER_HOPS.index(kind)
        rows = pl.ds(piece * height, height)
        return pltpu.make_async_remote_copy(
            src_ref=hop_out.at[index, rows],
            dst_ref=hop_in.at[index, rows],
            send_sem=hop_send.at[index, piece],
            recv_sem=hop_recv.at[index, piece],
            device_id=device[kind],
            device_id_type=MESH,
        )

    def compute(step, kind):
        mine, theirs = SCATTER_SWAPS.index(kind), SCATTER_SWAPS.index(sibling_kind[kind])

        def put(columns, value):
            both_ref[...] = value
            total_ref[mine, :, columns] = both_ref[tile(core, sub), :]
            give_ref[theirs, :, columns] = both_ref[tile(1 - core, sub), :].astype(BF)

        partial(step, where[kind][0], put)
        copy = swap(sibling_kind[kind])
        copy.start()
        sent.append(copy)

    def settle(kind):
        index = SCATTER_SWAPS.index(kind)
        swap(kind).wait_recv()
        for piece in range(PIECES):
            rows = pl.ds(piece * height, height)
            value = total_ref[index, rows, :] + take_ref[index, rows, :].astype(F32)
            if kind == "P":
                hop("D", piece).wait_recv()
                value += hop_in[SCATTER_HOPS.index("D"), rows, :].astype(F32)
            if kind == "O":
                for source in ("Q", "P"):
                    hop(source, piece).wait_recv()
                    value += hop_in[SCATTER_HOPS.index(source), rows, :].astype(F32)
                finish(piece, rows, value)
            else:
                hop_out[SCATTER_HOPS.index(kind), rows, :] = value.astype(BF)
                copy = hop(kind, piece)
                copy.start()
                sent.append(copy)

    compute(0, "D")
    compute(1, "Q")
    settle("D")
    compute(2, "P")
    settle("Q")
    compute(3, "O")
    if meanwhile is not None:
        meanwhile()
    settle("P")
    settle("O")
    for copy in sent:
        copy.wait_send()


SPAN = 512


def scatter_scratch(sub):
    return [
        pltpu.VMEM((4, sub, D), F32),
        pltpu.VMEM((4, sub, D), BF),
        pltpu.VMEM((4, sub, D), BF),
        pltpu.VMEM((3, sub, D), BF),
        pltpu.VMEM((3, sub, D), BF),
        pltpu.VMEM((2 * sub, SPAN), F32),
        DMA((4,)),
        DMA((4,)),
        DMA((3, PIECES)),
        DMA((3, PIECES)),
    ]


SCATTER_REFS = 10


def home_ends(row, col, cols):
    return [(col, other) for other in range(cols)], [(other, row) for other in range(cols)]


def greet(pairs_to, row, col, waits):
    barrier = pltpu.get_barrier_semaphore()
    for to_row, to_col in pairs_to:

        @pl.when((to_row != row) | (to_col != col))
        def _():
            pl.semaphore_signal(
                barrier, inc=1, device_id={"row": to_row, "col": to_col}, device_id_type=MESH
            )

    pl.semaphore_wait(barrier, waits - (row == col).astype(jnp.int32))


def home_scratch(sub, rows):
    return [
        pltpu.VMEM((sub, D), BF),
        pltpu.VMEM((sub * COLS, D // rows), BF),
        DMA((rows, PIECES)),
        DMA((COLS, PIECES)),
        DMA((PIECES,)),
    ]


HOME_REFS = 5


class Home:
    def __init__(self, scratch):
        self.stage, self.home, self.send_sems, self.recv_sems, self.local_sems = scratch
        self.row, self.col = lax.axis_index("row"), lax.axis_index("col")
        self.rows = lax.axis_size("row")
        self.sub = self.stage.shape[0]
        self.height, self.width = self.sub // PIECES, D // self.rows
        self.senders, self.targets = home_ends(self.row, self.col, COLS)

    def meet(self, others):
        greet(self.senders, self.row, self.col, COLS + others)

    def target(self, piece):
        first = pl.multiple_of(self.col * self.sub + piece * self.height, self.height)
        return self.home.at[pl.ds(first, self.height)]

    def copies(self, piece, index):
        to_row, to_col = self.targets[index]
        source = self.stage.at[pl.ds(piece * self.height, self.height), pl.ds(index * self.width, self.width)]
        remote = pltpu.make_async_remote_copy(
            src_ref=source,
            dst_ref=self.target(piece),
            send_sem=self.send_sems.at[index, piece],
            recv_sem=self.recv_sems.at[self.col, piece],
            device_id={"row": to_row, "col": to_col},
            device_id_type=MESH,
        )
        local = pltpu.make_async_copy(source, self.target(piece), self.local_sems.at[piece])
        return (to_row == self.row) & (to_col == self.col), remote, local

    def send(self, piece):
        for index in range(self.rows):
            own, remote, local = self.copies(piece, index)

            @pl.when(own)
            def _():
                local.start()

            @pl.when(jnp.logical_not(own))
            def _():
                remote.start()

    def wait(self):
        for piece in range(PIECES):
            for index in range(self.rows):
                own, remote, local = self.copies(piece, index)

                @pl.when(own)
                def _():
                    local.wait()

                @pl.when(jnp.logical_not(own))
                def _():
                    remote.wait_send()

            for index in range(COLS):
                from_row, from_col = self.senders[index]
                spot = self.home.at[pl.ds(index * self.sub + piece * self.height, self.height)]
                arrived = pltpu.make_async_remote_copy(
                    src_ref=spot,
                    dst_ref=spot,
                    send_sem=self.send_sems.at[0, piece],
                    recv_sem=self.recv_sems.at[index, piece],
                    device_id={"row": from_row, "col": from_col},
                    device_id_type=MESH,
                )

                @pl.when((from_row != self.row) | (from_col != self.col))
                def _():
                    arrived.wait_recv()


def head_rows(block):
    turned = block.astype(F32).T
    return [turned[head * HD : (head + 1) * HD].astype(BF) for head in range(GROUP)]


def allowed_entries(key_block, low_ref, query_first):
    tokens = low_ref.shape[-1]
    key_slot = key_block * KEYS + lax.broadcasted_iota(jnp.int32, (KEYS, tokens), 0)
    query_slot = query_first + lax.broadcasted_iota(jnp.int32, (KEYS, tokens), 1)
    return (key_slot >= low_ref[...]) & (key_slot <= query_slot)


def key_rows(block):
    return pl.ds(pl.multiple_of(block * KEYS, KEYS), KEYS)


def attend_kernel(bounds, query_ref, pair_ref, low_ref, out_ref, log_ref, score_ref, mix_ref):
    step = pl.program_id(1)
    place = pl.program_id(0) * pl.num_programs(1) + step
    first, last, query_first = bounds[0, place], bounds[1, place], bounds[2, place]
    tokens = query_ref.shape[0]
    blank = jnp.zeros((HD, tokens), BF)
    queries = [jnp.concatenate([rows, blank], axis=0) for rows in head_rows(query_ref[...])]

    def score_block(block, tops):
        pairs = pair_ref[key_rows(block), :]
        allowed = allowed_entries(block, low_ref, query_first)
        new_tops = []
        for head in range(GROUP):
            scores = jnp.where(allowed, dot(pairs, queries[head], 1, 0), MASKED)
            score_ref[head, key_rows(block - first), :] = scores
            new_tops.append(jnp.maximum(tops[head], jnp.max(scores, axis=0, keepdims=True)))
        return tuple(new_tops)

    start = tuple(jnp.full((1, tokens), MASKED, F32) for _ in range(GROUP))
    tops = lax.fori_loop(first, last, score_block, start)
    mix_ref[...] = jnp.zeros_like(mix_ref)

    def mix_block(block, totals):
        pairs = pair_ref[key_rows(block), :]
        new_totals = []
        for head in range(GROUP):
            terms = jnp.exp(score_ref[head, key_rows(block - first), :] - tops[head])
            new_totals.append(totals[head] + jnp.sum(terms, axis=0, keepdims=True))
            mix_ref[head] += dot(pairs, terms.astype(BF), 0, 0)
        return tuple(new_totals)

    start = tuple(jnp.zeros((1, tokens), F32) for _ in range(GROUP))
    totals = lax.fori_loop(first, last, mix_block, start)
    mixed = jnp.concatenate(
        [mix_ref[head, HD:, :] / totals[head] for head in range(GROUP)], axis=0
    )
    out_ref[...] = mixed.T.astype(BF)
    for head in range(GROUP):
        log_ref[head : head + 1, :] = tops[head] + jnp.log(totals[head])


def attend_back_kernel(
    bounds, query_ref, grad_ref, pair_ref, low_ref, log_ref, dquery_ref, dpair_ref, prob_ref, dprob_ref, dmix_ref
):
    step = pl.program_id(1)
    place = pl.program_id(0) * pl.num_programs(1) + step
    first, last, query_first = bounds[0, place], bounds[1, place], bounds[2, place]
    tokens = query_ref.shape[0]
    blank = jnp.zeros((HD, tokens), BF)
    queries = [jnp.concatenate([rows, blank], axis=0) for rows in head_rows(query_ref[...])]
    grads = [jnp.concatenate([blank, rows], axis=0) for rows in head_rows(grad_ref[...])]

    @pl.when(step == 0)
    def _():
        dpair_ref[...] = jnp.zeros_like(dpair_ref)

    def prob_block(block, inners):
        pairs = pair_ref[key_rows(block), :]
        allowed = allowed_entries(block, low_ref, query_first)
        new_inners = []
        for head in range(GROUP):
            scores = dot(pairs, queries[head], 1, 0)
            probs = jnp.where(allowed, jnp.exp(scores - log_ref[head : head + 1, :]), 0.0)
            dprobs = dot(pairs, grads[head], 1, 0)
            prob_ref[head, key_rows(block - first), :] = probs
            dprob_ref[head, key_rows(block - first), :] = dprobs
            new_inners.append(inners[head] + jnp.sum(probs * dprobs, axis=0, keepdims=True))
        return tuple(new_inners)

    start = tuple(jnp.zeros((1, tokens), F32) for _ in range(GROUP))
    inners = lax.fori_loop(first, last, prob_block, start)
    dmix_ref[...] = jnp.zeros_like(dmix_ref)
    all_queries = jnp.concatenate(queries, axis=1)
    all_grads = jnp.concatenate(grads, axis=1)

    def back_block(block, carry):
        rows = key_rows(block)
        pairs = pair_ref[rows, :]
        all_probs, all_scores = [], []
        for head in range(GROUP):
            probs = prob_ref[head, key_rows(block - first), :]
            dprobs = dprob_ref[head, key_rows(block - first), :]
            dscores = (probs * (dprobs - inners[head])).astype(BF)
            dmix_ref[head] += dot(pairs, dscores, 0, 0)
            all_probs.append(probs.astype(BF))
            all_scores.append(dscores)
        dpair_ref[rows, :] += dot(jnp.concatenate(all_scores, axis=1), all_queries, 1, 1) + dot(
            jnp.concatenate(all_probs, axis=1), all_grads, 1, 1
        )
        return carry

    lax.fori_loop(first, last, back_block, 0)
    dquery = jnp.concatenate([dmix_ref[head, :HD, :] for head in range(GROUP)], axis=0)
    dquery_ref[...] = dquery.T * SCALE


def attend(queries, pairs, low, bounds):
    tokens, width = queries.shape
    replicas, slots, _ = pairs.shape
    rows = low.shape[2]
    blocks = low.shape[0] // replicas
    span = LMAX + KEYS
    return pl.pallas_call(
        attend_kernel,
        grid_spec=pltpu.PrefetchScalarGridSpec(
            num_scalar_prefetch=1,
            grid=(replicas, blocks),
            in_specs=[
                pl.BlockSpec((rows, GROUP * HD), lambda rep, block, _: (rep * blocks + block, 0)),
                pl.BlockSpec((None, slots, 2 * HD), lambda rep, block, _: (rep, 0, 0)),
                pl.BlockSpec((None, 1, rows), lambda rep, block, _: (rep * blocks + block, 0, 0)),
            ],
            out_specs=[
                pl.BlockSpec((rows, GROUP * HD), lambda rep, block, _: (rep * blocks + block, 0)),
                pl.BlockSpec((None, None, GROUP, rows), lambda rep, block, _: (rep, block, 0, 0)),
            ],
            scratch_shapes=[
                pltpu.VMEM((GROUP, span, rows), F32),
                pltpu.VMEM((GROUP, 2 * HD, rows), F32),
            ],
        ),
        out_shape=[
            jax.ShapeDtypeStruct((tokens, width), BF),
            jax.ShapeDtypeStruct((replicas, blocks, GROUP, rows), F32),
        ],
        compiler_params=pltpu.CompilerParams(vmem_limit_bytes=48 * 2**20),
        cost_estimate=takes(14),
        name="attend",
    )(bounds, queries, pairs, low)


def attend_back(queries, grads, pairs, low, log_total, bounds):
    tokens, width = queries.shape
    replicas, slots, _ = pairs.shape
    rows = low.shape[2]
    blocks = low.shape[0] // replicas
    span = LMAX + KEYS
    return pl.pallas_call(
        attend_back_kernel,
        grid_spec=pltpu.PrefetchScalarGridSpec(
            num_scalar_prefetch=1,
            grid=(replicas, blocks),
            in_specs=[
                pl.BlockSpec((rows, GROUP * HD), lambda rep, block, _: (rep * blocks + block, 0)),
                pl.BlockSpec((rows, GROUP * HD), lambda rep, block, _: (rep * blocks + block, 0)),
                pl.BlockSpec((None, slots, 2 * HD), lambda rep, block, _: (rep, 0, 0)),
                pl.BlockSpec((None, 1, rows), lambda rep, block, _: (rep * blocks + block, 0, 0)),
                pl.BlockSpec((None, None, GROUP, rows), lambda rep, block, _: (rep, block, 0, 0)),
            ],
            out_specs=[
                pl.BlockSpec((rows, GROUP * HD), lambda rep, block, _: (rep * blocks + block, 0)),
                pl.BlockSpec((None, slots, 2 * HD), lambda rep, block, _: (rep, 0, 0)),
            ],
            scratch_shapes=[
                pltpu.VMEM((GROUP, span, rows), F32),
                pltpu.VMEM((GROUP, span, rows), F32),
                pltpu.VMEM((GROUP, 2 * HD, rows), F32),
            ],
        ),
        out_shape=[
            jax.ShapeDtypeStruct((tokens, width), F32),
            jax.ShapeDtypeStruct((replicas, slots, 2 * HD), F32),
        ],
        compiler_params=pltpu.CompilerParams(vmem_limit_bytes=48 * 2**20),
        cost_estimate=takes(23),
        name="attend_back",
    )(bounds, queries, grads, pairs, low, log_total)


def norm_of(vectors):
    scaling = lax.rsqrt(jnp.mean(vectors * vectors, axis=1, keepdims=True) + EPS_NORM)
    return vectors * scaling, scaling


def norm_back(value, vectors, gain):
    unit, scaling = norm_of(vectors)
    weighted = value * gain
    inner = jnp.mean(weighted * unit, axis=1, keepdims=True)
    return scaling * (weighted - unit * inner), jnp.sum(value * unit, axis=0, keepdims=True)


def exchange_kernel(
    token_ref, top_ref, gain_ref, usable_ref, source_ref, normed_ref, grad_top_ref, gains_ref,
    held, held_top, mid, mid_top, held_gains, col_send, col_recv, row_send, row_recv, gain_send, gain_recv, local_sems,
):
    row, col, rows, cols = lax.axis_index("row"), lax.axis_index("col"), lax.axis_size("row"), lax.axis_size("col")
    sub, width = held.shape[0], token_ref.shape[1]
    row_of = row_partners()
    col_of = [lax.rem(col + shift, cols) for shift in range(1, cols)]
    meet([{"row": partner} for partner in row_of] + [{"col": partner} for partner in col_of])
    own_cols = tile(row, width)

    def run(copies):
        for copy in copies:
            copy.start()
        return copies

    def finish(copies):
        for copy in copies:
            copy.wait()

    def remote(source, target, send_sem, recv_sem, device):
        return pltpu.make_async_remote_copy(
            src_ref=source, dst_ref=target, send_sem=send_sem, recv_sem=recv_sem, device_id=device, device_id_type=MESH
        )

    def to_columns(array, source, target):
        return run(
            [
                remote(
                    source.at[tile(partner, sub)], target.at[col],
                    col_send.at[array, shift], col_recv.at[array, shift], {"col": partner},
                )
                for shift, partner in enumerate(col_of)
            ]
            + [pltpu.make_async_copy(source.at[tile(col, sub)], target.at[col], local_sems.at[array, 0])]
        )

    def to_rows(array, source, target):
        return run(
            [
                remote(
                    source.at[partner], target.at[:, own_cols],
                    row_send.at[array, shift], row_recv.at[array, shift], {"row": partner},
                )
                for shift, partner in enumerate(row_of)
            ]
            + [pltpu.make_async_copy(source.at[row], target.at[:, own_cols], local_sems.at[array, 1])]
        )

    tokens = to_columns(0, token_ref, mid)
    gains = run(
        [
            remote(gain_ref, held_gains.at[:, own_cols], gain_send.at[shift], gain_recv.at[shift], {"row": partner})
            for shift, partner in enumerate(row_of)
        ]
        + [pltpu.make_async_copy(gain_ref, held_gains.at[:, own_cols], local_sems.at[2, 0])]
    )
    tops = to_columns(1, top_ref, mid_top)
    finish(tokens)
    tokens = to_rows(0, mid, held)
    finish(tops)
    tops = to_rows(1, mid_top, held_top)
    finish(gains)
    finish(tokens)
    source_ref[...] = held[...]
    gains_ref[...] = held_gains[...]
    unit, _ = norm_of(held[...].astype(F32))
    normed_ref[...] = (unit * held_gains[0:1, :]).astype(BF)
    finish(tops)
    grad_top_ref[...] = (held_top[...].astype(F32) * usable_ref[...]).astype(BF)


def exchange(tokens, top, gains, usable, rows):
    sub, width = tokens.shape[0] // COLS, tokens.shape[1]
    block = jax.ShapeDtypeStruct((sub, rows * width), BF)
    return pl.pallas_call(
        exchange_kernel,
        out_shape=[block, block, block, jax.ShapeDtypeStruct((gains.shape[0], rows * width), F32)],
        in_specs=[VMEM] * 4,
        out_specs=[VMEM] * 4,
        scratch_shapes=[pltpu.VMEM((sub, rows * width), BF)] * 2
        + [pltpu.VMEM((COLS, sub, width), BF)] * 2
        + [
            pltpu.VMEM((gains.shape[0], rows * width), F32),
            DMA((2, COLS - 1)),
            DMA((2, COLS - 1)),
            DMA((2, rows - 1)),
            DMA((2, rows - 1)),
            DMA((rows - 1,)),
            DMA((rows - 1,)),
            DMA((3, 2)),
        ],
        compiler_params=params(1),
        cost_estimate=takes(65),
        name="exchange",
    )(tokens, top, gains, usable)


def project_kernel(
    reps, own_ref, top_ref, weight_ref, cosine_ref, sine_ref,
    all_ref, top_all_ref, query_ref, pair_ref,
    held, send_sems, recv_sems, local_sem, top_held, top_send, top_recv, top_local,
    queries, pairs, halo, out_sems, pair_sems, halo_sems, pair_send, pair_recv,
):
    row, rows = lax.axis_index("row"), lax.axis_size("row")
    meet(near(reps) + [{"row": partner} for partner in row_partners()])
    sub = own_ref.shape[0]
    copies, chips = [], []
    has_next, has_last = row < rows - 1, row > 0

    @pl.when(row == 0)
    def _():
        halo[...] = jnp.zeros_like(halo)

    def out(source, target, sem):
        copy = pltpu.make_async_copy(source, target, sem)
        copy.start()
        copies.append(copy)

    def push(step, chip):
        return pltpu.make_async_remote_copy(
            src_ref=pairs.at[chip],
            dst_ref=halo.at[chip],
            send_sem=pair_send.at[step],
            recv_sem=pair_recv.at[step],
            device_id={"row": lax.rem(row + 1, rows)},
            device_id_type=MESH,
        )

    def use(step, chip):
        chips.append(chip)
        out(held.at[chip], all_ref.at[chip], out_sems.at[step])
        places = tile(chip, 2 * sub)
        turned = rotate(dot(held[chip], weight_ref[...], 1, 0), cosine_ref[places, :], sine_ref[places, :])
        queries[chip] = (turned[:, : GROUP * HD] * SCALE).astype(BF)
        out(queries.at[chip], query_ref.at[chip], out_sems.at[COLS + step])
        pairs[chip] = turned[:, GROUP * HD :].astype(BF)
        out(pairs.at[chip], pair_ref.at[lax.div(chip, 2), 1, lax.rem(chip, 2)], pair_sems.at[step])

        @pl.when(has_next)
        def _():
            push(step, chip).start()

    run_gather(reps, own_ref, held, (send_sems, recv_sems, local_sem), use)

    def use_top(step, chip):
        out(top_held.at[chip], top_all_ref.at[chip], out_sems.at[2 * COLS + step])

    run_gather(reps, top_ref, top_held, (top_send, top_recv, top_local), use_top)
    for step, chip in enumerate(chips):

        @pl.when(has_next)
        def _():
            push(step, chip).wait_send()

        @pl.when(has_last)
        def _():
            push(step, chip).wait_recv()

    for chip in range(COLS):
        out(halo.at[chip], pair_ref.at[chip // 2, 0, chip % 2], halo_sems.at[chip])
    for copy in copies:
        copy.wait()


def project(normed_own, top_own, weight, cosine, sine, reps):
    sub = normed_own.shape[0]
    return pl.pallas_call(
        functools.partial(project_kernel, reps),
        out_shape=[
            jax.ShapeDtypeStruct((COLS, 2 * sub, D), BF),
            jax.ShapeDtypeStruct((COLS, 2 * sub, D), BF),
            jax.ShapeDtypeStruct((COLS, 2 * sub, GROUP * HD), BF),
            jax.ShapeDtypeStruct((2, 2, COLS // 2, 2 * sub, 2 * HD), BF),
        ],
        in_specs=[VMEM] * 5,
        out_specs=[HBM] * 4,
        scratch_shapes=gather_scratch(sub)
        + gather_scratch(sub)
        + [
            pltpu.VMEM((COLS, 2 * sub, GROUP * HD), BF),
            pltpu.VMEM((COLS, 2 * sub, 2 * HD), BF),
            pltpu.VMEM((COLS, 2 * sub, 2 * HD), BF),
            DMA((3 * COLS,)),
            DMA((COLS,)),
            DMA((COLS,)),
            DMA((COLS,)),
            DMA((COLS,)),
        ],
        compiler_params=params(2),
        cost_estimate=takes(75),
        name="project",
    )(normed_own, top_own, weight, cosine, sine)


def mix_out_kernel(reps, attended_ref, weight_ref, source_ref, gains_ref, middle_ref, normed_ref, *scratch):
    meet(near(reps))
    parts, _, width = weight_ref.shape

    def partial(step, chip, put):
        for part in range(parts):
            put(pl.ds(part * width, width), dot(attended_ref[chip], weight_ref[part], 1, 0))

    def finish(piece, rows, value):
        middle = source_ref[rows, :].astype(F32) + value
        middle_ref[rows, :] = middle
        normed_ref[rows, :] = (norm_of(middle)[0] * gains_ref[1:2, :]).astype(BF)

    run_scatter(reps, partial, finish, scratch)


def mix_out(attended, weight, source, gains, reps):
    sub = source.shape[0]
    return pl.pallas_call(
        functools.partial(mix_out_kernel, reps),
        out_shape=[jax.ShapeDtypeStruct((sub, D), F32), jax.ShapeDtypeStruct((sub, D), BF)],
        in_specs=[VMEM] * 4,
        out_specs=[VMEM] * 2,
        scratch_shapes=scatter_scratch(sub),
        compiler_params=params(3),
        cost_estimate=takes(44),
        name="mix_out",
    )(attended, weight, source, gains)


def gated(tokens, top, weight_ref, put):
    parts, rows, width = weight_ref.shape
    units, span = rows // 3, 256

    def one_tile(index, carry):
        columns = tile(index, span)
        gate_w = weight_ref[:, :units, columns].reshape(D, span)
        up_w = weight_ref[:, units : 2 * units, columns].reshape(D, span)
        gate = dot(tokens, gate_w, 1, 0)
        up = dot(tokens, up_w, 1, 0)
        down_rows = pl.ds(pl.multiple_of(2 * units + index * span, span), span)
        grad = dot(top[:, :width], weight_ref[0, down_rows, :], 1, 1)
        for part in range(1, parts):
            grad += dot(top[:, part * width : (part + 1) * width], weight_ref[part, down_rows, :], 1, 1)
        sigma = 1.0 / (1.0 + jnp.exp(-gate))
        active = gate * sigma
        put(
            columns,
            (active * up).astype(BF),
            (grad * up * sigma * (1.0 + gate * (1.0 - sigma))).astype(BF),
            (grad * active).astype(BF),
        )
        return carry

    lax.fori_loop(0, units // span, one_tile, 0)


def first_slice_kernel(
    reps, own_ref, top_ref, weight_ref, all_ref, hidden_ref, ggate_ref, gup_ref,
    held, send_sems, recv_sems, local_sem, tops, hiddens, ggates, gups, top_sems, out_sems,
):
    meet(near(reps))
    where = plane(reps)
    order = [where[kind][0] for kind in ("O", "P", "Q", "D")]
    loads = [pltpu.make_async_copy(top_ref.at[chip], tops.at[chip], top_sems.at[step]) for step, chip in enumerate(order)]
    for copy in loads:
        copy.start()
    copies = []

    def use(step, chip):
        def out(source, target, index):
            copy = pltpu.make_async_copy(source.at[chip], target.at[chip], out_sems.at[index, step])
            copy.start()
            copies.append(copy)

        out(held, all_ref, 0)
        loads[step].wait()

        def put(columns, hidden, ggate, gup):
            hiddens[chip, :, columns] = hidden
            ggates[chip, :, columns] = ggate
            gups[chip, :, columns] = gup

        gated(held[chip], tops[chip], weight_ref, put)
        out(hiddens, hidden_ref, 1)
        out(ggates, ggate_ref, 2)
        out(gups, gup_ref, 3)

    run_gather(reps, own_ref, held, (send_sems, recv_sems, local_sem), use)
    for copy in copies:
        copy.wait()


def first_slice(normed_own, top_all, weight, reps):
    sub = normed_own.shape[0]
    units = weight.shape[1] // 3
    piece = jax.ShapeDtypeStruct((COLS, 2 * sub, units), BF)
    return pl.pallas_call(
        functools.partial(first_slice_kernel, reps),
        out_shape=[jax.ShapeDtypeStruct((COLS, 2 * sub, D), BF)] + [piece] * 3,
        in_specs=[VMEM, HBM, VMEM],
        out_specs=[HBM] * 4,
        scratch_shapes=gather_scratch(sub)
        + [pltpu.VMEM((COLS, 2 * sub, D), BF)]
        + [pltpu.VMEM((COLS, 2 * sub, units), BF)] * 3
        + [DMA((COLS,)), DMA((4, COLS))],
        compiler_params=params(4),
        cost_estimate=takes(50),
        name="first_slice",
    )(normed_own, top_all, weight)


def second_slice_kernel(
    reps, token_ref, top_ref, ggate_one_ref, gup_one_ref, weight_one_ref, weight_ref, middle_ref, own_top_ref, gains_ref,
    hidden_ref, ggate_ref, gup_ref, grad_ref, low_ref, gain_ref, *scratch,
):
    tokens, tops, ggate_ones, gup_ones, weight_one, hiddens, ggates, gups, in_sems, out_sems, weight_sem = scratch[SCATTER_REFS:]
    meet(near(reps))
    order = scatter_order(reps)
    parts, rows, width = weight_ref.shape
    units = rows // 3
    loads, copies = {}, []
    sources = ((token_ref, tokens), (top_ref, tops), (ggate_one_ref, ggate_ones), (gup_one_ref, gup_ones))

    def load(step):
        loads[step] = []
        for index, (source, target) in enumerate(sources):
            copy = pltpu.make_async_copy(source.at[order[step]], target.at[step % 2], in_sems.at[index, step % 2])
            copy.start()
            loads[step].append(copy)

    load(0)
    weight_copy = pltpu.make_async_copy(weight_one_ref.at[:, pl.ds(0, 2 * units)], weight_one, weight_sem)
    weight_copy.start()
    gain_ref[...] = jnp.zeros_like(gain_ref)

    def partial(step, chip, put):
        slot = step % 2
        for copy in loads[step]:
            copy.wait()
        if step < 3:
            load(step + 1)

        def keep(columns, hidden, ggate, gup):
            hiddens[chip, :, columns] = hidden
            ggates[chip, :, columns] = ggate
            gups[chip, :, columns] = gup

        gated(tokens[slot], tops[slot], weight_ref, keep)
        for index, (source, target) in enumerate(((hiddens, hidden_ref), (ggates, ggate_ref), (gups, gup_ref))):
            copy = pltpu.make_async_copy(source.at[chip], target.at[chip], out_sems.at[index, step])
            copy.start()
            copies.append(copy)
        if step == 0:
            weight_copy.wait()
        for part in range(parts):
            value = dot(ggates[chip], weight_ref[part, :units, :], 1, 1)
            value += dot(gups[chip], weight_ref[part, units : 2 * units, :], 1, 1)
            value += dot(ggate_ones[slot], weight_one[part, :units, :], 1, 1)
            value += dot(gup_ones[slot], weight_one[part, units:, :], 1, 1)
            put(pl.ds(part * width, width), value)

    def finish(piece, rows_of, value):
        back, gain_part = norm_back(value, middle_ref[rows_of, :], gains_ref[1:2, :])
        grad = own_top_ref[rows_of, :].astype(F32) + back
        grad_ref[rows_of, :] = grad
        low_ref[rows_of, :] = grad.astype(BF)
        gain_ref[0:1, :] += gain_part

    run_scatter(reps, partial, finish, scratch[:SCATTER_REFS])
    for copy in copies:
        copy.wait()


def second_slice(normed_all, top_all, ggate_one, gup_one, weight_one, weight, middle, own_top, gains, reps):
    sub = middle.shape[0]
    parts, rows, width = weight.shape
    units = rows // 3
    piece = jax.ShapeDtypeStruct((COLS, 2 * sub, units), BF)
    return pl.pallas_call(
        functools.partial(second_slice_kernel, reps),
        out_shape=[piece] * 3
        + [
            jax.ShapeDtypeStruct((sub, D), F32),
            jax.ShapeDtypeStruct((sub, D), BF),
            jax.ShapeDtypeStruct((8, D), F32),
        ],
        in_specs=[HBM] * 5 + [VMEM] * 4,
        out_specs=[HBM] * 3 + [VMEM] * 3,
        scratch_shapes=scatter_scratch(sub)
        + [pltpu.VMEM((2, 2 * sub, D), BF)] * 2
        + [pltpu.VMEM((2, 2 * sub, units), BF)] * 2
        + [pltpu.VMEM((parts, 2 * units, width), BF)]
        + [pltpu.VMEM((COLS, 2 * sub, units), BF)] * 3
        + [DMA((4, 2)), DMA((3, COLS)), DMA],
        compiler_params=params(5),
        cost_estimate=takes(65),
        name="second_slice",
    )(normed_all, top_all, ggate_one, gup_one, weight_one, weight, middle, own_top, gains)


def back_out_kernel(
    reps, own_ref, weight_ref, all_ref, grad_ref, held, send_sems, recv_sems, local_sem, grads, out_sems
):
    meet(near(reps))
    parts, _, width = weight_ref.shape
    copies = []

    def use(step, chip):
        def out(source, target, index):
            copy = pltpu.make_async_copy(source.at[chip], target.at[chip], out_sems.at[index, step])
            copy.start()
            copies.append(copy)

        out(held, all_ref, 0)
        total = dot(held[chip, :, :width], weight_ref[0], 1, 1)
        for part in range(1, parts):
            total += dot(held[chip, :, part * width : (part + 1) * width], weight_ref[part], 1, 1)
        grads[chip] = total.astype(BF)
        out(grads, grad_ref, 1)

    run_gather(reps, own_ref, held, (send_sems, recv_sems, local_sem), use)
    for copy in copies:
        copy.wait()


def back_out(grad_own, weight, reps):
    sub = grad_own.shape[0]
    return pl.pallas_call(
        functools.partial(back_out_kernel, reps),
        out_shape=[
            jax.ShapeDtypeStruct((COLS, 2 * sub, D), BF),
            jax.ShapeDtypeStruct((COLS, 2 * sub, weight.shape[1]), BF),
        ],
        in_specs=[VMEM] * 2,
        out_specs=[HBM] * 2,
        scratch_shapes=gather_scratch(sub)
        + [pltpu.VMEM((COLS, 2 * sub, weight.shape[1]), BF), DMA((2, COLS))],
        compiler_params=params(6),
        cost_estimate=takes(41),
        name="back_out",
    )(grad_own, weight)


def lift_kernel(
    reps, hidden_one_ref, hidden_two_ref, weight_one_ref, weight_two_ref, middle_ref,
    dquery_ref, dpair_ref, cosine_ref, sine_ref, result_ref, proj_ref, *scratch,
):
    weight_one, weight_two, weight_sems, low, taken, push_send, push_recv = scratch[SCATTER_REFS + HOME_REFS :]
    parts, units, width = weight_one.shape
    row, rows = lax.axis_index("row"), lax.axis_size("row")
    loads = []
    for index, (source, target) in enumerate(((weight_one_ref, weight_one), (weight_two_ref, weight_two))):
        copy = pltpu.make_async_copy(source.at[:, pl.ds(2 * units, units)], target, weight_sems.at[index])
        copy.start()
        loads.append(copy)
    partners = row_partners()
    signal(near(reps) + [{"row": partner} for partner in partners])
    home = Home(scratch[SCATTER_REFS : SCATTER_REFS + HOME_REFS])
    home.meet(3 + len(partners))
    low[...] = dpair_ref[:, 0].astype(BF)
    push = pltpu.make_async_remote_copy(
        src_ref=low,
        dst_ref=taken,
        send_sem=push_send,
        recv_sem=push_recv,
        device_id={"row": lax.rem(row + rows - 1, rows)},
        device_id_type=MESH,
    )

    @pl.when(row > 0)
    def _():
        push.start()

    for copy in loads:
        copy.wait()

    def partial(step, chip, put):
        for part in range(parts):
            value = dot(hidden_one_ref[chip], weight_one[part], 1, 0)
            put(pl.ds(part * width, width), value + dot(hidden_two_ref[chip], weight_two[part], 1, 0))

    def finish(piece, rows_of, value):
        home.stage[rows_of, :] = (middle_ref[rows_of, :] + value).astype(BF)
        home.send(piece)

    def turn_back():
        @pl.when(row == rows - 1)
        def _():
            taken[...] = jnp.zeros_like(taken)

        @pl.when(row < rows - 1)
        def _():
            push.wait_recv()

        chips, height, _ = proj_ref.shape
        for chip in range(chips):
            places = pl.ds(chip * height, height)
            pair_rows = pl.ds(chip % 2 * height, height)
            pair = dpair_ref[chip // 2, 1, pair_rows, :] + taken[chip // 2, pair_rows, :].astype(F32)
            grad = jnp.concatenate([dquery_ref[places, :], pair], axis=1)
            proj_ref[chip] = rotate(grad, cosine_ref[places, :], -sine_ref[places, :]).astype(BF)

    run_scatter(reps, partial, finish, scratch[:SCATTER_REFS], turn_back)

    @pl.when(row > 0)
    def _():
        push.wait_send()

    home.wait()
    result_ref[...] = home.home[...]


def lift(hidden_one, hidden_two, weight_one, weight_two, middle, dquery, dpairs, cosine, sine, reps):
    sub = middle.shape[0]
    parts, rows, width = weight_one.shape
    tokens, heads = dquery.shape
    halves, _, slots, lanes = dpairs.shape
    return pl.pallas_call(
        functools.partial(lift_kernel, reps),
        out_shape=[
            jax.ShapeDtypeStruct((sub * COLS, width), BF),
            jax.ShapeDtypeStruct((COLS, tokens // COLS, heads + lanes), BF),
        ],
        in_specs=[VMEM] * 2 + [HBM] * 2 + [VMEM] * 5,
        out_specs=[VMEM] * 2,
        scratch_shapes=scatter_scratch(sub)
        + home_scratch(sub, parts)
        + [pltpu.VMEM((parts, rows // 3, width), BF)] * 2
        + [DMA((2,))]
        + [pltpu.VMEM((halves, slots, lanes), BF)] * 2
        + [DMA, DMA],
        compiler_params=params(7),
        cost_estimate=takes(70),
        name="lift",
    )(hidden_one, hidden_two, weight_one, weight_two, middle, dquery, dpairs, cosine, sine)


PEERS = ("SO", "P", "SP", "Q", "SQ", "D", "SD")


def project_back_kernel(
    reps, proj_ref, weight_ref, source_ref, middle_ref, gains_ref, gain_two_ref, resid_ref, gain_ref, *scratch
):
    gain_own, gain_rows, gain_plane, row_send, row_recv, plane_send, plane_recv = scratch[SCATTER_REFS + HOME_REFS :]
    where = plane(reps)
    row = lax.axis_index("row")
    partners = row_partners()
    signal([where[kind][2] for kind in PEERS] + [{"row": partner} for partner in partners])
    home = Home(scratch[SCATTER_REFS : SCATTER_REFS + HOME_REFS])
    home.meet(len(PEERS) + len(partners))
    gain_own[...] = jnp.zeros_like(gain_own)
    gain_own[1:2, :] = gain_two_ref[0:1, :]

    def partial(step, chip, put):
        for index in range(D // SPAN):
            columns = pl.ds(index * SPAN, SPAN)
            put(columns, dot(proj_ref[chip], weight_ref[columns, :], 1, 1))

    def finish(piece, rows, value):
        back, gain_part = norm_back(value, source_ref[rows, :].astype(F32), gains_ref[0:1, :])
        home.stage[rows, :] = (middle_ref[rows, :] + back).astype(BF)
        home.send(piece)
        gain_own[0:1, :] += gain_part

    run_scatter(reps, partial, finish, scratch[:SCATTER_REFS])
    width = gain_ref.shape[1]
    copies = []
    for shift, partner in enumerate(partners):
        copy = pltpu.make_async_remote_copy(
            src_ref=gain_own.at[:, tile(partner, width)],
            dst_ref=gain_rows.at[shift],
            send_sem=row_send.at[shift],
            recv_sem=row_recv.at[shift],
            device_id={"row": partner},
            device_id_type=MESH,
        )
        copy.start()
        copies.append(copy)
    for copy in copies:
        copy.wait()
    total = gain_own[:, tile(row, width)]
    for shift in range(len(partners)):
        total += gain_rows[shift]
    own = where["O"][0] * 2 + where["O"][1]
    gain_plane[own] = total

    def share(index, place):
        return pltpu.make_async_remote_copy(
            src_ref=gain_plane.at[place],
            dst_ref=gain_plane.at[place],
            send_sem=plane_send.at[index],
            recv_sem=plane_recv.at[place],
            device_id=where[PEERS[index]][2],
            device_id_type=MESH,
        )

    for index in range(len(PEERS)):
        share(index, own).start()
    for index, kind in enumerate(PEERS):
        share(index, where[kind][0] * 2 + where[kind][1]).wait_recv()
    total = gain_plane[0]
    for place in range(1, 2 * COLS):
        total += gain_plane[place]
    gain_ref[...] = total
    for index in range(len(PEERS)):
        share(index, own).wait_send()
    home.wait()
    resid_ref[...] = home.home[...]


def project_back(grad_proj, weight, source, grad_middle, gains, gain_two, reps, rows):
    sub = source.shape[0]
    width = D // rows
    return pl.pallas_call(
        functools.partial(project_back_kernel, reps),
        out_shape=[jax.ShapeDtypeStruct((sub * COLS, width), BF), jax.ShapeDtypeStruct((8, width), F32)],
        in_specs=[VMEM] * 6,
        out_specs=[VMEM] * 2,
        scratch_shapes=scatter_scratch(sub)
        + home_scratch(sub, rows)
        + [
            pltpu.VMEM((8, D), F32),
            pltpu.VMEM((rows - 1, 8, width), F32),
            pltpu.VMEM((2 * COLS, 8, width), F32),
            DMA((rows - 1,)),
            DMA((rows - 1,)),
            DMA((len(PEERS),)),
            DMA((2 * COLS,)),
        ],
        compiler_params=params(8),
        cost_estimate=takes(55),
        name="project_back",
    )(grad_proj, weight, source, grad_middle, gains, gain_two)


def adamw(weights, gradient, moment, square, step_rate, decay_rate):
    gradient = gradient.astype(F32)
    moment_new = BETA_ONE * moment + (1.0 - BETA_ONE) * gradient
    square_new = BETA_TWO * square + (1.0 - BETA_TWO) * gradient * gradient
    moment_hat = moment_new / (1.0 - BETA_ONE**STEP)
    square_hat = square_new / (1.0 - BETA_TWO**STEP)
    weights_new = weights - step_rate * (
        moment_hat / (jnp.sqrt(square_hat) + ADAM_EPS) + decay_rate * weights
    )
    return (weights_new, moment_new, square_new)


def local(
    resid_in,
    cotangent,
    seq_lens,
    qkv_weight,
    qkv_moment,
    qkv_square,
    out_weight,
    out_moment,
    out_square,
    gate_weight,
    gate_moment,
    gate_square,
    up_weight,
    up_moment,
    up_square,
    down_weight,
    down_moment,
    down_square,
    norm_gains,
    gain_moment,
    gain_square,
):
    cols, rows, replicas = lax.axis_size("col"), lax.axis_size("row"), lax.axis_size("dp")
    reps = replicas // 2
    half = lax.axis_index("dp") // reps
    row, col = lax.axis_index("row"), lax.axis_index("col")
    chunk = resid_in.shape[0]
    sub = chunk // cols
    blocks = 2 * cols
    plane_tokens = sub * blocks
    head_width = (GROUP + 2) * HD

    qkv_block = half_columns(qkv_weight, reps)
    out_block = tall_block(out_weight, reps)
    split = out_block.shape[1] // 2
    stacked = jnp.concatenate([out_block[:, :split], out_block[:, split:]], axis=0)
    first_w = lax.all_gather(jnp.concatenate([qkv_block, stacked], axis=1), "row", axis=0)
    qkv_w = first_w[:, :, :head_width].reshape(D, head_width)
    heads = out_block.shape[0]
    out_w = jnp.concatenate([first_w[:, :heads, head_width:], first_w[:, heads:, head_width:]], axis=2)
    lengths = both_halves(seq_lens, partner_swap(seq_lens, reps), half, 0)
    ends = jnp.cumsum(lengths, axis=1, dtype=jnp.int32)
    slot = (row * chunk + jnp.arange(chunk, dtype=jnp.int32)).reshape(1, chunk)
    passed = (slot[:, :, None] >= ends[:, None, :]).astype(jnp.int32)
    seq_start = jnp.sum(passed * lengths[:, None, :], axis=2, dtype=jnp.int32)
    usable = slot < ends[:, -1:]
    cosine, sine = rope_tables((slot - seq_start).reshape(plane_tokens))
    low = (jnp.where(usable, seq_start, slot) - (row - 1) * chunk).reshape(blocks, 1, sub)
    firsts = jnp.tile(chunk + jnp.arange(cols, dtype=jnp.int32) * sub, 2)
    bounds = jnp.stack([low[:, 0, 0] // KEYS, (firsts + sub - 1) // KEYS + 1, firsts]).astype(jnp.int32)
    usable_mine = (row * chunk + col * sub + jnp.arange(sub, dtype=jnp.int32)) < jnp.sum(seq_lens)

    padded = jnp.concatenate([norm_gains, jnp.zeros((6, norm_gains.shape[1]), F32)])
    source, normed_own, grad_top, gains = exchange(
        resid_in, cotangent, padded, usable_mine.astype(F32)[:, None], rows
    )
    gate_block = half_columns(gate_weight, reps, source)
    up_block = half_columns(up_weight, reps, source)
    down_block = tall_block(down_weight, reps)
    units = gate_block.shape[1] // SLICES
    slice_w = []
    for index in range(SLICES):
        span = slice(index * units, (index + 1) * units)
        block = jnp.concatenate([gate_block[:, span], up_block[:, span], down_block[span]], axis=0)
        slice_w.append(lax.all_gather(block, "row", axis=0))
    normed_one, grad_top_all, queries, pairs = project(normed_own, grad_top, qkv_w, cosine, sine, reps)
    queries = queries.reshape(plane_tokens, GROUP * HD)
    pairs = pairs.reshape(2, 2 * chunk, 2 * HD)
    attended, log_total = attend(queries, pairs, low, bounds)
    middle, normed_own = mix_out(attended.reshape(cols, 2 * sub, GROUP * HD), out_w, source, gains, reps)

    flat_top = grad_top_all.reshape(plane_tokens, D)

    def slice_grads(normed_all, hidden, ggate, gup):
        flat = normed_all.reshape(plane_tokens, D)
        parts = [
            dot(flat, ggate.reshape(plane_tokens, units), 0, 0).astype(BF).reshape(rows, -1, units),
            dot(flat, gup.reshape(plane_tokens, units), 0, 0).astype(BF).reshape(rows, -1, units),
            row_blocks(dot(hidden.reshape(plane_tokens, units), flat_top, 0, 0).astype(BF), rows),
        ]
        return jnp.concatenate(parts, axis=1)

    normed_two, hidden_one, ggate_one, gup_one = first_slice(normed_own, grad_top_all, slice_w[0], reps)
    grads_one = slice_grads(normed_two, hidden_one, ggate_one, gup_one)
    normed_two, grads_one = lax.optimization_barrier((normed_two, grads_one))
    hidden_two, ggate_two, gup_two, grad_middle, grad_middle_own, gain_grad_two = second_slice(
        normed_two, grad_top_all, ggate_one, gup_one, slice_w[0], slice_w[1], middle, grad_top, gains, reps
    )
    grads_two = slice_grads(normed_two, hidden_two, ggate_two, gup_two)
    grad_middle_own, grads_two = lax.optimization_barrier((grad_middle_own, grads_two))
    slice_g = [lax.psum_scatter(part, "row", scatter_dimension=0) for part in (grads_one, grads_two)]

    grad_middle_all, grad_attended = back_out(grad_middle_own, out_w, reps)
    grad_attended, slice_g[0] = lax.optimization_barrier((grad_attended, slice_g[0]))
    grad_query, grad_pairs = attend_back(
        queries, grad_attended.reshape(plane_tokens, GROUP * HD), pairs, low, log_total, bounds
    )
    result, grad_proj = lift(
        hidden_one, hidden_two, slice_w[0], slice_w[1], middle,
        grad_query, grad_pairs.reshape(2, 2, chunk, 2 * HD), cosine, sine, reps,
    )
    grad_qkv = dot(normed_one.reshape(plane_tokens, D), grad_proj.reshape(plane_tokens, head_width), 0, 0).astype(BF)
    grad_proj, grad_qkv = lax.optimization_barrier((grad_proj, grad_qkv))
    resid_grad, gain_grads = project_back(
        grad_proj, qkv_w, source, grad_middle, gains, gain_grad_two, reps, rows
    )
    resid_grad = resid_grad.astype(F32)
    attended, slice_g[1] = lax.optimization_barrier((attended, slice_g[1]))
    grad_out = row_blocks(dot(attended, grad_middle_all.reshape(plane_tokens, D), 0, 0).astype(BF), rows)
    grad_out = own_tall(lax.psum_scatter(grad_out, "row", scatter_dimension=0), reps)
    grad_qkv = own_rows(lax.psum_scatter(grad_qkv, "row", scatter_dimension=0, tiled=True), reps)
    wide = sum(part.shape[0] for part in slice_g) // (3 * SLICES)
    grad_gate = own_rows(jnp.concatenate([part[:wide] for part in slice_g], axis=1), reps)
    grad_up = own_rows(jnp.concatenate([part[wide : 2 * wide] for part in slice_g], axis=1), reps)
    grad_down = own_tall(jnp.concatenate([part[2 * wide :] for part in slice_g], axis=0), reps)

    gain_grads = gain_grads[:2]
    if reps > 1:
        gain_grads = lax.psum(gain_grads, "dp", axis_index_groups=rep_groups(reps))
    qkv_set = adamw(qkv_weight, grad_qkv, qkv_moment, qkv_square, RATE_MATRIX, WEIGHT_DECAY)
    out_set = adamw(out_weight, grad_out, out_moment, out_square, RATE_OUTPUT, WEIGHT_DECAY)
    gate_set = adamw(gate_weight, grad_gate, gate_moment, gate_square, RATE_MATRIX, WEIGHT_DECAY)
    up_set = adamw(up_weight, grad_up, up_moment, up_square, RATE_MATRIX, WEIGHT_DECAY)
    down_set = adamw(down_weight, grad_down, down_moment, down_square, RATE_MATRIX, WEIGHT_DECAY)
    gain_set = adamw(norm_gains, gain_grads, gain_moment, gain_square, RATE_GAIN, 0.0)
    return (result, resid_grad, *qkv_set, *out_set, *gate_set, *up_set, *down_set, *gain_set)


def solution(mesh):
    tokens = P(("dp", "col"), "row")
    wide = P(("row", "dp"), "col")
    tall = P(("col", "dp"), "row")
    gain = P(None, "row")
    weights = (wide,) * 3 + (tall,) * 3 + (wide,) * 6 + (tall,) * 3 + (gain,) * 3
    return jax.shard_map(
        local,
        mesh=mesh,
        in_specs=(tokens, tokens, P("dp", None)) + weights,
        out_specs=(tokens, tokens) + weights,
        check_vma=False,
    )
```

```python
import functools

import jax
import jax.numpy as jnp
from jax import lax
from jax.experimental import pallas as pl
from jax.experimental.pallas import tpu as pltpu
from jax.sharding import PartitionSpec as P

D = 2048
FF = 8192
HD = 64
GROUP = 4
LMAX = 1024
STEP = 10
KEYS = 256
SLICES = 2
PIECES = 4
COLS = 4

EPS_NORM = 1e-05
ROPE_BASE = 500000.0
BETA_ONE = 0.9
BETA_TWO = 0.95
ADAM_EPS = 1e-08
WEIGHT_DECAY = 0.1
RATE_MATRIX = 0.05
RATE_OUTPUT = 0.4
RATE_GAIN = 0.8
MASKED = -1e30
SCALE = HD ** (-0.5)

BF = jnp.bfloat16
F32 = jnp.float32


def dot(left, right, left_dim, right_dim):
    return lax.dot_general(
        left, right, (((left_dim,), (right_dim,)), ((), ())), preferred_element_type=F32
    )


def half_groups(reps):
    return [[rep, rep + reps] for rep in range(reps)]


def rep_groups(reps):
    return [[half * reps + rep for rep in range(reps)] for half in range(2)]


def partner_swap(values_in, reps):
    pairs = [pair for rep in range(reps) for pair in ((rep, rep + reps), (rep + reps, rep))]
    return lax.ppermute(values_in, "dp", pairs)


def both_halves(mine, theirs, half, axis):
    first = jnp.where(half == 0, mine, theirs)
    second = jnp.where(half == 0, theirs, mine)
    return jnp.concatenate([first, second], axis=axis)


def half_columns(weight, reps, after=None):
    half = lax.axis_index("dp") // reps
    own, width = weight.shape[0], weight.shape[1] // 2
    low = weight.astype(BF)
    mine = lax.dynamic_slice_in_dim(low, half * width, width, 1)
    theirs = partner_swap(lax.dynamic_slice_in_dim(low, (1 - half) * width, width, 1), reps)
    if after is not None:
        theirs, _ = lax.optimization_barrier((theirs, after))
    both = both_halves(mine, theirs, half, 0)
    if reps > 1:
        both = lax.all_gather(both, "dp", axis=0, axis_index_groups=rep_groups(reps))
        both = both.reshape(reps, 2, own, width).swapaxes(0, 1).reshape(2 * reps * own, width)
    return both


def own_rows(part, reps):
    half = lax.axis_index("dp") // reps
    height = part.shape[0] // 2
    mine = lax.dynamic_slice_in_dim(part, half * height, height, 0)
    theirs = partner_swap(lax.dynamic_slice_in_dim(part, (1 - half) * height, height, 0), reps)
    part = both_halves(mine, theirs, half, 1)
    if reps > 1:
        part = lax.psum_scatter(
            part, "dp", scatter_dimension=0, tiled=True, axis_index_groups=rep_groups(reps)
        )
    return part


def tall_block(weight, reps):
    own = weight.astype(BF)
    if reps > 1:
        own = lax.all_gather(own, "dp", axis=0, tiled=True, axis_index_groups=rep_groups(reps))
    return own


def own_tall(part, reps):
    if reps > 1:
        part = lax.psum_scatter(
            part, "dp", scatter_dimension=0, tiled=True, axis_index_groups=rep_groups(reps)
        )
    return part


def row_blocks(matrix, rows):
    return matrix.reshape(matrix.shape[0], rows, -1).swapaxes(0, 1)


def rope_tables(position):
    exponent = jnp.arange(0, HD, 2, dtype=F32) / HD
    freq_table = 1.0 / ROPE_BASE**exponent
    angle = position.astype(F32)[:, None] * freq_table[None, :]
    cosine = jnp.cos(angle)
    sine = jnp.sin(angle)
    return (jnp.concatenate([cosine] * 4, axis=1), jnp.concatenate([-sine, sine, -sine, sine], axis=1))


def rotate(vectors, cosine, sine):
    width = vectors.shape[1]
    lane = lax.broadcasted_iota(jnp.int32, vectors.shape, 1)
    lower = lax.rem(lane, HD) < HD // 2
    turned = jnp.where(
        lower, pltpu.roll(vectors, width - HD // 2, 1), pltpu.roll(vectors, HD // 2, 1)
    )
    copies = width // cosine.shape[1]
    cosine = jnp.concatenate([cosine] * copies, axis=1)
    sine = jnp.concatenate([sine] * copies, axis=1)
    return jnp.where(lane < (GROUP + 1) * HD, vectors * cosine + turned * sine, vectors)


MESH = pl.DeviceIdType.MESH
HBM = pl.BlockSpec(memory_space=pl.ANY)
VMEM = pl.BlockSpec(memory_space=pltpu.VMEM)
DMA = pltpu.SemaphoreType.DMA


def takes(micros):
    return pl.CostEstimate(flops=1, bytes_accessed=int(micros * 3.6e6), transcendentals=0)


def params(collective_id):
    return pltpu.CompilerParams(
        collective_id=collective_id, has_side_effects=True, vmem_limit_bytes=60 * 2**20
    )


def tile(index, width):
    return pl.ds(pl.multiple_of(index * width, width), width)


def plane(reps):
    replica, col = lax.axis_index("dp"), lax.axis_index("col")
    half, rep = lax.div(replica, reps), lax.rem(replica, reps)
    core = lax.rem(col, 2)
    other = col + 1 - 2 * core

    def place(half_of, col_of):
        chip = half_of * (COLS // 2) + lax.div(col_of, 2)
        return (chip, lax.rem(col_of, 2), {"dp": half_of * reps + rep, "col": col_of})

    def turn(value, by, modulus):
        return lax.rem(value + by, modulus)

    return {
        "O": place(half, col),
        "P": place(turn(half, 1 - core, 2), turn(col, 2 * core, COLS)),
        "Q": place(turn(half, core, 2), turn(col, 2 - 2 * core, COLS)),
        "D": place(1 - half, turn(col, 2, COLS)),
        "SO": place(half, other),
        "SP": place(turn(half, core, 2), turn(other, 2 - 2 * core, COLS)),
        "SQ": place(turn(half, 1 - core, 2), turn(other, 2 * core, COLS)),
        "SD": place(1 - half, turn(other, 2, COLS)),
    }


def near(reps):
    where = plane(reps)
    return [where["P"][2], where["Q"][2], where["SO"][2]]


def row_partners():
    rows, row = lax.axis_size("row"), lax.axis_index("row")
    return [lax.rem(row + shift, rows) for shift in range(1, rows)]


def signal(devices):
    barrier = pltpu.get_barrier_semaphore()
    for device in devices:
        pl.semaphore_signal(barrier, inc=1, device_id=device, device_id_type=MESH)


def meet(devices):
    signal(devices)
    pl.semaphore_wait(pltpu.get_barrier_semaphore(), len(devices))


GATHER_KINDS = ("P", "Q", "D", "SO", "SP", "SQ", "SD")


def run_gather(reps, own_ref, held_ref, sems, use):
    send_sems, recv_sems, local_sem = sems
    where = plane(reps)
    sub = own_ref.shape[0]
    height = sub // PIECES

    def spot(kind, piece):
        chip, core, _ = where[kind]
        return held_ref.at[chip, pl.ds(pl.multiple_of(core * sub + piece * height, height), height)]

    def message(kind, piece, source, target, device):
        index = GATHER_KINDS.index(kind)
        return pltpu.make_async_remote_copy(
            src_ref=source,
            dst_ref=target,
            send_sem=send_sems.at[index, piece],
            recv_sem=recv_sems.at[index, piece],
            device_id=device,
            device_id_type=MESH,
        )

    near_p, near_q, sibling = where["P"][2], where["Q"][2], where["SO"][2]
    sent = []

    def send(kind, piece, source, held_by, device):
        copy = message(kind, piece, source, spot(held_by, piece), device)
        copy.start()
        sent.append(copy)

    def arrive(kind, piece):
        message(kind, piece, spot(kind, piece), spot(kind, piece), sibling).wait_recv()

    own_copy = pltpu.make_async_copy(own_ref, held_ref.at[where["O"][0], tile(where["O"][1], sub)], local_sem)
    own_copy.start()
    for piece in range(PIECES):
        source = own_ref.at[pl.ds(piece * height, height)]
        send("P", piece, source, "O", near_p)
        send("Q", piece, source, "O", near_q)
        send("SO", piece, source, "O", sibling)
    own_copy.wait()
    for piece in range(PIECES):
        arrive("SO", piece)
    use(0, where["O"][0])
    for piece in range(PIECES):
        arrive("P", piece)
        send("D", piece, spot("P", piece), "P", near_q)
        send("SP", piece, spot("P", piece), "P", sibling)
    for piece in range(PIECES):
        arrive("Q", piece)
        send("SQ", piece, spot("Q", piece), "Q", sibling)
    for piece in range(PIECES):
        arrive("SQ", piece)
    use(1, where["P"][0])
    for piece in range(PIECES):
        arrive("SP", piece)
    use(2, where["Q"][0])
    for piece in range(PIECES):
        arrive("D", piece)
        send("SD", piece, spot("D", piece), "D", sibling)
    for piece in range(PIECES):
        arrive("SD", piece)
    use(3, where["D"][0])
    for copy in sent:
        copy.wait_send()


def gather_scratch(sub):
    count = len(GATHER_KINDS)
    return [pltpu.VMEM((COLS, 2 * sub, D), BF), DMA((count, PIECES)), DMA((count, PIECES)), DMA]


SCATTER_SWAPS = ("D", "Q", "P", "O")
SCATTER_HOPS = ("D", "Q", "P")


def scatter_order(reps):
    where = plane(reps)
    return [where[kind][0] for kind in SCATTER_SWAPS]


def run_scatter(reps, partial, finish, scratch, meanwhile=None):
    total_ref, give_ref, take_ref, hop_out, hop_in, both_ref, swap_send, swap_recv, hop_send, hop_recv = scratch
    where = plane(reps)
    core = where["O"][1]
    device = {"P": where["P"][2], "Q": where["Q"][2], "D": where["Q"][2]}
    sibling = where["SO"][2]
    sub = total_ref.shape[1]
    height = sub // PIECES
    sibling_kind = {"D": "D", "Q": "P", "P": "Q", "O": "O"}
    sent = []

    def swap(kind):
        index = SCATTER_SWAPS.index(kind)
        return pltpu.make_async_remote_copy(
            src_ref=give_ref.at[index],
            dst_ref=take_ref.at[index],
            send_sem=swap_send.at[index],
            recv_sem=swap_recv.at[index],
            device_id=sibling,
            device_id_type=MESH,
        )

    def hop(kind, piece):
        index = SCATTER_HOPS.index(kind)
        rows = pl.ds(piece * height, height)
        return pltpu.make_async_remote_copy(
            src_ref=hop_out.at[index, rows],
            dst_ref=hop_in.at[index, rows],
            send_sem=hop_send.at[index, piece],
            recv_sem=hop_recv.at[index, piece],
            device_id=device[kind],
            device_id_type=MESH,
        )

    def compute(step, kind):
        mine, theirs = SCATTER_SWAPS.index(kind), SCATTER_SWAPS.index(sibling_kind[kind])

        def put(columns, value):
            both_ref[...] = value
            total_ref[mine, :, columns] = both_ref[tile(core, sub), :]
            give_ref[theirs, :, columns] = both_ref[tile(1 - core, sub), :].astype(BF)

        partial(step, where[kind][0], put)
        copy = swap(sibling_kind[kind])
        copy.start()
        sent.append(copy)

    def settle(kind):
        index = SCATTER_SWAPS.index(kind)
        swap(kind).wait_recv()
        for piece in range(PIECES):
            rows = pl.ds(piece * height, height)
            value = total_ref[index, rows, :] + take_ref[index, rows, :].astype(F32)
            if kind == "P":
                hop("D", piece).wait_recv()
                value += hop_in[SCATTER_HOPS.index("D"), rows, :].astype(F32)
            if kind == "O":
                for source in ("Q", "P"):
                    hop(source, piece).wait_recv()
                    value += hop_in[SCATTER_HOPS.index(source), rows, :].astype(F32)
                finish(piece, rows, value)
            else:
                hop_out[SCATTER_HOPS.index(kind), rows, :] = value.astype(BF)
                copy = hop(kind, piece)
                copy.start()
                sent.append(copy)

    compute(0, "D")
    compute(1, "Q")
    settle("D")
    compute(2, "P")
    settle("Q")
    compute(3, "O")
    if meanwhile is not None:
        meanwhile()
    settle("P")
    settle("O")
    for copy in sent:
        copy.wait_send()


SPAN = 512


def scatter_scratch(sub):
    return [
        pltpu.VMEM((4, sub, D), F32),
        pltpu.VMEM((4, sub, D), BF),
        pltpu.VMEM((4, sub, D), BF),
        pltpu.VMEM((3, sub, D), BF),
        pltpu.VMEM((3, sub, D), BF),
        pltpu.VMEM((2 * sub, SPAN), F32),
        DMA((4,)),
        DMA((4,)),
        DMA((3, PIECES)),
        DMA((3, PIECES)),
    ]


SCATTER_REFS = 10


def col_partners():
    cols, col = lax.axis_size("col"), lax.axis_index("col")
    return [lax.rem(col + shift, cols) for shift in range(1, cols)]


def home_scratch(sub, rows):
    return [
        pltpu.VMEM((rows, sub, D // rows), BF),
        pltpu.VMEM((sub * COLS, D // rows), BF),
        DMA((rows - 1, PIECES)),
        DMA((rows - 1, PIECES)),
        DMA((COLS - 1,)),
        DMA((COLS - 1,)),
    ]


HOME_REFS = 6


class Home:
    def __init__(self, stage, scratch):
        self.stage = stage
        self.mid, self.home, self.row_send, self.row_recv, self.col_send, self.col_recv = scratch
        self.row, self.col = lax.axis_index("row"), lax.axis_index("col")
        self.sub = stage.shape[0]
        self.height, self.width = self.sub // PIECES, self.mid.shape[2]
        self.sent = []

    def row_copies(self, piece):
        rows = pl.ds(piece * self.height, self.height)
        return [
            pltpu.make_async_remote_copy(
                src_ref=self.stage.at[rows, tile(partner, self.width)],
                dst_ref=self.mid.at[self.row, rows],
                send_sem=self.row_send.at[shift, piece],
                recv_sem=self.row_recv.at[shift, piece],
                device_id={"row": partner},
                device_id_type=MESH,
            )
            for shift, partner in enumerate(row_partners())
        ]

    def send(self, piece):
        rows = pl.ds(piece * self.height, self.height)
        copies = self.row_copies(piece)
        for copy in copies:
            copy.start()
        self.sent += copies
        self.mid[self.row, rows, :] = self.stage[rows, tile(self.row, self.width)]

    def turn(self):
        for copy in self.sent:
            copy.wait()
        self.sent = []
        for shift, partner in enumerate(col_partners()):
            copy = pltpu.make_async_remote_copy(
                src_ref=self.mid.at[partner],
                dst_ref=self.home.at[tile(self.col, self.sub)],
                send_sem=self.col_send.at[shift],
                recv_sem=self.col_recv.at[shift],
                device_id={"col": partner},
                device_id_type=MESH,
            )
            copy.start()
            self.sent.append(copy)
        self.home[tile(self.col, self.sub), :] = self.mid[self.col]

    def wait(self):
        for copy in self.sent:
            copy.wait()


def head_rows(block):
    turned = block.astype(F32).T
    return [turned[head * HD : (head + 1) * HD].astype(BF) for head in range(GROUP)]


def allowed_entries(key_block, low_ref, query_first):
    tokens = low_ref.shape[-1]
    key_slot = key_block * KEYS + lax.broadcasted_iota(jnp.int32, (KEYS, tokens), 0)
    query_slot = query_first + lax.broadcasted_iota(jnp.int32, (KEYS, tokens), 1)
    return (key_slot >= low_ref[...]) & (key_slot <= query_slot)


def key_rows(block):
    return pl.ds(pl.multiple_of(block * KEYS, KEYS), KEYS)


def attend_kernel(bounds, query_ref, pair_ref, low_ref, out_ref, log_ref, score_ref, mix_ref):
    step = pl.program_id(1)
    place = pl.program_id(0) * pl.num_programs(1) + step
    first, last, query_first = bounds[0, place], bounds[1, place], bounds[2, place]
    tokens = query_ref.shape[0]
    blank = jnp.zeros((HD, tokens), BF)
    queries = [jnp.concatenate([rows, blank], axis=0) for rows in head_rows(query_ref[...])]

    def score_block(block, tops):
        pairs = pair_ref[key_rows(block), :]
        allowed = allowed_entries(block, low_ref, query_first)
        new_tops = []
        for head in range(GROUP):
            scores = jnp.where(allowed, dot(pairs, queries[head], 1, 0), MASKED)
            score_ref[head, key_rows(block - first), :] = scores
            new_tops.append(jnp.maximum(tops[head], jnp.max(scores, axis=0, keepdims=True)))
        return tuple(new_tops)

    start = tuple(jnp.full((1, tokens), MASKED, F32) for _ in range(GROUP))
    tops = lax.fori_loop(first, last, score_block, start)
    mix_ref[...] = jnp.zeros_like(mix_ref)

    def mix_block(block, totals):
        pairs = pair_ref[key_rows(block), :]
        new_totals = []
        for head in range(GROUP):
            terms = jnp.exp(score_ref[head, key_rows(block - first), :] - tops[head])
            new_totals.append(totals[head] + jnp.sum(terms, axis=0, keepdims=True))
            mix_ref[head] += dot(pairs, terms.astype(BF), 0, 0)
        return tuple(new_totals)

    start = tuple(jnp.zeros((1, tokens), F32) for _ in range(GROUP))
    totals = lax.fori_loop(first, last, mix_block, start)
    mixed = jnp.concatenate(
        [mix_ref[head, HD:, :] / totals[head] for head in range(GROUP)], axis=0
    )
    out_ref[...] = mixed.T.astype(BF)
    for head in range(GROUP):
        log_ref[head : head + 1, :] = tops[head] + jnp.log(totals[head])


def attend_back_kernel(
    bounds, query_ref, grad_ref, pair_ref, low_ref, log_ref, dquery_ref, dpair_ref, prob_ref, dprob_ref, dmix_ref
):
    step = pl.program_id(1)
    place = pl.program_id(0) * pl.num_programs(1) + step
    first, last, query_first = bounds[0, place], bounds[1, place], bounds[2, place]
    tokens = query_ref.shape[0]
    blank = jnp.zeros((HD, tokens), BF)
    queries = [jnp.concatenate([rows, blank], axis=0) for rows in head_rows(query_ref[...])]
    grads = [jnp.concatenate([blank, rows], axis=0) for rows in head_rows(grad_ref[...])]

    @pl.when(step == 0)
    def _():
        dpair_ref[...] = jnp.zeros_like(dpair_ref)

    def prob_block(block, inners):
        pairs = pair_ref[key_rows(block), :]
        allowed = allowed_entries(block, low_ref, query_first)
        new_inners = []
        for head in range(GROUP):
            scores = dot(pairs, queries[head], 1, 0)
            probs = jnp.where(allowed, jnp.exp(scores - log_ref[head : head + 1, :]), 0.0)
            dprobs = dot(pairs, grads[head], 1, 0)
            prob_ref[head, key_rows(block - first), :] = probs
            dprob_ref[head, key_rows(block - first), :] = dprobs
            new_inners.append(inners[head] + jnp.sum(probs * dprobs, axis=0, keepdims=True))
        return tuple(new_inners)

    start = tuple(jnp.zeros((1, tokens), F32) for _ in range(GROUP))
    inners = lax.fori_loop(first, last, prob_block, start)
    dmix_ref[...] = jnp.zeros_like(dmix_ref)
    all_queries = jnp.concatenate(queries, axis=1)
    all_grads = jnp.concatenate(grads, axis=1)

    def back_block(block, carry):
        rows = key_rows(block)
        pairs = pair_ref[rows, :]
        all_probs, all_scores = [], []
        for head in range(GROUP):
            probs = prob_ref[head, key_rows(block - first), :]
            dprobs = dprob_ref[head, key_rows(block - first), :]
            dscores = (probs * (dprobs - inners[head])).astype(BF)
            dmix_ref[head] += dot(pairs, dscores, 0, 0)
            all_probs.append(probs.astype(BF))
            all_scores.append(dscores)
        dpair_ref[rows, :] += dot(jnp.concatenate(all_scores, axis=1), all_queries, 1, 1) + dot(
            jnp.concatenate(all_probs, axis=1), all_grads, 1, 1
        )
        return carry

    lax.fori_loop(first, last, back_block, 0)
    dquery = jnp.concatenate([dmix_ref[head, :HD, :] for head in range(GROUP)], axis=0)
    dquery_ref[...] = dquery.T * SCALE


def attend(queries, pairs, low, bounds):
    tokens, width = queries.shape
    replicas, slots, _ = pairs.shape
    rows = low.shape[2]
    blocks = low.shape[0] // replicas
    span = LMAX + KEYS
    return pl.pallas_call(
        attend_kernel,
        grid_spec=pltpu.PrefetchScalarGridSpec(
            num_scalar_prefetch=1,
            grid=(replicas, blocks),
            in_specs=[
                pl.BlockSpec((rows, GROUP * HD), lambda rep, block, _: (rep * blocks + block, 0)),
                pl.BlockSpec((None, slots, 2 * HD), lambda rep, block, _: (rep, 0, 0)),
                pl.BlockSpec((None, 1, rows), lambda rep, block, _: (rep * blocks + block, 0, 0)),
            ],
            out_specs=[
                pl.BlockSpec((rows, GROUP * HD), lambda rep, block, _: (rep * blocks + block, 0)),
                pl.BlockSpec((None, None, GROUP, rows), lambda rep, block, _: (rep, block, 0, 0)),
            ],
            scratch_shapes=[
                pltpu.VMEM((GROUP, span, rows), F32),
                pltpu.VMEM((GROUP, 2 * HD, rows), F32),
            ],
        ),
        out_shape=[
            jax.ShapeDtypeStruct((tokens, width), BF),
            jax.ShapeDtypeStruct((replicas, blocks, GROUP, rows), F32),
        ],
        compiler_params=pltpu.CompilerParams(vmem_limit_bytes=48 * 2**20),
        cost_estimate=takes(14),
        name="attend",
    )(bounds, queries, pairs, low)


def attend_back(queries, grads, pairs, low, log_total, bounds):
    tokens, width = queries.shape
    replicas, slots, _ = pairs.shape
    rows = low.shape[2]
    blocks = low.shape[0] // replicas
    span = LMAX + KEYS
    return pl.pallas_call(
        attend_back_kernel,
        grid_spec=pltpu.PrefetchScalarGridSpec(
            num_scalar_prefetch=1,
            grid=(replicas, blocks),
            in_specs=[
                pl.BlockSpec((rows, GROUP * HD), lambda rep, block, _: (rep * blocks + block, 0)),
                pl.BlockSpec((rows, GROUP * HD), lambda rep, block, _: (rep * blocks + block, 0)),
                pl.BlockSpec((None, slots, 2 * HD), lambda rep, block, _: (rep, 0, 0)),
                pl.BlockSpec((None, 1, rows), lambda rep, block, _: (rep * blocks + block, 0, 0)),
                pl.BlockSpec((None, None, GROUP, rows), lambda rep, block, _: (rep, block, 0, 0)),
            ],
            out_specs=[
                pl.BlockSpec((rows, GROUP * HD), lambda rep, block, _: (rep * blocks + block, 0)),
                pl.BlockSpec((None, slots, 2 * HD), lambda rep, block, _: (rep, 0, 0)),
            ],
            scratch_shapes=[
                pltpu.VMEM((GROUP, span, rows), F32),
                pltpu.VMEM((GROUP, span, rows), F32),
                pltpu.VMEM((GROUP, 2 * HD, rows), F32),
            ],
        ),
        out_shape=[
            jax.ShapeDtypeStruct((tokens, width), F32),
            jax.ShapeDtypeStruct((replicas, slots, 2 * HD), F32),
        ],
        compiler_params=pltpu.CompilerParams(vmem_limit_bytes=48 * 2**20),
        cost_estimate=takes(23),
        name="attend_back",
    )(bounds, queries, grads, pairs, low, log_total)


def norm_of(vectors):
    scaling = lax.rsqrt(jnp.mean(vectors * vectors, axis=1, keepdims=True) + EPS_NORM)
    return vectors * scaling, scaling


def norm_back(value, vectors, gain):
    unit, scaling = norm_of(vectors)
    weighted = value * gain
    inner = jnp.mean(weighted * unit, axis=1, keepdims=True)
    return scaling * (weighted - unit * inner), jnp.sum(value * unit, axis=0, keepdims=True)


def exchange_kernel(
    token_ref, top_ref, gain_ref, usable_ref, source_ref, normed_ref, grad_top_ref, gains_ref,
    held, held_top, mid, mid_top, held_gains, col_send, col_recv, row_send, row_recv, gain_send, gain_recv, local_sems,
):
    row, col = lax.axis_index("row"), lax.axis_index("col")
    sub, width = held.shape[0], token_ref.shape[1]
    row_of = row_partners()
    col_of = col_partners()
    meet([{"row": partner} for partner in row_of] + [{"col": partner} for partner in col_of])
    own_cols = tile(row, width)

    def run(copies):
        for copy in copies:
            copy.start()
        return copies

    def finish(copies):
        for copy in copies:
            copy.wait()

    def remote(source, target, send_sem, recv_sem, device):
        return pltpu.make_async_remote_copy(
            src_ref=source, dst_ref=target, send_sem=send_sem, recv_sem=recv_sem, device_id=device, device_id_type=MESH
        )

    def to_columns(array, source, target):
        return run(
            [
                remote(
                    source.at[tile(partner, sub)], target.at[col],
                    col_send.at[array, shift], col_recv.at[array, shift], {"col": partner},
                )
                for shift, partner in enumerate(col_of)
            ]
            + [pltpu.make_async_copy(source.at[tile(col, sub)], target.at[col], local_sems.at[array, 0])]
        )

    def to_rows(array, source, target):
        return run(
            [
                remote(
                    source.at[partner], target.at[:, own_cols],
                    row_send.at[array, shift], row_recv.at[array, shift], {"row": partner},
                )
                for shift, partner in enumerate(row_of)
            ]
            + [pltpu.make_async_copy(source.at[row], target.at[:, own_cols], local_sems.at[array, 1])]
        )

    tokens = to_columns(0, token_ref, mid)
    gains = run(
        [
            remote(gain_ref, held_gains.at[:, own_cols], gain_send.at[shift], gain_recv.at[shift], {"row": partner})
            for shift, partner in enumerate(row_of)
        ]
        + [pltpu.make_async_copy(gain_ref, held_gains.at[:, own_cols], local_sems.at[2, 0])]
    )
    tops = to_columns(1, top_ref, mid_top)
    finish(tokens)
    tokens = to_rows(0, mid, held)
    finish(tops)
    tops = to_rows(1, mid_top, held_top)
    finish(gains)
    finish(tokens)
    source_ref[...] = held[...]
    gains_ref[...] = held_gains[...]
    unit, _ = norm_of(held[...].astype(F32))
    normed_ref[...] = (unit * held_gains[0:1, :]).astype(BF)
    finish(tops)
    grad_top_ref[...] = (held_top[...].astype(F32) * usable_ref[...]).astype(BF)


def exchange(tokens, top, gains, usable, rows):
    sub, width = tokens.shape[0] // COLS, tokens.shape[1]
    block = jax.ShapeDtypeStruct((sub, rows * width), BF)
    return pl.pallas_call(
        exchange_kernel,
        out_shape=[block, block, block, jax.ShapeDtypeStruct((gains.shape[0], rows * width), F32)],
        in_specs=[VMEM] * 4,
        out_specs=[VMEM] * 4,
        scratch_shapes=[pltpu.VMEM((sub, rows * width), BF)] * 2
        + [pltpu.VMEM((COLS, sub, width), BF)] * 2
        + [
            pltpu.VMEM((gains.shape[0], rows * width), F32),
            DMA((2, COLS - 1)),
            DMA((2, COLS - 1)),
            DMA((2, rows - 1)),
            DMA((2, rows - 1)),
            DMA((rows - 1,)),
            DMA((rows - 1,)),
            DMA((3, 2)),
        ],
        compiler_params=params(1),
        cost_estimate=takes(65),
        name="exchange",
    )(tokens, top, gains, usable)


def project_kernel(
    reps, own_ref, top_ref, weight_ref, cosine_ref, sine_ref,
    all_ref, top_all_ref, query_ref, pair_ref,
    held, send_sems, recv_sems, local_sem, top_held, top_send, top_recv, top_local,
    queries, pairs, halo, out_sems, pair_sems, halo_sems, pair_send, pair_recv,
):
    row, rows = lax.axis_index("row"), lax.axis_size("row")
    meet(near(reps) + [{"row": partner} for partner in row_partners()])
    sub = own_ref.shape[0]
    copies, chips = [], []
    has_next, has_last = row < rows - 1, row > 0

    @pl.when(row == 0)
    def _():
        halo[...] = jnp.zeros_like(halo)

    def out(source, target, sem):
        copy = pltpu.make_async_copy(source, target, sem)
        copy.start()
        copies.append(copy)

    def push(step, chip):
        return pltpu.make_async_remote_copy(
            src_ref=pairs.at[chip],
            dst_ref=halo.at[chip],
            send_sem=pair_send.at[step],
            recv_sem=pair_recv.at[step],
            device_id={"row": lax.rem(row + 1, rows)},
            device_id_type=MESH,
        )

    def use(step, chip):
        chips.append(chip)
        out(held.at[chip], all_ref.at[chip], out_sems.at[step])
        places = tile(chip, 2 * sub)
        turned = rotate(dot(held[chip], weight_ref[...], 1, 0), cosine_ref[places, :], sine_ref[places, :])
        queries[chip] = (turned[:, : GROUP * HD] * SCALE).astype(BF)
        out(queries.at[chip], query_ref.at[chip], out_sems.at[COLS + step])
        pairs[chip] = turned[:, GROUP * HD :].astype(BF)
        out(pairs.at[chip], pair_ref.at[lax.div(chip, 2), 1, lax.rem(chip, 2)], pair_sems.at[step])

        @pl.when(has_next)
        def _():
            push(step, chip).start()

    run_gather(reps, own_ref, held, (send_sems, recv_sems, local_sem), use)

    def use_top(step, chip):
        out(top_held.at[chip], top_all_ref.at[chip], out_sems.at[2 * COLS + step])

    run_gather(reps, top_ref, top_held, (top_send, top_recv, top_local), use_top)
    for step, chip in enumerate(chips):

        @pl.when(has_next)
        def _():
            push(step, chip).wait_send()

        @pl.when(has_last)
        def _():
            push(step, chip).wait_recv()

    for chip in range(COLS):
        out(halo.at[chip], pair_ref.at[chip // 2, 0, chip % 2], halo_sems.at[chip])
    for copy in copies:
        copy.wait()


def project(normed_own, top_own, weight, cosine, sine, reps):
    sub = normed_own.shape[0]
    return pl.pallas_call(
        functools.partial(project_kernel, reps),
        out_shape=[
            jax.ShapeDtypeStruct((COLS, 2 * sub, D), BF),
            jax.ShapeDtypeStruct((COLS, 2 * sub, D), BF),
            jax.ShapeDtypeStruct((COLS, 2 * sub, GROUP * HD), BF),
            jax.ShapeDtypeStruct((2, 2, COLS // 2, 2 * sub, 2 * HD), BF),
        ],
        in_specs=[VMEM] * 5,
        out_specs=[HBM] * 4,
        scratch_shapes=gather_scratch(sub)
        + gather_scratch(sub)
        + [
            pltpu.VMEM((COLS, 2 * sub, GROUP * HD), BF),
            pltpu.VMEM((COLS, 2 * sub, 2 * HD), BF),
            pltpu.VMEM((COLS, 2 * sub, 2 * HD), BF),
            DMA((3 * COLS,)),
            DMA((COLS,)),
            DMA((COLS,)),
            DMA((COLS,)),
            DMA((COLS,)),
        ],
        compiler_params=params(2),
        cost_estimate=takes(75),
        name="project",
    )(normed_own, top_own, weight, cosine, sine)


def mix_out_kernel(reps, attended_ref, weight_ref, source_ref, gains_ref, middle_ref, normed_ref, *scratch):
    meet(near(reps))
    parts, _, width = weight_ref.shape

    def partial(step, chip, put):
        for part in range(parts):
            put(pl.ds(part * width, width), dot(attended_ref[chip], weight_ref[part], 1, 0))

    def finish(piece, rows, value):
        middle = source_ref[rows, :].astype(F32) + value
        middle_ref[rows, :] = middle
        normed_ref[rows, :] = (norm_of(middle)[0] * gains_ref[1:2, :]).astype(BF)

    run_scatter(reps, partial, finish, scratch)


def mix_out(attended, weight, source, gains, reps):
    sub = source.shape[0]
    return pl.pallas_call(
        functools.partial(mix_out_kernel, reps),
        out_shape=[jax.ShapeDtypeStruct((sub, D), F32), jax.ShapeDtypeStruct((sub, D), BF)],
        in_specs=[VMEM] * 4,
        out_specs=[VMEM] * 2,
        scratch_shapes=scatter_scratch(sub),
        compiler_params=params(3),
        cost_estimate=takes(44),
        name="mix_out",
    )(attended, weight, source, gains)


def gated(tokens, top, weight_ref, put):
    parts, rows, width = weight_ref.shape
    units, span = rows // 3, 256

    def one_tile(index, carry):
        columns = tile(index, span)
        gate_w = weight_ref[:, :units, columns].reshape(D, span)
        up_w = weight_ref[:, units : 2 * units, columns].reshape(D, span)
        gate = dot(tokens, gate_w, 1, 0)
        up = dot(tokens, up_w, 1, 0)
        down_rows = pl.ds(pl.multiple_of(2 * units + index * span, span), span)
        grad = dot(top[:, :width], weight_ref[0, down_rows, :], 1, 1)
        for part in range(1, parts):
            grad += dot(top[:, part * width : (part + 1) * width], weight_ref[part, down_rows, :], 1, 1)
        sigma = 1.0 / (1.0 + jnp.exp(-gate))
        active = gate * sigma
        put(
            columns,
            (active * up).astype(BF),
            (grad * up * sigma * (1.0 + gate * (1.0 - sigma))).astype(BF),
            (grad * active).astype(BF),
        )
        return carry

    lax.fori_loop(0, units // span, one_tile, 0)


def first_slice_kernel(
    reps, own_ref, top_ref, weight_ref, all_ref, hidden_ref, ggate_ref, gup_ref,
    held, send_sems, recv_sems, local_sem, tops, hiddens, ggates, gups, top_sems, out_sems,
):
    meet(near(reps))
    where = plane(reps)
    order = [where[kind][0] for kind in ("O", "P", "Q", "D")]
    loads = [pltpu.make_async_copy(top_ref.at[chip], tops.at[chip], top_sems.at[step]) for step, chip in enumerate(order)]
    for copy in loads:
        copy.start()
    copies = []

    def use(step, chip):
        def out(source, target, index):
            copy = pltpu.make_async_copy(source.at[chip], target.at[chip], out_sems.at[index, step])
            copy.start()
            copies.append(copy)

        out(held, all_ref, 0)
        loads[step].wait()

        def put(columns, hidden, ggate, gup):
            hiddens[chip, :, columns] = hidden
            ggates[chip, :, columns] = ggate
            gups[chip, :, columns] = gup

        gated(held[chip], tops[chip], weight_ref, put)
        out(hiddens, hidden_ref, 1)
        out(ggates, ggate_ref, 2)
        out(gups, gup_ref, 3)

    run_gather(reps, own_ref, held, (send_sems, recv_sems, local_sem), use)
    for copy in copies:
        copy.wait()


def first_slice(normed_own, top_all, weight, reps):
    sub = normed_own.shape[0]
    units = weight.shape[1] // 3
    piece = jax.ShapeDtypeStruct((COLS, 2 * sub, units), BF)
    return pl.pallas_call(
        functools.partial(first_slice_kernel, reps),
        out_shape=[jax.ShapeDtypeStruct((COLS, 2 * sub, D), BF)] + [piece] * 3,
        in_specs=[VMEM, HBM, VMEM],
        out_specs=[HBM] * 4,
        scratch_shapes=gather_scratch(sub)
        + [pltpu.VMEM((COLS, 2 * sub, D), BF)]
        + [pltpu.VMEM((COLS, 2 * sub, units), BF)] * 3
        + [DMA((COLS,)), DMA((4, COLS))],
        compiler_params=params(4),
        cost_estimate=takes(50),
        name="first_slice",
    )(normed_own, top_all, weight)


def second_slice_kernel(
    reps, token_ref, top_ref, ggate_one_ref, gup_one_ref, weight_one_ref, weight_ref, middle_ref, own_top_ref, gains_ref,
    hidden_ref, ggate_ref, gup_ref, grad_ref, low_ref, gain_ref, *scratch,
):
    tokens, tops, ggate_ones, gup_ones, weight_one, hiddens, ggates, gups, in_sems, out_sems, weight_sem = scratch[SCATTER_REFS:]
    meet(near(reps))
    order = scatter_order(reps)
    parts, rows, width = weight_ref.shape
    units = rows // 3
    loads, copies = {}, []
    sources = ((token_ref, tokens), (top_ref, tops), (ggate_one_ref, ggate_ones), (gup_one_ref, gup_ones))

    def load(step):
        loads[step] = []
        for index, (source, target) in enumerate(sources):
            copy = pltpu.make_async_copy(source.at[order[step]], target.at[step % 2], in_sems.at[index, step % 2])
            copy.start()
            loads[step].append(copy)

    load(0)
    weight_copy = pltpu.make_async_copy(weight_one_ref.at[:, pl.ds(0, 2 * units)], weight_one, weight_sem)
    weight_copy.start()
    gain_ref[...] = jnp.zeros_like(gain_ref)

    def partial(step, chip, put):
        slot = step % 2
        for copy in loads[step]:
            copy.wait()
        if step < 3:
            load(step + 1)

        def keep(columns, hidden, ggate, gup):
            hiddens[chip, :, columns] = hidden
            ggates[chip, :, columns] = ggate
            gups[chip, :, columns] = gup

        gated(tokens[slot], tops[slot], weight_ref, keep)
        for index, (source, target) in enumerate(((hiddens, hidden_ref), (ggates, ggate_ref), (gups, gup_ref))):
            copy = pltpu.make_async_copy(source.at[chip], target.at[chip], out_sems.at[index, step])
            copy.start()
            copies.append(copy)
        if step == 0:
            weight_copy.wait()
        for part in range(parts):
            value = dot(ggates[chip], weight_ref[part, :units, :], 1, 1)
            value += dot(gups[chip], weight_ref[part, units : 2 * units, :], 1, 1)
            value += dot(ggate_ones[slot], weight_one[part, :units, :], 1, 1)
            value += dot(gup_ones[slot], weight_one[part, units:, :], 1, 1)
            put(pl.ds(part * width, width), value)

    def finish(piece, rows_of, value):
        back, gain_part = norm_back(value, middle_ref[rows_of, :], gains_ref[1:2, :])
        grad = own_top_ref[rows_of, :].astype(F32) + back
        grad_ref[rows_of, :] = grad
        low_ref[rows_of, :] = grad.astype(BF)
        gain_ref[0:1, :] += gain_part

    run_scatter(reps, partial, finish, scratch[:SCATTER_REFS])
    for copy in copies:
        copy.wait()


def second_slice(normed_all, top_all, ggate_one, gup_one, weight_one, weight, middle, own_top, gains, reps):
    sub = middle.shape[0]
    parts, rows, width = weight.shape
    units = rows // 3
    piece = jax.ShapeDtypeStruct((COLS, 2 * sub, units), BF)
    return pl.pallas_call(
        functools.partial(second_slice_kernel, reps),
        out_shape=[piece] * 3
        + [
            jax.ShapeDtypeStruct((sub, D), F32),
            jax.ShapeDtypeStruct((sub, D), BF),
            jax.ShapeDtypeStruct((8, D), F32),
        ],
        in_specs=[HBM] * 5 + [VMEM] * 4,
        out_specs=[HBM] * 3 + [VMEM] * 3,
        scratch_shapes=scatter_scratch(sub)
        + [pltpu.VMEM((2, 2 * sub, D), BF)] * 2
        + [pltpu.VMEM((2, 2 * sub, units), BF)] * 2
        + [pltpu.VMEM((parts, 2 * units, width), BF)]
        + [pltpu.VMEM((COLS, 2 * sub, units), BF)] * 3
        + [DMA((4, 2)), DMA((3, COLS)), DMA],
        compiler_params=params(5),
        cost_estimate=takes(65),
        name="second_slice",
    )(normed_all, top_all, ggate_one, gup_one, weight_one, weight, middle, own_top, gains)


def back_out_kernel(
    reps, own_ref, weight_ref, token_ref, top_ref, hidden_ref, ggate_ref, gup_ref, all_ref, grad_ref, slice_ref,
    held, send_sems, recv_sems, local_sem, grads, out_sems, tokens, tops, slices, in_sems, slice_sems,
):
    meet(near(reps))
    parts, _, width = weight_ref.shape
    units = hidden_ref.shape[1]
    chips, height = token_ref.shape[:2]
    copies, loads, stores = [], {}, {}

    def load(part):
        loads[part] = []
        columns = pl.ds(part * width, width)
        for index, (source, target) in enumerate(((token_ref, tokens), (top_ref, tops))):
            copy = pltpu.make_async_copy(source.at[:, :, columns], target.at[part % 2], in_sems.at[index, part % 2])
            copy.start()
            loads[part].append(copy)

    load(0)

    def slice_grads(part):
        slot = part % 2
        for copy in loads[part]:
            copy.wait()
        if part < parts - 1:
            load(part + 1)
        if part >= 2:
            stores[part - 2].wait()
        features = tokens[slot].reshape(chips * height, width)
        slices[slot, :units] = dot(features, ggate_ref[...], 0, 0).astype(BF)
        slices[slot, units : 2 * units] = dot(features, gup_ref[...], 0, 0).astype(BF)
        slices[slot, 2 * units :] = dot(hidden_ref[...], tops[slot].reshape(chips * height, width), 0, 0).astype(BF)
        stores[part] = pltpu.make_async_copy(slices.at[slot], slice_ref.at[part], slice_sems.at[slot])
        stores[part].start()

    def use(step, chip):
        def out(source, target, index):
            copy = pltpu.make_async_copy(source.at[chip], target.at[chip], out_sems.at[index, step])
            copy.start()
            copies.append(copy)

        out(held, all_ref, 0)
        total = dot(held[chip, :, :width], weight_ref[0], 1, 1)
        for part in range(1, parts):
            total += dot(held[chip, :, part * width : (part + 1) * width], weight_ref[part], 1, 1)
        grads[chip] = total.astype(BF)
        out(grads, grad_ref, 1)
        slice_grads(step)

    run_gather(reps, own_ref, held, (send_sems, recv_sems, local_sem), use)
    for copy in copies + [stores[parts - 2], stores[parts - 1]]:
        copy.wait()


def back_out(grad_own, weight, normed_all, top_all, hidden, ggate, gup, reps):
    sub = grad_own.shape[0]
    parts, _, width = weight.shape
    chips, height, units = hidden.shape
    flat = [array.reshape(chips * height, units) for array in (hidden, ggate, gup)]
    return pl.pallas_call(
        functools.partial(back_out_kernel, reps),
        out_shape=[
            jax.ShapeDtypeStruct((COLS, 2 * sub, D), BF),
            jax.ShapeDtypeStruct((COLS, 2 * sub, weight.shape[1]), BF),
            jax.ShapeDtypeStruct((parts, 3 * units, width), BF),
        ],
        in_specs=[VMEM] * 2 + [HBM] * 2 + [VMEM] * 3,
        out_specs=[HBM] * 3,
        scratch_shapes=gather_scratch(sub)
        + [pltpu.VMEM((COLS, 2 * sub, weight.shape[1]), BF), DMA((2, COLS))]
        + [pltpu.VMEM((2, chips, height, width), BF)] * 2
        + [pltpu.VMEM((2, 3 * units, width), BF), DMA((2, 2)), DMA((2,))],
        compiler_params=params(6),
        cost_estimate=takes(50),
        name="back_out",
    )(grad_own, weight, normed_all, top_all, *flat)


def lift_kernel(
    reps, hidden_one_ref, hidden_two_ref, weight_one_ref, weight_two_ref, middle_ref,
    dquery_ref, dpair_ref, cosine_ref, sine_ref, result_ref, proj_ref, *scratch,
):
    weight_one, weight_two, weight_sems, low, taken, push_send, push_recv = scratch[SCATTER_REFS:]
    parts, units, width = weight_one.shape
    row, rows = lax.axis_index("row"), lax.axis_size("row")
    loads = []
    for index, (source, target) in enumerate(((weight_one_ref, weight_one), (weight_two_ref, weight_two))):
        copy = pltpu.make_async_copy(source.at[:, pl.ds(2 * units, units)], target, weight_sems.at[index])
        copy.start()
        loads.append(copy)
    partners = row_partners()
    meet(near(reps) + [{"row": partner} for partner in partners])
    low[...] = dpair_ref[:, 0].astype(BF)
    push = pltpu.make_async_remote_copy(
        src_ref=low,
        dst_ref=taken,
        send_sem=push_send,
        recv_sem=push_recv,
        device_id={"row": lax.rem(row + rows - 1, rows)},
        device_id_type=MESH,
    )

    @pl.when(row > 0)
    def _():
        push.start()

    for copy in loads:
        copy.wait()

    def partial(step, chip, put):
        for part in range(parts):
            value = dot(hidden_one_ref[chip], weight_one[part], 1, 0)
            put(pl.ds(part * width, width), value + dot(hidden_two_ref[chip], weight_two[part], 1, 0))

    def finish(piece, rows_of, value):
        result_ref[rows_of, :] = (middle_ref[rows_of, :] + value).astype(BF)

    def turn_back():
        @pl.when(row == rows - 1)
        def _():
            taken[...] = jnp.zeros_like(taken)

        @pl.when(row < rows - 1)
        def _():
            push.wait_recv()

        chips, height, _ = proj_ref.shape
        for chip in range(chips):
            places = pl.ds(chip * height, height)
            pair_rows = pl.ds(chip % 2 * height, height)
            pair = dpair_ref[chip // 2, 1, pair_rows, :] + taken[chip // 2, pair_rows, :].astype(F32)
            grad = jnp.concatenate([dquery_ref[places, :], pair], axis=1)
            proj_ref[chip] = rotate(grad, cosine_ref[places, :], -sine_ref[places, :]).astype(BF)

    run_scatter(reps, partial, finish, scratch[:SCATTER_REFS], turn_back)

    @pl.when(row > 0)
    def _():
        push.wait_send()


def lift(hidden_one, hidden_two, weight_one, weight_two, middle, dquery, dpairs, cosine, sine, reps):
    sub = middle.shape[0]
    parts, rows, width = weight_one.shape
    tokens, heads = dquery.shape
    halves, _, slots, lanes = dpairs.shape
    return pl.pallas_call(
        functools.partial(lift_kernel, reps),
        out_shape=[
            jax.ShapeDtypeStruct((sub, D), BF),
            jax.ShapeDtypeStruct((COLS, tokens // COLS, heads + lanes), BF),
        ],
        in_specs=[VMEM] * 2 + [HBM] * 2 + [VMEM] * 5,
        out_specs=[VMEM] * 2,
        scratch_shapes=scatter_scratch(sub)
        + [pltpu.VMEM((parts, rows // 3, width), BF)] * 2
        + [DMA((2,))]
        + [pltpu.VMEM((halves, slots, lanes), BF)] * 2
        + [DMA, DMA],
        compiler_params=params(7),
        cost_estimate=takes(50),
        name="lift",
    )(hidden_one, hidden_two, weight_one, weight_two, middle, dquery, dpairs, cosine, sine)


PEERS = ("SO", "P", "SP", "Q", "SQ", "D", "SD")


def project_back_kernel(
    reps, proj_ref, weight_ref, source_ref, middle_ref, gains_ref, gain_two_ref, result_in_ref,
    resid_ref, gain_ref, result_ref, *scratch,
):
    stage, *scratch = scratch
    result_home = Home(result_in_ref, scratch[SCATTER_REFS : SCATTER_REFS + HOME_REFS])
    home = Home(stage, scratch[SCATTER_REFS + HOME_REFS : SCATTER_REFS + 2 * HOME_REFS])
    gain_own, gain_rows, gain_plane, row_send, row_recv, plane_send, plane_recv = scratch[SCATTER_REFS + 2 * HOME_REFS :]
    where = plane(reps)
    row = lax.axis_index("row")
    partners = row_partners()
    meet([where[kind][2] for kind in PEERS] + [{"row": partner} for partner in partners])
    for piece in range(PIECES):
        result_home.send(piece)
    gain_own[...] = jnp.zeros_like(gain_own)
    gain_own[1:2, :] = gain_two_ref[0:1, :]

    def partial(step, chip, put):
        for index in range(D // SPAN):
            columns = pl.ds(index * SPAN, SPAN)
            put(columns, dot(proj_ref[chip], weight_ref[columns, :], 1, 1))

    def finish(piece, rows, value):
        back, gain_part = norm_back(value, source_ref[rows, :].astype(F32), gains_ref[0:1, :])
        home.stage[rows, :] = (middle_ref[rows, :] + back).astype(BF)
        home.send(piece)
        gain_own[0:1, :] += gain_part

    run_scatter(reps, partial, finish, scratch[:SCATTER_REFS], result_home.turn)
    width = gain_ref.shape[1]
    copies = []
    for shift, partner in enumerate(partners):
        copy = pltpu.make_async_remote_copy(
            src_ref=gain_own.at[:, tile(partner, width)],
            dst_ref=gain_rows.at[shift],
            send_sem=row_send.at[shift],
            recv_sem=row_recv.at[shift],
            device_id={"row": partner},
            device_id_type=MESH,
        )
        copy.start()
        copies.append(copy)
    home.turn()
    for copy in copies:
        copy.wait()
    total = gain_own[:, tile(row, width)]
    for shift in range(len(partners)):
        total += gain_rows[shift]
    own = where["O"][0] * 2 + where["O"][1]
    gain_plane[own] = total

    def share(index, place):
        return pltpu.make_async_remote_copy(
            src_ref=gain_plane.at[place],
            dst_ref=gain_plane.at[place],
            send_sem=plane_send.at[index],
            recv_sem=plane_recv.at[place],
            device_id=where[PEERS[index]][2],
            device_id_type=MESH,
        )

    for index in range(len(PEERS)):
        share(index, own).start()
    for index, kind in enumerate(PEERS):
        share(index, where[kind][0] * 2 + where[kind][1]).wait_recv()
    total = gain_plane[0]
    for place in range(1, 2 * COLS):
        total += gain_plane[place]
    gain_ref[...] = total
    for index in range(len(PEERS)):
        share(index, own).wait_send()
    result_home.wait()
    result_ref[...] = result_home.home[...]
    home.wait()
    resid_ref[...] = home.home[...]


def project_back(grad_proj, weight, source, grad_middle, gains, gain_two, result, reps, rows):
    sub = source.shape[0]
    width = D // rows
    return pl.pallas_call(
        functools.partial(project_back_kernel, reps),
        out_shape=[
            jax.ShapeDtypeStruct((sub * COLS, width), BF),
            jax.ShapeDtypeStruct((8, width), F32),
            jax.ShapeDtypeStruct((sub * COLS, width), BF),
        ],
        in_specs=[VMEM] * 7,
        out_specs=[VMEM] * 3,
        scratch_shapes=[pltpu.VMEM((sub, D), BF)]
        + scatter_scratch(sub)
        + home_scratch(sub, rows)
        + home_scratch(sub, rows)
        + [
            pltpu.VMEM((8, D), F32),
            pltpu.VMEM((rows - 1, 8, width), F32),
            pltpu.VMEM((2 * COLS, 8, width), F32),
            DMA((rows - 1,)),
            DMA((rows - 1,)),
            DMA((len(PEERS),)),
            DMA((2 * COLS,)),
        ],
        compiler_params=params(8),
        cost_estimate=takes(55),
        name="project_back",
    )(grad_proj, weight, source, grad_middle, gains, gain_two, result)


def adamw(weights, gradient, moment, square, step_rate, decay_rate):
    gradient = gradient.astype(F32)
    moment_new = BETA_ONE * moment + (1.0 - BETA_ONE) * gradient
    square_new = BETA_TWO * square + (1.0 - BETA_TWO) * gradient * gradient
    moment_hat = moment_new / (1.0 - BETA_ONE**STEP)
    square_hat = square_new / (1.0 - BETA_TWO**STEP)
    weights_new = weights - step_rate * (
        moment_hat / (jnp.sqrt(square_hat) + ADAM_EPS) + decay_rate * weights
    )
    return (weights_new, moment_new, square_new)


def local(
    resid_in,
    cotangent,
    seq_lens,
    qkv_weight,
    qkv_moment,
    qkv_square,
    out_weight,
    out_moment,
    out_square,
    gate_weight,
    gate_moment,
    gate_square,
    up_weight,
    up_moment,
    up_square,
    down_weight,
    down_moment,
    down_square,
    norm_gains,
    gain_moment,
    gain_square,
):
    cols, rows, replicas = lax.axis_size("col"), lax.axis_size("row"), lax.axis_size("dp")
    reps = replicas // 2
    half = lax.axis_index("dp") // reps
    row, col = lax.axis_index("row"), lax.axis_index("col")
    chunk = resid_in.shape[0]
    sub = chunk // cols
    blocks = 2 * cols
    plane_tokens = sub * blocks
    head_width = (GROUP + 2) * HD

    qkv_block = half_columns(qkv_weight, reps)
    out_block = tall_block(out_weight, reps)
    split = out_block.shape[1] // 2
    stacked = jnp.concatenate([out_block[:, :split], out_block[:, split:]], axis=0)
    first_w = lax.all_gather(jnp.concatenate([qkv_block, stacked], axis=1), "row", axis=0)
    qkv_w = first_w[:, :, :head_width].reshape(D, head_width)
    heads = out_block.shape[0]
    out_w = jnp.concatenate([first_w[:, :heads, head_width:], first_w[:, heads:, head_width:]], axis=2)
    lengths = both_halves(seq_lens, partner_swap(seq_lens, reps), half, 0)
    ends = jnp.cumsum(lengths, axis=1, dtype=jnp.int32)
    slot = (row * chunk + jnp.arange(chunk, dtype=jnp.int32)).reshape(1, chunk)
    passed = (slot[:, :, None] >= ends[:, None, :]).astype(jnp.int32)
    seq_start = jnp.sum(passed * lengths[:, None, :], axis=2, dtype=jnp.int32)
    usable = slot < ends[:, -1:]
    cosine, sine = rope_tables((slot - seq_start).reshape(plane_tokens))
    low = (jnp.where(usable, seq_start, slot) - (row - 1) * chunk).reshape(blocks, 1, sub)
    firsts = jnp.tile(chunk + jnp.arange(cols, dtype=jnp.int32) * sub, 2)
    bounds = jnp.stack([low[:, 0, 0] // KEYS, (firsts + sub - 1) // KEYS + 1, firsts]).astype(jnp.int32)
    usable_mine = (row * chunk + col * sub + jnp.arange(sub, dtype=jnp.int32)) < jnp.sum(seq_lens)

    padded = jnp.concatenate([norm_gains, jnp.zeros((6, norm_gains.shape[1]), F32)])
    source, normed_own, grad_top, gains = exchange(
        resid_in, cotangent, padded, usable_mine.astype(F32)[:, None], rows
    )
    gate_block = half_columns(gate_weight, reps, source)
    up_block = half_columns(up_weight, reps, source)
    down_block = tall_block(down_weight, reps)
    units = gate_block.shape[1] // SLICES
    slice_w = []
    for index in range(SLICES):
        span = slice(index * units, (index + 1) * units)
        block = jnp.concatenate([gate_block[:, span], up_block[:, span], down_block[span]], axis=0)
        slice_w.append(lax.all_gather(block, "row", axis=0))
    normed_one, grad_top_all, queries, pairs = project(normed_own, grad_top, qkv_w, cosine, sine, reps)
    queries = queries.reshape(plane_tokens, GROUP * HD)
    pairs = pairs.reshape(2, 2 * chunk, 2 * HD)
    attended, log_total = attend(queries, pairs, low, bounds)
    middle, normed_own = mix_out(attended.reshape(cols, 2 * sub, GROUP * HD), out_w, source, gains, reps)

    flat_top = grad_top_all.reshape(plane_tokens, D)

    def slice_grads(normed_all, hidden, ggate, gup):
        flat = normed_all.reshape(plane_tokens, D)
        parts = [
            dot(flat, ggate.reshape(plane_tokens, units), 0, 0).astype(BF).reshape(rows, -1, units),
            dot(flat, gup.reshape(plane_tokens, units), 0, 0).astype(BF).reshape(rows, -1, units),
            row_blocks(dot(hidden.reshape(plane_tokens, units), flat_top, 0, 0).astype(BF), rows),
        ]
        return jnp.concatenate(parts, axis=1)

    normed_two, hidden_one, ggate_one, gup_one = first_slice(normed_own, grad_top_all, slice_w[0], reps)
    grads_one = slice_grads(normed_two, hidden_one, ggate_one, gup_one)
    normed_two, grads_one = lax.optimization_barrier((normed_two, grads_one))
    hidden_two, ggate_two, gup_two, grad_middle, grad_middle_own, gain_grad_two = second_slice(
        normed_two, grad_top_all, ggate_one, gup_one, slice_w[0], slice_w[1], middle, grad_top, gains, reps
    )
    grad_middle_all, grad_attended, grads_two = back_out(
        grad_middle_own, out_w, normed_two, grad_top_all, hidden_two, ggate_two, gup_two, reps
    )
    slice_g = [lax.psum_scatter(part, "row", scatter_dimension=0) for part in (grads_one, grads_two)]
    grad_attended, slice_g[0] = lax.optimization_barrier((grad_attended, slice_g[0]))
    grad_query, grad_pairs = attend_back(
        queries, grad_attended.reshape(plane_tokens, GROUP * HD), pairs, low, log_total, bounds
    )
    result, grad_proj = lift(
        hidden_one, hidden_two, slice_w[0], slice_w[1], middle,
        grad_query, grad_pairs.reshape(2, 2, chunk, 2 * HD), cosine, sine, reps,
    )
    grad_qkv = dot(normed_one.reshape(plane_tokens, D), grad_proj.reshape(plane_tokens, head_width), 0, 0).astype(BF)
    grad_proj, grad_qkv = lax.optimization_barrier((grad_proj, grad_qkv))
    resid_grad, gain_grads, result = project_back(
        grad_proj, qkv_w, source, grad_middle, gains, gain_grad_two, result, reps, rows
    )
    resid_grad = resid_grad.astype(F32)
    attended, slice_g[0] = lax.optimization_barrier((attended, slice_g[0]))
    grad_out = row_blocks(dot(attended, grad_middle_all.reshape(plane_tokens, D), 0, 0).astype(BF), rows)
    grad_out = own_tall(lax.psum_scatter(grad_out, "row", scatter_dimension=0), reps)
    grad_qkv = own_rows(lax.psum_scatter(grad_qkv, "row", scatter_dimension=0, tiled=True), reps)
    wide = sum(part.shape[0] for part in slice_g) // (3 * SLICES)
    grad_gate = own_rows(jnp.concatenate([part[:wide] for part in slice_g], axis=1), reps)
    grad_up = own_rows(jnp.concatenate([part[wide : 2 * wide] for part in slice_g], axis=1), reps)
    grad_down = own_tall(jnp.concatenate([part[2 * wide :] for part in slice_g], axis=0), reps)

    gain_grads = gain_grads[:2]
    if reps > 1:
        gain_grads = lax.psum(gain_grads, "dp", axis_index_groups=rep_groups(reps))
    qkv_set = adamw(qkv_weight, grad_qkv, qkv_moment, qkv_square, RATE_MATRIX, WEIGHT_DECAY)
    out_set = adamw(out_weight, grad_out, out_moment, out_square, RATE_OUTPUT, WEIGHT_DECAY)
    gate_set = adamw(gate_weight, grad_gate, gate_moment, gate_square, RATE_MATRIX, WEIGHT_DECAY)
    up_set = adamw(up_weight, grad_up, up_moment, up_square, RATE_MATRIX, WEIGHT_DECAY)
    down_set = adamw(down_weight, grad_down, down_moment, down_square, RATE_MATRIX, WEIGHT_DECAY)
    gain_set = adamw(norm_gains, gain_grads, gain_moment, gain_square, RATE_GAIN, 0.0)
    return (result, resid_grad, *qkv_set, *out_set, *gate_set, *up_set, *down_set, *gain_set)


def solution(mesh):
    tokens = P(("dp", "col"), "row")
    wide = P(("row", "dp"), "col")
    tall = P(("col", "dp"), "row")
    gain = P(None, "row")
    weights = (wide,) * 3 + (tall,) * 3 + (wide,) * 6 + (tall,) * 3 + (gain,) * 3
    return jax.shard_map(
        local,
        mesh=mesh,
        in_specs=(tokens, tokens, P("dp", None)) + weights,
        out_specs=(tokens, tokens) + weights,
        check_vma=False,
    )
```

```python
import functools

import jax
import jax.numpy as jnp
from jax import lax
from jax.experimental import pallas as pl
from jax.experimental.pallas import tpu as pltpu
from jax.sharding import PartitionSpec as P

D = 2048
FF = 8192
HD = 64
GROUP = 4
LMAX = 1024
STEP = 10
KEYS = 256
SLICES = 2
PIECES = 4
COLS = 4

EPS_NORM = 1e-05
ROPE_BASE = 500000.0
BETA_ONE = 0.9
BETA_TWO = 0.95
ADAM_EPS = 1e-08
WEIGHT_DECAY = 0.1
RATE_MATRIX = 0.05
RATE_OUTPUT = 0.4
RATE_GAIN = 0.8
MASKED = -1e30
SCALE = HD ** (-0.5)

BF = jnp.bfloat16
F32 = jnp.float32


def dot(left, right, left_dim, right_dim):
    return lax.dot_general(
        left, right, (((left_dim,), (right_dim,)), ((), ())), preferred_element_type=F32
    )


def half_groups(reps):
    return [[rep, rep + reps] for rep in range(reps)]


def rep_groups(reps):
    return [[half * reps + rep for rep in range(reps)] for half in range(2)]


def partner_swap(values_in, reps):
    pairs = [pair for rep in range(reps) for pair in ((rep, rep + reps), (rep + reps, rep))]
    return lax.ppermute(values_in, "dp", pairs)


def both_halves(mine, theirs, half, axis):
    first = jnp.where(half == 0, mine, theirs)
    second = jnp.where(half == 0, theirs, mine)
    return jnp.concatenate([first, second], axis=axis)


def half_columns(weight, reps, after=None):
    half = lax.axis_index("dp") // reps
    own, width = weight.shape[0], weight.shape[1] // 2
    low = weight.astype(BF)
    mine = lax.dynamic_slice_in_dim(low, half * width, width, 1)
    theirs = partner_swap(lax.dynamic_slice_in_dim(low, (1 - half) * width, width, 1), reps)
    if after is not None:
        theirs, _ = lax.optimization_barrier((theirs, after))
    both = both_halves(mine, theirs, half, 0)
    if reps > 1:
        both = lax.all_gather(both, "dp", axis=0, axis_index_groups=rep_groups(reps))
        both = both.reshape(reps, 2, own, width).swapaxes(0, 1).reshape(2 * reps * own, width)
    return both


def own_rows(part, reps):
    half = lax.axis_index("dp") // reps
    height = part.shape[0] // 2
    mine = lax.dynamic_slice_in_dim(part, half * height, height, 0)
    theirs = partner_swap(lax.dynamic_slice_in_dim(part, (1 - half) * height, height, 0), reps)
    part = both_halves(mine, theirs, half, 1)
    if reps > 1:
        part = lax.psum_scatter(
            part, "dp", scatter_dimension=0, tiled=True, axis_index_groups=rep_groups(reps)
        )
    return part


def own_slice(part, reps):
    half = lax.axis_index("dp") // reps
    units = part.shape[1]
    split = part.reshape(2, 2, -1, units)
    mine = lax.dynamic_index_in_dim(split, half, 1, False)
    theirs = partner_swap(lax.dynamic_index_in_dim(split, 1 - half, 1, False), reps)
    halves = [jnp.where(half == 0, mine, theirs), jnp.where(half == 0, theirs, mine)]
    if reps > 1:
        halves = [
            lax.psum_scatter(piece, "dp", scatter_dimension=1, tiled=True, axis_index_groups=rep_groups(reps))
            for piece in halves
        ]
    return halves


def tall_block(weight, reps):
    own = weight.astype(BF)
    if reps > 1:
        own = lax.all_gather(own, "dp", axis=0, tiled=True, axis_index_groups=rep_groups(reps))
    return own


def own_tall(part, reps):
    if reps > 1:
        part = lax.psum_scatter(
            part, "dp", scatter_dimension=0, tiled=True, axis_index_groups=rep_groups(reps)
        )
    return part


def row_blocks(matrix, rows):
    return matrix.reshape(matrix.shape[0], rows, -1).swapaxes(0, 1)


def rope_tables(position):
    exponent = jnp.arange(0, HD, 2, dtype=F32) / HD
    freq_table = 1.0 / ROPE_BASE**exponent
    angle = position.astype(F32)[:, None] * freq_table[None, :]
    cosine = jnp.cos(angle)
    sine = jnp.sin(angle)
    return (jnp.concatenate([cosine] * 4, axis=1), jnp.concatenate([-sine, sine, -sine, sine], axis=1))


def rotate(vectors, cosine, sine):
    width = vectors.shape[1]
    lane = lax.broadcasted_iota(jnp.int32, vectors.shape, 1)
    lower = lax.rem(lane, HD) < HD // 2
    turned = jnp.where(
        lower, pltpu.roll(vectors, width - HD // 2, 1), pltpu.roll(vectors, HD // 2, 1)
    )
    copies = width // cosine.shape[1]
    cosine = jnp.concatenate([cosine] * copies, axis=1)
    sine = jnp.concatenate([sine] * copies, axis=1)
    return jnp.where(lane < (GROUP + 1) * HD, vectors * cosine + turned * sine, vectors)


MESH = pl.DeviceIdType.MESH
HBM = pl.BlockSpec(memory_space=pl.ANY)
VMEM = pl.BlockSpec(memory_space=pltpu.VMEM)
DMA = pltpu.SemaphoreType.DMA


def takes(micros):
    return pl.CostEstimate(flops=1, bytes_accessed=int(micros * 3.6e6), transcendentals=0)


def params(collective_id):
    return pltpu.CompilerParams(
        collective_id=collective_id, has_side_effects=True, vmem_limit_bytes=60 * 2**20
    )


def tile(index, width):
    return pl.ds(pl.multiple_of(index * width, width), width)


def plane(reps):
    replica, col = lax.axis_index("dp"), lax.axis_index("col")
    half, rep = lax.div(replica, reps), lax.rem(replica, reps)
    core = lax.rem(col, 2)
    other = col + 1 - 2 * core

    def place(half_of, col_of):
        chip = half_of * (COLS // 2) + lax.div(col_of, 2)
        return (chip, lax.rem(col_of, 2), {"dp": half_of * reps + rep, "col": col_of})

    def turn(value, by, modulus):
        return lax.rem(value + by, modulus)

    return {
        "O": place(half, col),
        "P": place(turn(half, 1 - core, 2), turn(col, 2 * core, COLS)),
        "Q": place(turn(half, core, 2), turn(col, 2 - 2 * core, COLS)),
        "D": place(1 - half, turn(col, 2, COLS)),
        "SO": place(half, other),
        "SP": place(turn(half, core, 2), turn(other, 2 - 2 * core, COLS)),
        "SQ": place(turn(half, 1 - core, 2), turn(other, 2 * core, COLS)),
        "SD": place(1 - half, turn(other, 2, COLS)),
    }


def near(reps):
    where = plane(reps)
    return [where["P"][2], where["Q"][2], where["SO"][2]]


def row_partners():
    rows, row = lax.axis_size("row"), lax.axis_index("row")
    return [lax.rem(row + shift, rows) for shift in range(1, rows)]


def signal(devices):
    barrier = pltpu.get_barrier_semaphore()
    for device in devices:
        pl.semaphore_signal(barrier, inc=1, device_id=device, device_id_type=MESH)


def meet(devices):
    signal(devices)
    pl.semaphore_wait(pltpu.get_barrier_semaphore(), len(devices))


GATHER_KINDS = ("P", "Q", "D", "SO", "SP", "SQ", "SD")


def run_gather(reps, own_ref, held_ref, sems, use):
    send_sems, recv_sems, local_sem = sems
    where = plane(reps)
    sub = own_ref.shape[0]
    height = sub // PIECES

    def spot(kind, piece):
        chip, core, _ = where[kind]
        return held_ref.at[chip, pl.ds(pl.multiple_of(core * sub + piece * height, height), height)]

    def message(kind, piece, source, target, device):
        index = GATHER_KINDS.index(kind)
        return pltpu.make_async_remote_copy(
            src_ref=source,
            dst_ref=target,
            send_sem=send_sems.at[index, piece],
            recv_sem=recv_sems.at[index, piece],
            device_id=device,
            device_id_type=MESH,
        )

    near_p, near_q, sibling = where["P"][2], where["Q"][2], where["SO"][2]
    sent = []

    def send(kind, piece, source, held_by, device):
        copy = message(kind, piece, source, spot(held_by, piece), device)
        copy.start()
        sent.append(copy)

    def arrive(kind, piece):
        message(kind, piece, spot(kind, piece), spot(kind, piece), sibling).wait_recv()

    own_copy = pltpu.make_async_copy(own_ref, held_ref.at[where["O"][0], tile(where["O"][1], sub)], local_sem)
    own_copy.start()
    for piece in range(PIECES):
        source = own_ref.at[pl.ds(piece * height, height)]
        send("P", piece, source, "O", near_p)
        send("Q", piece, source, "O", near_q)
        send("SO", piece, source, "O", sibling)
    own_copy.wait()
    for piece in range(PIECES):
        arrive("SO", piece)
    use(0, where["O"][0])
    for piece in range(PIECES):
        arrive("P", piece)
        send("D", piece, spot("P", piece), "P", near_q)
        send("SP", piece, spot("P", piece), "P", sibling)
    for piece in range(PIECES):
        arrive("Q", piece)
        send("SQ", piece, spot("Q", piece), "Q", sibling)
    for piece in range(PIECES):
        arrive("SQ", piece)
    use(1, where["P"][0])
    for piece in range(PIECES):
        arrive("SP", piece)
    use(2, where["Q"][0])
    for piece in range(PIECES):
        arrive("D", piece)
        send("SD", piece, spot("D", piece), "D", sibling)
    for piece in range(PIECES):
        arrive("SD", piece)
    use(3, where["D"][0])
    for copy in sent:
        copy.wait_send()


def gather_scratch(sub):
    count = len(GATHER_KINDS)
    return [pltpu.VMEM((COLS, 2 * sub, D), BF), DMA((count, PIECES)), DMA((count, PIECES)), DMA]


SCATTER_SWAPS = ("D", "Q", "P", "O")
SCATTER_HOPS = ("D", "Q", "P")


def scatter_order(reps):
    where = plane(reps)
    return [where[kind][0] for kind in SCATTER_SWAPS]


def run_scatter(reps, partial, finish, scratch, meanwhile=None):
    total_ref, give_ref, take_ref, hop_out, hop_in, both_ref, swap_send, swap_recv, hop_send, hop_recv = scratch
    where = plane(reps)
    core = where["O"][1]
    device = {"P": where["P"][2], "Q": where["Q"][2], "D": where["Q"][2]}
    sibling = where["SO"][2]
    sub = total_ref.shape[1]
    height = sub // PIECES
    sibling_kind = {"D": "D", "Q": "P", "P": "Q", "O": "O"}
    sent = []

    def swap(kind):
        index = SCATTER_SWAPS.index(kind)
        return pltpu.make_async_remote_copy(
            src_ref=give_ref.at[index],
            dst_ref=take_ref.at[index],
            send_sem=swap_send.at[index],
            recv_sem=swap_recv.at[index],
            device_id=sibling,
            device_id_type=MESH,
        )

    def hop(kind, piece):
        index = SCATTER_HOPS.index(kind)
        rows = pl.ds(piece * height, height)
        return pltpu.make_async_remote_copy(
            src_ref=hop_out.at[index, rows],
            dst_ref=hop_in.at[index, rows],
            send_sem=hop_send.at[index, piece],
            recv_sem=hop_recv.at[index, piece],
            device_id=device[kind],
            device_id_type=MESH,
        )

    def compute(step, kind):
        mine, theirs = SCATTER_SWAPS.index(kind), SCATTER_SWAPS.index(sibling_kind[kind])

        def put(columns, value):
            both_ref[...] = value
            total_ref[mine, :, columns] = both_ref[tile(core, sub), :]
            give_ref[theirs, :, columns] = both_ref[tile(1 - core, sub), :].astype(BF)

        partial(step, where[kind][0], put)
        copy = swap(sibling_kind[kind])
        copy.start()
        sent.append(copy)

    def settle(kind):
        index = SCATTER_SWAPS.index(kind)
        swap(kind).wait_recv()
        for piece in range(PIECES):
            rows = pl.ds(piece * height, height)
            value = total_ref[index, rows, :] + take_ref[index, rows, :].astype(F32)
            if kind == "P":
                hop("D", piece).wait_recv()
                value += hop_in[SCATTER_HOPS.index("D"), rows, :].astype(F32)
            if kind == "O":
                for source in ("Q", "P"):
                    hop(source, piece).wait_recv()
                    value += hop_in[SCATTER_HOPS.index(source), rows, :].astype(F32)
                finish(piece, rows, value)
            else:
                hop_out[SCATTER_HOPS.index(kind), rows, :] = value.astype(BF)
                copy = hop(kind, piece)
                copy.start()
                sent.append(copy)

    compute(0, "D")
    compute(1, "Q")
    settle("D")
    compute(2, "P")
    settle("Q")
    compute(3, "O")
    if meanwhile is not None:
        meanwhile()
    settle("P")
    settle("O")
    for copy in sent:
        copy.wait_send()


SPAN = 512


def scatter_scratch(sub):
    return [
        pltpu.VMEM((4, sub, D), F32),
        pltpu.VMEM((4, sub, D), BF),
        pltpu.VMEM((4, sub, D), BF),
        pltpu.VMEM((3, sub, D), BF),
        pltpu.VMEM((3, sub, D), BF),
        pltpu.VMEM((2 * sub, SPAN), F32),
        DMA((4,)),
        DMA((4,)),
        DMA((3, PIECES)),
        DMA((3, PIECES)),
    ]


SCATTER_REFS = 10


def col_partners():
    cols, col = lax.axis_size("col"), lax.axis_index("col")
    return [lax.rem(col + shift, cols) for shift in range(1, cols)]


def home_scratch(sub, rows):
    return [
        pltpu.VMEM((rows, sub, D // rows), BF),
        pltpu.VMEM((sub * COLS, D // rows), BF),
        DMA((rows - 1, PIECES)),
        DMA((rows - 1, PIECES)),
        DMA((COLS - 1,)),
        DMA((COLS - 1,)),
    ]


HOME_REFS = 6


class Home:
    def __init__(self, stage, scratch):
        self.stage = stage
        self.mid, self.home, self.row_send, self.row_recv, self.col_send, self.col_recv = scratch
        self.row, self.col = lax.axis_index("row"), lax.axis_index("col")
        self.sub = stage.shape[0]
        self.height, self.width = self.sub // PIECES, self.mid.shape[2]
        self.sent = []

    def row_copies(self, piece):
        rows = pl.ds(piece * self.height, self.height)
        return [
            pltpu.make_async_remote_copy(
                src_ref=self.stage.at[rows, tile(partner, self.width)],
                dst_ref=self.mid.at[self.row, rows],
                send_sem=self.row_send.at[shift, piece],
                recv_sem=self.row_recv.at[shift, piece],
                device_id={"row": partner},
                device_id_type=MESH,
            )
            for shift, partner in enumerate(row_partners())
        ]

    def send(self, piece):
        rows = pl.ds(piece * self.height, self.height)
        copies = self.row_copies(piece)
        for copy in copies:
            copy.start()
        self.sent += copies
        self.mid[self.row, rows, :] = self.stage[rows, tile(self.row, self.width)]

    def turn(self):
        for copy in self.sent:
            copy.wait()
        self.sent = []
        for shift, partner in enumerate(col_partners()):
            copy = pltpu.make_async_remote_copy(
                src_ref=self.mid.at[partner],
                dst_ref=self.home.at[tile(self.col, self.sub)],
                send_sem=self.col_send.at[shift],
                recv_sem=self.col_recv.at[shift],
                device_id={"col": partner},
                device_id_type=MESH,
            )
            copy.start()
            self.sent.append(copy)
        self.home[tile(self.col, self.sub), :] = self.mid[self.col]

    def wait(self):
        for copy in self.sent:
            copy.wait()


def head_rows(block):
    turned = block.astype(F32).T
    return [turned[head * HD : (head + 1) * HD].astype(BF) for head in range(GROUP)]


def allowed_entries(key_block, low_ref, query_first):
    tokens = low_ref.shape[-1]
    key_slot = key_block * KEYS + lax.broadcasted_iota(jnp.int32, (KEYS, tokens), 0)
    query_slot = query_first + lax.broadcasted_iota(jnp.int32, (KEYS, tokens), 1)
    return (key_slot >= low_ref[...]) & (key_slot <= query_slot)


def key_rows(block):
    return pl.ds(pl.multiple_of(block * KEYS, KEYS), KEYS)


def attend_kernel(bounds, query_ref, pair_ref, low_ref, out_ref, log_ref, score_ref, mix_ref):
    step = pl.program_id(1)
    place = pl.program_id(0) * pl.num_programs(1) + step
    first, last, query_first = bounds[0, place], bounds[1, place], bounds[2, place]
    tokens = query_ref.shape[0]
    blank = jnp.zeros((HD, tokens), BF)
    queries = [jnp.concatenate([rows, blank], axis=0) for rows in head_rows(query_ref[...])]

    def score_block(block, tops):
        pairs = pair_ref[key_rows(block), :]
        allowed = allowed_entries(block, low_ref, query_first)
        new_tops = []
        for head in range(GROUP):
            scores = jnp.where(allowed, dot(pairs, queries[head], 1, 0), MASKED)
            score_ref[head, key_rows(block - first), :] = scores
            new_tops.append(jnp.maximum(tops[head], jnp.max(scores, axis=0, keepdims=True)))
        return tuple(new_tops)

    start = tuple(jnp.full((1, tokens), MASKED, F32) for _ in range(GROUP))
    tops = lax.fori_loop(first, last, score_block, start)
    mix_ref[...] = jnp.zeros_like(mix_ref)

    def mix_block(block, totals):
        pairs = pair_ref[key_rows(block), :]
        new_totals = []
        for head in range(GROUP):
            terms = jnp.exp(score_ref[head, key_rows(block - first), :] - tops[head])
            new_totals.append(totals[head] + jnp.sum(terms, axis=0, keepdims=True))
            mix_ref[head] += dot(pairs, terms.astype(BF), 0, 0)
        return tuple(new_totals)

    start = tuple(jnp.zeros((1, tokens), F32) for _ in range(GROUP))
    totals = lax.fori_loop(first, last, mix_block, start)
    mixed = jnp.concatenate(
        [mix_ref[head, HD:, :] / totals[head] for head in range(GROUP)], axis=0
    )
    out_ref[...] = mixed.T.astype(BF)
    for head in range(GROUP):
        log_ref[head : head + 1, :] = tops[head] + jnp.log(totals[head])


def attend_back_kernel(
    bounds, query_ref, grad_ref, pair_ref, low_ref, log_ref, dquery_ref, dpair_ref, prob_ref, dprob_ref, dmix_ref
):
    step = pl.program_id(1)
    place = pl.program_id(0) * pl.num_programs(1) + step
    first, last, query_first = bounds[0, place], bounds[1, place], bounds[2, place]
    tokens = query_ref.shape[0]
    blank = jnp.zeros((HD, tokens), BF)
    queries = [jnp.concatenate([rows, blank], axis=0) for rows in head_rows(query_ref[...])]
    grads = [jnp.concatenate([blank, rows], axis=0) for rows in head_rows(grad_ref[...])]

    @pl.when(step == 0)
    def _():
        dpair_ref[...] = jnp.zeros_like(dpair_ref)

    def prob_block(block, inners):
        pairs = pair_ref[key_rows(block), :]
        allowed = allowed_entries(block, low_ref, query_first)
        new_inners = []
        for head in range(GROUP):
            scores = dot(pairs, queries[head], 1, 0)
            probs = jnp.where(allowed, jnp.exp(scores - log_ref[head : head + 1, :]), 0.0)
            dprobs = dot(pairs, grads[head], 1, 0)
            prob_ref[head, key_rows(block - first), :] = probs
            dprob_ref[head, key_rows(block - first), :] = dprobs
            new_inners.append(inners[head] + jnp.sum(probs * dprobs, axis=0, keepdims=True))
        return tuple(new_inners)

    start = tuple(jnp.zeros((1, tokens), F32) for _ in range(GROUP))
    inners = lax.fori_loop(first, last, prob_block, start)
    dmix_ref[...] = jnp.zeros_like(dmix_ref)
    all_queries = jnp.concatenate(queries, axis=1)
    all_grads = jnp.concatenate(grads, axis=1)

    def back_block(block, carry):
        rows = key_rows(block)
        pairs = pair_ref[rows, :]
        all_probs, all_scores = [], []
        for head in range(GROUP):
            probs = prob_ref[head, key_rows(block - first), :]
            dprobs = dprob_ref[head, key_rows(block - first), :]
            dscores = (probs * (dprobs - inners[head])).astype(BF)
            dmix_ref[head] += dot(pairs, dscores, 0, 0)
            all_probs.append(probs.astype(BF))
            all_scores.append(dscores)
        dpair_ref[rows, :] += dot(jnp.concatenate(all_scores, axis=1), all_queries, 1, 1) + dot(
            jnp.concatenate(all_probs, axis=1), all_grads, 1, 1
        )
        return carry

    lax.fori_loop(first, last, back_block, 0)
    dquery = jnp.concatenate([dmix_ref[head, :HD, :] for head in range(GROUP)], axis=0)
    dquery_ref[...] = dquery.T * SCALE


def attend(queries, pairs, low, bounds):
    tokens, width = queries.shape
    replicas, slots, _ = pairs.shape
    rows = low.shape[2]
    blocks = low.shape[0] // replicas
    span = LMAX + KEYS
    return pl.pallas_call(
        attend_kernel,
        grid_spec=pltpu.PrefetchScalarGridSpec(
            num_scalar_prefetch=1,
            grid=(replicas, blocks),
            in_specs=[
                pl.BlockSpec((rows, GROUP * HD), lambda rep, block, _: (rep * blocks + block, 0)),
                pl.BlockSpec((None, slots, 2 * HD), lambda rep, block, _: (rep, 0, 0)),
                pl.BlockSpec((None, 1, rows), lambda rep, block, _: (rep * blocks + block, 0, 0)),
            ],
            out_specs=[
                pl.BlockSpec((rows, GROUP * HD), lambda rep, block, _: (rep * blocks + block, 0)),
                pl.BlockSpec((None, None, GROUP, rows), lambda rep, block, _: (rep, block, 0, 0)),
            ],
            scratch_shapes=[
                pltpu.VMEM((GROUP, span, rows), F32),
                pltpu.VMEM((GROUP, 2 * HD, rows), F32),
            ],
        ),
        out_shape=[
            jax.ShapeDtypeStruct((tokens, width), BF),
            jax.ShapeDtypeStruct((replicas, blocks, GROUP, rows), F32),
        ],
        compiler_params=pltpu.CompilerParams(vmem_limit_bytes=48 * 2**20),
        cost_estimate=takes(14),
        name="attend",
    )(bounds, queries, pairs, low)


def attend_back(queries, grads, pairs, low, log_total, bounds):
    tokens, width = queries.shape
    replicas, slots, _ = pairs.shape
    rows = low.shape[2]
    blocks = low.shape[0] // replicas
    span = LMAX + KEYS
    return pl.pallas_call(
        attend_back_kernel,
        grid_spec=pltpu.PrefetchScalarGridSpec(
            num_scalar_prefetch=1,
            grid=(replicas, blocks),
            in_specs=[
                pl.BlockSpec((rows, GROUP * HD), lambda rep, block, _: (rep * blocks + block, 0)),
                pl.BlockSpec((rows, GROUP * HD), lambda rep, block, _: (rep * blocks + block, 0)),
                pl.BlockSpec((None, slots, 2 * HD), lambda rep, block, _: (rep, 0, 0)),
                pl.BlockSpec((None, 1, rows), lambda rep, block, _: (rep * blocks + block, 0, 0)),
                pl.BlockSpec((None, None, GROUP, rows), lambda rep, block, _: (rep, block, 0, 0)),
            ],
            out_specs=[
                pl.BlockSpec((rows, GROUP * HD), lambda rep, block, _: (rep * blocks + block, 0)),
                pl.BlockSpec((None, slots, 2 * HD), lambda rep, block, _: (rep, 0, 0)),
            ],
            scratch_shapes=[
                pltpu.VMEM((GROUP, span, rows), F32),
                pltpu.VMEM((GROUP, span, rows), F32),
                pltpu.VMEM((GROUP, 2 * HD, rows), F32),
            ],
        ),
        out_shape=[
            jax.ShapeDtypeStruct((tokens, width), F32),
            jax.ShapeDtypeStruct((replicas, slots, 2 * HD), F32),
        ],
        compiler_params=pltpu.CompilerParams(vmem_limit_bytes=48 * 2**20),
        cost_estimate=takes(23),
        name="attend_back",
    )(bounds, queries, grads, pairs, low, log_total)


def norm_of(vectors):
    scaling = lax.rsqrt(jnp.mean(vectors * vectors, axis=1, keepdims=True) + EPS_NORM)
    return vectors * scaling, scaling


def norm_back(value, vectors, gain):
    unit, scaling = norm_of(vectors)
    weighted = value * gain
    inner = jnp.mean(weighted * unit, axis=1, keepdims=True)
    return scaling * (weighted - unit * inner), jnp.sum(value * unit, axis=0, keepdims=True)


def exchange_kernel(
    token_ref, top_ref, gain_ref, usable_ref, source_ref, normed_ref, grad_top_ref, gains_ref,
    held, held_top, mid, mid_top, held_gains, col_send, col_recv, row_send, row_recv, gain_send, gain_recv, local_sems,
):
    row, col = lax.axis_index("row"), lax.axis_index("col")
    sub, width = held.shape[0], token_ref.shape[1]
    row_of = row_partners()
    col_of = col_partners()
    meet([{"row": partner} for partner in row_of] + [{"col": partner} for partner in col_of])
    own_cols = tile(row, width)

    def run(copies):
        for copy in copies:
            copy.start()
        return copies

    def finish(copies):
        for copy in copies:
            copy.wait()

    def remote(source, target, send_sem, recv_sem, device):
        return pltpu.make_async_remote_copy(
            src_ref=source, dst_ref=target, send_sem=send_sem, recv_sem=recv_sem, device_id=device, device_id_type=MESH
        )

    def to_columns(array, source, target):
        return run(
            [
                remote(
                    source.at[tile(partner, sub)], target.at[col],
                    col_send.at[array, shift], col_recv.at[array, shift], {"col": partner},
                )
                for shift, partner in enumerate(col_of)
            ]
            + [pltpu.make_async_copy(source.at[tile(col, sub)], target.at[col], local_sems.at[array, 0])]
        )

    def to_rows(array, source, target):
        return run(
            [
                remote(
                    source.at[partner], target.at[:, own_cols],
                    row_send.at[array, shift], row_recv.at[array, shift], {"row": partner},
                )
                for shift, partner in enumerate(row_of)
            ]
            + [pltpu.make_async_copy(source.at[row], target.at[:, own_cols], local_sems.at[array, 1])]
        )

    tokens = to_columns(0, token_ref, mid)
    gains = run(
        [
            remote(gain_ref, held_gains.at[:, own_cols], gain_send.at[shift], gain_recv.at[shift], {"row": partner})
            for shift, partner in enumerate(row_of)
        ]
        + [pltpu.make_async_copy(gain_ref, held_gains.at[:, own_cols], local_sems.at[2, 0])]
    )
    tops = to_columns(1, top_ref, mid_top)
    finish(tokens)
    tokens = to_rows(0, mid, held)
    finish(tops)
    tops = to_rows(1, mid_top, held_top)
    finish(gains)
    finish(tokens)
    source_ref[...] = held[...]
    gains_ref[...] = held_gains[...]
    unit, _ = norm_of(held[...].astype(F32))
    normed_ref[...] = (unit * held_gains[0:1, :]).astype(BF)
    finish(tops)
    grad_top_ref[...] = (held_top[...].astype(F32) * usable_ref[...]).astype(BF)


def exchange(tokens, top, gains, usable, rows):
    sub, width = tokens.shape[0] // COLS, tokens.shape[1]
    block = jax.ShapeDtypeStruct((sub, rows * width), BF)
    return pl.pallas_call(
        exchange_kernel,
        out_shape=[block, block, block, jax.ShapeDtypeStruct((gains.shape[0], rows * width), F32)],
        in_specs=[VMEM] * 4,
        out_specs=[VMEM] * 4,
        scratch_shapes=[pltpu.VMEM((sub, rows * width), BF)] * 2
        + [pltpu.VMEM((COLS, sub, width), BF)] * 2
        + [
            pltpu.VMEM((gains.shape[0], rows * width), F32),
            DMA((2, COLS - 1)),
            DMA((2, COLS - 1)),
            DMA((2, rows - 1)),
            DMA((2, rows - 1)),
            DMA((rows - 1,)),
            DMA((rows - 1,)),
            DMA((3, 2)),
        ],
        compiler_params=params(1),
        cost_estimate=takes(65),
        name="exchange",
    )(tokens, top, gains, usable)


def project_kernel(
    reps, own_ref, top_ref, weight_ref, cosine_ref, sine_ref,
    all_ref, top_all_ref, query_ref, pair_ref,
    held, send_sems, recv_sems, local_sem, top_held, top_send, top_recv, top_local,
    queries, pairs, halo, out_sems, pair_sems, halo_sems, pair_send, pair_recv,
):
    row, rows = lax.axis_index("row"), lax.axis_size("row")
    meet(near(reps) + [{"row": partner} for partner in row_partners()])
    sub = own_ref.shape[0]
    copies, chips = [], []
    has_next, has_last = row < rows - 1, row > 0

    @pl.when(row == 0)
    def _():
        halo[...] = jnp.zeros_like(halo)

    def out(source, target, sem):
        copy = pltpu.make_async_copy(source, target, sem)
        copy.start()
        copies.append(copy)

    def push(step, chip):
        return pltpu.make_async_remote_copy(
            src_ref=pairs.at[chip],
            dst_ref=halo.at[chip],
            send_sem=pair_send.at[step],
            recv_sem=pair_recv.at[step],
            device_id={"row": lax.rem(row + 1, rows)},
            device_id_type=MESH,
        )

    def use(step, chip):
        chips.append(chip)
        out(held.at[chip], all_ref.at[chip], out_sems.at[step])
        places = tile(chip, 2 * sub)
        turned = rotate(dot(held[chip], weight_ref[...], 1, 0), cosine_ref[places, :], sine_ref[places, :])
        queries[chip] = (turned[:, : GROUP * HD] * SCALE).astype(BF)
        out(queries.at[chip], query_ref.at[chip], out_sems.at[COLS + step])
        pairs[chip] = turned[:, GROUP * HD :].astype(BF)
        out(pairs.at[chip], pair_ref.at[lax.div(chip, 2), 1, lax.rem(chip, 2)], pair_sems.at[step])

        @pl.when(has_next)
        def _():
            push(step, chip).start()

    run_gather(reps, own_ref, held, (send_sems, recv_sems, local_sem), use)

    def use_top(step, chip):
        out(top_held.at[chip], top_all_ref.at[chip], out_sems.at[2 * COLS + step])

    run_gather(reps, top_ref, top_held, (top_send, top_recv, top_local), use_top)
    for step, chip in enumerate(chips):

        @pl.when(has_next)
        def _():
            push(step, chip).wait_send()

        @pl.when(has_last)
        def _():
            push(step, chip).wait_recv()

    for chip in range(COLS):
        out(halo.at[chip], pair_ref.at[chip // 2, 0, chip % 2], halo_sems.at[chip])
    for copy in copies:
        copy.wait()


def project(normed_own, top_own, weight, cosine, sine, reps):
    sub = normed_own.shape[0]
    return pl.pallas_call(
        functools.partial(project_kernel, reps),
        out_shape=[
            jax.ShapeDtypeStruct((COLS, 2 * sub, D), BF),
            jax.ShapeDtypeStruct((COLS, 2 * sub, D), BF),
            jax.ShapeDtypeStruct((COLS, 2 * sub, GROUP * HD), BF),
            jax.ShapeDtypeStruct((2, 2, COLS // 2, 2 * sub, 2 * HD), BF),
        ],
        in_specs=[VMEM] * 5,
        out_specs=[HBM] * 4,
        scratch_shapes=gather_scratch(sub)
        + gather_scratch(sub)
        + [
            pltpu.VMEM((COLS, 2 * sub, GROUP * HD), BF),
            pltpu.VMEM((COLS, 2 * sub, 2 * HD), BF),
            pltpu.VMEM((COLS, 2 * sub, 2 * HD), BF),
            DMA((3 * COLS,)),
            DMA((COLS,)),
            DMA((COLS,)),
            DMA((COLS,)),
            DMA((COLS,)),
        ],
        compiler_params=params(2),
        cost_estimate=takes(75),
        name="project",
    )(normed_own, top_own, weight, cosine, sine)


def mix_out_kernel(reps, attended_ref, weight_ref, source_ref, gains_ref, middle_ref, normed_ref, *scratch):
    meet(near(reps))
    parts, _, width = weight_ref.shape

    def partial(step, chip, put):
        for part in range(parts):
            put(pl.ds(part * width, width), dot(attended_ref[chip], weight_ref[part], 1, 0))

    def finish(piece, rows, value):
        middle = source_ref[rows, :].astype(F32) + value
        middle_ref[rows, :] = middle
        normed_ref[rows, :] = (norm_of(middle)[0] * gains_ref[1:2, :]).astype(BF)

    run_scatter(reps, partial, finish, scratch)


def mix_out(attended, weight, source, gains, reps):
    sub = source.shape[0]
    return pl.pallas_call(
        functools.partial(mix_out_kernel, reps),
        out_shape=[jax.ShapeDtypeStruct((sub, D), F32), jax.ShapeDtypeStruct((sub, D), BF)],
        in_specs=[VMEM] * 4,
        out_specs=[VMEM] * 2,
        scratch_shapes=scatter_scratch(sub),
        compiler_params=params(3),
        cost_estimate=takes(44),
        name="mix_out",
    )(attended, weight, source, gains)


def gated(tokens, top, weight_ref, put):
    parts, rows, width = weight_ref.shape
    units, span = rows // 3, 256

    def one_tile(index, carry):
        columns = tile(index, span)
        gate_w = weight_ref[:, :units, columns].reshape(D, span)
        up_w = weight_ref[:, units : 2 * units, columns].reshape(D, span)
        gate = dot(tokens, gate_w, 1, 0)
        up = dot(tokens, up_w, 1, 0)
        down_rows = pl.ds(pl.multiple_of(2 * units + index * span, span), span)
        grad = dot(top[:, :width], weight_ref[0, down_rows, :], 1, 1)
        for part in range(1, parts):
            grad += dot(top[:, part * width : (part + 1) * width], weight_ref[part, down_rows, :], 1, 1)
        sigma = 1.0 / (1.0 + jnp.exp(-gate))
        active = gate * sigma
        put(
            columns,
            (active * up).astype(BF),
            (grad * up * sigma * (1.0 + gate * (1.0 - sigma))).astype(BF),
            (grad * active).astype(BF),
        )
        return carry

    lax.fori_loop(0, units // span, one_tile, 0)


def first_slice_kernel(
    reps, own_ref, top_ref, weight_ref, all_ref, hidden_ref, ggate_ref, gup_ref,
    held, send_sems, recv_sems, local_sem, tops, hiddens, ggates, gups, top_sems, out_sems,
):
    meet(near(reps))
    where = plane(reps)
    order = [where[kind][0] for kind in ("O", "P", "Q", "D")]
    loads = [pltpu.make_async_copy(top_ref.at[chip], tops.at[chip], top_sems.at[step]) for step, chip in enumerate(order)]
    for copy in loads:
        copy.start()
    copies = []

    def use(step, chip):
        def out(source, target, index):
            copy = pltpu.make_async_copy(source.at[chip], target.at[chip], out_sems.at[index, step])
            copy.start()
            copies.append(copy)

        out(held, all_ref, 0)
        loads[step].wait()

        def put(columns, hidden, ggate, gup):
            hiddens[chip, :, columns] = hidden
            ggates[chip, :, columns] = ggate
            gups[chip, :, columns] = gup

        gated(held[chip], tops[chip], weight_ref, put)
        out(hiddens, hidden_ref, 1)
        out(ggates, ggate_ref, 2)
        out(gups, gup_ref, 3)

    run_gather(reps, own_ref, held, (send_sems, recv_sems, local_sem), use)
    for copy in copies:
        copy.wait()


def first_slice(normed_own, top_all, weight, reps):
    sub = normed_own.shape[0]
    units = weight.shape[1] // 3
    piece = jax.ShapeDtypeStruct((COLS, 2 * sub, units), BF)
    return pl.pallas_call(
        functools.partial(first_slice_kernel, reps),
        out_shape=[jax.ShapeDtypeStruct((COLS, 2 * sub, D), BF)] + [piece] * 3,
        in_specs=[VMEM, HBM, VMEM],
        out_specs=[HBM] * 4,
        scratch_shapes=gather_scratch(sub)
        + [pltpu.VMEM((COLS, 2 * sub, D), BF)]
        + [pltpu.VMEM((COLS, 2 * sub, units), BF)] * 3
        + [DMA((COLS,)), DMA((4, COLS))],
        compiler_params=params(4),
        cost_estimate=takes(50),
        name="first_slice",
    )(normed_own, top_all, weight)


def second_slice_kernel(
    reps, token_ref, top_ref, ggate_one_ref, gup_one_ref, weight_one_ref, weight_ref, middle_ref, own_top_ref, gains_ref,
    hidden_ref, ggate_ref, gup_ref, grad_ref, low_ref, gain_ref, *scratch,
):
    tokens, tops, ggate_ones, gup_ones, weight_one, hiddens, ggates, gups, in_sems, out_sems, weight_sem = scratch[SCATTER_REFS:]
    meet(near(reps))
    order = scatter_order(reps)
    parts, rows, width = weight_ref.shape
    units = rows // 3
    loads, copies = {}, []
    sources = ((token_ref, tokens), (top_ref, tops), (ggate_one_ref, ggate_ones), (gup_one_ref, gup_ones))

    def load(step):
        loads[step] = []
        for index, (source, target) in enumerate(sources):
            copy = pltpu.make_async_copy(source.at[order[step]], target.at[step % 2], in_sems.at[index, step % 2])
            copy.start()
            loads[step].append(copy)

    load(0)
    weight_copy = pltpu.make_async_copy(weight_one_ref.at[:, pl.ds(0, 2 * units)], weight_one, weight_sem)
    weight_copy.start()
    gain_ref[...] = jnp.zeros_like(gain_ref)

    def partial(step, chip, put):
        slot = step % 2
        for copy in loads[step]:
            copy.wait()
        if step < 3:
            load(step + 1)

        def keep(columns, hidden, ggate, gup):
            hiddens[chip, :, columns] = hidden
            ggates[chip, :, columns] = ggate
            gups[chip, :, columns] = gup

        gated(tokens[slot], tops[slot], weight_ref, keep)
        for index, (source, target) in enumerate(((hiddens, hidden_ref), (ggates, ggate_ref), (gups, gup_ref))):
            copy = pltpu.make_async_copy(source.at[chip], target.at[chip], out_sems.at[index, step])
            copy.start()
            copies.append(copy)
        if step == 0:
            weight_copy.wait()
        for part in range(parts):
            value = dot(ggates[chip], weight_ref[part, :units, :], 1, 1)
            value += dot(gups[chip], weight_ref[part, units : 2 * units, :], 1, 1)
            value += dot(ggate_ones[slot], weight_one[part, :units, :], 1, 1)
            value += dot(gup_ones[slot], weight_one[part, units:, :], 1, 1)
            put(pl.ds(part * width, width), value)

    def finish(piece, rows_of, value):
        back, gain_part = norm_back(value, middle_ref[rows_of, :], gains_ref[1:2, :])
        grad = own_top_ref[rows_of, :].astype(F32) + back
        grad_ref[rows_of, :] = grad
        low_ref[rows_of, :] = grad.astype(BF)
        gain_ref[0:1, :] += gain_part

    run_scatter(reps, partial, finish, scratch[:SCATTER_REFS])
    for copy in copies:
        copy.wait()


def second_slice(normed_all, top_all, ggate_one, gup_one, weight_one, weight, middle, own_top, gains, reps):
    sub = middle.shape[0]
    parts, rows, width = weight.shape
    units = rows // 3
    piece = jax.ShapeDtypeStruct((COLS, 2 * sub, units), BF)
    return pl.pallas_call(
        functools.partial(second_slice_kernel, reps),
        out_shape=[piece] * 3
        + [
            jax.ShapeDtypeStruct((sub, D), F32),
            jax.ShapeDtypeStruct((sub, D), BF),
            jax.ShapeDtypeStruct((8, D), F32),
        ],
        in_specs=[HBM] * 5 + [VMEM] * 4,
        out_specs=[HBM] * 3 + [VMEM] * 3,
        scratch_shapes=scatter_scratch(sub)
        + [pltpu.VMEM((2, 2 * sub, D), BF)] * 2
        + [pltpu.VMEM((2, 2 * sub, units), BF)] * 2
        + [pltpu.VMEM((parts, 2 * units, width), BF)]
        + [pltpu.VMEM((COLS, 2 * sub, units), BF)] * 3
        + [DMA((4, 2)), DMA((3, COLS)), DMA],
        compiler_params=params(5),
        cost_estimate=takes(65),
        name="second_slice",
    )(normed_all, top_all, ggate_one, gup_one, weight_one, weight, middle, own_top, gains)


def slice_grads_kernel(token_ref, top_ref, hidden_ref, ggate_ref, gup_ref, out_ref):
    units = hidden_ref.shape[1]
    tokens, width = hidden_ref.shape[0], token_ref.shape[2]
    features = token_ref[...].reshape(tokens, width)
    out_ref[:units] = dot(features, ggate_ref[...], 0, 0).astype(BF)
    out_ref[units : 2 * units] = dot(features, gup_ref[...], 0, 0).astype(BF)
    out_ref[2 * units :] = dot(hidden_ref[...], top_ref[...].reshape(tokens, width), 0, 0).astype(BF)


def slice_grads(normed_all, top_all, hidden, ggate, gup, rows):
    chips, height, units = hidden.shape
    width = D // rows
    flat = [array.reshape(chips * height, units) for array in (hidden, ggate, gup)]
    block = pl.BlockSpec((chips, height, width), lambda part: (0, 0, part))
    whole = pl.BlockSpec((chips * height, units), lambda part: (0, 0))
    return pl.pallas_call(
        slice_grads_kernel,
        grid=(rows,),
        out_shape=jax.ShapeDtypeStruct((rows, 3 * units, width), BF),
        in_specs=[block, block, whole, whole, whole],
        out_specs=pl.BlockSpec((None, 3 * units, width), lambda part: (part, 0, 0)),
        compiler_params=pltpu.CompilerParams(vmem_limit_bytes=48 * 2**20),
        cost_estimate=takes(20),
        name="slice_grads",
    )(normed_all, top_all, *flat)


def back_out_kernel(
    reps, own_ref, weight_ref, token_ref, top_ref, hidden_ref, ggate_ref, gup_ref, attended_ref, grad_ref, slice_ref,
    held, send_sems, recv_sems, local_sem, grads, out_sems, tokens, tops, slices, in_sems, slice_sems, outs, out_low, tail_sem,
):
    meet(near(reps))
    parts, _, width = weight_ref.shape
    units = hidden_ref.shape[1]
    chips, height = token_ref.shape[:2]
    copies, loads, stores = [], {}, {}

    def load(part):
        loads[part] = []
        columns = pl.ds(part * width, width)
        for index, (source, target) in enumerate(((token_ref, tokens), (top_ref, tops))):
            copy = pltpu.make_async_copy(source.at[:, :, columns], target.at[part % 2], in_sems.at[index, part % 2])
            copy.start()
            loads[part].append(copy)

    load(0)

    def slice_grads(part):
        slot = part % 2
        for copy in loads[part]:
            copy.wait()
        if part < parts - 1:
            load(part + 1)
        if part >= 2:
            stores[part - 2].wait()
        features = tokens[slot].reshape(chips * height, width)
        slices[slot, :units] = dot(features, ggate_ref[...], 0, 0).astype(BF)
        slices[slot, units : 2 * units] = dot(features, gup_ref[...], 0, 0).astype(BF)
        slices[slot, 2 * units :] = dot(hidden_ref[...], tops[slot].reshape(chips * height, width), 0, 0).astype(BF)
        stores[part] = pltpu.make_async_copy(
            slices.at[slot], slice_ref.at[part, pl.ds(0, 3 * units)], slice_sems.at[slot]
        )
        stores[part].start()

    def use(step, chip):
        def out(source, target, index):
            copy = pltpu.make_async_copy(source.at[chip], target.at[chip], out_sems.at[index, step])
            copy.start()
            copies.append(copy)

        for part in range(parts):
            columns = pl.ds(part * width, width)
            value = dot(attended_ref[chip], held[chip, :, columns], 0, 0)
            outs[:, columns] = value if step == 0 else outs[:, columns] + value
        total = dot(held[chip, :, :width], weight_ref[0], 1, 1)
        for part in range(1, parts):
            total += dot(held[chip, :, part * width : (part + 1) * width], weight_ref[part], 1, 1)
        grads[chip] = total.astype(BF)
        out(grads, grad_ref, 0)
        slice_grads(step)

    run_gather(reps, own_ref, held, (send_sems, recv_sems, local_sem), use)
    for part in range(parts):
        out_low[part] = outs[:, part * width : (part + 1) * width].astype(BF)
    tail = pltpu.make_async_copy(out_low, slice_ref.at[:, pl.ds(3 * units, outs.shape[0])], tail_sem)
    tail.start()
    for copy in copies + [stores[parts - 2], stores[parts - 1], tail]:
        copy.wait()


def back_out(grad_own, weight, normed_all, top_all, hidden, ggate, gup, attended, reps):
    sub = grad_own.shape[0]
    parts, heads, width = weight.shape
    chips, height, units = hidden.shape
    flat = [array.reshape(chips * height, units) for array in (hidden, ggate, gup)]
    return pl.pallas_call(
        functools.partial(back_out_kernel, reps),
        out_shape=[
            jax.ShapeDtypeStruct((COLS, 2 * sub, heads), BF),
            jax.ShapeDtypeStruct((parts, 3 * units + heads, width), BF),
        ],
        in_specs=[VMEM] * 2 + [HBM] * 2 + [VMEM] * 4,
        out_specs=[HBM] * 2,
        scratch_shapes=gather_scratch(sub)
        + [pltpu.VMEM((COLS, 2 * sub, heads), BF), DMA((1, COLS))]
        + [pltpu.VMEM((2, chips, height, width), BF)] * 2
        + [pltpu.VMEM((2, 3 * units, width), BF), DMA((2, 2)), DMA((2,))]
        + [pltpu.VMEM((heads, D), F32), pltpu.VMEM((parts, heads, width), BF), DMA],
        compiler_params=params(6),
        cost_estimate=takes(50),
        name="back_out",
    )(grad_own, weight, normed_all, top_all, *flat, attended)


def lift_kernel(
    reps, hidden_one_ref, hidden_two_ref, weight_one_ref, weight_two_ref, middle_ref,
    dquery_ref, dpair_ref, cosine_ref, sine_ref, result_ref, proj_ref, *scratch,
):
    weight_one, weight_two, weight_sems, low, taken, push_send, push_recv = scratch[SCATTER_REFS:]
    parts, units, width = weight_one.shape
    row, rows = lax.axis_index("row"), lax.axis_size("row")
    loads = []
    for index, (source, target) in enumerate(((weight_one_ref, weight_one), (weight_two_ref, weight_two))):
        copy = pltpu.make_async_copy(source.at[:, pl.ds(2 * units, units)], target, weight_sems.at[index])
        copy.start()
        loads.append(copy)
    partners = row_partners()
    meet(near(reps) + [{"row": partner} for partner in partners])
    low[...] = dpair_ref[:, 0].astype(BF)
    push = pltpu.make_async_remote_copy(
        src_ref=low,
        dst_ref=taken,
        send_sem=push_send,
        recv_sem=push_recv,
        device_id={"row": lax.rem(row + rows - 1, rows)},
        device_id_type=MESH,
    )

    @pl.when(row > 0)
    def _():
        push.start()

    for copy in loads:
        copy.wait()

    def partial(step, chip, put):
        for part in range(parts):
            value = dot(hidden_one_ref[chip], weight_one[part], 1, 0)
            put(pl.ds(part * width, width), value + dot(hidden_two_ref[chip], weight_two[part], 1, 0))

    def finish(piece, rows_of, value):
        result_ref[rows_of, :] = (middle_ref[rows_of, :] + value).astype(BF)

    def turn_back():
        @pl.when(row == rows - 1)
        def _():
            taken[...] = jnp.zeros_like(taken)

        @pl.when(row < rows - 1)
        def _():
            push.wait_recv()

        chips, height, _ = proj_ref.shape
        for chip in range(chips):
            places = pl.ds(chip * height, height)
            pair_rows = pl.ds(chip % 2 * height, height)
            pair = dpair_ref[chip // 2, 1, pair_rows, :] + taken[chip // 2, pair_rows, :].astype(F32)
            grad = jnp.concatenate([dquery_ref[places, :], pair], axis=1)
            proj_ref[chip] = rotate(grad, cosine_ref[places, :], -sine_ref[places, :]).astype(BF)

    run_scatter(reps, partial, finish, scratch[:SCATTER_REFS], turn_back)

    @pl.when(row > 0)
    def _():
        push.wait_send()


def lift(hidden_one, hidden_two, weight_one, weight_two, middle, dquery, dpairs, cosine, sine, reps):
    sub = middle.shape[0]
    parts, rows, width = weight_one.shape
    tokens, heads = dquery.shape
    halves, _, slots, lanes = dpairs.shape
    return pl.pallas_call(
        functools.partial(lift_kernel, reps),
        out_shape=[
            jax.ShapeDtypeStruct((sub, D), BF),
            jax.ShapeDtypeStruct((COLS, tokens // COLS, heads + lanes), BF),
        ],
        in_specs=[VMEM] * 2 + [HBM] * 2 + [VMEM] * 5,
        out_specs=[VMEM] * 2,
        scratch_shapes=scatter_scratch(sub)
        + [pltpu.VMEM((parts, rows // 3, width), BF)] * 2
        + [DMA((2,))]
        + [pltpu.VMEM((halves, slots, lanes), BF)] * 2
        + [DMA, DMA],
        compiler_params=params(7),
        cost_estimate=takes(50),
        name="lift",
    )(hidden_one, hidden_two, weight_one, weight_two, middle, dquery, dpairs, cosine, sine)


PEERS = ("SO", "P", "SP", "Q", "SQ", "D", "SD")


def project_back_kernel(
    reps, proj_ref, weight_ref, source_ref, middle_ref, gains_ref, gain_two_ref, result_in_ref,
    resid_ref, gain_ref, result_ref, *scratch,
):
    stage, *scratch = scratch
    result_home = Home(result_in_ref, scratch[SCATTER_REFS : SCATTER_REFS + HOME_REFS])
    home = Home(stage, scratch[SCATTER_REFS + HOME_REFS : SCATTER_REFS + 2 * HOME_REFS])
    gain_own, gain_rows, gain_plane, row_send, row_recv, plane_send, plane_recv = scratch[SCATTER_REFS + 2 * HOME_REFS :]
    where = plane(reps)
    row = lax.axis_index("row")
    partners = row_partners()
    meet([where[kind][2] for kind in PEERS] + [{"row": partner} for partner in partners])
    for piece in range(PIECES):
        result_home.send(piece)
    gain_own[...] = jnp.zeros_like(gain_own)
    gain_own[1:2, :] = gain_two_ref[0:1, :]

    def partial(step, chip, put):
        for index in range(D // SPAN):
            columns = pl.ds(index * SPAN, SPAN)
            put(columns, dot(proj_ref[chip], weight_ref[columns, :], 1, 1))

    def finish(piece, rows, value):
        back, gain_part = norm_back(value, source_ref[rows, :].astype(F32), gains_ref[0:1, :])
        home.stage[rows, :] = (middle_ref[rows, :] + back).astype(BF)
        home.send(piece)
        gain_own[0:1, :] += gain_part

    run_scatter(reps, partial, finish, scratch[:SCATTER_REFS], result_home.turn)
    width = gain_ref.shape[1]
    copies = []
    for shift, partner in enumerate(partners):
        copy = pltpu.make_async_remote_copy(
            src_ref=gain_own.at[:, tile(partner, width)],
            dst_ref=gain_rows.at[shift],
            send_sem=row_send.at[shift],
            recv_sem=row_recv.at[shift],
            device_id={"row": partner},
            device_id_type=MESH,
        )
        copy.start()
        copies.append(copy)
    home.turn()
    for copy in copies:
        copy.wait()
    total = gain_own[:, tile(row, width)]
    for shift in range(len(partners)):
        total += gain_rows[shift]
    own = where["O"][0] * 2 + where["O"][1]
    gain_plane[own] = total

    def share(index, place):
        return pltpu.make_async_remote_copy(
            src_ref=gain_plane.at[place],
            dst_ref=gain_plane.at[place],
            send_sem=plane_send.at[index],
            recv_sem=plane_recv.at[place],
            device_id=where[PEERS[index]][2],
            device_id_type=MESH,
        )

    for index in range(len(PEERS)):
        share(index, own).start()
    for index, kind in enumerate(PEERS):
        share(index, where[kind][0] * 2 + where[kind][1]).wait_recv()
    total = gain_plane[0]
    for place in range(1, 2 * COLS):
        total += gain_plane[place]
    gain_ref[...] = total
    for index in range(len(PEERS)):
        share(index, own).wait_send()
    result_home.wait()
    result_ref[...] = result_home.home[...]
    home.wait()
    resid_ref[...] = home.home[...]


def project_back(grad_proj, weight, source, grad_middle, gains, gain_two, result, reps, rows):
    sub = source.shape[0]
    width = D // rows
    return pl.pallas_call(
        functools.partial(project_back_kernel, reps),
        out_shape=[
            jax.ShapeDtypeStruct((sub * COLS, width), BF),
            jax.ShapeDtypeStruct((8, width), F32),
            jax.ShapeDtypeStruct((sub * COLS, width), BF),
        ],
        in_specs=[VMEM] * 7,
        out_specs=[VMEM] * 3,
        scratch_shapes=[pltpu.VMEM((sub, D), BF)]
        + scatter_scratch(sub)
        + home_scratch(sub, rows)
        + home_scratch(sub, rows)
        + [
            pltpu.VMEM((8, D), F32),
            pltpu.VMEM((rows - 1, 8, width), F32),
            pltpu.VMEM((2 * COLS, 8, width), F32),
            DMA((rows - 1,)),
            DMA((rows - 1,)),
            DMA((len(PEERS),)),
            DMA((2 * COLS,)),
        ],
        compiler_params=params(8),
        cost_estimate=takes(55),
        name="project_back",
    )(grad_proj, weight, source, grad_middle, gains, gain_two, result)


def adamw(weights, gradient, moment, square, step_rate, decay_rate):
    gradient = gradient.astype(F32)
    moment_new = BETA_ONE * moment + (1.0 - BETA_ONE) * gradient
    square_new = BETA_TWO * square + (1.0 - BETA_TWO) * gradient * gradient
    moment_hat = moment_new / (1.0 - BETA_ONE**STEP)
    square_hat = square_new / (1.0 - BETA_TWO**STEP)
    weights_new = weights - step_rate * (
        moment_hat / (jnp.sqrt(square_hat) + ADAM_EPS) + decay_rate * weights
    )
    return (weights_new, moment_new, square_new)


def local(
    resid_in,
    cotangent,
    seq_lens,
    qkv_weight,
    qkv_moment,
    qkv_square,
    out_weight,
    out_moment,
    out_square,
    gate_weight,
    gate_moment,
    gate_square,
    up_weight,
    up_moment,
    up_square,
    down_weight,
    down_moment,
    down_square,
    norm_gains,
    gain_moment,
    gain_square,
):
    cols, rows, replicas = lax.axis_size("col"), lax.axis_size("row"), lax.axis_size("dp")
    reps = replicas // 2
    half = lax.axis_index("dp") // reps
    row, col = lax.axis_index("row"), lax.axis_index("col")
    chunk = resid_in.shape[0]
    sub = chunk // cols
    blocks = 2 * cols
    plane_tokens = sub * blocks
    head_width = (GROUP + 2) * HD

    qkv_block = half_columns(qkv_weight, reps)
    out_block = tall_block(out_weight, reps)
    split = out_block.shape[1] // 2
    stacked = jnp.concatenate([out_block[:, :split], out_block[:, split:]], axis=0)
    first_w = lax.all_gather(jnp.concatenate([qkv_block, stacked], axis=1), "row", axis=0)
    qkv_w = first_w[:, :, :head_width].reshape(D, head_width)
    heads = out_block.shape[0]
    out_w = jnp.concatenate([first_w[:, :heads, head_width:], first_w[:, heads:, head_width:]], axis=2)
    lengths = both_halves(seq_lens, partner_swap(seq_lens, reps), half, 0)
    ends = jnp.cumsum(lengths, axis=1, dtype=jnp.int32)
    slot = (row * chunk + jnp.arange(chunk, dtype=jnp.int32)).reshape(1, chunk)
    passed = (slot[:, :, None] >= ends[:, None, :]).astype(jnp.int32)
    seq_start = jnp.sum(passed * lengths[:, None, :], axis=2, dtype=jnp.int32)
    usable = slot < ends[:, -1:]
    cosine, sine = rope_tables((slot - seq_start).reshape(plane_tokens))
    low = (jnp.where(usable, seq_start, slot) - (row - 1) * chunk).reshape(blocks, 1, sub)
    firsts = jnp.tile(chunk + jnp.arange(cols, dtype=jnp.int32) * sub, 2)
    bounds = jnp.stack([low[:, 0, 0] // KEYS, (firsts + sub - 1) // KEYS + 1, firsts]).astype(jnp.int32)
    usable_mine = (row * chunk + col * sub + jnp.arange(sub, dtype=jnp.int32)) < jnp.sum(seq_lens)

    padded = jnp.concatenate([norm_gains, jnp.zeros((6, norm_gains.shape[1]), F32)])
    source, normed_own, grad_top, gains = exchange(
        resid_in, cotangent, padded, usable_mine.astype(F32)[:, None], rows
    )
    gate_block = half_columns(gate_weight, reps, source)
    up_block = half_columns(up_weight, reps, source)
    down_block = tall_block(down_weight, reps)
    units = gate_block.shape[1] // SLICES
    slice_w = []
    for index in range(SLICES):
        span = slice(index * units, (index + 1) * units)
        block = jnp.concatenate([gate_block[:, span], up_block[:, span], down_block[span]], axis=0)
        slice_w.append(lax.all_gather(block, "row", axis=0))
    normed_one, grad_top_all, queries, pairs = project(normed_own, grad_top, qkv_w, cosine, sine, reps)
    queries = queries.reshape(plane_tokens, GROUP * HD)
    pairs = pairs.reshape(2, 2 * chunk, 2 * HD)
    attended, log_total = attend(queries, pairs, low, bounds)
    middle, normed_own = mix_out(attended.reshape(cols, 2 * sub, GROUP * HD), out_w, source, gains, reps)

    normed_two, hidden_one, ggate_one, gup_one = first_slice(normed_own, grad_top_all, slice_w[0], reps)
    grads_one = slice_grads(normed_two, grad_top_all, hidden_one, ggate_one, gup_one, rows)
    normed_two, grads_one = lax.optimization_barrier((normed_two, grads_one))
    hidden_two, ggate_two, gup_two, grad_middle, grad_middle_own, gain_grad_two = second_slice(
        normed_two, grad_top_all, ggate_one, gup_one, slice_w[0], slice_w[1], middle, grad_top, gains, reps
    )
    grad_attended, grads_two = back_out(
        grad_middle_own, out_w, normed_two, grad_top_all, hidden_two, ggate_two, gup_two,
        attended.reshape(cols, 2 * sub, GROUP * HD), reps,
    )
    slice_g = [lax.psum_scatter(part, "row", scatter_dimension=0) for part in (grads_one, grads_two)]
    grad_attended, slice_g[0] = lax.optimization_barrier((grad_attended, slice_g[0]))
    grad_query, grad_pairs = attend_back(
        queries, grad_attended.reshape(plane_tokens, GROUP * HD), pairs, low, log_total, bounds
    )
    result, grad_proj = lift(
        hidden_one, hidden_two, slice_w[0], slice_w[1], middle,
        grad_query, grad_pairs.reshape(2, 2, chunk, 2 * HD), cosine, sine, reps,
    )
    grad_qkv = dot(normed_one.reshape(plane_tokens, D), grad_proj.reshape(plane_tokens, head_width), 0, 0).astype(BF)
    grad_proj, grad_qkv = lax.optimization_barrier((grad_proj, grad_qkv))
    resid_grad, gain_grads, result = project_back(
        grad_proj, qkv_w, source, grad_middle, gains, gain_grad_two, result, reps, rows
    )
    resid_grad = resid_grad.astype(F32)
    grad_qkv = lax.psum_scatter(grad_qkv, "row", scatter_dimension=0, tiled=True)
    wide = 2 * (D // rows)
    slice_g[1], resid_grad = lax.optimization_barrier((slice_g[1], resid_grad))
    halves = [own_slice(part[:wide], reps) for part in slice_g]
    grad_qkv, halves, slice_g[0] = lax.optimization_barrier((grad_qkv, halves, slice_g[0]))
    grad_qkv = own_rows(grad_qkv, reps)
    pieces = [halves[index][place] for place in range(2) for index in range(SLICES)]
    grad_gate, grad_up = [jnp.concatenate([piece[index] for piece in pieces], axis=1) for index in range(2)]
    grad_down = own_tall(jnp.concatenate([part[wide : wide + units] for part in slice_g], axis=0), reps)
    grad_out = own_tall(slice_g[1][wide + units :], reps)

    gain_grads = gain_grads[:2]
    if reps > 1:
        gain_grads = lax.psum(gain_grads, "dp", axis_index_groups=rep_groups(reps))
    qkv_set = adamw(qkv_weight, grad_qkv, qkv_moment, qkv_square, RATE_MATRIX, WEIGHT_DECAY)
    out_set = adamw(out_weight, grad_out, out_moment, out_square, RATE_OUTPUT, WEIGHT_DECAY)
    gate_set = adamw(gate_weight, grad_gate, gate_moment, gate_square, RATE_MATRIX, WEIGHT_DECAY)
    up_set = adamw(up_weight, grad_up, up_moment, up_square, RATE_MATRIX, WEIGHT_DECAY)
    down_set = adamw(down_weight, grad_down, down_moment, down_square, RATE_MATRIX, WEIGHT_DECAY)
    gain_set = adamw(norm_gains, gain_grads, gain_moment, gain_square, RATE_GAIN, 0.0)
    return (result, resid_grad, *qkv_set, *out_set, *gate_set, *up_set, *down_set, *gain_set)


def solution(mesh):
    tokens = P(("dp", "col"), "row")
    wide = P(("row", "dp"), "col")
    tall = P(("col", "dp"), "row")
    gain = P(None, "row")
    weights = (wide,) * 3 + (tall,) * 3 + (wide,) * 6 + (tall,) * 3 + (gain,) * 3
    return jax.shard_map(
        local,
        mesh=mesh,
        in_specs=(tokens, tokens, P("dp", None)) + weights,
        out_specs=(tokens, tokens) + weights,
        check_vma=False,
    )
```

```python
import functools

import jax
import jax.numpy as jnp
from jax import lax
from jax.experimental import pallas as pl
from jax.experimental.pallas import tpu as pltpu
from jax.sharding import PartitionSpec as P

D = 2048
FF = 8192
HD = 64
GROUP = 4
LMAX = 1024
STEP = 10
KEYS = 256
SLICES = 2
PIECES = 4
COLS = 4

EPS_NORM = 1e-05
ROPE_BASE = 500000.0
BETA_ONE = 0.9
BETA_TWO = 0.95
ADAM_EPS = 1e-08
WEIGHT_DECAY = 0.1
RATE_MATRIX = 0.05
RATE_OUTPUT = 0.4
RATE_GAIN = 0.8
MASKED = -1e30
SCALE = HD ** (-0.5)

BF = jnp.bfloat16
F32 = jnp.float32


def dot(left, right, left_dim, right_dim):
    return lax.dot_general(
        left, right, (((left_dim,), (right_dim,)), ((), ())), preferred_element_type=F32
    )


def half_groups(reps):
    return [[rep, rep + reps] for rep in range(reps)]


def rep_groups(reps):
    return [[half * reps + rep for rep in range(reps)] for half in range(2)]


def partner_swap(values_in, reps):
    pairs = [pair for rep in range(reps) for pair in ((rep, rep + reps), (rep + reps, rep))]
    return lax.ppermute(values_in, "dp", pairs)


def both_halves(mine, theirs, half, axis):
    first = jnp.where(half == 0, mine, theirs)
    second = jnp.where(half == 0, theirs, mine)
    return jnp.concatenate([first, second], axis=axis)


def half_columns(weight, reps, after=None):
    half = lax.axis_index("dp") // reps
    own, width = weight.shape[0], weight.shape[1] // 2
    low = weight.astype(BF)
    mine = lax.dynamic_slice_in_dim(low, half * width, width, 1)
    theirs = partner_swap(lax.dynamic_slice_in_dim(low, (1 - half) * width, width, 1), reps)
    if after is not None:
        theirs, _ = lax.optimization_barrier((theirs, after))
    both = both_halves(mine, theirs, half, 0)
    if reps > 1:
        both = lax.all_gather(both, "dp", axis=0, axis_index_groups=rep_groups(reps))
        both = both.reshape(reps, 2, own, width).swapaxes(0, 1).reshape(2 * reps * own, width)
    return both


def own_rows(part, reps):
    half = lax.axis_index("dp") // reps
    height = part.shape[0] // 2
    mine = lax.dynamic_slice_in_dim(part, half * height, height, 0)
    theirs = partner_swap(lax.dynamic_slice_in_dim(part, (1 - half) * height, height, 0), reps)
    part = both_halves(mine, theirs, half, 1)
    if reps > 1:
        part = lax.psum_scatter(
            part, "dp", scatter_dimension=0, tiled=True, axis_index_groups=rep_groups(reps)
        )
    return part


def own_slice(part, reps):
    half = lax.axis_index("dp") // reps
    units = part.shape[1]
    split = part.reshape(2, 2, -1, units)
    mine = lax.dynamic_index_in_dim(split, half, 1, False)
    theirs = partner_swap(lax.dynamic_index_in_dim(split, 1 - half, 1, False), reps)
    halves = [jnp.where(half == 0, mine, theirs), jnp.where(half == 0, theirs, mine)]
    if reps > 1:
        halves = [
            lax.psum_scatter(piece, "dp", scatter_dimension=1, tiled=True, axis_index_groups=rep_groups(reps))
            for piece in halves
        ]
    return halves


def tall_block(weight, reps):
    own = weight.astype(BF)
    if reps > 1:
        own = lax.all_gather(own, "dp", axis=0, tiled=True, axis_index_groups=rep_groups(reps))
    return own


def own_tall(part, reps):
    if reps > 1:
        part = lax.psum_scatter(
            part, "dp", scatter_dimension=0, tiled=True, axis_index_groups=rep_groups(reps)
        )
    return part


def row_blocks(matrix, rows):
    return matrix.reshape(matrix.shape[0], rows, -1).swapaxes(0, 1)


def rope_tables(position):
    exponent = jnp.arange(0, HD, 2, dtype=F32) / HD
    freq_table = 1.0 / ROPE_BASE**exponent
    angle = position.astype(F32)[:, None] * freq_table[None, :]
    cosine = jnp.cos(angle)
    sine = jnp.sin(angle)
    return (jnp.concatenate([cosine] * 4, axis=1), jnp.concatenate([-sine, sine, -sine, sine], axis=1))


def rotate(vectors, cosine, sine):
    width = vectors.shape[1]
    lane = lax.broadcasted_iota(jnp.int32, vectors.shape, 1)
    lower = lax.rem(lane, HD) < HD // 2
    turned = jnp.where(
        lower, pltpu.roll(vectors, width - HD // 2, 1), pltpu.roll(vectors, HD // 2, 1)
    )
    copies = width // cosine.shape[1]
    cosine = jnp.concatenate([cosine] * copies, axis=1)
    sine = jnp.concatenate([sine] * copies, axis=1)
    return jnp.where(lane < (GROUP + 1) * HD, vectors * cosine + turned * sine, vectors)


MESH = pl.DeviceIdType.MESH
HBM = pl.BlockSpec(memory_space=pl.ANY)
VMEM = pl.BlockSpec(memory_space=pltpu.VMEM)
DMA = pltpu.SemaphoreType.DMA


def takes(micros):
    return pl.CostEstimate(flops=1, bytes_accessed=int(micros * 3.6e6), transcendentals=0)


def params(collective_id):
    return pltpu.CompilerParams(
        collective_id=collective_id, has_side_effects=True, vmem_limit_bytes=60 * 2**20
    )


def tile(index, width):
    return pl.ds(pl.multiple_of(index * width, width), width)


def plane(reps):
    replica, col = lax.axis_index("dp"), lax.axis_index("col")
    half, rep = lax.div(replica, reps), lax.rem(replica, reps)
    core = lax.rem(col, 2)
    other = col + 1 - 2 * core

    def place(half_of, col_of):
        chip = half_of * (COLS // 2) + lax.div(col_of, 2)
        return (chip, lax.rem(col_of, 2), {"dp": half_of * reps + rep, "col": col_of})

    def turn(value, by, modulus):
        return lax.rem(value + by, modulus)

    return {
        "O": place(half, col),
        "P": place(turn(half, 1 - core, 2), turn(col, 2 * core, COLS)),
        "Q": place(turn(half, core, 2), turn(col, 2 - 2 * core, COLS)),
        "D": place(1 - half, turn(col, 2, COLS)),
        "SO": place(half, other),
        "SP": place(turn(half, core, 2), turn(other, 2 - 2 * core, COLS)),
        "SQ": place(turn(half, 1 - core, 2), turn(other, 2 * core, COLS)),
        "SD": place(1 - half, turn(other, 2, COLS)),
    }


def near(reps):
    where = plane(reps)
    return [where["P"][2], where["Q"][2], where["SO"][2]]


def row_partners():
    rows, row = lax.axis_size("row"), lax.axis_index("row")
    return [lax.rem(row + shift, rows) for shift in range(1, rows)]


def signal(devices):
    barrier = pltpu.get_barrier_semaphore()
    for device in devices:
        pl.semaphore_signal(barrier, inc=1, device_id=device, device_id_type=MESH)


def meet(devices):
    signal(devices)
    pl.semaphore_wait(pltpu.get_barrier_semaphore(), len(devices))


GATHER_KINDS = ("P", "Q", "D", "SO", "SP", "SQ", "SD")


def run_gather(reps, own_ref, held_ref, sems, use):
    send_sems, recv_sems, local_sem = sems
    where = plane(reps)
    sub = own_ref.shape[0]
    height = sub // PIECES

    def spot(kind, piece):
        chip, core, _ = where[kind]
        return held_ref.at[chip, pl.ds(pl.multiple_of(core * sub + piece * height, height), height)]

    def message(kind, piece, source, target, device):
        index = GATHER_KINDS.index(kind)
        return pltpu.make_async_remote_copy(
            src_ref=source,
            dst_ref=target,
            send_sem=send_sems.at[index, piece],
            recv_sem=recv_sems.at[index, piece],
            device_id=device,
            device_id_type=MESH,
        )

    near_p, near_q, sibling = where["P"][2], where["Q"][2], where["SO"][2]
    sent = []

    def send(kind, piece, source, held_by, device):
        copy = message(kind, piece, source, spot(held_by, piece), device)
        copy.start()
        sent.append(copy)

    def arrive(kind, piece):
        message(kind, piece, spot(kind, piece), spot(kind, piece), sibling).wait_recv()

    own_copy = pltpu.make_async_copy(own_ref, held_ref.at[where["O"][0], tile(where["O"][1], sub)], local_sem)
    own_copy.start()
    for piece in range(PIECES):
        source = own_ref.at[pl.ds(piece * height, height)]
        send("P", piece, source, "O", near_p)
        send("Q", piece, source, "O", near_q)
        send("SO", piece, source, "O", sibling)
    own_copy.wait()
    for piece in range(PIECES):
        arrive("SO", piece)
    use(0, where["O"][0])
    for piece in range(PIECES):
        arrive("P", piece)
        send("D", piece, spot("P", piece), "P", near_q)
        send("SP", piece, spot("P", piece), "P", sibling)
    for piece in range(PIECES):
        arrive("Q", piece)
        send("SQ", piece, spot("Q", piece), "Q", sibling)
    for piece in range(PIECES):
        arrive("SQ", piece)
    use(1, where["P"][0])
    for piece in range(PIECES):
        arrive("SP", piece)
    use(2, where["Q"][0])
    for piece in range(PIECES):
        arrive("D", piece)
        send("SD", piece, spot("D", piece), "D", sibling)
    for piece in range(PIECES):
        arrive("SD", piece)
    use(3, where["D"][0])
    for copy in sent:
        copy.wait_send()


def gather_scratch(sub):
    count = len(GATHER_KINDS)
    return [pltpu.VMEM((COLS, 2 * sub, D), BF), DMA((count, PIECES)), DMA((count, PIECES)), DMA]


SCATTER_SWAPS = ("D", "Q", "P", "O")
SCATTER_HOPS = ("D", "Q", "P")


def scatter_order(reps):
    where = plane(reps)
    return [where[kind][0] for kind in SCATTER_SWAPS]


def run_scatter(reps, partial, finish, scratch, meanwhile=None):
    total_ref, give_ref, take_ref, hop_out, hop_in, both_ref, swap_send, swap_recv, hop_send, hop_recv = scratch
    where = plane(reps)
    core = where["O"][1]
    device = {"P": where["P"][2], "Q": where["Q"][2], "D": where["Q"][2]}
    sibling = where["SO"][2]
    sub = total_ref.shape[1]
    height = sub // PIECES
    sibling_kind = {"D": "D", "Q": "P", "P": "Q", "O": "O"}
    sent = []

    def swap(kind):
        index = SCATTER_SWAPS.index(kind)
        return pltpu.make_async_remote_copy(
            src_ref=give_ref.at[index],
            dst_ref=take_ref.at[index],
            send_sem=swap_send.at[index],
            recv_sem=swap_recv.at[index],
            device_id=sibling,
            device_id_type=MESH,
        )

    def hop(kind, piece):
        index = SCATTER_HOPS.index(kind)
        rows = pl.ds(piece * height, height)
        return pltpu.make_async_remote_copy(
            src_ref=hop_out.at[index, rows],
            dst_ref=hop_in.at[index, rows],
            send_sem=hop_send.at[index, piece],
            recv_sem=hop_recv.at[index, piece],
            device_id=device[kind],
            device_id_type=MESH,
        )

    def compute(step, kind):
        mine, theirs = SCATTER_SWAPS.index(kind), SCATTER_SWAPS.index(sibling_kind[kind])

        def put(columns, value):
            both_ref[...] = value
            total_ref[mine, :, columns] = both_ref[tile(core, sub), :]
            give_ref[theirs, :, columns] = both_ref[tile(1 - core, sub), :].astype(BF)

        partial(step, where[kind][0], put)
        copy = swap(sibling_kind[kind])
        copy.start()
        sent.append(copy)

    def settle(kind):
        index = SCATTER_SWAPS.index(kind)
        swap(kind).wait_recv()
        for piece in range(PIECES):
            rows = pl.ds(piece * height, height)
            value = total_ref[index, rows, :] + take_ref[index, rows, :].astype(F32)
            if kind == "P":
                hop("D", piece).wait_recv()
                value += hop_in[SCATTER_HOPS.index("D"), rows, :].astype(F32)
            if kind == "O":
                for source in ("Q", "P"):
                    hop(source, piece).wait_recv()
                    value += hop_in[SCATTER_HOPS.index(source), rows, :].astype(F32)
                finish(piece, rows, value)
            else:
                hop_out[SCATTER_HOPS.index(kind), rows, :] = value.astype(BF)
                copy = hop(kind, piece)
                copy.start()
                sent.append(copy)

    compute(0, "D")
    compute(1, "Q")
    settle("D")
    compute(2, "P")
    settle("Q")
    compute(3, "O")
    if meanwhile is not None:
        meanwhile()
    settle("P")
    settle("O")
    for copy in sent:
        copy.wait_send()


SPAN = 512


def scatter_scratch(sub):
    return [
        pltpu.VMEM((4, sub, D), F32),
        pltpu.VMEM((4, sub, D), BF),
        pltpu.VMEM((4, sub, D), BF),
        pltpu.VMEM((3, sub, D), BF),
        pltpu.VMEM((3, sub, D), BF),
        pltpu.VMEM((2 * sub, SPAN), F32),
        DMA((4,)),
        DMA((4,)),
        DMA((3, PIECES)),
        DMA((3, PIECES)),
    ]


SCATTER_REFS = 10


def col_partners():
    cols, col = lax.axis_size("col"), lax.axis_index("col")
    return [lax.rem(col + shift, cols) for shift in range(1, cols)]


def put_by_row(out_ref, piece, value):
    height, width = value.shape[0], out_ref.shape[1]
    parts = D // width
    sub = out_ref.shape[0] // parts
    for part in range(parts):
        out_ref[pl.ds(part * sub + piece * height, height), :] = value[:, part * width : (part + 1) * width].astype(BF)


def to_rows(block):
    return lax.all_to_all(block, "row", split_axis=0, concat_axis=0, tiled=True)


def to_columns(block):
    return lax.all_to_all(block, "col", split_axis=0, concat_axis=0, tiled=True)


def head_rows(block):
    turned = block.astype(F32).T
    return [turned[head * HD : (head + 1) * HD].astype(BF) for head in range(GROUP)]


def allowed_entries(key_block, low_ref, query_first):
    tokens = low_ref.shape[-1]
    key_slot = key_block * KEYS + lax.broadcasted_iota(jnp.int32, (KEYS, tokens), 0)
    query_slot = query_first + lax.broadcasted_iota(jnp.int32, (KEYS, tokens), 1)
    return (key_slot >= low_ref[...]) & (key_slot <= query_slot)


def key_rows(block):
    return pl.ds(pl.multiple_of(block * KEYS, KEYS), KEYS)


def attend_kernel(bounds, query_ref, pair_ref, low_ref, out_ref, log_ref, score_ref, mix_ref):
    step = pl.program_id(1)
    place = pl.program_id(0) * pl.num_programs(1) + step
    first, last, query_first = bounds[0, place], bounds[1, place], bounds[2, place]
    tokens = query_ref.shape[0]
    blank = jnp.zeros((HD, tokens), BF)
    queries = [jnp.concatenate([rows, blank], axis=0) for rows in head_rows(query_ref[...])]

    def score_block(block, tops):
        pairs = pair_ref[key_rows(block), :]
        allowed = allowed_entries(block, low_ref, query_first)
        new_tops = []
        for head in range(GROUP):
            scores = jnp.where(allowed, dot(pairs, queries[head], 1, 0), MASKED)
            score_ref[head, key_rows(block - first), :] = scores
            new_tops.append(jnp.maximum(tops[head], jnp.max(scores, axis=0, keepdims=True)))
        return tuple(new_tops)

    start = tuple(jnp.full((1, tokens), MASKED, F32) for _ in range(GROUP))
    tops = lax.fori_loop(first, last, score_block, start)
    mix_ref[...] = jnp.zeros_like(mix_ref)

    def mix_block(block, totals):
        pairs = pair_ref[key_rows(block), :]
        new_totals = []
        for head in range(GROUP):
            terms = jnp.exp(score_ref[head, key_rows(block - first), :] - tops[head])
            new_totals.append(totals[head] + jnp.sum(terms, axis=0, keepdims=True))
            mix_ref[head] += dot(pairs, terms.astype(BF), 0, 0)
        return tuple(new_totals)

    start = tuple(jnp.zeros((1, tokens), F32) for _ in range(GROUP))
    totals = lax.fori_loop(first, last, mix_block, start)
    mixed = jnp.concatenate(
        [mix_ref[head, HD:, :] / totals[head] for head in range(GROUP)], axis=0
    )
    out_ref[...] = mixed.T.astype(BF)
    for head in range(GROUP):
        log_ref[head : head + 1, :] = tops[head] + jnp.log(totals[head])


def attend_back_kernel(
    bounds, query_ref, grad_ref, pair_ref, low_ref, log_ref, dquery_ref, dpair_ref, prob_ref, dprob_ref, dmix_ref
):
    step = pl.program_id(1)
    place = pl.program_id(0) * pl.num_programs(1) + step
    first, last, query_first = bounds[0, place], bounds[1, place], bounds[2, place]
    tokens = query_ref.shape[0]
    blank = jnp.zeros((HD, tokens), BF)
    queries = [jnp.concatenate([rows, blank], axis=0) for rows in head_rows(query_ref[...])]
    grads = [jnp.concatenate([blank, rows], axis=0) for rows in head_rows(grad_ref[...])]

    @pl.when(step == 0)
    def _():
        dpair_ref[...] = jnp.zeros_like(dpair_ref)

    def prob_block(block, inners):
        pairs = pair_ref[key_rows(block), :]
        allowed = allowed_entries(block, low_ref, query_first)
        new_inners = []
        for head in range(GROUP):
            scores = dot(pairs, queries[head], 1, 0)
            probs = jnp.where(allowed, jnp.exp(scores - log_ref[head : head + 1, :]), 0.0)
            dprobs = dot(pairs, grads[head], 1, 0)
            prob_ref[head, key_rows(block - first), :] = probs
            dprob_ref[head, key_rows(block - first), :] = dprobs
            new_inners.append(inners[head] + jnp.sum(probs * dprobs, axis=0, keepdims=True))
        return tuple(new_inners)

    start = tuple(jnp.zeros((1, tokens), F32) for _ in range(GROUP))
    inners = lax.fori_loop(first, last, prob_block, start)
    dmix_ref[...] = jnp.zeros_like(dmix_ref)
    all_queries = jnp.concatenate(queries, axis=1)
    all_grads = jnp.concatenate(grads, axis=1)

    def back_block(block, carry):
        rows = key_rows(block)
        pairs = pair_ref[rows, :]
        all_probs, all_scores = [], []
        for head in range(GROUP):
            probs = prob_ref[head, key_rows(block - first), :]
            dprobs = dprob_ref[head, key_rows(block - first), :]
            dscores = (probs * (dprobs - inners[head])).astype(BF)
            dmix_ref[head] += dot(pairs, dscores, 0, 0)
            all_probs.append(probs.astype(BF))
            all_scores.append(dscores)
        dpair_ref[rows, :] += dot(jnp.concatenate(all_scores, axis=1), all_queries, 1, 1) + dot(
            jnp.concatenate(all_probs, axis=1), all_grads, 1, 1
        )
        return carry

    lax.fori_loop(first, last, back_block, 0)
    dquery = jnp.concatenate([dmix_ref[head, :HD, :] for head in range(GROUP)], axis=0)
    dquery_ref[...] = dquery.T * SCALE


def attend(queries, pairs, low, bounds):
    tokens, width = queries.shape
    replicas, slots, _ = pairs.shape
    rows = low.shape[2]
    blocks = low.shape[0] // replicas
    span = LMAX + KEYS
    return pl.pallas_call(
        attend_kernel,
        grid_spec=pltpu.PrefetchScalarGridSpec(
            num_scalar_prefetch=1,
            grid=(replicas, blocks),
            in_specs=[
                pl.BlockSpec((rows, GROUP * HD), lambda rep, block, _: (rep * blocks + block, 0)),
                pl.BlockSpec((None, slots, 2 * HD), lambda rep, block, _: (rep, 0, 0)),
                pl.BlockSpec((None, 1, rows), lambda rep, block, _: (rep * blocks + block, 0, 0)),
            ],
            out_specs=[
                pl.BlockSpec((rows, GROUP * HD), lambda rep, block, _: (rep * blocks + block, 0)),
                pl.BlockSpec((None, None, GROUP, rows), lambda rep, block, _: (rep, block, 0, 0)),
            ],
            scratch_shapes=[
                pltpu.VMEM((GROUP, span, rows), F32),
                pltpu.VMEM((GROUP, 2 * HD, rows), F32),
            ],
        ),
        out_shape=[
            jax.ShapeDtypeStruct((tokens, width), BF),
            jax.ShapeDtypeStruct((replicas, blocks, GROUP, rows), F32),
        ],
        compiler_params=pltpu.CompilerParams(vmem_limit_bytes=48 * 2**20),
        cost_estimate=takes(14),
        name="attend",
    )(bounds, queries, pairs, low)


def attend_back(queries, grads, pairs, low, log_total, bounds):
    tokens, width = queries.shape
    replicas, slots, _ = pairs.shape
    rows = low.shape[2]
    blocks = low.shape[0] // replicas
    span = LMAX + KEYS
    return pl.pallas_call(
        attend_back_kernel,
        grid_spec=pltpu.PrefetchScalarGridSpec(
            num_scalar_prefetch=1,
            grid=(replicas, blocks),
            in_specs=[
                pl.BlockSpec((rows, GROUP * HD), lambda rep, block, _: (rep * blocks + block, 0)),
                pl.BlockSpec((rows, GROUP * HD), lambda rep, block, _: (rep * blocks + block, 0)),
                pl.BlockSpec((None, slots, 2 * HD), lambda rep, block, _: (rep, 0, 0)),
                pl.BlockSpec((None, 1, rows), lambda rep, block, _: (rep * blocks + block, 0, 0)),
                pl.BlockSpec((None, None, GROUP, rows), lambda rep, block, _: (rep, block, 0, 0)),
            ],
            out_specs=[
                pl.BlockSpec((rows, GROUP * HD), lambda rep, block, _: (rep * blocks + block, 0)),
                pl.BlockSpec((None, slots, 2 * HD), lambda rep, block, _: (rep, 0, 0)),
            ],
            scratch_shapes=[
                pltpu.VMEM((GROUP, span, rows), F32),
                pltpu.VMEM((GROUP, span, rows), F32),
                pltpu.VMEM((GROUP, 2 * HD, rows), F32),
            ],
        ),
        out_shape=[
            jax.ShapeDtypeStruct((tokens, width), F32),
            jax.ShapeDtypeStruct((replicas, slots, 2 * HD), F32),
        ],
        compiler_params=pltpu.CompilerParams(vmem_limit_bytes=48 * 2**20),
        cost_estimate=takes(23),
        name="attend_back",
    )(bounds, queries, grads, pairs, low, log_total)


def norm_of(vectors):
    scaling = lax.rsqrt(jnp.mean(vectors * vectors, axis=1, keepdims=True) + EPS_NORM)
    return vectors * scaling, scaling


def norm_back(value, vectors, gain):
    unit, scaling = norm_of(vectors)
    weighted = value * gain
    inner = jnp.mean(weighted * unit, axis=1, keepdims=True)
    return scaling * (weighted - unit * inner), jnp.sum(value * unit, axis=0, keepdims=True)


def exchange_kernel(
    token_ref, top_ref, gain_ref, usable_ref, source_ref, normed_ref, grad_top_ref, gains_ref,
    held, held_top, mid, mid_top, held_gains, col_send, col_recv, row_send, row_recv, gain_send, gain_recv, local_sems,
):
    row, col = lax.axis_index("row"), lax.axis_index("col")
    sub, width = held.shape[0], token_ref.shape[1]
    row_of = row_partners()
    col_of = col_partners()
    meet([{"row": partner} for partner in row_of] + [{"col": partner} for partner in col_of])
    own_cols = tile(row, width)

    def run(copies):
        for copy in copies:
            copy.start()
        return copies

    def finish(copies):
        for copy in copies:
            copy.wait()

    def remote(source, target, send_sem, recv_sem, device):
        return pltpu.make_async_remote_copy(
            src_ref=source, dst_ref=target, send_sem=send_sem, recv_sem=recv_sem, device_id=device, device_id_type=MESH
        )

    def to_columns(array, source, target):
        return run(
            [
                remote(
                    source.at[tile(partner, sub)], target.at[col],
                    col_send.at[array, shift], col_recv.at[array, shift], {"col": partner},
                )
                for shift, partner in enumerate(col_of)
            ]
            + [pltpu.make_async_copy(source.at[tile(col, sub)], target.at[col], local_sems.at[array, 0])]
        )

    def to_rows(array, source, target):
        return run(
            [
                remote(
                    source.at[partner], target.at[:, own_cols],
                    row_send.at[array, shift], row_recv.at[array, shift], {"row": partner},
                )
                for shift, partner in enumerate(row_of)
            ]
            + [pltpu.make_async_copy(source.at[row], target.at[:, own_cols], local_sems.at[array, 1])]
        )

    tokens = to_columns(0, token_ref, mid)
    gains = run(
        [
            remote(gain_ref, held_gains.at[:, own_cols], gain_send.at[shift], gain_recv.at[shift], {"row": partner})
            for shift, partner in enumerate(row_of)
        ]
        + [pltpu.make_async_copy(gain_ref, held_gains.at[:, own_cols], local_sems.at[2, 0])]
    )
    tops = to_columns(1, top_ref, mid_top)
    finish(tokens)
    tokens = to_rows(0, mid, held)
    finish(tops)
    tops = to_rows(1, mid_top, held_top)
    finish(gains)
    finish(tokens)
    source_ref[...] = held[...]
    gains_ref[...] = held_gains[...]
    unit, _ = norm_of(held[...].astype(F32))
    normed_ref[...] = (unit * held_gains[0:1, :]).astype(BF)
    finish(tops)
    grad_top_ref[...] = (held_top[...].astype(F32) * usable_ref[...]).astype(BF)


def exchange(tokens, top, gains, usable, rows):
    sub, width = tokens.shape[0] // COLS, tokens.shape[1]
    block = jax.ShapeDtypeStruct((sub, rows * width), BF)
    return pl.pallas_call(
        exchange_kernel,
        out_shape=[block, block, block, jax.ShapeDtypeStruct((gains.shape[0], rows * width), F32)],
        in_specs=[VMEM] * 4,
        out_specs=[VMEM] * 4,
        scratch_shapes=[pltpu.VMEM((sub, rows * width), BF)] * 2
        + [pltpu.VMEM((COLS, sub, width), BF)] * 2
        + [
            pltpu.VMEM((gains.shape[0], rows * width), F32),
            DMA((2, COLS - 1)),
            DMA((2, COLS - 1)),
            DMA((2, rows - 1)),
            DMA((2, rows - 1)),
            DMA((rows - 1,)),
            DMA((rows - 1,)),
            DMA((3, 2)),
        ],
        compiler_params=params(1),
        cost_estimate=takes(65),
        name="exchange",
    )(tokens, top, gains, usable)


def project_kernel(
    reps, own_ref, top_ref, weight_ref, cosine_ref, sine_ref,
    all_ref, top_all_ref, query_ref, pair_ref,
    held, send_sems, recv_sems, local_sem, top_held, top_send, top_recv, top_local,
    queries, pairs, halo, out_sems, pair_sems, halo_sems, pair_send, pair_recv,
):
    row, rows = lax.axis_index("row"), lax.axis_size("row")
    meet(near(reps) + [{"row": partner} for partner in row_partners()])
    sub = own_ref.shape[0]
    copies, chips = [], []
    has_next, has_last = row < rows - 1, row > 0

    @pl.when(row == 0)
    def _():
        halo[...] = jnp.zeros_like(halo)

    def out(source, target, sem):
        copy = pltpu.make_async_copy(source, target, sem)
        copy.start()
        copies.append(copy)

    def push(step, chip):
        return pltpu.make_async_remote_copy(
            src_ref=pairs.at[chip],
            dst_ref=halo.at[chip],
            send_sem=pair_send.at[step],
            recv_sem=pair_recv.at[step],
            device_id={"row": lax.rem(row + 1, rows)},
            device_id_type=MESH,
        )

    def use(step, chip):
        chips.append(chip)
        out(held.at[chip], all_ref.at[chip], out_sems.at[step])
        places = tile(chip, 2 * sub)
        turned = rotate(dot(held[chip], weight_ref[...], 1, 0), cosine_ref[places, :], sine_ref[places, :])
        queries[chip] = (turned[:, : GROUP * HD] * SCALE).astype(BF)
        out(queries.at[chip], query_ref.at[chip], out_sems.at[COLS + step])
        pairs[chip] = turned[:, GROUP * HD :].astype(BF)
        out(pairs.at[chip], pair_ref.at[lax.div(chip, 2), 1, lax.rem(chip, 2)], pair_sems.at[step])

        @pl.when(has_next)
        def _():
            push(step, chip).start()

    run_gather(reps, own_ref, held, (send_sems, recv_sems, local_sem), use)

    def use_top(step, chip):
        out(top_held.at[chip], top_all_ref.at[chip], out_sems.at[2 * COLS + step])

    run_gather(reps, top_ref, top_held, (top_send, top_recv, top_local), use_top)
    for step, chip in enumerate(chips):

        @pl.when(has_next)
        def _():
            push(step, chip).wait_send()

        @pl.when(has_last)
        def _():
            push(step, chip).wait_recv()

    for chip in range(COLS):
        out(halo.at[chip], pair_ref.at[chip // 2, 0, chip % 2], halo_sems.at[chip])
    for copy in copies:
        copy.wait()


def project(normed_own, top_own, weight, cosine, sine, reps):
    sub = normed_own.shape[0]
    return pl.pallas_call(
        functools.partial(project_kernel, reps),
        out_shape=[
            jax.ShapeDtypeStruct((COLS, 2 * sub, D), BF),
            jax.ShapeDtypeStruct((COLS, 2 * sub, D), BF),
            jax.ShapeDtypeStruct((COLS, 2 * sub, GROUP * HD), BF),
            jax.ShapeDtypeStruct((2, 2, COLS // 2, 2 * sub, 2 * HD), BF),
        ],
        in_specs=[VMEM] * 5,
        out_specs=[HBM] * 4,
        scratch_shapes=gather_scratch(sub)
        + gather_scratch(sub)
        + [
            pltpu.VMEM((COLS, 2 * sub, GROUP * HD), BF),
            pltpu.VMEM((COLS, 2 * sub, 2 * HD), BF),
            pltpu.VMEM((COLS, 2 * sub, 2 * HD), BF),
            DMA((3 * COLS,)),
            DMA((COLS,)),
            DMA((COLS,)),
            DMA((COLS,)),
            DMA((COLS,)),
        ],
        compiler_params=params(2),
        cost_estimate=takes(75),
        name="project",
    )(normed_own, top_own, weight, cosine, sine)


def mix_out_kernel(reps, attended_ref, weight_ref, source_ref, gains_ref, middle_ref, normed_ref, *scratch):
    meet(near(reps))
    parts, _, width = weight_ref.shape

    def partial(step, chip, put):
        for part in range(parts):
            put(pl.ds(part * width, width), dot(attended_ref[chip], weight_ref[part], 1, 0))

    def finish(piece, rows, value):
        middle = source_ref[rows, :].astype(F32) + value
        middle_ref[rows, :] = middle
        normed_ref[rows, :] = (norm_of(middle)[0] * gains_ref[1:2, :]).astype(BF)

    run_scatter(reps, partial, finish, scratch)


def mix_out(attended, weight, source, gains, reps):
    sub = source.shape[0]
    return pl.pallas_call(
        functools.partial(mix_out_kernel, reps),
        out_shape=[jax.ShapeDtypeStruct((sub, D), F32), jax.ShapeDtypeStruct((sub, D), BF)],
        in_specs=[VMEM] * 4,
        out_specs=[VMEM] * 2,
        scratch_shapes=scatter_scratch(sub),
        compiler_params=params(3),
        cost_estimate=takes(44),
        name="mix_out",
    )(attended, weight, source, gains)


def gated(tokens, top, weight_ref, put):
    parts, rows, width = weight_ref.shape
    units, span = rows // 3, 256

    def one_tile(index, carry):
        columns = tile(index, span)
        gate_w = weight_ref[:, :units, columns].reshape(D, span)
        up_w = weight_ref[:, units : 2 * units, columns].reshape(D, span)
        gate = dot(tokens, gate_w, 1, 0)
        up = dot(tokens, up_w, 1, 0)
        down_rows = pl.ds(pl.multiple_of(2 * units + index * span, span), span)
        grad = dot(top[:, :width], weight_ref[0, down_rows, :], 1, 1)
        for part in range(1, parts):
            grad += dot(top[:, part * width : (part + 1) * width], weight_ref[part, down_rows, :], 1, 1)
        sigma = 1.0 / (1.0 + jnp.exp(-gate))
        active = gate * sigma
        put(
            columns,
            (active * up).astype(BF),
            (grad * up * sigma * (1.0 + gate * (1.0 - sigma))).astype(BF),
            (grad * active).astype(BF),
        )
        return carry

    lax.fori_loop(0, units // span, one_tile, 0)


def first_slice_kernel(
    reps, own_ref, top_ref, weight_ref, all_ref, hidden_ref, ggate_ref, gup_ref,
    held, send_sems, recv_sems, local_sem, tops, hiddens, ggates, gups, top_sems, out_sems,
):
    meet(near(reps))
    where = plane(reps)
    order = [where[kind][0] for kind in ("O", "P", "Q", "D")]
    loads = [pltpu.make_async_copy(top_ref.at[chip], tops.at[chip], top_sems.at[step]) for step, chip in enumerate(order)]
    for copy in loads:
        copy.start()
    copies = []

    def use(step, chip):
        def out(source, target, index):
            copy = pltpu.make_async_copy(source.at[chip], target.at[chip], out_sems.at[index, step])
            copy.start()
            copies.append(copy)

        out(held, all_ref, 0)
        loads[step].wait()

        def put(columns, hidden, ggate, gup):
            hiddens[chip, :, columns] = hidden
            ggates[chip, :, columns] = ggate
            gups[chip, :, columns] = gup

        gated(held[chip], tops[chip], weight_ref, put)
        out(hiddens, hidden_ref, 1)
        out(ggates, ggate_ref, 2)
        out(gups, gup_ref, 3)

    run_gather(reps, own_ref, held, (send_sems, recv_sems, local_sem), use)
    for copy in copies:
        copy.wait()


def first_slice(normed_own, top_all, weight, reps):
    sub = normed_own.shape[0]
    units = weight.shape[1] // 3
    piece = jax.ShapeDtypeStruct((COLS, 2 * sub, units), BF)
    return pl.pallas_call(
        functools.partial(first_slice_kernel, reps),
        out_shape=[jax.ShapeDtypeStruct((COLS, 2 * sub, D), BF)] + [piece] * 3,
        in_specs=[VMEM, HBM, VMEM],
        out_specs=[HBM] * 4,
        scratch_shapes=gather_scratch(sub)
        + [pltpu.VMEM((COLS, 2 * sub, D), BF)]
        + [pltpu.VMEM((COLS, 2 * sub, units), BF)] * 3
        + [DMA((COLS,)), DMA((4, COLS))],
        compiler_params=params(4),
        cost_estimate=takes(50),
        name="first_slice",
    )(normed_own, top_all, weight)


def second_slice_kernel(
    reps, token_ref, top_ref, ggate_one_ref, gup_one_ref, weight_one_ref, weight_ref, middle_ref, own_top_ref, gains_ref,
    hidden_ref, ggate_ref, gup_ref, grad_ref, low_ref, gain_ref, *scratch,
):
    tokens, tops, ggate_ones, gup_ones, weight_one, hiddens, ggates, gups, in_sems, out_sems, weight_sem = scratch[SCATTER_REFS:]
    meet(near(reps))
    order = scatter_order(reps)
    parts, rows, width = weight_ref.shape
    units = rows // 3
    loads, copies = {}, []
    sources = ((token_ref, tokens), (top_ref, tops), (ggate_one_ref, ggate_ones), (gup_one_ref, gup_ones))

    def load(step):
        loads[step] = []
        for index, (source, target) in enumerate(sources):
            copy = pltpu.make_async_copy(source.at[order[step]], target.at[step % 2], in_sems.at[index, step % 2])
            copy.start()
            loads[step].append(copy)

    load(0)
    weight_copy = pltpu.make_async_copy(weight_one_ref.at[:, pl.ds(0, 2 * units)], weight_one, weight_sem)
    weight_copy.start()
    gain_ref[...] = jnp.zeros_like(gain_ref)

    def partial(step, chip, put):
        slot = step % 2
        for copy in loads[step]:
            copy.wait()
        if step < 3:
            load(step + 1)

        def keep(columns, hidden, ggate, gup):
            hiddens[chip, :, columns] = hidden
            ggates[chip, :, columns] = ggate
            gups[chip, :, columns] = gup

        gated(tokens[slot], tops[slot], weight_ref, keep)
        for index, (source, target) in enumerate(((hiddens, hidden_ref), (ggates, ggate_ref), (gups, gup_ref))):
            copy = pltpu.make_async_copy(source.at[chip], target.at[chip], out_sems.at[index, step])
            copy.start()
            copies.append(copy)
        if step == 0:
            weight_copy.wait()
        for part in range(parts):
            value = dot(ggates[chip], weight_ref[part, :units, :], 1, 1)
            value += dot(gups[chip], weight_ref[part, units : 2 * units, :], 1, 1)
            value += dot(ggate_ones[slot], weight_one[part, :units, :], 1, 1)
            value += dot(gup_ones[slot], weight_one[part, units:, :], 1, 1)
            put(pl.ds(part * width, width), value)

    def finish(piece, rows_of, value):
        back, gain_part = norm_back(value, middle_ref[rows_of, :], gains_ref[1:2, :])
        grad = own_top_ref[rows_of, :].astype(F32) + back
        grad_ref[rows_of, :] = grad
        low_ref[rows_of, :] = grad.astype(BF)
        gain_ref[0:1, :] += gain_part

    run_scatter(reps, partial, finish, scratch[:SCATTER_REFS])
    for copy in copies:
        copy.wait()


def second_slice(normed_all, top_all, ggate_one, gup_one, weight_one, weight, middle, own_top, gains, reps):
    sub = middle.shape[0]
    parts, rows, width = weight.shape
    units = rows // 3
    piece = jax.ShapeDtypeStruct((COLS, 2 * sub, units), BF)
    return pl.pallas_call(
        functools.partial(second_slice_kernel, reps),
        out_shape=[piece] * 3
        + [
            jax.ShapeDtypeStruct((sub, D), F32),
            jax.ShapeDtypeStruct((sub, D), BF),
            jax.ShapeDtypeStruct((8, D), F32),
        ],
        in_specs=[HBM] * 5 + [VMEM] * 4,
        out_specs=[HBM] * 3 + [VMEM] * 3,
        scratch_shapes=scatter_scratch(sub)
        + [pltpu.VMEM((2, 2 * sub, D), BF)] * 2
        + [pltpu.VMEM((2, 2 * sub, units), BF)] * 2
        + [pltpu.VMEM((parts, 2 * units, width), BF)]
        + [pltpu.VMEM((COLS, 2 * sub, units), BF)] * 3
        + [DMA((4, 2)), DMA((3, COLS)), DMA],
        compiler_params=params(5),
        cost_estimate=takes(65),
        name="second_slice",
    )(normed_all, top_all, ggate_one, gup_one, weight_one, weight, middle, own_top, gains)


def slice_grads_kernel(token_ref, top_ref, hidden_ref, ggate_ref, gup_ref, out_ref):
    units = hidden_ref.shape[1]
    tokens, width = hidden_ref.shape[0], token_ref.shape[2]
    features = token_ref[...].reshape(tokens, width)
    out_ref[:units] = dot(features, ggate_ref[...], 0, 0).astype(BF)
    out_ref[units : 2 * units] = dot(features, gup_ref[...], 0, 0).astype(BF)
    out_ref[2 * units :] = dot(hidden_ref[...], top_ref[...].reshape(tokens, width), 0, 0).astype(BF)


def slice_grads(normed_all, top_all, hidden, ggate, gup, rows):
    chips, height, units = hidden.shape
    width = D // rows
    flat = [array.reshape(chips * height, units) for array in (hidden, ggate, gup)]
    block = pl.BlockSpec((chips, height, width), lambda part: (0, 0, part))
    whole = pl.BlockSpec((chips * height, units), lambda part: (0, 0))
    return pl.pallas_call(
        slice_grads_kernel,
        grid=(rows,),
        out_shape=jax.ShapeDtypeStruct((rows, 3 * units, width), BF),
        in_specs=[block, block, whole, whole, whole],
        out_specs=pl.BlockSpec((None, 3 * units, width), lambda part: (part, 0, 0)),
        compiler_params=pltpu.CompilerParams(vmem_limit_bytes=48 * 2**20),
        cost_estimate=takes(20),
        name="slice_grads",
    )(normed_all, top_all, *flat)


def back_out_kernel(
    reps, own_ref, weight_ref, token_ref, top_ref, hidden_ref, ggate_ref, gup_ref, attended_ref, grad_ref, slice_ref,
    held, send_sems, recv_sems, local_sem, grads, out_sems, tokens, tops, slices, in_sems, slice_sems, outs, out_low, tail_sem,
):
    meet(near(reps))
    parts, _, width = weight_ref.shape
    units = hidden_ref.shape[1]
    chips, height = token_ref.shape[:2]
    copies, loads, stores = [], {}, {}

    def load(part):
        loads[part] = []
        columns = pl.ds(part * width, width)
        for index, (source, target) in enumerate(((token_ref, tokens), (top_ref, tops))):
            copy = pltpu.make_async_copy(source.at[:, :, columns], target.at[part % 2], in_sems.at[index, part % 2])
            copy.start()
            loads[part].append(copy)

    load(0)

    def slice_grads(part):
        slot = part % 2
        for copy in loads[part]:
            copy.wait()
        if part < parts - 1:
            load(part + 1)
        if part >= 2:
            stores[part - 2].wait()
        features = tokens[slot].reshape(chips * height, width)
        slices[slot, :units] = dot(features, ggate_ref[...], 0, 0).astype(BF)
        slices[slot, units : 2 * units] = dot(features, gup_ref[...], 0, 0).astype(BF)
        slices[slot, 2 * units :] = dot(hidden_ref[...], tops[slot].reshape(chips * height, width), 0, 0).astype(BF)
        stores[part] = pltpu.make_async_copy(
            slices.at[slot], slice_ref.at[part, pl.ds(0, 3 * units)], slice_sems.at[slot]
        )
        stores[part].start()

    def use(step, chip):
        def out(source, target, index):
            copy = pltpu.make_async_copy(source.at[chip], target.at[chip], out_sems.at[index, step])
            copy.start()
            copies.append(copy)

        for part in range(parts):
            columns = pl.ds(part * width, width)
            value = dot(attended_ref[chip], held[chip, :, columns], 0, 0)
            outs[:, columns] = value if step == 0 else outs[:, columns] + value
        total = dot(held[chip, :, :width], weight_ref[0], 1, 1)
        for part in range(1, parts):
            total += dot(held[chip, :, part * width : (part + 1) * width], weight_ref[part], 1, 1)
        grads[chip] = total.astype(BF)
        out(grads, grad_ref, 0)
        slice_grads(step)

    run_gather(reps, own_ref, held, (send_sems, recv_sems, local_sem), use)
    for part in range(parts):
        out_low[part] = outs[:, part * width : (part + 1) * width].astype(BF)
    tail = pltpu.make_async_copy(out_low, slice_ref.at[:, pl.ds(3 * units, outs.shape[0])], tail_sem)
    tail.start()
    for copy in copies + [stores[parts - 2], stores[parts - 1], tail]:
        copy.wait()


def back_out(grad_own, weight, normed_all, top_all, hidden, ggate, gup, attended, reps):
    sub = grad_own.shape[0]
    parts, heads, width = weight.shape
    chips, height, units = hidden.shape
    flat = [array.reshape(chips * height, units) for array in (hidden, ggate, gup)]
    return pl.pallas_call(
        functools.partial(back_out_kernel, reps),
        out_shape=[
            jax.ShapeDtypeStruct((COLS, 2 * sub, heads), BF),
            jax.ShapeDtypeStruct((parts, 3 * units + heads, width), BF),
        ],
        in_specs=[VMEM] * 2 + [HBM] * 2 + [VMEM] * 4,
        out_specs=[HBM] * 2,
        scratch_shapes=gather_scratch(sub)
        + [pltpu.VMEM((COLS, 2 * sub, heads), BF), DMA((1, COLS))]
        + [pltpu.VMEM((2, chips, height, width), BF)] * 2
        + [pltpu.VMEM((2, 3 * units, width), BF), DMA((2, 2)), DMA((2,))]
        + [pltpu.VMEM((heads, D), F32), pltpu.VMEM((parts, heads, width), BF), DMA],
        compiler_params=params(6),
        cost_estimate=takes(50),
        name="back_out",
    )(grad_own, weight, normed_all, top_all, *flat, attended)


def lift_kernel(
    reps, hidden_one_ref, hidden_two_ref, weight_one_ref, weight_two_ref, middle_ref,
    dquery_ref, dpair_ref, cosine_ref, sine_ref, result_ref, proj_ref, *scratch,
):
    weight_one, weight_two, weight_sems, low, taken, push_send, push_recv = scratch[SCATTER_REFS:]
    parts, units, width = weight_one.shape
    row, rows = lax.axis_index("row"), lax.axis_size("row")
    loads = []
    for index, (source, target) in enumerate(((weight_one_ref, weight_one), (weight_two_ref, weight_two))):
        copy = pltpu.make_async_copy(source.at[:, pl.ds(2 * units, units)], target, weight_sems.at[index])
        copy.start()
        loads.append(copy)
    partners = row_partners()
    meet(near(reps) + [{"row": partner} for partner in partners])
    low[...] = dpair_ref[:, 0].astype(BF)
    push = pltpu.make_async_remote_copy(
        src_ref=low,
        dst_ref=taken,
        send_sem=push_send,
        recv_sem=push_recv,
        device_id={"row": lax.rem(row + rows - 1, rows)},
        device_id_type=MESH,
    )

    @pl.when(row > 0)
    def _():
        push.start()

    for copy in loads:
        copy.wait()

    def partial(step, chip, put):
        for part in range(parts):
            value = dot(hidden_one_ref[chip], weight_one[part], 1, 0)
            put(pl.ds(part * width, width), value + dot(hidden_two_ref[chip], weight_two[part], 1, 0))

    def finish(piece, rows_of, value):
        put_by_row(result_ref, piece, middle_ref[rows_of, :] + value)

    def turn_back():
        @pl.when(row == rows - 1)
        def _():
            taken[...] = jnp.zeros_like(taken)

        @pl.when(row < rows - 1)
        def _():
            push.wait_recv()

        chips, height, _ = proj_ref.shape
        for chip in range(chips):
            places = pl.ds(chip * height, height)
            pair_rows = pl.ds(chip % 2 * height, height)
            pair = dpair_ref[chip // 2, 1, pair_rows, :] + taken[chip // 2, pair_rows, :].astype(F32)
            grad = jnp.concatenate([dquery_ref[places, :], pair], axis=1)
            proj_ref[chip] = rotate(grad, cosine_ref[places, :], -sine_ref[places, :]).astype(BF)

    run_scatter(reps, partial, finish, scratch[:SCATTER_REFS], turn_back)

    @pl.when(row > 0)
    def _():
        push.wait_send()


def lift(hidden_one, hidden_two, weight_one, weight_two, middle, dquery, dpairs, cosine, sine, reps):
    sub = middle.shape[0]
    parts, rows, width = weight_one.shape
    tokens, heads = dquery.shape
    halves, _, slots, lanes = dpairs.shape
    return pl.pallas_call(
        functools.partial(lift_kernel, reps),
        out_shape=[
            jax.ShapeDtypeStruct((sub * parts, width), BF),
            jax.ShapeDtypeStruct((COLS, tokens // COLS, heads + lanes), BF),
        ],
        in_specs=[VMEM] * 2 + [HBM] * 2 + [VMEM] * 5,
        out_specs=[VMEM] * 2,
        scratch_shapes=scatter_scratch(sub)
        + [pltpu.VMEM((parts, rows // 3, width), BF)] * 2
        + [DMA((2,))]
        + [pltpu.VMEM((halves, slots, lanes), BF)] * 2
        + [DMA, DMA],
        compiler_params=params(7),
        cost_estimate=takes(50),
        name="lift",
    )(hidden_one, hidden_two, weight_one, weight_two, middle, dquery, dpairs, cosine, sine)


PEERS = ("SO", "P", "SP", "Q", "SQ", "D", "SD")


def project_back_kernel(
    reps, proj_ref, weight_ref, source_ref, middle_ref, gains_ref, gain_two_ref, resid_ref, gain_ref, *scratch
):
    gain_own, gain_rows, gain_plane, row_send, row_recv, plane_send, plane_recv = scratch[SCATTER_REFS:]
    where = plane(reps)
    row = lax.axis_index("row")
    partners = row_partners()
    meet([where[kind][2] for kind in PEERS] + [{"row": partner} for partner in partners])
    gain_own[...] = jnp.zeros_like(gain_own)
    gain_own[1:2, :] = gain_two_ref[0:1, :]

    def partial(step, chip, put):
        for index in range(D // SPAN):
            columns = pl.ds(index * SPAN, SPAN)
            put(columns, dot(proj_ref[chip], weight_ref[columns, :], 1, 1))

    def finish(piece, rows, value):
        back, gain_part = norm_back(value, source_ref[rows, :].astype(F32), gains_ref[0:1, :])
        put_by_row(resid_ref, piece, middle_ref[rows, :] + back)
        gain_own[0:1, :] += gain_part

    run_scatter(reps, partial, finish, scratch[:SCATTER_REFS])
    width = gain_ref.shape[1]
    copies = []
    for shift, partner in enumerate(partners):
        copy = pltpu.make_async_remote_copy(
            src_ref=gain_own.at[:, tile(partner, width)],
            dst_ref=gain_rows.at[shift],
            send_sem=row_send.at[shift],
            recv_sem=row_recv.at[shift],
            device_id={"row": partner},
            device_id_type=MESH,
        )
        copy.start()
        copies.append(copy)
    for copy in copies:
        copy.wait()
    total = gain_own[:, tile(row, width)]
    for shift in range(len(partners)):
        total += gain_rows[shift]
    own = where["O"][0] * 2 + where["O"][1]
    gain_plane[own] = total

    def share(index, place):
        return pltpu.make_async_remote_copy(
            src_ref=gain_plane.at[place],
            dst_ref=gain_plane.at[place],
            send_sem=plane_send.at[index],
            recv_sem=plane_recv.at[place],
            device_id=where[PEERS[index]][2],
            device_id_type=MESH,
        )

    for index in range(len(PEERS)):
        share(index, own).start()
    for index, kind in enumerate(PEERS):
        share(index, where[kind][0] * 2 + where[kind][1]).wait_recv()
    total = gain_plane[0]
    for place in range(1, 2 * COLS):
        total += gain_plane[place]
    gain_ref[...] = total
    for index in range(len(PEERS)):
        share(index, own).wait_send()


def project_back(grad_proj, weight, source, grad_middle, gains, gain_two, reps, rows):
    sub = source.shape[0]
    width = D // rows
    return pl.pallas_call(
        functools.partial(project_back_kernel, reps),
        out_shape=[
            jax.ShapeDtypeStruct((sub * rows, width), BF),
            jax.ShapeDtypeStruct((8, width), F32),
        ],
        in_specs=[VMEM] * 6,
        out_specs=[VMEM] * 2,
        scratch_shapes=scatter_scratch(sub)
        + [
            pltpu.VMEM((8, D), F32),
            pltpu.VMEM((rows - 1, 8, width), F32),
            pltpu.VMEM((2 * COLS, 8, width), F32),
            DMA((rows - 1,)),
            DMA((rows - 1,)),
            DMA((len(PEERS),)),
            DMA((2 * COLS,)),
        ],
        compiler_params=params(8),
        cost_estimate=takes(55),
        name="project_back",
    )(grad_proj, weight, source, grad_middle, gains, gain_two)


def adamw(weights, gradient, moment, square, step_rate, decay_rate):
    gradient = gradient.astype(F32)
    moment_new = BETA_ONE * moment + (1.0 - BETA_ONE) * gradient
    square_new = BETA_TWO * square + (1.0 - BETA_TWO) * gradient * gradient
    moment_hat = moment_new / (1.0 - BETA_ONE**STEP)
    square_hat = square_new / (1.0 - BETA_TWO**STEP)
    weights_new = weights - step_rate * (
        moment_hat / (jnp.sqrt(square_hat) + ADAM_EPS) + decay_rate * weights
    )
    return (weights_new, moment_new, square_new)


def local(
    resid_in,
    cotangent,
    seq_lens,
    qkv_weight,
    qkv_moment,
    qkv_square,
    out_weight,
    out_moment,
    out_square,
    gate_weight,
    gate_moment,
    gate_square,
    up_weight,
    up_moment,
    up_square,
    down_weight,
    down_moment,
    down_square,
    norm_gains,
    gain_moment,
    gain_square,
):
    cols, rows, replicas = lax.axis_size("col"), lax.axis_size("row"), lax.axis_size("dp")
    reps = replicas // 2
    half = lax.axis_index("dp") // reps
    row, col = lax.axis_index("row"), lax.axis_index("col")
    chunk = resid_in.shape[0]
    sub = chunk // cols
    blocks = 2 * cols
    plane_tokens = sub * blocks
    head_width = (GROUP + 2) * HD

    qkv_block = half_columns(qkv_weight, reps)
    out_block = tall_block(out_weight, reps)
    split = out_block.shape[1] // 2
    stacked = jnp.concatenate([out_block[:, :split], out_block[:, split:]], axis=0)
    first_w = lax.all_gather(jnp.concatenate([qkv_block, stacked], axis=1), "row", axis=0)
    qkv_w = first_w[:, :, :head_width].reshape(D, head_width)
    heads = out_block.shape[0]
    out_w = jnp.concatenate([first_w[:, :heads, head_width:], first_w[:, heads:, head_width:]], axis=2)
    lengths = both_halves(seq_lens, partner_swap(seq_lens, reps), half, 0)
    ends = jnp.cumsum(lengths, axis=1, dtype=jnp.int32)
    slot = (row * chunk + jnp.arange(chunk, dtype=jnp.int32)).reshape(1, chunk)
    passed = (slot[:, :, None] >= ends[:, None, :]).astype(jnp.int32)
    seq_start = jnp.sum(passed * lengths[:, None, :], axis=2, dtype=jnp.int32)
    usable = slot < ends[:, -1:]
    cosine, sine = rope_tables((slot - seq_start).reshape(plane_tokens))
    low = (jnp.where(usable, seq_start, slot) - (row - 1) * chunk).reshape(blocks, 1, sub)
    firsts = jnp.tile(chunk + jnp.arange(cols, dtype=jnp.int32) * sub, 2)
    bounds = jnp.stack([low[:, 0, 0] // KEYS, (firsts + sub - 1) // KEYS + 1, firsts]).astype(jnp.int32)
    usable_mine = (row * chunk + col * sub + jnp.arange(sub, dtype=jnp.int32)) < jnp.sum(seq_lens)

    padded = jnp.concatenate([norm_gains, jnp.zeros((6, norm_gains.shape[1]), F32)])
    source, normed_own, grad_top, gains = exchange(
        resid_in, cotangent, padded, usable_mine.astype(F32)[:, None], rows
    )
    gate_block = half_columns(gate_weight, reps, source)
    up_block = half_columns(up_weight, reps, source)
    down_block = tall_block(down_weight, reps)
    units = gate_block.shape[1] // SLICES
    slice_w = []
    for index in range(SLICES):
        span = slice(index * units, (index + 1) * units)
        block = jnp.concatenate([gate_block[:, span], up_block[:, span], down_block[span]], axis=0)
        slice_w.append(lax.all_gather(block, "row", axis=0))
    normed_one, grad_top_all, queries, pairs = project(normed_own, grad_top, qkv_w, cosine, sine, reps)
    queries = queries.reshape(plane_tokens, GROUP * HD)
    pairs = pairs.reshape(2, 2 * chunk, 2 * HD)
    attended, log_total = attend(queries, pairs, low, bounds)
    middle, normed_own = mix_out(attended.reshape(cols, 2 * sub, GROUP * HD), out_w, source, gains, reps)

    normed_two, hidden_one, ggate_one, gup_one = first_slice(normed_own, grad_top_all, slice_w[0], reps)
    grads_one = slice_grads(normed_two, grad_top_all, hidden_one, ggate_one, gup_one, rows)
    normed_two, grads_one = lax.optimization_barrier((normed_two, grads_one))
    hidden_two, ggate_two, gup_two, grad_middle, grad_middle_own, gain_grad_two = second_slice(
        normed_two, grad_top_all, ggate_one, gup_one, slice_w[0], slice_w[1], middle, grad_top, gains, reps
    )
    grad_attended, grads_two = back_out(
        grad_middle_own, out_w, normed_two, grad_top_all, hidden_two, ggate_two, gup_two,
        attended.reshape(cols, 2 * sub, GROUP * HD), reps,
    )
    slice_g = [lax.psum_scatter(part, "row", scatter_dimension=0) for part in (grads_one, grads_two)]
    grad_attended, slice_g[0] = lax.optimization_barrier((grad_attended, slice_g[0]))
    grad_query, grad_pairs = attend_back(
        queries, grad_attended.reshape(plane_tokens, GROUP * HD), pairs, low, log_total, bounds
    )
    result, grad_proj = lift(
        hidden_one, hidden_two, slice_w[0], slice_w[1], middle,
        grad_query, grad_pairs.reshape(2, 2, chunk, 2 * HD), cosine, sine, reps,
    )
    grad_qkv = dot(normed_one.reshape(plane_tokens, D), grad_proj.reshape(plane_tokens, head_width), 0, 0).astype(BF)
    grad_proj, grad_qkv = lax.optimization_barrier((grad_proj, grad_qkv))
    resid_grad, gain_grads = project_back(
        grad_proj, qkv_w, source, grad_middle, gains, gain_grad_two, reps, rows
    )
    result, resid_grad = lax.optimization_barrier((to_rows(result), resid_grad))
    result = to_columns(result)
    grad_qkv = lax.psum_scatter(grad_qkv, "row", scatter_dimension=0, tiled=True)
    wide = 2 * (D // rows)
    slice_g[1], resid_grad = lax.optimization_barrier((slice_g[1], resid_grad))
    halves = [own_slice(part[:wide], reps) for part in slice_g]
    grad_qkv, halves, slice_g[0] = lax.optimization_barrier((grad_qkv, halves, slice_g[0]))
    grad_qkv = own_rows(grad_qkv, reps)
    resid_grad = to_columns(to_rows(resid_grad)).astype(F32)
    pieces = [halves[index][place] for place in range(2) for index in range(SLICES)]
    grad_gate, grad_up = [jnp.concatenate([piece[index] for piece in pieces], axis=1) for index in range(2)]
    grad_down = own_tall(jnp.concatenate([part[wide : wide + units] for part in slice_g], axis=0), reps)
    grad_out = own_tall(slice_g[1][wide + units :], reps)

    gain_grads = gain_grads[:2]
    if reps > 1:
        gain_grads = lax.psum(gain_grads, "dp", axis_index_groups=rep_groups(reps))
    qkv_set = adamw(qkv_weight, grad_qkv, qkv_moment, qkv_square, RATE_MATRIX, WEIGHT_DECAY)
    out_set = adamw(out_weight, grad_out, out_moment, out_square, RATE_OUTPUT, WEIGHT_DECAY)
    gate_set = adamw(gate_weight, grad_gate, gate_moment, gate_square, RATE_MATRIX, WEIGHT_DECAY)
    up_set = adamw(up_weight, grad_up, up_moment, up_square, RATE_MATRIX, WEIGHT_DECAY)
    down_set = adamw(down_weight, grad_down, down_moment, down_square, RATE_MATRIX, WEIGHT_DECAY)
    gain_set = adamw(norm_gains, gain_grads, gain_moment, gain_square, RATE_GAIN, 0.0)
    return (result, resid_grad, *qkv_set, *out_set, *gate_set, *up_set, *down_set, *gain_set)


def solution(mesh):
    tokens = P(("dp", "col"), "row")
    wide = P(("row", "dp"), "col")
    tall = P(("col", "dp"), "row")
    gain = P(None, "row")
    weights = (wide,) * 3 + (tall,) * 3 + (wide,) * 6 + (tall,) * 3 + (gain,) * 3
    return jax.shard_map(
        local,
        mesh=mesh,
        in_specs=(tokens, tokens, P("dp", None)) + weights,
        out_specs=(tokens, tokens) + weights,
        check_vma=False,
    )
```

```python
import functools

import jax
import jax.numpy as jnp
from jax import lax
from jax.experimental import pallas as pl
from jax.experimental.pallas import tpu as pltpu
from jax.sharding import PartitionSpec as P

D = 2048
FF = 8192
HD = 64
GROUP = 4
LMAX = 1024
STEP = 10
KEYS = 256
SLICES = 2
PIECES = 4
COLS = 4

EPS_NORM = 1e-05
ROPE_BASE = 500000.0
BETA_ONE = 0.9
BETA_TWO = 0.95
ADAM_EPS = 1e-08
WEIGHT_DECAY = 0.1
RATE_MATRIX = 0.05
RATE_OUTPUT = 0.4
RATE_GAIN = 0.8
MASKED = -1e30
SCALE = HD ** (-0.5)

BF = jnp.bfloat16
F32 = jnp.float32


def dot(left, right, left_dim, right_dim):
    return lax.dot_general(
        left, right, (((left_dim,), (right_dim,)), ((), ())), preferred_element_type=F32
    )


def half_groups(reps):
    return [[rep, rep + reps] for rep in range(reps)]


def rep_groups(reps):
    return [[half * reps + rep for rep in range(reps)] for half in range(2)]


def partner_swap(values_in, reps):
    pairs = [pair for rep in range(reps) for pair in ((rep, rep + reps), (rep + reps, rep))]
    return lax.ppermute(values_in, "dp", pairs)


def both_halves(mine, theirs, half, axis):
    first = jnp.where(half == 0, mine, theirs)
    second = jnp.where(half == 0, theirs, mine)
    return jnp.concatenate([first, second], axis=axis)


def half_columns(weight, reps, after=None):
    half = lax.axis_index("dp") // reps
    own, width = weight.shape[0], weight.shape[1] // 2
    low = weight.astype(BF)
    mine = lax.dynamic_slice_in_dim(low, half * width, width, 1)
    theirs = partner_swap(lax.dynamic_slice_in_dim(low, (1 - half) * width, width, 1), reps)
    if after is not None:
        theirs, _ = lax.optimization_barrier((theirs, after))
    both = both_halves(mine, theirs, half, 0)
    if reps > 1:
        both = lax.all_gather(both, "dp", axis=0, axis_index_groups=rep_groups(reps))
        both = both.reshape(reps, 2, own, width).swapaxes(0, 1).reshape(2 * reps * own, width)
    return both


def own_rows(part, reps):
    half = lax.axis_index("dp") // reps
    height = part.shape[0] // 2
    mine = lax.dynamic_slice_in_dim(part, half * height, height, 0)
    theirs = partner_swap(lax.dynamic_slice_in_dim(part, (1 - half) * height, height, 0), reps)
    part = both_halves(mine, theirs, half, 1)
    if reps > 1:
        part = lax.psum_scatter(
            part, "dp", scatter_dimension=0, tiled=True, axis_index_groups=rep_groups(reps)
        )
    return part


def own_slice(part, reps):
    half = lax.axis_index("dp") // reps
    units = part.shape[1]
    split = part.reshape(2, 2, -1, units)
    mine = lax.dynamic_index_in_dim(split, half, 1, False)
    theirs = partner_swap(lax.dynamic_index_in_dim(split, 1 - half, 1, False), reps)
    halves = [jnp.where(half == 0, mine, theirs), jnp.where(half == 0, theirs, mine)]
    if reps > 1:
        halves = [
            lax.psum_scatter(piece, "dp", scatter_dimension=1, tiled=True, axis_index_groups=rep_groups(reps))
            for piece in halves
        ]
    return halves


def tall_block(weight, reps):
    own = weight.astype(BF)
    if reps > 1:
        own = lax.all_gather(own, "dp", axis=0, tiled=True, axis_index_groups=rep_groups(reps))
    return own


def own_tall(part, reps):
    if reps > 1:
        part = lax.psum_scatter(
            part, "dp", scatter_dimension=0, tiled=True, axis_index_groups=rep_groups(reps)
        )
    return part


def row_blocks(matrix, rows):
    return matrix.reshape(matrix.shape[0], rows, -1).swapaxes(0, 1)


def rope_tables(position):
    exponent = jnp.arange(0, HD, 2, dtype=F32) / HD
    freq_table = 1.0 / ROPE_BASE**exponent
    angle = position.astype(F32)[:, None] * freq_table[None, :]
    cosine = jnp.cos(angle)
    sine = jnp.sin(angle)
    return (jnp.concatenate([cosine] * 4, axis=1), jnp.concatenate([-sine, sine, -sine, sine], axis=1))


def rotate(vectors, cosine, sine):
    width = vectors.shape[1]
    lane = lax.broadcasted_iota(jnp.int32, vectors.shape, 1)
    lower = lax.rem(lane, HD) < HD // 2
    turned = jnp.where(
        lower, pltpu.roll(vectors, width - HD // 2, 1), pltpu.roll(vectors, HD // 2, 1)
    )
    copies = width // cosine.shape[1]
    cosine = jnp.concatenate([cosine] * copies, axis=1)
    sine = jnp.concatenate([sine] * copies, axis=1)
    return jnp.where(lane < (GROUP + 1) * HD, vectors * cosine + turned * sine, vectors)


MESH = pl.DeviceIdType.MESH
HBM = pl.BlockSpec(memory_space=pl.ANY)
VMEM = pl.BlockSpec(memory_space=pltpu.VMEM)
DMA = pltpu.SemaphoreType.DMA


def takes(micros):
    return pl.CostEstimate(flops=1, bytes_accessed=int(micros * 3.6e6), transcendentals=0)


def params(collective_id):
    return pltpu.CompilerParams(
        collective_id=collective_id, has_side_effects=True, vmem_limit_bytes=60 * 2**20
    )


def tile(index, width):
    return pl.ds(pl.multiple_of(index * width, width), width)


def plane(reps):
    replica, col = lax.axis_index("dp"), lax.axis_index("col")
    half, rep = lax.div(replica, reps), lax.rem(replica, reps)
    core = lax.rem(col, 2)
    other = col + 1 - 2 * core

    def place(half_of, col_of):
        chip = half_of * (COLS // 2) + lax.div(col_of, 2)
        return (chip, lax.rem(col_of, 2), {"dp": half_of * reps + rep, "col": col_of})

    def turn(value, by, modulus):
        return lax.rem(value + by, modulus)

    return {
        "O": place(half, col),
        "P": place(turn(half, 1 - core, 2), turn(col, 2 * core, COLS)),
        "Q": place(turn(half, core, 2), turn(col, 2 - 2 * core, COLS)),
        "D": place(1 - half, turn(col, 2, COLS)),
        "SO": place(half, other),
        "SP": place(turn(half, core, 2), turn(other, 2 - 2 * core, COLS)),
        "SQ": place(turn(half, 1 - core, 2), turn(other, 2 * core, COLS)),
        "SD": place(1 - half, turn(other, 2, COLS)),
    }


def near(reps):
    where = plane(reps)
    return [where["P"][2], where["Q"][2], where["SO"][2]]


def row_partners():
    rows, row = lax.axis_size("row"), lax.axis_index("row")
    return [lax.rem(row + shift, rows) for shift in range(1, rows)]


def signal(devices):
    barrier = pltpu.get_barrier_semaphore()
    for device in devices:
        pl.semaphore_signal(barrier, inc=1, device_id=device, device_id_type=MESH)


def meet(devices):
    signal(devices)
    pl.semaphore_wait(pltpu.get_barrier_semaphore(), len(devices))


GATHER_KINDS = ("P", "Q", "D", "SO", "SP", "SQ", "SD")


def run_gather(reps, own_ref, held_ref, sems, use):
    send_sems, recv_sems, local_sem = sems
    where = plane(reps)
    sub = own_ref.shape[0]
    height = sub // PIECES

    def spot(kind, piece):
        chip, core, _ = where[kind]
        return held_ref.at[chip, pl.ds(pl.multiple_of(core * sub + piece * height, height), height)]

    def message(kind, piece, source, target, device):
        index = GATHER_KINDS.index(kind)
        return pltpu.make_async_remote_copy(
            src_ref=source,
            dst_ref=target,
            send_sem=send_sems.at[index, piece],
            recv_sem=recv_sems.at[index, piece],
            device_id=device,
            device_id_type=MESH,
        )

    near_p, near_q, sibling = where["P"][2], where["Q"][2], where["SO"][2]
    sent = []

    def send(kind, piece, source, held_by, device):
        copy = message(kind, piece, source, spot(held_by, piece), device)
        copy.start()
        sent.append(copy)

    def arrive(kind, piece):
        message(kind, piece, spot(kind, piece), spot(kind, piece), sibling).wait_recv()

    own_copy = pltpu.make_async_copy(own_ref, held_ref.at[where["O"][0], tile(where["O"][1], sub)], local_sem)
    own_copy.start()
    for piece in range(PIECES):
        source = own_ref.at[pl.ds(piece * height, height)]
        send("P", piece, source, "O", near_p)
        send("Q", piece, source, "O", near_q)
        send("SO", piece, source, "O", sibling)
    own_copy.wait()
    for piece in range(PIECES):
        arrive("SO", piece)
    use(0, where["O"][0])
    for piece in range(PIECES):
        arrive("P", piece)
        send("D", piece, spot("P", piece), "P", near_q)
        send("SP", piece, spot("P", piece), "P", sibling)
    for piece in range(PIECES):
        arrive("Q", piece)
        send("SQ", piece, spot("Q", piece), "Q", sibling)
    for piece in range(PIECES):
        arrive("SQ", piece)
    use(1, where["P"][0])
    for piece in range(PIECES):
        arrive("SP", piece)
    use(2, where["Q"][0])
    for piece in range(PIECES):
        arrive("D", piece)
        send("SD", piece, spot("D", piece), "D", sibling)
    for piece in range(PIECES):
        arrive("SD", piece)
    use(3, where["D"][0])
    for copy in sent:
        copy.wait_send()


def gather_scratch(sub):
    count = len(GATHER_KINDS)
    return [pltpu.VMEM((COLS, 2 * sub, D), BF), DMA((count, PIECES)), DMA((count, PIECES)), DMA]


SCATTER_SWAPS = ("D", "Q", "P", "O")
SCATTER_HOPS = ("D", "Q", "P")


def scatter_order(reps):
    where = plane(reps)
    return [where[kind][0] for kind in SCATTER_SWAPS]


def run_scatter(reps, partial, finish, scratch, meanwhile=None):
    total_ref, give_ref, take_ref, hop_out, hop_in, both_ref, swap_send, swap_recv, hop_send, hop_recv = scratch
    where = plane(reps)
    core = where["O"][1]
    device = {"P": where["P"][2], "Q": where["Q"][2], "D": where["Q"][2]}
    sibling = where["SO"][2]
    sub = total_ref.shape[1]
    height = sub // PIECES
    sibling_kind = {"D": "D", "Q": "P", "P": "Q", "O": "O"}
    sent = []

    def swap(kind):
        index = SCATTER_SWAPS.index(kind)
        return pltpu.make_async_remote_copy(
            src_ref=give_ref.at[index],
            dst_ref=take_ref.at[index],
            send_sem=swap_send.at[index],
            recv_sem=swap_recv.at[index],
            device_id=sibling,
            device_id_type=MESH,
        )

    def hop(kind, piece):
        index = SCATTER_HOPS.index(kind)
        rows = pl.ds(piece * height, height)
        return pltpu.make_async_remote_copy(
            src_ref=hop_out.at[index, rows],
            dst_ref=hop_in.at[index, rows],
            send_sem=hop_send.at[index, piece],
            recv_sem=hop_recv.at[index, piece],
            device_id=device[kind],
            device_id_type=MESH,
        )

    def compute(step, kind):
        mine, theirs = SCATTER_SWAPS.index(kind), SCATTER_SWAPS.index(sibling_kind[kind])

        def put(columns, value):
            both_ref[...] = value
            total_ref[mine, :, columns] = both_ref[tile(core, sub), :]
            give_ref[theirs, :, columns] = both_ref[tile(1 - core, sub), :].astype(BF)

        partial(step, where[kind][0], put)
        copy = swap(sibling_kind[kind])
        copy.start()
        sent.append(copy)

    def settle(kind):
        index = SCATTER_SWAPS.index(kind)
        swap(kind).wait_recv()
        for piece in range(PIECES):
            rows = pl.ds(piece * height, height)
            value = total_ref[index, rows, :] + take_ref[index, rows, :].astype(F32)
            if kind == "P":
                hop("D", piece).wait_recv()
                value += hop_in[SCATTER_HOPS.index("D"), rows, :].astype(F32)
            if kind == "O":
                for source in ("Q", "P"):
                    hop(source, piece).wait_recv()
                    value += hop_in[SCATTER_HOPS.index(source), rows, :].astype(F32)
                finish(piece, rows, value)
            else:
                hop_out[SCATTER_HOPS.index(kind), rows, :] = value.astype(BF)
                copy = hop(kind, piece)
                copy.start()
                sent.append(copy)

    compute(0, "D")
    compute(1, "Q")
    settle("D")
    compute(2, "P")
    settle("Q")
    compute(3, "O")
    if meanwhile is not None:
        meanwhile()
    settle("P")
    settle("O")
    for copy in sent:
        copy.wait_send()


SPAN = 512


def scatter_scratch(sub):
    return [
        pltpu.VMEM((4, sub, D), F32),
        pltpu.VMEM((4, sub, D), BF),
        pltpu.VMEM((4, sub, D), BF),
        pltpu.VMEM((3, sub, D), BF),
        pltpu.VMEM((3, sub, D), BF),
        pltpu.VMEM((2 * sub, SPAN), F32),
        DMA((4,)),
        DMA((4,)),
        DMA((3, PIECES)),
        DMA((3, PIECES)),
    ]


SCATTER_REFS = 10


def col_partners():
    cols, col = lax.axis_size("col"), lax.axis_index("col")
    return [lax.rem(col + shift, cols) for shift in range(1, cols)]


def put_by_row(out_ref, piece, value):
    height, width = value.shape[0], out_ref.shape[1]
    parts = D // width
    sub = out_ref.shape[0] // parts
    for part in range(parts):
        out_ref[pl.ds(part * sub + piece * height, height), :] = value[:, part * width : (part + 1) * width].astype(BF)


def to_rows(block):
    return lax.all_to_all(block, "row", split_axis=0, concat_axis=0, tiled=True)


def to_columns(block):
    return lax.all_to_all(block, "col", split_axis=0, concat_axis=0, tiled=True)


def head_rows(block):
    turned = block.astype(F32).T
    return [turned[head * HD : (head + 1) * HD].astype(BF) for head in range(GROUP)]


def allowed_entries(key_block, low_ref, query_first):
    tokens = low_ref.shape[-1]
    key_slot = key_block * KEYS + lax.broadcasted_iota(jnp.int32, (KEYS, tokens), 0)
    query_slot = query_first + lax.broadcasted_iota(jnp.int32, (KEYS, tokens), 1)
    return (key_slot >= low_ref[...]) & (key_slot <= query_slot)


def key_rows(block):
    return pl.ds(pl.multiple_of(block * KEYS, KEYS), KEYS)


def attend_kernel(bounds, query_ref, pair_ref, low_ref, out_ref, log_ref, score_ref, mix_ref):
    step = pl.program_id(1)
    place = pl.program_id(0) * pl.num_programs(1) + step
    first, last, query_first = bounds[0, place], bounds[1, place], bounds[2, place]
    tokens = query_ref.shape[0]
    blank = jnp.zeros((HD, tokens), BF)
    queries = [jnp.concatenate([rows, blank], axis=0) for rows in head_rows(query_ref[...])]

    def score_block(block, tops):
        pairs = pair_ref[key_rows(block), :]
        allowed = allowed_entries(block, low_ref, query_first)
        new_tops = []
        for head in range(GROUP):
            scores = jnp.where(allowed, dot(pairs, queries[head], 1, 0), MASKED)
            score_ref[head, key_rows(block - first), :] = scores
            new_tops.append(jnp.maximum(tops[head], jnp.max(scores, axis=0, keepdims=True)))
        return tuple(new_tops)

    start = tuple(jnp.full((1, tokens), MASKED, F32) for _ in range(GROUP))
    tops = lax.fori_loop(first, last, score_block, start)
    mix_ref[...] = jnp.zeros_like(mix_ref)

    def mix_block(block, totals):
        pairs = pair_ref[key_rows(block), :]
        new_totals = []
        for head in range(GROUP):
            terms = jnp.exp(score_ref[head, key_rows(block - first), :] - tops[head])
            new_totals.append(totals[head] + jnp.sum(terms, axis=0, keepdims=True))
            mix_ref[head] += dot(pairs, terms.astype(BF), 0, 0)
        return tuple(new_totals)

    start = tuple(jnp.zeros((1, tokens), F32) for _ in range(GROUP))
    totals = lax.fori_loop(first, last, mix_block, start)
    mixed = jnp.concatenate(
        [mix_ref[head, HD:, :] / totals[head] for head in range(GROUP)], axis=0
    )
    out_ref[...] = mixed.T.astype(BF)
    for head in range(GROUP):
        log_ref[head : head + 1, :] = tops[head] + jnp.log(totals[head])


def attend_back_kernel(
    bounds, query_ref, grad_ref, pair_ref, low_ref, log_ref, dquery_ref, dpair_ref, prob_ref, dprob_ref, dmix_ref
):
    step = pl.program_id(1)
    place = pl.program_id(0) * pl.num_programs(1) + step
    first, last, query_first = bounds[0, place], bounds[1, place], bounds[2, place]
    tokens = query_ref.shape[0]
    blank = jnp.zeros((HD, tokens), BF)
    queries = [jnp.concatenate([rows, blank], axis=0) for rows in head_rows(query_ref[...])]
    grads = [jnp.concatenate([blank, rows], axis=0) for rows in head_rows(grad_ref[...])]

    @pl.when(step == 0)
    def _():
        dpair_ref[...] = jnp.zeros_like(dpair_ref)

    def prob_block(block, inners):
        pairs = pair_ref[key_rows(block), :]
        allowed = allowed_entries(block, low_ref, query_first)
        new_inners = []
        for head in range(GROUP):
            scores = dot(pairs, queries[head], 1, 0)
            probs = jnp.where(allowed, jnp.exp(scores - log_ref[head : head + 1, :]), 0.0)
            dprobs = dot(pairs, grads[head], 1, 0)
            prob_ref[head, key_rows(block - first), :] = probs
            dprob_ref[head, key_rows(block - first), :] = dprobs
            new_inners.append(inners[head] + jnp.sum(probs * dprobs, axis=0, keepdims=True))
        return tuple(new_inners)

    start = tuple(jnp.zeros((1, tokens), F32) for _ in range(GROUP))
    inners = lax.fori_loop(first, last, prob_block, start)
    dmix_ref[...] = jnp.zeros_like(dmix_ref)
    all_queries = jnp.concatenate(queries, axis=1)
    all_grads = jnp.concatenate(grads, axis=1)

    def back_block(block, carry):
        rows = key_rows(block)
        pairs = pair_ref[rows, :]
        all_probs, all_scores = [], []
        for head in range(GROUP):
            probs = prob_ref[head, key_rows(block - first), :]
            dprobs = dprob_ref[head, key_rows(block - first), :]
            dscores = (probs * (dprobs - inners[head])).astype(BF)
            dmix_ref[head] += dot(pairs, dscores, 0, 0)
            all_probs.append(probs.astype(BF))
            all_scores.append(dscores)
        dpair_ref[rows, :] += dot(jnp.concatenate(all_scores, axis=1), all_queries, 1, 1) + dot(
            jnp.concatenate(all_probs, axis=1), all_grads, 1, 1
        )
        return carry

    lax.fori_loop(first, last, back_block, 0)
    dquery = jnp.concatenate([dmix_ref[head, :HD, :] for head in range(GROUP)], axis=0)
    dquery_ref[...] = dquery.T * SCALE


def attend(queries, pairs, low, bounds):
    tokens, width = queries.shape
    replicas, slots, _ = pairs.shape
    rows = low.shape[2]
    blocks = low.shape[0] // replicas
    span = LMAX + KEYS
    return pl.pallas_call(
        attend_kernel,
        grid_spec=pltpu.PrefetchScalarGridSpec(
            num_scalar_prefetch=1,
            grid=(replicas, blocks),
            in_specs=[
                pl.BlockSpec((rows, GROUP * HD), lambda rep, block, _: (rep * blocks + block, 0)),
                pl.BlockSpec((None, slots, 2 * HD), lambda rep, block, _: (rep, 0, 0)),
                pl.BlockSpec((None, 1, rows), lambda rep, block, _: (rep * blocks + block, 0, 0)),
            ],
            out_specs=[
                pl.BlockSpec((rows, GROUP * HD), lambda rep, block, _: (rep * blocks + block, 0)),
                pl.BlockSpec((None, None, GROUP, rows), lambda rep, block, _: (rep, block, 0, 0)),
            ],
            scratch_shapes=[
                pltpu.VMEM((GROUP, span, rows), F32),
                pltpu.VMEM((GROUP, 2 * HD, rows), F32),
            ],
        ),
        out_shape=[
            jax.ShapeDtypeStruct((tokens, width), BF),
            jax.ShapeDtypeStruct((replicas, blocks, GROUP, rows), F32),
        ],
        compiler_params=pltpu.CompilerParams(vmem_limit_bytes=48 * 2**20),
        cost_estimate=takes(14),
        name="attend",
    )(bounds, queries, pairs, low)


def attend_back(queries, grads, pairs, low, log_total, bounds):
    tokens, width = queries.shape
    replicas, slots, _ = pairs.shape
    rows = low.shape[2]
    blocks = low.shape[0] // replicas
    span = LMAX + KEYS
    return pl.pallas_call(
        attend_back_kernel,
        grid_spec=pltpu.PrefetchScalarGridSpec(
            num_scalar_prefetch=1,
            grid=(replicas, blocks),
            in_specs=[
                pl.BlockSpec((rows, GROUP * HD), lambda rep, block, _: (rep * blocks + block, 0)),
                pl.BlockSpec((rows, GROUP * HD), lambda rep, block, _: (rep * blocks + block, 0)),
                pl.BlockSpec((None, slots, 2 * HD), lambda rep, block, _: (rep, 0, 0)),
                pl.BlockSpec((None, 1, rows), lambda rep, block, _: (rep * blocks + block, 0, 0)),
                pl.BlockSpec((None, None, GROUP, rows), lambda rep, block, _: (rep, block, 0, 0)),
            ],
            out_specs=[
                pl.BlockSpec((rows, GROUP * HD), lambda rep, block, _: (rep * blocks + block, 0)),
                pl.BlockSpec((None, slots, 2 * HD), lambda rep, block, _: (rep, 0, 0)),
            ],
            scratch_shapes=[
                pltpu.VMEM((GROUP, span, rows), F32),
                pltpu.VMEM((GROUP, span, rows), F32),
                pltpu.VMEM((GROUP, 2 * HD, rows), F32),
            ],
        ),
        out_shape=[
            jax.ShapeDtypeStruct((tokens, width), F32),
            jax.ShapeDtypeStruct((replicas, slots, 2 * HD), F32),
        ],
        compiler_params=pltpu.CompilerParams(vmem_limit_bytes=48 * 2**20),
        cost_estimate=takes(23),
        name="attend_back",
    )(bounds, queries, grads, pairs, low, log_total)


def norm_of(vectors):
    scaling = lax.rsqrt(jnp.mean(vectors * vectors, axis=1, keepdims=True) + EPS_NORM)
    return vectors * scaling, scaling


def norm_back(value, vectors, gain):
    unit, scaling = norm_of(vectors)
    weighted = value * gain
    inner = jnp.mean(weighted * unit, axis=1, keepdims=True)
    return scaling * (weighted - unit * inner), jnp.sum(value * unit, axis=0, keepdims=True)


def exchange_kernel(
    token_ref, top_ref, gain_ref, usable_ref, source_ref, normed_ref, grad_top_ref, gains_ref,
    held, held_top, mid, mid_top, held_gains, col_send, col_recv, row_send, row_recv, gain_send, gain_recv, local_sems,
):
    row, col = lax.axis_index("row"), lax.axis_index("col")
    sub, width = held.shape[0], token_ref.shape[1]
    row_of = row_partners()
    col_of = col_partners()
    meet([{"row": partner} for partner in row_of] + [{"col": partner} for partner in col_of])
    own_cols = tile(row, width)

    def run(copies):
        for copy in copies:
            copy.start()
        return copies

    def finish(copies):
        for copy in copies:
            copy.wait()

    def remote(source, target, send_sem, recv_sem, device):
        return pltpu.make_async_remote_copy(
            src_ref=source, dst_ref=target, send_sem=send_sem, recv_sem=recv_sem, device_id=device, device_id_type=MESH
        )

    def to_columns(array, source, target):
        return run(
            [
                remote(
                    source.at[tile(partner, sub)], target.at[col],
                    col_send.at[array, shift], col_recv.at[array, shift], {"col": partner},
                )
                for shift, partner in enumerate(col_of)
            ]
            + [pltpu.make_async_copy(source.at[tile(col, sub)], target.at[col], local_sems.at[array, 0])]
        )

    def to_rows(array, source, target):
        return run(
            [
                remote(
                    source.at[partner], target.at[:, own_cols],
                    row_send.at[array, shift], row_recv.at[array, shift], {"row": partner},
                )
                for shift, partner in enumerate(row_of)
            ]
            + [pltpu.make_async_copy(source.at[row], target.at[:, own_cols], local_sems.at[array, 1])]
        )

    tokens = to_columns(0, token_ref, mid)
    gains = run(
        [
            remote(gain_ref, held_gains.at[:, own_cols], gain_send.at[shift], gain_recv.at[shift], {"row": partner})
            for shift, partner in enumerate(row_of)
        ]
        + [pltpu.make_async_copy(gain_ref, held_gains.at[:, own_cols], local_sems.at[2, 0])]
    )
    tops = to_columns(1, top_ref, mid_top)
    finish(tokens)
    tokens = to_rows(0, mid, held)
    finish(tops)
    tops = to_rows(1, mid_top, held_top)
    finish(gains)
    finish(tokens)
    source_ref[...] = held[...]
    gains_ref[...] = held_gains[...]
    unit, _ = norm_of(held[...].astype(F32))
    normed_ref[...] = (unit * held_gains[0:1, :]).astype(BF)
    finish(tops)
    grad_top_ref[...] = (held_top[...].astype(F32) * usable_ref[...]).astype(BF)


def exchange(tokens, top, gains, usable, rows):
    sub, width = tokens.shape[0] // COLS, tokens.shape[1]
    block = jax.ShapeDtypeStruct((sub, rows * width), BF)
    return pl.pallas_call(
        exchange_kernel,
        out_shape=[block, block, block, jax.ShapeDtypeStruct((gains.shape[0], rows * width), F32)],
        in_specs=[VMEM] * 4,
        out_specs=[VMEM] * 4,
        scratch_shapes=[pltpu.VMEM((sub, rows * width), BF)] * 2
        + [pltpu.VMEM((COLS, sub, width), BF)] * 2
        + [
            pltpu.VMEM((gains.shape[0], rows * width), F32),
            DMA((2, COLS - 1)),
            DMA((2, COLS - 1)),
            DMA((2, rows - 1)),
            DMA((2, rows - 1)),
            DMA((rows - 1,)),
            DMA((rows - 1,)),
            DMA((3, 2)),
        ],
        compiler_params=params(1),
        cost_estimate=takes(65),
        name="exchange",
    )(tokens, top, gains, usable)


def project_kernel(
    reps, own_ref, top_ref, weight_ref, cosine_ref, sine_ref,
    all_ref, top_all_ref, query_ref, pair_ref,
    held, send_sems, recv_sems, local_sem, top_held, top_send, top_recv, top_local,
    queries, pairs, halo, out_sems, pair_sems, halo_sems, pair_send, pair_recv,
):
    row, rows = lax.axis_index("row"), lax.axis_size("row")
    meet(near(reps) + [{"row": partner} for partner in row_partners()])
    sub = own_ref.shape[0]
    copies, chips = [], []
    has_next, has_last = row < rows - 1, row > 0

    @pl.when(row == 0)
    def _():
        halo[...] = jnp.zeros_like(halo)

    def out(source, target, sem):
        copy = pltpu.make_async_copy(source, target, sem)
        copy.start()
        copies.append(copy)

    def push(step, chip):
        return pltpu.make_async_remote_copy(
            src_ref=pairs.at[chip],
            dst_ref=halo.at[chip],
            send_sem=pair_send.at[step],
            recv_sem=pair_recv.at[step],
            device_id={"row": lax.rem(row + 1, rows)},
            device_id_type=MESH,
        )

    def use(step, chip):
        chips.append(chip)
        out(held.at[chip], all_ref.at[chip], out_sems.at[step])
        places = tile(chip, 2 * sub)
        turned = rotate(dot(held[chip], weight_ref[...], 1, 0), cosine_ref[places, :], sine_ref[places, :])
        queries[chip] = (turned[:, : GROUP * HD] * SCALE).astype(BF)
        out(queries.at[chip], query_ref.at[chip], out_sems.at[COLS + step])
        pairs[chip] = turned[:, GROUP * HD :].astype(BF)
        out(pairs.at[chip], pair_ref.at[lax.div(chip, 2), 1, lax.rem(chip, 2)], pair_sems.at[step])

        @pl.when(has_next)
        def _():
            push(step, chip).start()

    run_gather(reps, own_ref, held, (send_sems, recv_sems, local_sem), use)

    def use_top(step, chip):
        out(top_held.at[chip], top_all_ref.at[chip], out_sems.at[2 * COLS + step])

    run_gather(reps, top_ref, top_held, (top_send, top_recv, top_local), use_top)
    for step, chip in enumerate(chips):

        @pl.when(has_next)
        def _():
            push(step, chip).wait_send()

        @pl.when(has_last)
        def _():
            push(step, chip).wait_recv()

    for chip in range(COLS):
        out(halo.at[chip], pair_ref.at[chip // 2, 0, chip % 2], halo_sems.at[chip])
    for copy in copies:
        copy.wait()


def project(normed_own, top_own, weight, cosine, sine, reps):
    sub = normed_own.shape[0]
    return pl.pallas_call(
        functools.partial(project_kernel, reps),
        out_shape=[
            jax.ShapeDtypeStruct((COLS, 2 * sub, D), BF),
            jax.ShapeDtypeStruct((COLS, 2 * sub, D), BF),
            jax.ShapeDtypeStruct((COLS, 2 * sub, GROUP * HD), BF),
            jax.ShapeDtypeStruct((2, 2, COLS // 2, 2 * sub, 2 * HD), BF),
        ],
        in_specs=[VMEM] * 5,
        out_specs=[HBM] * 4,
        scratch_shapes=gather_scratch(sub)
        + gather_scratch(sub)
        + [
            pltpu.VMEM((COLS, 2 * sub, GROUP * HD), BF),
            pltpu.VMEM((COLS, 2 * sub, 2 * HD), BF),
            pltpu.VMEM((COLS, 2 * sub, 2 * HD), BF),
            DMA((3 * COLS,)),
            DMA((COLS,)),
            DMA((COLS,)),
            DMA((COLS,)),
            DMA((COLS,)),
        ],
        compiler_params=params(2),
        cost_estimate=takes(75),
        name="project",
    )(normed_own, top_own, weight, cosine, sine)


def mix_out_kernel(reps, attended_ref, weight_ref, source_ref, gains_ref, middle_ref, normed_ref, *scratch):
    meet(near(reps))
    parts, _, width = weight_ref.shape

    def partial(step, chip, put):
        for part in range(parts):
            put(pl.ds(part * width, width), dot(attended_ref[chip], weight_ref[part], 1, 0))

    def finish(piece, rows, value):
        middle = source_ref[rows, :].astype(F32) + value
        middle_ref[rows, :] = middle
        normed_ref[rows, :] = (norm_of(middle)[0] * gains_ref[1:2, :]).astype(BF)

    run_scatter(reps, partial, finish, scratch)


def mix_out(attended, weight, source, gains, reps):
    sub = source.shape[0]
    return pl.pallas_call(
        functools.partial(mix_out_kernel, reps),
        out_shape=[jax.ShapeDtypeStruct((sub, D), F32), jax.ShapeDtypeStruct((sub, D), BF)],
        in_specs=[VMEM] * 4,
        out_specs=[VMEM] * 2,
        scratch_shapes=scatter_scratch(sub),
        compiler_params=params(3),
        cost_estimate=takes(44),
        name="mix_out",
    )(attended, weight, source, gains)


def gated(tokens, top, weight_ref, put):
    parts, rows, width = weight_ref.shape
    units, span = rows // 3, 256

    def one_tile(index, carry):
        columns = tile(index, span)
        gate_w = weight_ref[:, :units, columns].reshape(D, span)
        up_w = weight_ref[:, units : 2 * units, columns].reshape(D, span)
        gate = dot(tokens, gate_w, 1, 0)
        up = dot(tokens, up_w, 1, 0)
        down_rows = pl.ds(pl.multiple_of(2 * units + index * span, span), span)
        grad = dot(top[:, :width], weight_ref[0, down_rows, :], 1, 1)
        for part in range(1, parts):
            grad += dot(top[:, part * width : (part + 1) * width], weight_ref[part, down_rows, :], 1, 1)
        sigma = 1.0 / (1.0 + jnp.exp(-gate))
        active = gate * sigma
        put(
            columns,
            (active * up).astype(BF),
            (grad * up * sigma * (1.0 + gate * (1.0 - sigma))).astype(BF),
            (grad * active).astype(BF),
        )
        return carry

    lax.fori_loop(0, units // span, one_tile, 0)


def first_slice_kernel(
    reps, own_ref, top_ref, weight_ref, all_ref, hidden_ref, ggate_ref, gup_ref,
    held, send_sems, recv_sems, local_sem, tops, hiddens, ggates, gups, top_sems, out_sems,
):
    meet(near(reps))
    where = plane(reps)
    order = [where[kind][0] for kind in ("O", "P", "Q", "D")]
    loads = [pltpu.make_async_copy(top_ref.at[chip], tops.at[chip], top_sems.at[step]) for step, chip in enumerate(order)]
    for copy in loads:
        copy.start()
    copies = []

    def use(step, chip):
        def out(source, target, index):
            copy = pltpu.make_async_copy(source.at[chip], target.at[chip], out_sems.at[index, step])
            copy.start()
            copies.append(copy)

        out(held, all_ref, 0)
        loads[step].wait()

        def put(columns, hidden, ggate, gup):
            hiddens[chip, :, columns] = hidden
            ggates[chip, :, columns] = ggate
            gups[chip, :, columns] = gup

        gated(held[chip], tops[chip], weight_ref, put)
        out(hiddens, hidden_ref, 1)
        out(ggates, ggate_ref, 2)
        out(gups, gup_ref, 3)

    run_gather(reps, own_ref, held, (send_sems, recv_sems, local_sem), use)
    for copy in copies:
        copy.wait()


def first_slice(normed_own, top_all, weight, reps):
    sub = normed_own.shape[0]
    units = weight.shape[1] // 3
    piece = jax.ShapeDtypeStruct((COLS, 2 * sub, units), BF)
    return pl.pallas_call(
        functools.partial(first_slice_kernel, reps),
        out_shape=[jax.ShapeDtypeStruct((COLS, 2 * sub, D), BF)] + [piece] * 3,
        in_specs=[VMEM, HBM, VMEM],
        out_specs=[HBM] * 4,
        scratch_shapes=gather_scratch(sub)
        + [pltpu.VMEM((COLS, 2 * sub, D), BF)]
        + [pltpu.VMEM((COLS, 2 * sub, units), BF)] * 3
        + [DMA((COLS,)), DMA((4, COLS))],
        compiler_params=params(4),
        cost_estimate=takes(50),
        name="first_slice",
    )(normed_own, top_all, weight)


def second_slice_kernel(
    reps, token_ref, top_ref, ggate_one_ref, gup_one_ref, weight_one_ref, weight_ref, middle_ref, own_top_ref, gains_ref,
    hidden_ref, ggate_ref, gup_ref, grad_ref, low_ref, gain_ref, *scratch,
):
    tokens, tops, ggate_ones, gup_ones, weight_one, hiddens, ggates, gups, in_sems, out_sems, weight_sem = scratch[SCATTER_REFS:]
    meet(near(reps))
    order = scatter_order(reps)
    parts, rows, width = weight_ref.shape
    units = rows // 3
    loads, copies = {}, []
    sources = ((token_ref, tokens), (top_ref, tops), (ggate_one_ref, ggate_ones), (gup_one_ref, gup_ones))

    def load(step):
        loads[step] = []
        for index, (source, target) in enumerate(sources):
            copy = pltpu.make_async_copy(source.at[order[step]], target.at[step % 2], in_sems.at[index, step % 2])
            copy.start()
            loads[step].append(copy)

    load(0)
    weight_copy = pltpu.make_async_copy(weight_one_ref.at[:, pl.ds(0, 2 * units)], weight_one, weight_sem)
    weight_copy.start()
    gain_ref[...] = jnp.zeros_like(gain_ref)

    def partial(step, chip, put):
        slot = step % 2
        for copy in loads[step]:
            copy.wait()
        if step < 3:
            load(step + 1)

        def keep(columns, hidden, ggate, gup):
            hiddens[chip, :, columns] = hidden
            ggates[chip, :, columns] = ggate
            gups[chip, :, columns] = gup

        gated(tokens[slot], tops[slot], weight_ref, keep)
        for index, (source, target) in enumerate(((hiddens, hidden_ref), (ggates, ggate_ref), (gups, gup_ref))):
            copy = pltpu.make_async_copy(source.at[chip], target.at[chip], out_sems.at[index, step])
            copy.start()
            copies.append(copy)
        if step == 0:
            weight_copy.wait()
        for part in range(parts):
            value = dot(ggates[chip], weight_ref[part, :units, :], 1, 1)
            value += dot(gups[chip], weight_ref[part, units : 2 * units, :], 1, 1)
            value += dot(ggate_ones[slot], weight_one[part, :units, :], 1, 1)
            value += dot(gup_ones[slot], weight_one[part, units:, :], 1, 1)
            put(pl.ds(part * width, width), value)

    def finish(piece, rows_of, value):
        back, gain_part = norm_back(value, middle_ref[rows_of, :], gains_ref[1:2, :])
        grad = own_top_ref[rows_of, :].astype(F32) + back
        grad_ref[rows_of, :] = grad
        low_ref[rows_of, :] = grad.astype(BF)
        gain_ref[0:1, :] += gain_part

    run_scatter(reps, partial, finish, scratch[:SCATTER_REFS])
    for copy in copies:
        copy.wait()


def second_slice(normed_all, top_all, ggate_one, gup_one, weight_one, weight, middle, own_top, gains, reps):
    sub = middle.shape[0]
    parts, rows, width = weight.shape
    units = rows // 3
    piece = jax.ShapeDtypeStruct((COLS, 2 * sub, units), BF)
    return pl.pallas_call(
        functools.partial(second_slice_kernel, reps),
        out_shape=[piece] * 3
        + [
            jax.ShapeDtypeStruct((sub, D), F32),
            jax.ShapeDtypeStruct((sub, D), BF),
            jax.ShapeDtypeStruct((8, D), F32),
        ],
        in_specs=[HBM] * 5 + [VMEM] * 4,
        out_specs=[HBM] * 3 + [VMEM] * 3,
        scratch_shapes=scatter_scratch(sub)
        + [pltpu.VMEM((2, 2 * sub, D), BF)] * 2
        + [pltpu.VMEM((2, 2 * sub, units), BF)] * 2
        + [pltpu.VMEM((parts, 2 * units, width), BF)]
        + [pltpu.VMEM((COLS, 2 * sub, units), BF)] * 3
        + [DMA((4, 2)), DMA((3, COLS)), DMA],
        compiler_params=params(5),
        cost_estimate=takes(65),
        name="second_slice",
    )(normed_all, top_all, ggate_one, gup_one, weight_one, weight, middle, own_top, gains)


def slice_grads_kernel(token_ref, top_ref, hidden_ref, ggate_ref, gup_ref, out_ref):
    units = hidden_ref.shape[1]
    tokens, width = hidden_ref.shape[0], token_ref.shape[2]
    features = token_ref[...].reshape(tokens, width)
    out_ref[:units] = dot(features, ggate_ref[...], 0, 0).astype(BF)
    out_ref[units : 2 * units] = dot(features, gup_ref[...], 0, 0).astype(BF)
    out_ref[2 * units :] = dot(hidden_ref[...], top_ref[...].reshape(tokens, width), 0, 0).astype(BF)


def slice_grads(normed_all, top_all, hidden, ggate, gup, rows):
    chips, height, units = hidden.shape
    width = D // rows
    flat = [array.reshape(chips * height, units) for array in (hidden, ggate, gup)]
    block = pl.BlockSpec((chips, height, width), lambda part: (0, 0, part))
    whole = pl.BlockSpec((chips * height, units), lambda part: (0, 0))
    return pl.pallas_call(
        slice_grads_kernel,
        grid=(rows,),
        out_shape=jax.ShapeDtypeStruct((rows, 3 * units, width), BF),
        in_specs=[block, block, whole, whole, whole],
        out_specs=pl.BlockSpec((None, 3 * units, width), lambda part: (part, 0, 0)),
        compiler_params=pltpu.CompilerParams(vmem_limit_bytes=48 * 2**20),
        cost_estimate=takes(20),
        name="slice_grads",
    )(normed_all, top_all, *flat)


def back_out_kernel(
    reps, own_ref, weight_ref, token_ref, top_ref, hidden_ref, ggate_ref, gup_ref, attended_ref, grad_ref, slice_ref,
    held, send_sems, recv_sems, local_sem, grads, out_sems, tokens, tops, slices, in_sems, slice_sems, outs, out_low, tail_sem,
):
    meet(near(reps))
    parts, _, width = weight_ref.shape
    units = hidden_ref.shape[1]
    chips, height = token_ref.shape[:2]
    copies, loads, stores = [], {}, {}

    def load(part):
        loads[part] = []
        columns = pl.ds(part * width, width)
        for index, (source, target) in enumerate(((token_ref, tokens), (top_ref, tops))):
            copy = pltpu.make_async_copy(source.at[:, :, columns], target.at[part % 2], in_sems.at[index, part % 2])
            copy.start()
            loads[part].append(copy)

    load(0)

    def slice_grads(part):
        slot = part % 2
        for copy in loads[part]:
            copy.wait()
        if part < parts - 1:
            load(part + 1)
        if part >= 2:
            stores[part - 2].wait()
        features = tokens[slot].reshape(chips * height, width)
        slices[slot, :units] = dot(features, ggate_ref[...], 0, 0).astype(BF)
        slices[slot, units : 2 * units] = dot(features, gup_ref[...], 0, 0).astype(BF)
        slices[slot, 2 * units :] = dot(hidden_ref[...], tops[slot].reshape(chips * height, width), 0, 0).astype(BF)
        stores[part] = pltpu.make_async_copy(
            slices.at[slot], slice_ref.at[part, pl.ds(0, 3 * units)], slice_sems.at[slot]
        )
        stores[part].start()

    def use(step, chip):
        def out(source, target, index):
            copy = pltpu.make_async_copy(source.at[chip], target.at[chip], out_sems.at[index, step])
            copy.start()
            copies.append(copy)

        for part in range(parts):
            columns = pl.ds(part * width, width)
            value = dot(attended_ref[chip], held[chip, :, columns], 0, 0)
            outs[:, columns] = value if step == 0 else outs[:, columns] + value
        total = dot(held[chip, :, :width], weight_ref[0], 1, 1)
        for part in range(1, parts):
            total += dot(held[chip, :, part * width : (part + 1) * width], weight_ref[part], 1, 1)
        grads[chip] = total.astype(BF)
        out(grads, grad_ref, 0)
        slice_grads(step)

    run_gather(reps, own_ref, held, (send_sems, recv_sems, local_sem), use)
    for part in range(parts):
        out_low[part] = outs[:, part * width : (part + 1) * width].astype(BF)
    tail = pltpu.make_async_copy(out_low, slice_ref.at[:, pl.ds(3 * units, outs.shape[0])], tail_sem)
    tail.start()
    for copy in copies + [stores[parts - 2], stores[parts - 1], tail]:
        copy.wait()


def back_out(grad_own, weight, normed_all, top_all, hidden, ggate, gup, attended, reps):
    sub = grad_own.shape[0]
    parts, heads, width = weight.shape
    chips, height, units = hidden.shape
    flat = [array.reshape(chips * height, units) for array in (hidden, ggate, gup)]
    return pl.pallas_call(
        functools.partial(back_out_kernel, reps),
        out_shape=[
            jax.ShapeDtypeStruct((COLS, 2 * sub, heads), BF),
            jax.ShapeDtypeStruct((parts, 3 * units + heads, width), BF),
        ],
        in_specs=[VMEM] * 2 + [HBM] * 2 + [VMEM] * 4,
        out_specs=[HBM] * 2,
        scratch_shapes=gather_scratch(sub)
        + [pltpu.VMEM((COLS, 2 * sub, heads), BF), DMA((1, COLS))]
        + [pltpu.VMEM((2, chips, height, width), BF)] * 2
        + [pltpu.VMEM((2, 3 * units, width), BF), DMA((2, 2)), DMA((2,))]
        + [pltpu.VMEM((heads, D), F32), pltpu.VMEM((parts, heads, width), BF), DMA],
        compiler_params=params(6),
        cost_estimate=takes(50),
        name="back_out",
    )(grad_own, weight, normed_all, top_all, *flat, attended)


def lift_kernel(
    reps, hidden_one_ref, hidden_two_ref, weight_one_ref, weight_two_ref, middle_ref,
    dquery_ref, dpair_ref, cosine_ref, sine_ref, result_ref, proj_ref, *scratch,
):
    weight_one, weight_two, weight_sems, low, taken, push_send, push_recv = scratch[SCATTER_REFS:]
    parts, units, width = weight_one.shape
    row, rows = lax.axis_index("row"), lax.axis_size("row")
    loads = []
    for index, (source, target) in enumerate(((weight_one_ref, weight_one), (weight_two_ref, weight_two))):
        copy = pltpu.make_async_copy(source.at[:, pl.ds(2 * units, units)], target, weight_sems.at[index])
        copy.start()
        loads.append(copy)
    partners = row_partners()
    meet(near(reps) + [{"row": partner} for partner in partners])
    low[...] = dpair_ref[:, 0].astype(BF)
    push = pltpu.make_async_remote_copy(
        src_ref=low,
        dst_ref=taken,
        send_sem=push_send,
        recv_sem=push_recv,
        device_id={"row": lax.rem(row + rows - 1, rows)},
        device_id_type=MESH,
    )

    @pl.when(row > 0)
    def _():
        push.start()

    for copy in loads:
        copy.wait()

    def partial(step, chip, put):
        for part in range(parts):
            value = dot(hidden_one_ref[chip], weight_one[part], 1, 0)
            put(pl.ds(part * width, width), value + dot(hidden_two_ref[chip], weight_two[part], 1, 0))

    def finish(piece, rows_of, value):
        put_by_row(result_ref, piece, middle_ref[rows_of, :] + value)

    def turn_back():
        @pl.when(row == rows - 1)
        def _():
            taken[...] = jnp.zeros_like(taken)

        @pl.when(row < rows - 1)
        def _():
            push.wait_recv()

        chips, height, _ = proj_ref.shape
        for chip in range(chips):
            places = pl.ds(chip * height, height)
            pair_rows = pl.ds(chip % 2 * height, height)
            pair = dpair_ref[chip // 2, 1, pair_rows, :] + taken[chip // 2, pair_rows, :].astype(F32)
            grad = jnp.concatenate([dquery_ref[places, :], pair], axis=1)
            proj_ref[chip] = rotate(grad, cosine_ref[places, :], -sine_ref[places, :]).astype(BF)

    run_scatter(reps, partial, finish, scratch[:SCATTER_REFS], turn_back)

    @pl.when(row > 0)
    def _():
        push.wait_send()


def lift(hidden_one, hidden_two, weight_one, weight_two, middle, dquery, dpairs, cosine, sine, reps):
    sub = middle.shape[0]
    parts, rows, width = weight_one.shape
    tokens, heads = dquery.shape
    halves, _, slots, lanes = dpairs.shape
    return pl.pallas_call(
        functools.partial(lift_kernel, reps),
        out_shape=[
            jax.ShapeDtypeStruct((sub * parts, width), BF),
            jax.ShapeDtypeStruct((COLS, tokens // COLS, heads + lanes), BF),
        ],
        in_specs=[VMEM] * 2 + [HBM] * 2 + [VMEM] * 5,
        out_specs=[VMEM] * 2,
        scratch_shapes=scatter_scratch(sub)
        + [pltpu.VMEM((parts, rows // 3, width), BF)] * 2
        + [DMA((2,))]
        + [pltpu.VMEM((halves, slots, lanes), BF)] * 2
        + [DMA, DMA],
        compiler_params=params(7),
        cost_estimate=takes(50),
        name="lift",
    )(hidden_one, hidden_two, weight_one, weight_two, middle, dquery, dpairs, cosine, sine)


PEERS = ("SO", "P", "SP", "Q", "SQ", "D", "SD")


def project_back_kernel(
    reps, proj_ref, weight_ref, source_ref, middle_ref, gains_ref, gain_two_ref, resid_ref, gain_ref, *scratch
):
    gain_own, gain_rows, gain_plane, row_send, row_recv, plane_send, plane_recv = scratch[SCATTER_REFS:]
    where = plane(reps)
    row = lax.axis_index("row")
    partners = row_partners()
    meet([where[kind][2] for kind in PEERS] + [{"row": partner} for partner in partners])
    gain_own[...] = jnp.zeros_like(gain_own)
    gain_own[1:2, :] = gain_two_ref[0:1, :]

    def partial(step, chip, put):
        for index in range(D // SPAN):
            columns = pl.ds(index * SPAN, SPAN)
            put(columns, dot(proj_ref[chip], weight_ref[columns, :], 1, 1))

    def finish(piece, rows, value):
        back, gain_part = norm_back(value, source_ref[rows, :].astype(F32), gains_ref[0:1, :])
        put_by_row(resid_ref, piece, middle_ref[rows, :] + back)
        gain_own[0:1, :] += gain_part

    run_scatter(reps, partial, finish, scratch[:SCATTER_REFS])
    width = gain_ref.shape[1]
    copies = []
    for shift, partner in enumerate(partners):
        copy = pltpu.make_async_remote_copy(
            src_ref=gain_own.at[:, tile(partner, width)],
            dst_ref=gain_rows.at[shift],
            send_sem=row_send.at[shift],
            recv_sem=row_recv.at[shift],
            device_id={"row": partner},
            device_id_type=MESH,
        )
        copy.start()
        copies.append(copy)
    for copy in copies:
        copy.wait()
    total = gain_own[:, tile(row, width)]
    for shift in range(len(partners)):
        total += gain_rows[shift]
    own = where["O"][0] * 2 + where["O"][1]
    gain_plane[own] = total

    def share(index, place):
        return pltpu.make_async_remote_copy(
            src_ref=gain_plane.at[place],
            dst_ref=gain_plane.at[place],
            send_sem=plane_send.at[index],
            recv_sem=plane_recv.at[place],
            device_id=where[PEERS[index]][2],
            device_id_type=MESH,
        )

    for index in range(len(PEERS)):
        share(index, own).start()
    for index, kind in enumerate(PEERS):
        share(index, where[kind][0] * 2 + where[kind][1]).wait_recv()
    total = gain_plane[0]
    for place in range(1, 2 * COLS):
        total += gain_plane[place]
    gain_ref[...] = total
    for index in range(len(PEERS)):
        share(index, own).wait_send()


def project_back(grad_proj, weight, source, grad_middle, gains, gain_two, reps, rows):
    sub = source.shape[0]
    width = D // rows
    return pl.pallas_call(
        functools.partial(project_back_kernel, reps),
        out_shape=[
            jax.ShapeDtypeStruct((sub * rows, width), BF),
            jax.ShapeDtypeStruct((8, width), F32),
        ],
        in_specs=[VMEM] * 6,
        out_specs=[VMEM] * 2,
        scratch_shapes=scatter_scratch(sub)
        + [
            pltpu.VMEM((8, D), F32),
            pltpu.VMEM((rows - 1, 8, width), F32),
            pltpu.VMEM((2 * COLS, 8, width), F32),
            DMA((rows - 1,)),
            DMA((rows - 1,)),
            DMA((len(PEERS),)),
            DMA((2 * COLS,)),
        ],
        compiler_params=params(8),
        cost_estimate=takes(55),
        name="project_back",
    )(grad_proj, weight, source, grad_middle, gains, gain_two)


def adamw(weights, gradient, moment, square, step_rate, decay_rate):
    gradient = gradient.astype(F32)
    moment_new = BETA_ONE * moment + (1.0 - BETA_ONE) * gradient
    square_new = BETA_TWO * square + (1.0 - BETA_TWO) * gradient * gradient
    moment_hat = moment_new / (1.0 - BETA_ONE**STEP)
    square_hat = square_new / (1.0 - BETA_TWO**STEP)
    weights_new = weights - step_rate * (
        moment_hat / (jnp.sqrt(square_hat) + ADAM_EPS) + decay_rate * weights
    )
    return (weights_new, moment_new, square_new)


def local(
    resid_in,
    cotangent,
    seq_lens,
    qkv_weight,
    qkv_moment,
    qkv_square,
    out_weight,
    out_moment,
    out_square,
    gate_weight,
    gate_moment,
    gate_square,
    up_weight,
    up_moment,
    up_square,
    down_weight,
    down_moment,
    down_square,
    norm_gains,
    gain_moment,
    gain_square,
):
    cols, rows, replicas = lax.axis_size("col"), lax.axis_size("row"), lax.axis_size("dp")
    reps = replicas // 2
    half = lax.axis_index("dp") // reps
    row, col = lax.axis_index("row"), lax.axis_index("col")
    chunk = resid_in.shape[0]
    sub = chunk // cols
    blocks = 2 * cols
    plane_tokens = sub * blocks
    head_width = (GROUP + 2) * HD

    qkv_block = half_columns(qkv_weight, reps)
    out_block = tall_block(out_weight, reps)
    split = out_block.shape[1] // 2
    stacked = jnp.concatenate([out_block[:, :split], out_block[:, split:]], axis=0)
    first_w = lax.all_gather(jnp.concatenate([qkv_block, stacked], axis=1), "row", axis=0)
    qkv_w = first_w[:, :, :head_width].reshape(D, head_width)
    heads = out_block.shape[0]
    out_w = jnp.concatenate([first_w[:, :heads, head_width:], first_w[:, heads:, head_width:]], axis=2)
    lengths = both_halves(seq_lens, partner_swap(seq_lens, reps), half, 0)
    ends = jnp.cumsum(lengths, axis=1, dtype=jnp.int32)
    slot = (row * chunk + jnp.arange(chunk, dtype=jnp.int32)).reshape(1, chunk)
    passed = (slot[:, :, None] >= ends[:, None, :]).astype(jnp.int32)
    seq_start = jnp.sum(passed * lengths[:, None, :], axis=2, dtype=jnp.int32)
    usable = slot < ends[:, -1:]
    cosine, sine = rope_tables((slot - seq_start).reshape(plane_tokens))
    low = (jnp.where(usable, seq_start, slot) - (row - 1) * chunk).reshape(blocks, 1, sub)
    firsts = jnp.tile(chunk + jnp.arange(cols, dtype=jnp.int32) * sub, 2)
    bounds = jnp.stack([low[:, 0, 0] // KEYS, (firsts + sub - 1) // KEYS + 1, firsts]).astype(jnp.int32)
    usable_mine = (row * chunk + col * sub + jnp.arange(sub, dtype=jnp.int32)) < jnp.sum(seq_lens)

    padded = jnp.concatenate([norm_gains, jnp.zeros((6, norm_gains.shape[1]), F32)])
    source, normed_own, grad_top, gains = exchange(
        resid_in, cotangent, padded, usable_mine.astype(F32)[:, None], rows
    )
    gate_block = half_columns(gate_weight, reps, source)
    up_block = half_columns(up_weight, reps, source)
    down_block = tall_block(down_weight, reps)
    units = gate_block.shape[1] // SLICES
    slice_w = []
    for index in range(SLICES):
        span = slice(index * units, (index + 1) * units)
        block = jnp.concatenate([gate_block[:, span], up_block[:, span], down_block[span]], axis=0)
        slice_w.append(lax.all_gather(block, "row", axis=0))
    normed_one, grad_top_all, queries, pairs = project(normed_own, grad_top, qkv_w, cosine, sine, reps)
    queries = queries.reshape(plane_tokens, GROUP * HD)
    pairs = pairs.reshape(2, 2 * chunk, 2 * HD)
    attended, log_total = attend(queries, pairs, low, bounds)
    middle, normed_own = mix_out(attended.reshape(cols, 2 * sub, GROUP * HD), out_w, source, gains, reps)

    normed_two, hidden_one, ggate_one, gup_one = first_slice(normed_own, grad_top_all, slice_w[0], reps)
    grads_one = slice_grads(normed_two, grad_top_all, hidden_one, ggate_one, gup_one, rows)
    normed_two, grads_one = lax.optimization_barrier((normed_two, grads_one))
    hidden_two, ggate_two, gup_two, grad_middle, grad_middle_own, gain_grad_two = second_slice(
        normed_two, grad_top_all, ggate_one, gup_one, slice_w[0], slice_w[1], middle, grad_top, gains, reps
    )
    grad_attended, grads_two = back_out(
        grad_middle_own, out_w, normed_two, grad_top_all, hidden_two, ggate_two, gup_two,
        attended.reshape(cols, 2 * sub, GROUP * HD), reps,
    )
    slice_g = [lax.psum_scatter(part, "row", scatter_dimension=0) for part in (grads_one, grads_two)]
    grad_attended, slice_g[0] = lax.optimization_barrier((grad_attended, slice_g[0]))
    grad_query, grad_pairs = attend_back(
        queries, grad_attended.reshape(plane_tokens, GROUP * HD), pairs, low, log_total, bounds
    )
    result, grad_proj = lift(
        hidden_one, hidden_two, slice_w[0], slice_w[1], middle,
        grad_query, grad_pairs.reshape(2, 2, chunk, 2 * HD), cosine, sine, reps,
    )
    grad_qkv = dot(normed_one.reshape(plane_tokens, D), grad_proj.reshape(plane_tokens, head_width), 0, 0).astype(BF)
    grad_proj, grad_qkv = lax.optimization_barrier((grad_proj, grad_qkv))
    resid_grad, gain_grads = project_back(
        grad_proj, qkv_w, source, grad_middle, gains, gain_grad_two, reps, rows
    )
    result, resid_grad = lax.optimization_barrier((to_rows(result), resid_grad))
    resid_grad = to_rows(resid_grad)
    grad_qkv = lax.psum_scatter(grad_qkv, "row", scatter_dimension=0, tiled=True)
    wide = 2 * (D // rows)
    slice_g[1], gain_grads = lax.optimization_barrier((slice_g[1], gain_grads))
    halves = [own_slice(part[:wide], reps) for part in slice_g]
    grad_qkv, halves, slice_g[0] = lax.optimization_barrier((grad_qkv, halves, slice_g[0]))
    grad_qkv = own_rows(grad_qkv, reps)
    outputs = jnp.concatenate([result.reshape(cols, sub, -1), resid_grad.reshape(cols, sub, -1)], axis=1)
    outputs = to_columns(outputs)
    result = outputs[:, :sub].reshape(chunk, -1)
    resid_grad = outputs[:, sub:].reshape(chunk, -1).astype(F32)
    pieces = [halves[index][place] for place in range(2) for index in range(SLICES)]
    grad_gate, grad_up = [jnp.concatenate([piece[index] for piece in pieces], axis=1) for index in range(2)]
    grad_down = own_tall(jnp.concatenate([part[wide : wide + units] for part in slice_g], axis=0), reps)
    grad_out = own_tall(slice_g[1][wide + units :], reps)

    gain_grads = gain_grads[:2]
    if reps > 1:
        gain_grads = lax.psum(gain_grads, "dp", axis_index_groups=rep_groups(reps))
    qkv_set = adamw(qkv_weight, grad_qkv, qkv_moment, qkv_square, RATE_MATRIX, WEIGHT_DECAY)
    out_set = adamw(out_weight, grad_out, out_moment, out_square, RATE_OUTPUT, WEIGHT_DECAY)
    gate_set = adamw(gate_weight, grad_gate, gate_moment, gate_square, RATE_MATRIX, WEIGHT_DECAY)
    up_set = adamw(up_weight, grad_up, up_moment, up_square, RATE_MATRIX, WEIGHT_DECAY)
    down_set = adamw(down_weight, grad_down, down_moment, down_square, RATE_MATRIX, WEIGHT_DECAY)
    gain_set = adamw(norm_gains, gain_grads, gain_moment, gain_square, RATE_GAIN, 0.0)
    return (result, resid_grad, *qkv_set, *out_set, *gate_set, *up_set, *down_set, *gain_set)


def solution(mesh):
    tokens = P(("dp", "col"), "row")
    wide = P(("row", "dp"), "col")
    tall = P(("col", "dp"), "row")
    gain = P(None, "row")
    weights = (wide,) * 3 + (tall,) * 3 + (wide,) * 6 + (tall,) * 3 + (gain,) * 3
    return jax.shard_map(
        local,
        mesh=mesh,
        in_specs=(tokens, tokens, P("dp", None)) + weights,
        out_specs=(tokens, tokens) + weights,
        check_vma=False,
    )
```
